32 devices in a mesh: facet: 4 (over y, x), bl: 4 (over z), chan: 2 (over core).
Axes of the slice: x: 2, y: 2, z: 4, core: 2. Of those that a mesh axis runs over, the one named last changes fastest.
Arguments:
- visibilities: bfloat16 [128, 8, 2, 128], P(('facet', 'bl'), 'chan'), may hold values from -6 to 6
- coords: bfloat16 [128, 2, 128], P(('facet', 'bl')), may hold values from 4 to 124
- plane_index: int32 [128], P(('facet', 'bl')), may hold values from 0 to 15, as said below
- block_group: int32 [128, 1], P(('facet', 'bl')), may hold values from 0 to 3, as said below
- offsets: int32 [4, 4, 2], replicated, may hold values from 0 to 7
- facet_centre: float32 [4, 2], replicated, may hold values from -8 to 8
- tables: bfloat16 [16, 2, 128, 2, 128], P(('facet', 'bl')), may hold values from -0.5 to 0.5
- antenna_gain: float32 [4, 2, 128], P('bl'), may hold values from 0.1 to 1.9
Outputs:
- subgrids: float32 [4, 4, 128, 2, 128], P('facet', 'bl', 'chan')
The draws below stay inside these ranges and needn't reach their ends.
Inputs may be any that keep to these rules, and one draw needn't show every extreme that they name: `block_group`: among the 8 blocks of one device at most 4 name the same baseline group, and on every device some group is named by exactly 4 of them. `plane_index`: A block whose baseline group is g names a w-plane p with p modulo 4 equal to g or to (g + 3) modulo 4.
All inputs are finite; a program needn't handle non-finite values.
Results may differ from the reference program's by a relative error of at most 0.0054.
Values may be sent and summed in bfloat16 or wider, within the bound.
No kernel may reach another device: no remote copies, remote signals or barrier semaphores. Data moves between devices by JAX's collectives and lax.ppermute only.
A program may use at most 64 MiB of HBM per device.

```python
import math
import jax
import jax.numpy as jnp
from jax import lax

SU = 128
BLK = 128
CH = 8
NB_DEV = 8
CAP = 4
FACETS = 4
GROUPS = 4
NB = 128
P_SIZE = 16


def group_rows(key):
    folded = jax.random.fold_in(key, 101)
    second_key = jax.random.fold_in(folded, 1)
    third_key = jax.random.fold_in(folded, 2)
    device_count = NB // NB_DEV
    slot_count = GROUPS * CAP
    chosen = (jnp.arange(device_count, dtype=jnp.int32) % GROUPS)[:, None]
    slot_ids = jnp.arange(slot_count, dtype=jnp.int32)
    jitter = jax.random.randint(second_key, (device_count, slot_count), 0, 1024)
    scores = jitter * slot_count + slot_ids[None, :] + jnp.where(slot_ids[None, :] // CAP == chosen, 0, 1024 * slot_count)
    ranked = jnp.argsort(scores, axis=1)
    picked = (ranked[:, :NB_DEV] // CAP).astype(jnp.int32)
    mixing = jax.random.randint(third_key, (device_count, NB_DEV), 0, 1024) * NB_DEV + jnp.arange(NB_DEV, dtype=jnp.int32)[None, :]
    shuffle = jnp.argsort(mixing, axis=1)
    result_rows = jnp.take_along_axis(picked, shuffle, axis=1)
    return result_rows.reshape(NB).astype(jnp.int32)


def draw_block_group(key, part):
    return group_rows(key)[:, None]


def draw_plane_index(key, part):
    group_ids = group_rows(key)
    folded = jax.random.fold_in(key, 202)
    first_key, second_key, third_key = jax.random.split(folded, 3)
    draw_a = jax.random.randint(first_key, (NB,), 0, FACETS)
    draw_b = jax.random.randint(second_key, (NB,), 0, 2 * FACETS)
    depth_level = jnp.minimum(draw_a, draw_b)
    advance = jax.random.randint(third_key, (NB,), 0, 2)
    normal_plane = depth_level * GROUPS + (group_ids + GROUPS - advance) % GROUPS
    device_count = NB // NB_DEV
    device_ids = jnp.arange(NB, dtype=jnp.int32) // NB_DEV
    own = (group_ids == device_ids % GROUPS).astype(jnp.int32).reshape(device_count, NB_DEV)
    first_own = ((jnp.cumsum(own, axis=1) == 1) & (own == 1)).reshape(NB)
    special = (device_ids + device_count - 1) % device_count
    return jnp.where(first_own, special, normal_plane).astype(jnp.int32)


def plant(result, stream_key, low, largest):
    longest = result.shape.index(max(result.shape))
    spots = []
    for shift in (0, 1):
        where = [jax.random.randint(jax.random.fold_in(stream_key, axis), (), 0, length) for axis, length in enumerate(result.shape)]
        where[longest] = (where[longest] + shift) % result.shape[longest]
        spots.append(tuple(where))
    return result.at[spots[0]].set(low).at[spots[1]].set(largest)


def block_levels(stream_key, dims, shards, least, top_value):
    loudness = 1.0
    for axis_at, parts in shards:
        draws = jax.random.uniform(jax.random.fold_in(jax.random.fold_in(stream_key, 6), axis_at), (parts,), jnp.float32, least / len(shards), top_value / len(shards))
        loudness = loudness * jnp.repeat(jnp.exp(draws), dims[axis_at] // parts).reshape((-1,) + (1,) * (len(dims) - 1 - axis_at))
    return loudness


def centred(own_key, extent, deviation, reach, shards=(), kind=jnp.bfloat16):
    values = deviation * jax.random.normal(own_key, extent, jnp.float32)
    if shards:
        values = values * block_levels(own_key, extent, shards, -0.22, 0.18)
    return jnp.clip(values, -reach, reach).astype(kind)


def setup_inputs(seed: int = 0) -> dict:
    arg_keys = jax.random.split(jax.random.key(seed), 9)
    return {
        "visibilities": centred(arg_keys[0], (NB, CH, 2, BLK), 1.0, 6.0, ((0, 16), (1, 2))),
        "coords": jnp.clip(4.0 + 120.0 * jax.random.uniform(arg_keys[1], (NB, 2, BLK), jnp.float32) ** block_levels(arg_keys[1], (NB, 2, BLK), ((0, 16),), -0.2, 0.2), 4.0, 124.0).astype(jnp.bfloat16),
        "plane_index": draw_plane_index(jax.random.fold_in(arg_keys[8], 71), 0),
        "block_group": draw_block_group(jax.random.fold_in(arg_keys[8], 71), 0),
        "offsets": plant(jax.random.randint(arg_keys[4], (FACETS, GROUPS, 2), 0, 8), jax.random.fold_in(arg_keys[4], 1), 0, 7).astype(jnp.int32),
        "facet_centre": jnp.clip(jax.random.uniform(arg_keys[5], (FACETS, 2), jnp.float32, -8.0, 8.0), -8.0, 8.0),
        "tables": centred(arg_keys[6], (P_SIZE, 2, SU, 2, SU), SU ** -0.5, 0.5, ((0, 16),)),
        "antenna_gain": jnp.clip(1.0 + 0.18 * jax.random.normal(arg_keys[7], (GROUPS, 2, SU), jnp.float32), 0.1, 1.9),
    }


kernel_spread = 1.5

def channel_scale(count, first):
    index = (first + jnp.arange(count, dtype=jnp.int32)).astype(jnp.float32)
    return 1.0 + 0.01 * (index - 0.5 * (CH - 1))

def grid_block(samples, place, kernel, shift, centre, scale):
    cells = jnp.arange(SU, dtype=jnp.int32).astype(jnp.float32)
    along_u = place[0].astype(jnp.float32)
    along_v = place[1].astype(jnp.float32)

    def profile(position, offset):
        spot = scale[:, None] * position[None, :] - offset
        apart = spot[:, :, None] - cells
        return jnp.exp(-apart * apart / (2.0 * kernel_spread * kernel_spread)).astype(jnp.bfloat16).reshape(CH * BLK, SU)
    spread_u = jnp.dot(profile(along_u, shift[0]), kernel[0].reshape(SU, 2 * SU), preferred_element_type=jnp.float32)
    spread_v = jnp.dot(profile(along_v, shift[1]), kernel[1].reshape(SU, 2 * SU), preferred_element_type=jnp.float32).astype(jnp.bfloat16)
    phase = 2.0 * math.pi / SU * (scale[:, None] * (along_u * centre[0] + along_v * centre[1])[None, :])
    phase = phase.reshape(CH * BLK, 1)
    real_part = samples[:, 0].astype(jnp.float32).reshape(CH * BLK, 1)
    imag_part = samples[:, 1].astype(jnp.float32).reshape(CH * BLK, 1)
    cosine = jnp.cos(phase)
    sine = jnp.sin(phase)
    turned_real = real_part * cosine - imag_part * sine
    turned_imag = real_part * sine + imag_part * cosine
    weighted_real = spread_u[:, :SU] * turned_real - spread_u[:, SU:] * turned_imag
    weighted_imag = spread_u[:, :SU] * turned_imag + spread_u[:, SU:] * turned_real
    weighted = jnp.concatenate([weighted_real, weighted_imag], axis=1).astype(jnp.bfloat16)
    product = jnp.dot(weighted.T, spread_v, preferred_element_type=jnp.float32)
    grid_real = product[:SU, :SU] - product[SU:, SU:]
    grid_imag = product[:SU, SU:] + product[SU:, :SU]
    return jnp.stack([grid_real, grid_imag], axis=1)

def reference(visibilities, coords, plane_index, block_group, offsets, facet_centre, tables, antenna_gain):
    scale = channel_scale(CH, 0)
    owners = block_group[:, 0]

    def one_facet(facet):
        shifts = offsets[facet].astype(jnp.float32)
        centre = facet_centre[facet]

        def step(carry, block):
            owner = owners[block]
            kernel = tables[plane_index[block]]
            part = grid_block(visibilities[block], coords[block], kernel, shifts[owner], centre, scale)
            return (carry.at[owner].add(part), None)
        start = jnp.zeros((GROUPS, SU, 2, SU), jnp.float32)
        total, _ = lax.scan(step, start, jnp.arange(NB, dtype=jnp.int32))
        return total
    raw = lax.map(one_facet, jnp.arange(FACETS, dtype=jnp.int32))
    norm = SU / math.sqrt(BLK * NB_DEV * FACETS * CH)
    gains = antenna_gain[:, 0][:, :, None, None] * antenna_gain[:, 1][:, None, None, :]
    return raw * gains[None] * norm
```

```python
import functools
import math

import jax
import jax.numpy as jnp
from jax import lax
from jax.experimental import pallas as pl
from jax.experimental.pallas import tpu as pltpu
from jax.sharding import PartitionSpec as P

SU = 128
CH = 8
KERNEL_SPREAD = 1.5
ALPHA = math.sqrt(math.log2(math.e) / (2.0 * KERNEL_SPREAD * KERNEL_SPREAD))
UNROLL = 2
NT = (((1,), (1,)), ((), ()))


def cos_sin(turns):
    quarter = jnp.floor(4.0 * turns + 0.5)
    angle = (2.0 * math.pi) * (turns - 0.25 * quarter)
    sq = angle * angle
    sine = angle * (
        1.0 + sq * (-1.0 / 6 + sq * (1.0 / 120 + sq * (-1.0 / 5040 + sq * (1.0 / 362880))))
    )
    cosine = 1.0 + sq * (
        -0.5 + sq * (1.0 / 24 + sq * (-1.0 / 720 + sq * (1.0 / 40320 + sq * (-1.0 / 3628800))))
    )
    turn = quarter.astype(jnp.int32) & 3
    odd = (turn & 1) == 1
    cos_out = jnp.where(odd, sine, cosine)
    sin_out = jnp.where(odd, cosine, sine)
    cos_out = jnp.where((turn == 1) | (turn == 2), -cos_out, cos_out)
    sin_out = jnp.where(turn >= 2, -sin_out, sin_out)
    return cos_out, sin_out


def split_bf16(x):
    high = x.astype(jnp.bfloat16)
    low = (x - high.astype(jnp.float32)).astype(jnp.bfloat16)
    return high, low


def grid_kernel(sizes, norm, packed_ref, offsets_ref, centre_ref, gain_ref, *refs):
    facets, groups, held, chans, rows = sizes
    slots = 2 * facets
    table_refs = refs[:slots]
    mine_ref, other_ref = refs[slots : slots + 2]
    flat, meta_v, meta_s, order, grids, stacked, table_f, total, sem = refs[slots + 2 :]
    devices = facets * groups
    facet = lax.axis_index("facet")
    group = lax.axis_index("bl")
    chan = lax.axis_index("chan")
    place_row = held * chans * 2
    meta_row = place_row + 2 * held

    def widen(d, carry):
        at = pl.multiple_of(d * rows, rows)
        flat[pl.ds(at, rows), :] = packed_ref[pl.ds(at, rows), :].astype(jnp.float32)
        return carry

    lax.fori_loop(0, devices, widen, 0)
    meta_v[...] = flat[pl.ds(meta_row, devices, stride=rows), :].astype(jnp.int32)
    copy = pltpu.make_async_copy(meta_v, meta_s, sem)
    copy.start()
    grids[...] = jnp.zeros_like(grids)
    copy.wait()

    def pick(d, count):
        for i in range(held):
            plane = meta_s[d, i]
            of_group = meta_s[d, held + i]
            set_id = jnp.where(lax.rem(plane, groups) == group, 0, 1)
            shift = lax.rem(facet - lax.div(plane, groups) + facets, facets)
            order[count] = (d * held + i) * slots + set_id * facets + shift
            count = count + jnp.where(of_group == group, 1, 0)
        return count

    count = lax.fori_loop(0, devices, pick, 0)
    for i in range(UNROLL):
        order[count + i] = 0

    offset_u = offsets_ref[facet, group, 0].astype(jnp.float32)
    offset_v = offsets_ref[facet, group, 1].astype(jnp.float32)
    along_l = centre_ref[facet, 0]
    along_m = centre_ref[facet, 1]
    channel = (chan * chans + lax.broadcasted_iota(jnp.int32, (chans, SU), 0)).astype(jnp.float32)
    scale = 1.0 + 0.01 * (channel - 0.5 * (CH - 1))
    cells = ALPHA * lax.broadcasted_iota(jnp.int32, (SU, SU), 0).astype(jnp.float32)

    def profile(spot):
        apart = spot - cells
        return jnp.exp2(-(apart * apart)).astype(jnp.bfloat16)

    def tiled(row):
        return jnp.broadcast_to(row, (16, SU)).astype(jnp.bfloat16)[None]

    def one_block(at):
        code = order[at]
        block = lax.div(code, slots)
        slot = lax.rem(code, slots)
        d = lax.div(block, held)
        i = lax.rem(block, held)
        keep = jnp.where(at < count, 1.0, 0.0)
        base = pl.multiple_of(d * rows + i * 2 * chans, 2 * chans)
        real = flat[pl.ds(base, chans, stride=2), :] * keep
        imag = flat[pl.ds(base + 1, chans, stride=2), :] * keep
        at_place = d * rows + place_row + 2 * i
        along_u = flat[pl.ds(at_place, 1), :]
        along_v = flat[pl.ds(at_place + 1, 1), :]
        spot_u = ALPHA * (scale * along_u - offset_u)
        spot_v = ALPHA * (scale * along_v - offset_v)
        turns = (1.0 / SU) * (scale * (along_u * along_l + along_v * along_m))
        cosine, sine = cos_sin(turns)
        turned_real = real * cosine - imag * sine
        turned_imag = real * sine + imag * cosine
        lefts_real, lefts_imag, rights = [], [], []
        for c in range(chans):
            left = profile(spot_u[c : c + 1]).reshape(SU // 16, 16, SU)
            lefts_real.append((left * tiled(turned_real[c : c + 1])).reshape(SU, SU))
            lefts_imag.append((left * tiled(turned_imag[c : c + 1])).reshape(SU, SU))
            rights.append(profile(spot_v[c : c + 1]))
        left = jnp.concatenate(
            [jnp.concatenate(lefts_real, axis=1), jnp.concatenate(lefts_imag, axis=1)], axis=0
        )
        right = jnp.concatenate(rights, axis=1)
        grids[slot] += lax.dot_general(left, right, NT, preferred_element_type=jnp.float32)

    def step(k, carry):
        for i in range(UNROLL):
            one_block(k * UNROLL + i)
        return carry

    lax.fori_loop(0, lax.div(count + UNROLL - 1, UNROLL), step, 0)

    result = jnp.zeros((SU, 2 * SU), jnp.float32)
    for s in range(slots):
        table_f[...] = table_refs[s][0].astype(jnp.float32)
        u_real = table_f[pl.ds(0, SU, stride=2), :]
        u_imag = table_f[pl.ds(1, SU, stride=2), :]
        u_side = jnp.concatenate([u_real.T, u_imag.T], axis=1).astype(jnp.bfloat16)
        grid_real = grids[s, :SU, :]
        grid_imag = grids[s, SU:, :]
        inner = jnp.concatenate(
            [
                jnp.concatenate([grid_real, grid_imag], axis=1),
                jnp.concatenate([-grid_imag, grid_real], axis=1),
            ],
            axis=0,
        )
        high, low = split_bf16(inner)
        half = jnp.dot(u_side, high, preferred_element_type=jnp.float32) + jnp.dot(
            u_side, low, preferred_element_type=jnp.float32
        )
        table_f[...] = table_refs[s][1].astype(jnp.float32)
        v_real = table_f[pl.ds(0, SU, stride=2), :]
        v_imag = table_f[pl.ds(1, SU, stride=2), :]
        v_side = jnp.concatenate(
            [
                jnp.concatenate([v_real, v_imag], axis=1),
                jnp.concatenate([-v_imag, v_real], axis=1),
            ],
            axis=0,
        ).astype(jnp.bfloat16)
        high, low = split_bf16(half)
        result = (
            result
            + jnp.dot(high, v_side, preferred_element_type=jnp.float32)
            + jnp.dot(low, v_side, preferred_element_type=jnp.float32)
        )
    gain_u = jnp.broadcast_to(gain_ref[0, 0:1, :], (SU, SU)).T
    gains = gain_u * gain_ref[0, 1:2, :] * norm
    total[...] = result * jnp.concatenate([gains, gains], axis=1)
    half_rows = mine_ref.shape[0]
    mine_ref[...] = total[pl.ds(pl.multiple_of(chan * half_rows, half_rows), half_rows), :]
    other_ref[...] = total[pl.ds(pl.multiple_of((1 - chan) * half_rows, half_rows), half_rows), :]


def body(
    visibilities, coords, plane_index, block_group, offsets, facet_centre, tables, antenna_gain
):
    facets = lax.axis_size("facet")
    groups = lax.axis_size("bl")
    chan_count = lax.axis_size("chan")
    held, chans = visibilities.shape[:2]
    devices = facets * groups
    norm = SU / math.sqrt(visibilities.shape[3] * held * facets * CH)

    own_table = tables.reshape(2, 2 * SU, SU)
    slot_tables = []
    for set_id in range(2):
        for shift in range(facets):
            if set_id == 0 and shift == 0:
                slot_tables.append(own_table)
                continue
            perm = [
                (f * groups + g, (f + shift) % facets * groups + (g + set_id) % groups)
                for f in range(facets)
                for g in range(groups)
            ]
            slot_tables.append(lax.ppermute(own_table, ("facet", "bl"), perm))

    numbers = jnp.concatenate([plane_index, block_group[:, 0]]).astype(jnp.bfloat16)
    numbers = jnp.pad(numbers[None, :], ((0, 15), (0, SU - 2 * held)))
    packed = jnp.concatenate(
        [
            visibilities.reshape(held * chans * 2, SU),
            coords.reshape(held * 2, SU),
            numbers,
        ],
        axis=0,
    )
    rows = packed.shape[0]
    gathered = lax.all_gather(packed, ("facet", "bl"), axis=0, tiled=True)

    slots = 2 * facets
    half_rows = SU // chan_count
    vmem = pl.BlockSpec(memory_space=pltpu.VMEM)
    smem = pl.BlockSpec(memory_space=pltpu.SMEM)
    mine, other = pl.pallas_call(
        functools.partial(grid_kernel, (facets, groups, held, chans, rows), norm),
        out_shape=[jax.ShapeDtypeStruct((half_rows, 2 * SU), jnp.float32)] * 2,
        in_specs=[vmem, smem, smem, vmem] + [vmem] * slots,
        out_specs=[vmem, vmem],
        scratch_shapes=[
            pltpu.VMEM((devices * rows, SU), jnp.float32),
            pltpu.VMEM((devices, SU), jnp.int32),
            pltpu.SMEM((devices, SU), jnp.int32),
            pltpu.SMEM((devices * held + UNROLL,), jnp.int32),
            pltpu.VMEM((slots, 2 * SU, SU), jnp.float32),
            pltpu.VMEM((2 * SU, 2 * SU), jnp.float32),
            pltpu.VMEM((2 * SU, SU), jnp.float32),
            pltpu.VMEM((SU, 2 * SU), jnp.float32),
            pltpu.SemaphoreType.DMA,
        ],
        compiler_params=pltpu.CompilerParams(vmem_limit_bytes=40 * 1024 * 1024),
        cost_estimate=pl.CostEstimate(
            flops=4_000_000_000, bytes_accessed=2_000_000, transcendentals=4_000_000
        ),
        name="grid",
    )(gathered, offsets, facet_centre, antenna_gain, *slot_tables)
    arrived = lax.ppermute(other, "chan", [(c, 1 - c) for c in range(chan_count)])
    return (mine + arrived).reshape(1, 1, half_rows, 2, SU)


def solution(mesh):
    in_specs = (
        P(("facet", "bl"), "chan", None, None),
        P(("facet", "bl"), None, None),
        P(("facet", "bl")),
        P(("facet", "bl"), None),
        P(),
        P(),
        P(("facet", "bl"), None, None, None, None),
        P("bl", None, None),
    )
    out_specs = P("facet", "bl", "chan", None, None)
    return jax.shard_map(body, mesh=mesh, in_specs=in_specs, out_specs=out_specs, check_vma=False)
```

```python
import functools
import math

import jax
import jax.numpy as jnp
from jax import lax
from jax.experimental import pallas as pl
from jax.experimental.pallas import tpu as pltpu
from jax.sharding import PartitionSpec as P

SU = 128
CH = 8
KERNEL_SPREAD = 1.5
ALPHA = math.sqrt(math.log2(math.e) / (2.0 * KERNEL_SPREAD * KERNEL_SPREAD))
UNROLL = 2
NT = (((1,), (1,)), ((), ()))
VMEM = pl.BlockSpec(memory_space=pltpu.VMEM)
SMEM = pl.BlockSpec(memory_space=pltpu.SMEM)
PARAMS = pltpu.CompilerParams(vmem_limit_bytes=32 * 1024 * 1024)


def cos_sin(turns):
    quarter = jnp.floor(4.0 * turns + 0.5)
    angle = (2.0 * math.pi) * (turns - 0.25 * quarter)
    sq = angle * angle
    sine = angle * (
        1.0 + sq * (-1.0 / 6 + sq * (1.0 / 120 + sq * (-1.0 / 5040 + sq * (1.0 / 362880))))
    )
    cosine = 1.0 + sq * (
        -0.5 + sq * (1.0 / 24 + sq * (-1.0 / 720 + sq * (1.0 / 40320 + sq * (-1.0 / 3628800))))
    )
    turn = quarter.astype(jnp.int32) & 3
    odd = (turn & 1) == 1
    cos_out = jnp.where(odd, sine, cosine)
    sin_out = jnp.where(odd, cosine, sine)
    cos_out = jnp.where((turn == 1) | (turn == 2), -cos_out, cos_out)
    sin_out = jnp.where(turn >= 2, -sin_out, sin_out)
    return cos_out, sin_out


def split_bf16(x):
    high = x.astype(jnp.bfloat16)
    low = (x - high.astype(jnp.float32)).astype(jnp.bfloat16)
    return high, low


def sort_kernel(sizes, plane_ref, group_ref, samples_ref, place_ref, out_ref, samples, place, sorted_, filled):
    facets, groups, held, chans, cap, rows = sizes
    per = 2 * chans
    samples[...] = samples_ref[...].astype(jnp.float32)
    place[...] = place_ref[...].astype(jnp.float32)
    sorted_[...] = jnp.zeros_like(sorted_)
    for g in range(groups):
        filled[g] = 0
    lane = lax.broadcasted_iota(jnp.int32, (1, SU), 1)
    for i in range(held):
        g = group_ref[0, i]
        k = filled[g]
        filled[g] = k + 1
        sorted_[g, pl.ds(pl.multiple_of(k * per, per), per), :] = samples[i * per : (i + 1) * per, :]
        sorted_[g, pl.ds(cap * per + 2 * k, 2), :] = place[2 * i : 2 * i + 2, :]
        sorted_[g, cap * (per + 2) : cap * (per + 2) + 1, :] += jnp.where(
            lane == k, (plane_ref[0, i] + 1).astype(jnp.float32), 0.0
        )
    for g in range(groups):
        mine = sorted_[g].astype(jnp.bfloat16)
        for f in range(facets):
            out_ref[f * groups + g] = mine


def grid_kernel(sizes, packed_ref, offsets_ref, centre_ref, grids, flat, meta_v, meta_s, order, sem):
    facets, groups, chans, cap, rows = sizes
    per = 2 * chans
    devices = facets * groups
    slots = 2 * facets
    facet = lax.axis_index("facet")
    group = lax.axis_index("bl")
    chan = lax.axis_index("chan")

    def widen(d, carry):
        flat[pl.ds(pl.multiple_of(d * rows, rows), rows), :] = packed_ref[d].astype(jnp.float32)
        return carry

    lax.fori_loop(0, devices, widen, 0)
    meta_v[...] = flat[pl.ds(cap * (per + 2), devices, stride=rows), :].astype(jnp.int32)
    copy = pltpu.make_async_copy(meta_v, meta_s, sem)
    copy.start()
    grids[...] = jnp.zeros_like(grids)
    copy.wait()

    def pick(d, count):
        for k in range(cap):
            plane = meta_s[d, k] - 1
            set_id = jnp.where(lax.rem(plane, groups) == group, 0, 1)
            order[count] = (d * cap + k) * slots + 2 * lax.div(plane, groups) + set_id
            count = count + jnp.where(plane >= 0, 1, 0)
        return count

    count = lax.fori_loop(0, devices, pick, 0)
    for i in range(UNROLL):
        order[count + i] = 0

    offset_u = offsets_ref[facet, 0, group].astype(jnp.float32)
    offset_v = offsets_ref[facet, 1, group].astype(jnp.float32)
    along_l = centre_ref[0, facet]
    along_m = centre_ref[1, facet]
    channel = (chan * chans + lax.broadcasted_iota(jnp.int32, (chans, SU), 0)).astype(jnp.float32)
    scale = 1.0 + 0.01 * (channel - 0.5 * (CH - 1))
    cells = ALPHA * lax.broadcasted_iota(jnp.int32, (SU, SU), 0).astype(jnp.float32)

    def profile(spot):
        apart = spot - cells
        return jnp.exp2(-(apart * apart)).astype(jnp.bfloat16)

    def tiled(row):
        return jnp.broadcast_to(row, (16, SU)).astype(jnp.bfloat16)[None]

    def one_block(at):
        code = order[at]
        block = lax.div(code, slots)
        slot = lax.rem(code, slots)
        d = lax.div(block, cap)
        k = lax.rem(block, cap)
        keep = jnp.where(at < count, 1.0, 0.0)
        base = pl.multiple_of(d * rows + k * per, per)
        real = flat[pl.ds(base, chans, stride=2), :] * keep
        imag = flat[pl.ds(base + 1, chans, stride=2), :] * keep
        at_place = d * rows + cap * per + 2 * k
        along_u = flat[pl.ds(at_place, 1), :]
        along_v = flat[pl.ds(at_place + 1, 1), :]
        spot_u = ALPHA * (scale * along_u - offset_u)
        spot_v = ALPHA * (scale * along_v - offset_v)
        turns = (1.0 / SU) * (scale * (along_u * along_l + along_v * along_m))
        cosine, sine = cos_sin(turns)
        turned_real = real * cosine - imag * sine
        turned_imag = real * sine + imag * cosine
        lefts_real, lefts_imag, rights = [], [], []
        for c in range(chans):
            left = profile(spot_u[c : c + 1]).reshape(SU // 16, 16, SU)
            lefts_real.append((left * tiled(turned_real[c : c + 1])).reshape(SU, SU))
            lefts_imag.append((left * tiled(turned_imag[c : c + 1])).reshape(SU, SU))
            rights.append(profile(spot_v[c : c + 1]))
        left = jnp.concatenate(
            [jnp.concatenate(lefts_real, axis=1), jnp.concatenate(lefts_imag, axis=1)], axis=0
        )
        right = jnp.concatenate(rights, axis=1)
        grids[slot] += lax.dot_general(left, right, NT, preferred_element_type=jnp.float32)

    def step(k, carry):
        for i in range(UNROLL):
            one_block(k * UNROLL + i)
        return carry

    lax.fori_loop(0, lax.div(count + UNROLL - 1, UNROLL), step, 0)


def table_kernel(slots, norm, grids, tables, gain_ref, mine_ref, other_ref, table_f, total):
    chan = lax.axis_index("chan")
    result = jnp.zeros((SU, 2 * SU), jnp.float32)
    for s in range(slots):
        table_f[...] = tables[s, 0].astype(jnp.float32)
        u_real = table_f[pl.ds(0, SU, stride=2), :]
        u_imag = table_f[pl.ds(1, SU, stride=2), :]
        u_side = jnp.concatenate([u_real.T, u_imag.T], axis=1).astype(jnp.bfloat16)
        grid_real = grids[s, :SU, :]
        grid_imag = grids[s, SU:, :]
        inner = jnp.concatenate(
            [
                jnp.concatenate([grid_real, grid_imag], axis=1),
                jnp.concatenate([-grid_imag, grid_real], axis=1),
            ],
            axis=0,
        )
        high, low = split_bf16(inner)
        half = jnp.dot(u_side, high, preferred_element_type=jnp.float32) + jnp.dot(
            u_side, low, preferred_element_type=jnp.float32
        )
        table_f[...] = tables[s, 1].astype(jnp.float32)
        v_real = table_f[pl.ds(0, SU, stride=2), :]
        v_imag = table_f[pl.ds(1, SU, stride=2), :]
        v_side = jnp.concatenate(
            [
                jnp.concatenate([v_real, v_imag], axis=1),
                jnp.concatenate([-v_imag, v_real], axis=1),
            ],
            axis=0,
        ).astype(jnp.bfloat16)
        high, low = split_bf16(half)
        result = (
            result
            + jnp.dot(high, v_side, preferred_element_type=jnp.float32)
            + jnp.dot(low, v_side, preferred_element_type=jnp.float32)
        )
    gain_u = jnp.broadcast_to(gain_ref[0, 0:1, :], (SU, SU)).T
    gains = gain_u * gain_ref[0, 1:2, :] * norm
    total[...] = result * jnp.concatenate([gains, gains], axis=1)
    half_rows = mine_ref.shape[0]
    mine_ref[...] = total[pl.ds(pl.multiple_of(chan * half_rows, half_rows), half_rows), :]
    other_ref[...] = total[pl.ds(pl.multiple_of((1 - chan) * half_rows, half_rows), half_rows), :]


def body(
    visibilities, coords, plane_index, block_group, offsets, facet_centre, tables, antenna_gain
):
    facets = lax.axis_size("facet")
    groups = lax.axis_size("bl")
    chan_count = lax.axis_size("chan")
    held, chans = visibilities.shape[:2]
    devices = facets * groups
    slots = 2 * facets
    cap = max(2, 2 * held // groups)
    per = 2 * chans
    rows = -(-(cap * (per + 2) + 1) // 16) * 16
    half_rows = SU // chan_count
    norm = SU / math.sqrt(visibilities.shape[3] * held * facets * CH)

    packed = pl.pallas_call(
        functools.partial(sort_kernel, (facets, groups, held, chans, cap, rows)),
        out_shape=jax.ShapeDtypeStruct((devices, rows, SU), jnp.bfloat16),
        in_specs=[SMEM, SMEM, VMEM, VMEM],
        out_specs=VMEM,
        scratch_shapes=[
            pltpu.VMEM((held * per, SU), jnp.float32),
            pltpu.VMEM((held * 2, SU), jnp.float32),
            pltpu.VMEM((groups, rows, SU), jnp.float32),
            pltpu.SMEM((groups,), jnp.int32),
        ],
        compiler_params=PARAMS,
        cost_estimate=pl.CostEstimate(flops=100_000, bytes_accessed=300_000, transcendentals=0),
        name="sort_blocks",
    )(
        plane_index.reshape(1, held),
        block_group.T,
        visibilities.reshape(held * per, SU),
        coords.reshape(held * 2, SU),
    )
    gathered = lax.all_to_all(packed, ("facet", "bl"), split_axis=0, concat_axis=0, tiled=True)

    own_table = tables.reshape(1, 2, 2 * SU, SU)
    perm = [(g, (g + 1) % groups) for g in range(groups)]
    both = jnp.concatenate([own_table, lax.ppermute(own_table, "bl", perm)], axis=0)
    spread = jnp.broadcast_to(both[None], (facets,) + both.shape)
    slot_tables = lax.all_to_all(spread, "facet", split_axis=0, concat_axis=0, tiled=True)

    grids = pl.pallas_call(
        functools.partial(grid_kernel, (facets, groups, chans, cap, rows)),
        out_shape=jax.ShapeDtypeStruct((slots, 2 * SU, SU), jnp.float32),
        in_specs=[VMEM, SMEM, SMEM],
        out_specs=VMEM,
        scratch_shapes=[
            pltpu.VMEM((devices * rows, SU), jnp.float32),
            pltpu.VMEM((devices, SU), jnp.int32),
            pltpu.SMEM((devices, SU), jnp.int32),
            pltpu.SMEM((devices * cap + UNROLL,), jnp.int32),
            pltpu.SemaphoreType.DMA,
        ],
        compiler_params=PARAMS,
        cost_estimate=pl.CostEstimate(
            flops=4_000_000_000, bytes_accessed=2_000_000, transcendentals=4_000_000
        ),
        name="grid",
    )(gathered, offsets.transpose(0, 2, 1), facet_centre.T)
    mine, other = pl.pallas_call(
        functools.partial(table_kernel, slots, norm),
        out_shape=[jax.ShapeDtypeStruct((half_rows, 2 * SU), jnp.float32)] * 2,
        in_specs=[VMEM, VMEM, VMEM],
        out_specs=[VMEM, VMEM],
        scratch_shapes=[
            pltpu.VMEM((2 * SU, SU), jnp.float32),
            pltpu.VMEM((SU, 2 * SU), jnp.float32),
        ],
        compiler_params=PARAMS,
        cost_estimate=pl.CostEstimate(
            flops=1_000_000_000, bytes_accessed=2_000_000, transcendentals=0
        ),
        name="apply_tables",
    )(grids, slot_tables.reshape(slots, 2, 2 * SU, SU), antenna_gain)
    arrived = lax.ppermute(other, "chan", [(c, 1 - c) for c in range(chan_count)])
    return (mine + arrived).reshape(1, 1, half_rows, 2, SU)


def solution(mesh):
    in_specs = (
        P(("facet", "bl"), "chan", None, None),
        P(("facet", "bl"), None, None),
        P(("facet", "bl")),
        P(("facet", "bl"), None),
        P(),
        P(),
        P(("facet", "bl"), None, None, None, None),
        P("bl", None, None),
    )
    out_specs = P("facet", "bl", "chan", None, None)
    return jax.shard_map(body, mesh=mesh, in_specs=in_specs, out_specs=out_specs, check_vma=False)
```

```python
import functools
import math

import jax
import jax.numpy as jnp
from jax import lax
from jax.experimental import pallas as pl
from jax.experimental.pallas import tpu as pltpu
from jax.sharding import PartitionSpec as P

SU = 128
CH = 8
KERNEL_SPREAD = 1.5
ALPHA = math.sqrt(math.log2(math.e) / (2.0 * KERNEL_SPREAD * KERNEL_SPREAD))
UNROLL = 4
NT = (((1,), (1,)), ((), ()))
VMEM = pl.BlockSpec(memory_space=pltpu.VMEM)
SMEM = pl.BlockSpec(memory_space=pltpu.SMEM)
HBM = pl.BlockSpec(memory_space=pltpu.HBM)
PARAMS = pltpu.CompilerParams(vmem_limit_bytes=32 * 1024 * 1024)
ALONE = pltpu.CompilerParams(vmem_limit_bytes=60 * 1024 * 1024)


def cos_sin(turns):
    quarter = jnp.floor(4.0 * turns + 0.5)
    angle = (2.0 * math.pi) * (turns - 0.25 * quarter)
    sq = angle * angle
    sine = angle * (
        1.0 + sq * (-1.0 / 6 + sq * (1.0 / 120 + sq * (-1.0 / 5040 + sq * (1.0 / 362880))))
    )
    cosine = 1.0 + sq * (
        -0.5 + sq * (1.0 / 24 + sq * (-1.0 / 720 + sq * (1.0 / 40320 + sq * (-1.0 / 3628800))))
    )
    turn = quarter.astype(jnp.int32) & 3
    odd = (turn & 1) == 1
    cos_out = jnp.where(odd, sine, cosine)
    sin_out = jnp.where(odd, cosine, sine)
    cos_out = jnp.where((turn == 1) | (turn == 2), -cos_out, cos_out)
    sin_out = jnp.where(turn >= 2, -sin_out, sin_out)
    return cos_out, sin_out


def split_bf16(x):
    high = x.astype(jnp.bfloat16)
    low = (x - high.astype(jnp.float32)).astype(jnp.bfloat16)
    return high, low


def sort_kernel(sizes, plane_hbm, group_hbm, samples_hbm, place_hbm, out_ref, *scratch):
    groups, held, chans, cap, rows = sizes
    plane_ref, group_ref, samples_b, place_b, samples, place, sorted_, filled, sems = scratch
    sources = (plane_hbm, group_hbm, samples_hbm, place_hbm)
    targets = (plane_ref, group_ref, samples_b, place_b)
    copies = [
        pltpu.make_async_copy(source, target, sems.at[n])
        for n, (source, target) in enumerate(zip(sources, targets))
    ]
    for copy in copies:
        copy.start()
    sorted_[...] = jnp.zeros_like(sorted_)
    for g in range(groups):
        filled[g] = 0
    for copy in copies:
        copy.wait()
    samples[...] = samples_b[...].astype(jnp.float32)
    place[...] = place_b[...].astype(jnp.float32)
    lane = lax.broadcasted_iota(jnp.int32, (1, SU), 1)
    for i in range(held):
        g = group_ref[0, i]
        k = filled[g]
        filled[g] = k + 1
        for part in range(2):
            at = part * cap * chans + k * chans
            sorted_[g, pl.ds(at, chans), :] = samples[pl.ds(2 * chans * i + part, chans, stride=2), :]
            at = 2 * cap * chans + part * cap + k
            sorted_[g, pl.ds(at, 1), :] = place[2 * i + part : 2 * i + part + 1, :]
        meta = 2 * cap * (chans + 1)
        sorted_[g, meta : meta + 1, :] += jnp.where(
            lane == k, (plane_ref[0, i] + 1).astype(jnp.float32), 0.0
        )
    out_ref[...] = sorted_[...].astype(jnp.bfloat16)


def grid_kernel(sizes, offsets_ref, centre_ref, *refs):
    facets, groups, chans, cap, rows = sizes
    packed_refs = refs[:facets]
    grids = refs[facets]
    meta_v, meta_s, order, spots_u, spots_v, turns_real, turns_imag, sem = refs[facets + 1 :]
    devices = facets * groups
    slots = 2 * facets
    lines = cap * chans
    facet = lax.axis_index("facet")
    group = lax.axis_index("bl")
    chan = lax.axis_index("chan")

    for f in range(facets):
        for g in range(groups):
            meta = packed_refs[f][g, rows - 16 : rows, :].astype(jnp.float32)
            at = 2 * (lines + cap) - (rows - 16)
            meta_v[f * groups + g : f * groups + g + 1, :] = meta[at : at + 1].astype(jnp.int32)
    copy = pltpu.make_async_copy(meta_v, meta_s, sem)
    copy.start()
    grids[...] = jnp.zeros_like(grids)

    offset_u = offsets_ref[facet, 0, group].astype(jnp.float32)
    offset_v = offsets_ref[facet, 1, group].astype(jnp.float32)
    along_l = centre_ref[0, facet]
    along_m = centre_ref[1, facet]
    line = lax.broadcasted_iota(jnp.int32, (lines, SU), 0)
    channel = (chan * chans + lax.rem(line, chans)).astype(jnp.float32)
    scale = 1.0 + 0.01 * (channel - 0.5 * (CH - 1))

    def spread_lines(place):
        return jnp.concatenate(
            [jnp.broadcast_to(place[k : k + 1], (chans, SU)) for k in range(cap)], axis=0
        )

    for f in range(facets):
        for g in range(groups):
            at = (f * groups + g) * lines
            wide = packed_refs[f][g].astype(jnp.float32)
            real = wide[:lines]
            imag = wide[lines : 2 * lines]
            along_u = spread_lines(wide[2 * lines : 2 * lines + cap])
            along_v = spread_lines(wide[2 * lines + cap : 2 * (lines + cap)])
            cosine, sine = cos_sin(
                (1.0 / SU) * (scale * (along_u * along_l + along_v * along_m))
            )
            spots_u[at : at + lines, :] = ALPHA * (scale * along_u - offset_u)
            spots_v[at : at + lines, :] = ALPHA * (scale * along_v - offset_v)
            turns_real[at : at + lines, :] = real * cosine - imag * sine
            turns_imag[at : at + lines, :] = real * sine + imag * cosine
    last = devices * lines
    for ref in (spots_u, spots_v, turns_real, turns_imag):
        ref[last : last + 8, :] = jnp.zeros((8, SU), jnp.float32)
    copy.wait()

    def pick(d, count):
        for k in range(cap):
            plane = meta_s[d, k] - 1
            set_id = jnp.where(lax.rem(plane, groups) == group, 0, 1)
            order[count] = (d * cap + k) * slots + 2 * lax.div(plane, groups) + set_id
            count = count + jnp.where(plane >= 0, 1, 0)
        return count

    count = lax.fori_loop(0, devices, pick, 0)
    for i in range(UNROLL):
        order[count + i] = devices * cap * slots

    cells = ALPHA * lax.broadcasted_iota(jnp.int32, (SU, SU), 0).astype(jnp.float32)

    def profile(spot):
        apart = spot - cells
        return jnp.exp2(-(apart * apart)).astype(jnp.bfloat16)

    def tiled(row):
        return jnp.broadcast_to(row, (16, SU)).astype(jnp.bfloat16)[None]

    def one_block(at):
        code = order[at]
        slot = lax.rem(code, slots)
        base = lax.div(code, slots) * chans
        lefts_real, lefts_imag, rights = [], [], []
        for c in range(chans):
            here = pl.ds(base + c, 1)
            left = profile(spots_u[here, :]).reshape(SU // 16, 16, SU)
            lefts_real.append((left * tiled(turns_real[here, :])).reshape(SU, SU))
            lefts_imag.append((left * tiled(turns_imag[here, :])).reshape(SU, SU))
            rights.append(profile(spots_v[here, :]))
        left = jnp.concatenate(
            [jnp.concatenate(lefts_real, axis=1), jnp.concatenate(lefts_imag, axis=1)], axis=0
        )
        right = jnp.concatenate(rights, axis=1)
        return slot, lax.dot_general(left, right, NT, preferred_element_type=jnp.float32)

    def step(k, carry):
        for slot, part in [one_block(k * UNROLL + i) for i in range(UNROLL)]:
            grids[slot] += part
        return carry

    lax.fori_loop(0, lax.div(count + UNROLL - 1, UNROLL), step, 0)


def table_kernel(slots, norm, grids, tables, gain_ref, mine_ref, other_ref, table_f, total):
    chan = lax.axis_index("chan")
    result = jnp.zeros((SU, 2 * SU), jnp.float32)
    for s in range(slots):
        table_f[...] = tables[s, 0].astype(jnp.float32)
        u_real = table_f[pl.ds(0, SU, stride=2), :]
        u_imag = table_f[pl.ds(1, SU, stride=2), :]
        u_side = jnp.concatenate([u_real.T, u_imag.T], axis=1).astype(jnp.bfloat16)
        grid_real = grids[s, :SU, :]
        grid_imag = grids[s, SU:, :]
        inner = jnp.concatenate(
            [
                jnp.concatenate([grid_real, grid_imag], axis=1),
                jnp.concatenate([-grid_imag, grid_real], axis=1),
            ],
            axis=0,
        )
        high, low = split_bf16(inner)
        half = jnp.dot(u_side, high, preferred_element_type=jnp.float32) + jnp.dot(
            u_side, low, preferred_element_type=jnp.float32
        )
        table_f[...] = tables[s, 1].astype(jnp.float32)
        v_real = table_f[pl.ds(0, SU, stride=2), :]
        v_imag = table_f[pl.ds(1, SU, stride=2), :]
        v_side = jnp.concatenate(
            [
                jnp.concatenate([v_real, v_imag], axis=1),
                jnp.concatenate([-v_imag, v_real], axis=1),
            ],
            axis=0,
        ).astype(jnp.bfloat16)
        high, low = split_bf16(half)
        result = (
            result
            + jnp.dot(high, v_side, preferred_element_type=jnp.float32)
            + jnp.dot(low, v_side, preferred_element_type=jnp.float32)
        )
    gain_u = jnp.broadcast_to(gain_ref[0, 0:1, :], (SU, SU)).T
    gains = gain_u * gain_ref[0, 1:2, :] * norm
    total[...] = result * jnp.concatenate([gains, gains], axis=1)
    half_rows = mine_ref.shape[0]
    mine_ref[...] = total[pl.ds(pl.multiple_of(chan * half_rows, half_rows), half_rows), :]
    other_ref[...] = total[pl.ds(pl.multiple_of((1 - chan) * half_rows, half_rows), half_rows), :]


def body(
    visibilities, coords, plane_index, block_group, offsets, facet_centre, tables, antenna_gain
):
    facets = lax.axis_size("facet")
    groups = lax.axis_size("bl")
    chan_count = lax.axis_size("chan")
    held, chans = visibilities.shape[:2]
    devices = facets * groups
    slots = 2 * facets
    cap = max(2, 2 * held // groups)
    rows = -(-(2 * cap * (chans + 1) + 1) // 16) * 16
    half_rows = SU // chan_count
    norm = SU / math.sqrt(visibilities.shape[3] * held * facets * CH)

    packed = pl.pallas_call(
        functools.partial(sort_kernel, (groups, held, chans, cap, rows)),
        out_shape=jax.ShapeDtypeStruct((groups, rows, SU), jnp.bfloat16),
        in_specs=[HBM] * 4,
        out_specs=VMEM,
        scratch_shapes=[
            pltpu.SMEM((1, held), jnp.int32),
            pltpu.SMEM((1, held), jnp.int32),
            pltpu.VMEM((held * 2 * chans, SU), jnp.bfloat16),
            pltpu.VMEM((held * 2, SU), jnp.bfloat16),
            pltpu.VMEM((held * 2 * chans, SU), jnp.float32),
            pltpu.VMEM((held * 2, SU), jnp.float32),
            pltpu.VMEM((groups, rows, SU), jnp.float32),
            pltpu.SMEM((groups,), jnp.int32),
            pltpu.SemaphoreType.DMA((4,)),
        ],
        compiler_params=ALONE,
        cost_estimate=pl.CostEstimate(flops=100_000, bytes_accessed=100_000, transcendentals=0),
        name="sort_blocks",
    )(
        plane_index.reshape(1, held),
        block_group.T,
        visibilities.reshape(held * 2 * chans, SU),
        coords.reshape(held * 2, SU),
    )
    here = lax.all_to_all(packed, "bl", split_axis=0, concat_axis=0, tiled=True)
    blocks = [here] + [
        lax.ppermute(here, "facet", [(f, (f + shift) % facets) for f in range(facets)])
        for shift in range(1, facets)
    ]

    own_table = tables.reshape(1, 2, 2 * SU, SU)
    perm = [(g, (g + 1) % groups) for g in range(groups)]
    both = jnp.concatenate([own_table, lax.ppermute(own_table, "bl", perm)], axis=0)
    spread = jnp.broadcast_to(both[None], (facets,) + both.shape)
    slot_tables = lax.all_to_all(spread, "facet", split_axis=0, concat_axis=0, tiled=True)

    grids = pl.pallas_call(
        functools.partial(grid_kernel, (facets, groups, chans, cap, rows)),
        out_shape=jax.ShapeDtypeStruct((slots, 2 * SU, SU), jnp.float32),
        in_specs=[SMEM, SMEM] + [VMEM] * facets,
        out_specs=VMEM,
        scratch_shapes=[
            pltpu.VMEM((devices, SU), jnp.int32),
            pltpu.SMEM((devices, SU), jnp.int32),
            pltpu.SMEM((devices * cap + UNROLL,), jnp.int32),
        ]
        + [pltpu.VMEM((devices * cap * chans + 8, SU), jnp.float32)] * 4
        + [pltpu.SemaphoreType.DMA],
        compiler_params=PARAMS,
        cost_estimate=pl.CostEstimate(
            flops=4_000_000_000, bytes_accessed=2_000_000, transcendentals=4_000_000
        ),
        name="grid",
    )(offsets.transpose(0, 2, 1), facet_centre.T, *blocks)
    mine, other = pl.pallas_call(
        functools.partial(table_kernel, slots, norm),
        out_shape=[jax.ShapeDtypeStruct((half_rows, 2 * SU), jnp.float32)] * 2,
        in_specs=[VMEM, VMEM, VMEM],
        out_specs=[VMEM, VMEM],
        scratch_shapes=[
            pltpu.VMEM((2 * SU, SU), jnp.float32),
            pltpu.VMEM((SU, 2 * SU), jnp.float32),
        ],
        compiler_params=PARAMS,
        cost_estimate=pl.CostEstimate(
            flops=1_000_000_000, bytes_accessed=2_000_000, transcendentals=0
        ),
        name="apply_tables",
    )(grids, slot_tables.reshape(slots, 2, 2 * SU, SU), antenna_gain)
    arrived = lax.ppermute(other, "chan", [(c, 1 - c) for c in range(chan_count)])
    return (mine + arrived).reshape(1, 1, half_rows, 2, SU)


def solution(mesh):
    in_specs = (
        P(("facet", "bl"), "chan", None, None),
        P(("facet", "bl"), None, None),
        P(("facet", "bl")),
        P(("facet", "bl"), None),
        P(),
        P(),
        P(("facet", "bl"), None, None, None, None),
        P("bl", None, None),
    )
    out_specs = P("facet", "bl", "chan", None, None)
    return jax.shard_map(body, mesh=mesh, in_specs=in_specs, out_specs=out_specs, check_vma=False)
```

```python
import functools
import math

import jax
import jax.numpy as jnp
from jax import lax
from jax.experimental import pallas as pl
from jax.experimental.pallas import tpu as pltpu
from jax.sharding import PartitionSpec as P

SU = 128
CH = 8
KERNEL_SPREAD = 1.5
ALPHA = math.sqrt(math.log2(math.e) / (2.0 * KERNEL_SPREAD * KERNEL_SPREAD))
UNROLL = 4
NT = (((1,), (1,)), ((), ()))
VMEM = pl.BlockSpec(memory_space=pltpu.VMEM)
HBM = pl.BlockSpec(memory_space=pltpu.HBM)
PARAMS = pltpu.CompilerParams(vmem_limit_bytes=32 * 1024 * 1024)
ALONE = pltpu.CompilerParams(vmem_limit_bytes=60 * 1024 * 1024)


def cos_sin(turns):
    quarter = jnp.floor(4.0 * turns + 0.5)
    angle = (2.0 * math.pi) * (turns - 0.25 * quarter)
    sq = angle * angle
    sine = angle * (
        1.0 + sq * (-1.0 / 6 + sq * (1.0 / 120 + sq * (-1.0 / 5040 + sq * (1.0 / 362880))))
    )
    cosine = 1.0 + sq * (
        -0.5 + sq * (1.0 / 24 + sq * (-1.0 / 720 + sq * (1.0 / 40320 + sq * (-1.0 / 3628800))))
    )
    turn = quarter.astype(jnp.int32) & 3
    odd = (turn & 1) == 1
    cos_out = jnp.where(odd, sine, cosine)
    sin_out = jnp.where(odd, cosine, sine)
    cos_out = jnp.where((turn == 1) | (turn == 2), -cos_out, cos_out)
    sin_out = jnp.where(turn >= 2, -sin_out, sin_out)
    return cos_out, sin_out


def split_bf16(x):
    high = x.astype(jnp.bfloat16)
    low = (x - high.astype(jnp.float32)).astype(jnp.bfloat16)
    return high, low


def three_parts(x):
    parts = []
    for _ in range(3):
        part = x.astype(jnp.bfloat16)
        x = x - part.astype(jnp.float32)
        parts.append(part.astype(jnp.float32))
    return parts


def sort_kernel(sizes, *refs):
    groups, held, chans, cap, rows = sizes
    out_ref = refs[7]
    plane_ref, group_ref, samples_b, place_b, offsets_ref, centre_ref, gain_ref = refs[8:15]
    samples, place, sorted_, filled, sems = refs[15:]
    facet = lax.axis_index("facet")
    copies = [
        pltpu.make_async_copy(source, target, sems.at[n])
        for n, (source, target) in enumerate(zip(refs[:7], refs[8:15]))
    ]
    for copy in copies:
        copy.start()
    sorted_[...] = jnp.zeros_like(sorted_)
    for g in range(groups):
        filled[g] = 0
    for copy in copies:
        copy.wait()
    samples[...] = samples_b[...].astype(jnp.float32)
    place[...] = place_b[...].astype(jnp.float32)
    lane = lax.broadcasted_iota(jnp.int32, (1, SU), 1)
    meta = 2 * cap * (chans + 1)
    centre = [
        part
        for axis in range(2)
        for part in three_parts(jnp.full((1, SU), centre_ref[axis, facet], jnp.float32))
    ]
    gains = three_parts(gain_ref[0])
    for g in range(groups):
        numbers = jnp.zeros((1, SU), jnp.float32)
        for axis in range(2):
            offset = offsets_ref[facet, axis, g].astype(jnp.float32)
            numbers = jnp.where(lane == axis, offset, numbers)
        for n, part in enumerate(centre):
            numbers = jnp.where(lane == 2 + n, part, numbers)
        sorted_[g, meta + 1 : meta + 2, :] = numbers
        for n, part in enumerate(gains):
            sorted_[g, meta + 2 + 2 * n : meta + 4 + 2 * n, :] = part
    for i in range(held):
        g = group_ref[0, i]
        k = filled[g]
        filled[g] = k + 1
        for part in range(2):
            at = part * cap * chans + k * chans
            sorted_[g, pl.ds(at, chans), :] = samples[pl.ds(2 * chans * i + part, chans, stride=2), :]
            at = 2 * cap * chans + part * cap + k
            sorted_[g, pl.ds(at, 1), :] = place[2 * i + part : 2 * i + part + 1, :]
        sorted_[g, meta : meta + 1, :] += jnp.where(
            lane == k, (plane_ref[0, i] + 1).astype(jnp.float32), 0.0
        )
    out_ref[...] = sorted_[...].astype(jnp.bfloat16)


def grid_kernel(sizes, *refs):
    facets, groups, chans, cap, rows = sizes
    packed_refs = refs[:facets]
    grids = refs[facets]
    meta_v, meta_s, order, spots_u, spots_v, turns_real, turns_imag, sem = refs[facets + 1 :]
    devices = facets * groups
    slots = 2 * facets
    lines = cap * chans
    meta_row = 2 * (lines + cap)
    tail = meta_row // 16 * 16
    group = lax.axis_index("bl")
    chan = lax.axis_index("chan")

    for f in range(facets):
        for g in range(groups):
            meta = packed_refs[f][g, tail : tail + 16, :].astype(jnp.float32)
            meta_v[f * groups + g : f * groups + g + 1, :] = meta[
                meta_row - tail : meta_row - tail + 1
            ].astype(jnp.int32)
            if f == 0 and g == 0:
                numbers = meta[meta_row - tail + 1 : meta_row - tail + 2]
    copy = pltpu.make_async_copy(meta_v, meta_s, sem)
    copy.start()
    grids[...] = jnp.zeros_like(grids)

    def number(n):
        return jnp.broadcast_to(numbers[:, n : n + 1], (lines, SU))

    offset_u = number(0)
    offset_v = number(1)
    along_l = number(2) + number(3) + number(4)
    along_m = number(5) + number(6) + number(7)
    line = lax.broadcasted_iota(jnp.int32, (lines, SU), 0)
    channel = (chan * chans + lax.rem(line, chans)).astype(jnp.float32)
    scale = 1.0 + 0.01 * (channel - 0.5 * (CH - 1))

    def spread_lines(place):
        return jnp.concatenate(
            [jnp.broadcast_to(place[k : k + 1], (chans, SU)) for k in range(cap)], axis=0
        )

    for f in range(facets):
        for g in range(groups):
            at = (f * groups + g) * lines
            wide = packed_refs[f][g].astype(jnp.float32)
            real = wide[:lines]
            imag = wide[lines : 2 * lines]
            along_u = spread_lines(wide[2 * lines : 2 * lines + cap])
            along_v = spread_lines(wide[2 * lines + cap : 2 * (lines + cap)])
            cosine, sine = cos_sin(
                (1.0 / SU) * (scale * (along_u * along_l + along_v * along_m))
            )
            spots_u[at : at + lines, :] = ALPHA * (scale * along_u - offset_u)
            spots_v[at : at + lines, :] = ALPHA * (scale * along_v - offset_v)
            turns_real[at : at + lines, :] = real * cosine - imag * sine
            turns_imag[at : at + lines, :] = real * sine + imag * cosine
    last = devices * lines
    for ref in (spots_u, spots_v, turns_real, turns_imag):
        ref[last : last + 8, :] = jnp.zeros((8, SU), jnp.float32)
    copy.wait()

    def pick(d, count):
        for k in range(cap):
            plane = meta_s[d, k] - 1
            set_id = jnp.where(lax.rem(plane, groups) == group, 0, 1)
            order[count] = (d * cap + k) * slots + 2 * lax.div(plane, groups) + set_id
            count = count + jnp.where(plane >= 0, 1, 0)
        return count

    count = lax.fori_loop(0, devices, pick, 0)
    for i in range(UNROLL):
        order[count + i] = devices * cap * slots

    cells = ALPHA * lax.broadcasted_iota(jnp.int32, (SU, SU), 0).astype(jnp.float32)

    def profile(spot):
        apart = (spot - cells).astype(jnp.bfloat16)
        return jnp.exp2(-(apart * apart))

    def tiled(row):
        return jnp.broadcast_to(row, (16, SU)).astype(jnp.bfloat16)[None]

    def one_block(at):
        code = order[at]
        slot = lax.rem(code, slots)
        base = lax.div(code, slots) * chans
        lefts_real, lefts_imag, rights = [], [], []
        for c in range(chans):
            here = pl.ds(base + c, 1)
            left = profile(spots_u[here, :]).reshape(SU // 16, 16, SU)
            lefts_real.append((left * tiled(turns_real[here, :])).reshape(SU, SU))
            lefts_imag.append((left * tiled(turns_imag[here, :])).reshape(SU, SU))
            rights.append(profile(spots_v[here, :]))
        left = jnp.concatenate(
            [jnp.concatenate(lefts_real, axis=1), jnp.concatenate(lefts_imag, axis=1)], axis=0
        )
        right = jnp.concatenate(rights, axis=1)
        return slot, lax.dot_general(left, right, NT, preferred_element_type=jnp.float32)

    def step(k, carry):
        for slot, part in [one_block(k * UNROLL + i) for i in range(UNROLL)]:
            grids[slot] += part
        return carry

    lax.fori_loop(0, lax.div(count + UNROLL - 1, UNROLL), step, 0)


def spread_kernel(own, shifted, out_ref):
    chan = lax.axis_index("chan")
    for n, ref in enumerate((own, shifted)):
        table = ref[chan]
        for f in range(out_ref.shape[0]):
            out_ref[f, n] = table


def table_kernel(sizes, norm, grids, own, swapped, packed, mine_ref, other_ref, table_f, total):
    slots, meta_row = sizes
    chan = lax.axis_index("chan")
    group = lax.axis_index("bl")
    first = chan == 0

    def parts(table):
        table_f[...] = table
        return table_f[pl.ds(0, SU, stride=2), :], table_f[pl.ds(1, SU, stride=2), :]

    result = jnp.zeros((SU, 2 * SU), jnp.float32)
    for s in range(slots):
        ours = own[s].astype(jnp.float32)
        theirs = swapped[s].astype(jnp.float32)
        u_real, u_imag = parts(jnp.where(first, ours, theirs))
        u_side = jnp.concatenate([u_real.T, u_imag.T], axis=1).astype(jnp.bfloat16)
        grid_real = grids[s, :SU, :]
        grid_imag = grids[s, SU:, :]
        inner = jnp.concatenate(
            [
                jnp.concatenate([grid_real, grid_imag], axis=1),
                jnp.concatenate([-grid_imag, grid_real], axis=1),
            ],
            axis=0,
        )
        high, low = split_bf16(inner)
        half = jnp.dot(u_side, high, preferred_element_type=jnp.float32) + jnp.dot(
            u_side, low, preferred_element_type=jnp.float32
        )
        v_real, v_imag = parts(jnp.where(first, theirs, ours))
        v_side = jnp.concatenate(
            [
                jnp.concatenate([v_real, v_imag], axis=1),
                jnp.concatenate([-v_imag, v_real], axis=1),
            ],
            axis=0,
        ).astype(jnp.bfloat16)
        high, low = split_bf16(half)
        result = (
            result
            + jnp.dot(high, v_side, preferred_element_type=jnp.float32)
            + jnp.dot(low, v_side, preferred_element_type=jnp.float32)
        )
    tail = meta_row // 16 * 16
    wide = packed[group, tail : tail + 16, :].astype(jnp.float32)
    at = meta_row - tail + 2
    gain = (wide[at : at + 2] + wide[at + 2 : at + 4]) + wide[at + 4 : at + 6]
    gain_u = jnp.broadcast_to(gain[0:1], (SU, SU)).T
    gains = gain_u * gain[1:2] * norm
    total[...] = result * jnp.concatenate([gains, gains], axis=1)
    half_rows = mine_ref.shape[0]
    mine_ref[...] = total[pl.ds(pl.multiple_of(chan * half_rows, half_rows), half_rows), :]
    other_ref[...] = total[pl.ds(pl.multiple_of((1 - chan) * half_rows, half_rows), half_rows), :]


def body(
    visibilities, coords, plane_index, block_group, offsets, facet_centre, tables, antenna_gain
):
    facets = lax.axis_size("facet")
    groups = lax.axis_size("bl")
    chan_count = lax.axis_size("chan")
    held, chans = visibilities.shape[:2]
    devices = facets * groups
    slots = 2 * facets
    cap = max(2, 2 * held // groups)
    meta_row = 2 * cap * (chans + 1)
    rows = -(-(meta_row + 8) // 16) * 16
    half_rows = SU // chan_count
    norm = SU / math.sqrt(visibilities.shape[3] * held * facets * CH)

    packed = pl.pallas_call(
        functools.partial(sort_kernel, (groups, held, chans, cap, rows)),
        out_shape=jax.ShapeDtypeStruct((groups, rows, SU), jnp.bfloat16),
        in_specs=[HBM] * 7,
        out_specs=VMEM,
        scratch_shapes=[
            pltpu.SMEM((1, held), jnp.int32),
            pltpu.SMEM((1, held), jnp.int32),
            pltpu.VMEM((held * 2 * chans, SU), jnp.bfloat16),
            pltpu.VMEM((held * 2, SU), jnp.bfloat16),
            pltpu.SMEM((facets, 2, groups), jnp.int32),
            pltpu.SMEM((2, facets), jnp.float32),
            pltpu.VMEM((1, 2, SU), jnp.float32),
            pltpu.VMEM((held * 2 * chans, SU), jnp.float32),
            pltpu.VMEM((held * 2, SU), jnp.float32),
            pltpu.VMEM((groups, rows, SU), jnp.float32),
            pltpu.SMEM((groups,), jnp.int32),
            pltpu.SemaphoreType.DMA((7,)),
        ],
        compiler_params=ALONE,
        cost_estimate=pl.CostEstimate(flops=100_000, bytes_accessed=100_000, transcendentals=0),
        name="sort_blocks",
    )(
        plane_index.reshape(1, held),
        block_group.T,
        visibilities.reshape(held * 2 * chans, SU),
        coords.reshape(held * 2, SU),
        offsets.transpose(0, 2, 1),
        facet_centre.T,
        antenna_gain,
    )
    here = lax.all_to_all(packed, "bl", split_axis=0, concat_axis=0, tiled=True)
    blocks = [here] + [
        lax.ppermute(here, "facet", [(f, (f + shift) % facets) for f in range(facets)])
        for shift in range(1, facets)
    ]

    swap = [(c, 1 - c) for c in range(chan_count)]
    own_table = tables.reshape(2, 2 * SU, SU)
    shifted = lax.ppermute(own_table, "bl", [(g, (g + 1) % groups) for g in range(groups)])
    spread = pl.pallas_call(
        spread_kernel,
        out_shape=jax.ShapeDtypeStruct((facets, 2, 2 * SU, SU), jnp.bfloat16),
        in_specs=[VMEM, VMEM],
        out_specs=VMEM,
        compiler_params=PARAMS,
        cost_estimate=pl.CostEstimate(flops=0, bytes_accessed=1_000_000, transcendentals=0),
        name="spread_tables",
    )(own_table, shifted)
    slot_tables = lax.all_to_all(spread, "facet", split_axis=0, concat_axis=0, tiled=True)
    slot_tables = slot_tables.reshape(slots, 2 * SU, SU)
    swapped_tables = lax.ppermute(slot_tables, "chan", swap)

    grids = pl.pallas_call(
        functools.partial(grid_kernel, (facets, groups, chans, cap, rows)),
        out_shape=jax.ShapeDtypeStruct((slots, 2 * SU, SU), jnp.float32),
        in_specs=[VMEM] * facets,
        out_specs=VMEM,
        scratch_shapes=[
            pltpu.VMEM((devices, SU), jnp.int32),
            pltpu.SMEM((devices, SU), jnp.int32),
            pltpu.SMEM((devices * cap + UNROLL,), jnp.int32),
        ]
        + [pltpu.VMEM((devices * cap * chans + 8, SU), jnp.float32)] * 4
        + [pltpu.SemaphoreType.DMA],
        compiler_params=PARAMS,
        cost_estimate=pl.CostEstimate(
            flops=4_000_000_000, bytes_accessed=2_000_000, transcendentals=4_000_000
        ),
        name="grid",
    )(*blocks)
    mine, other = pl.pallas_call(
        functools.partial(table_kernel, (slots, meta_row), norm),
        out_shape=[jax.ShapeDtypeStruct((half_rows, 2 * SU), jnp.float32)] * 2,
        in_specs=[VMEM] * 4,
        out_specs=[VMEM, VMEM],
        scratch_shapes=[
            pltpu.VMEM((2 * SU, SU), jnp.float32),
            pltpu.VMEM((SU, 2 * SU), jnp.float32),
        ],
        compiler_params=PARAMS,
        cost_estimate=pl.CostEstimate(
            flops=1_000_000_000, bytes_accessed=2_000_000, transcendentals=0
        ),
        name="apply_tables",
    )(grids, slot_tables, swapped_tables, here)
    arrived = lax.ppermute(other, "chan", swap)
    return (mine + arrived).reshape(1, 1, half_rows, 2, SU)


def solution(mesh):
    in_specs = (
        P(("facet", "bl"), "chan", None, None),
        P(("facet", "bl"), None, None),
        P(("facet", "bl")),
        P(("facet", "bl"), None),
        P(),
        P(),
        P(("facet", "bl"), None, None, None, None),
        P("bl", None, None),
    )
    out_specs = P("facet", "bl", "chan", None, None)
    return jax.shard_map(body, mesh=mesh, in_specs=in_specs, out_specs=out_specs, check_vma=False)
```

```python
import functools
import math

import jax
import jax.numpy as jnp
from jax import lax
from jax.experimental import pallas as pl
from jax.experimental.pallas import tpu as pltpu
from jax.sharding import PartitionSpec as P

SU = 128
CH = 8
KERNEL_SPREAD = 1.5
ALPHA = math.sqrt(math.log2(math.e) / (2.0 * KERNEL_SPREAD * KERNEL_SPREAD))
UNROLL = 2
NT = (((1,), (1,)), ((), ()))
VMEM = pl.BlockSpec(memory_space=pltpu.VMEM)
HBM = pl.BlockSpec(memory_space=pltpu.HBM)
PARAMS = pltpu.CompilerParams(vmem_limit_bytes=32 * 1024 * 1024)
ALONE = pltpu.CompilerParams(vmem_limit_bytes=60 * 1024 * 1024)


def cos_sin(turns):
    quarter = jnp.floor(4.0 * turns + 0.5)
    angle = (2.0 * math.pi) * (turns - 0.25 * quarter)
    sq = angle * angle
    sine = angle * (
        1.0 + sq * (-1.0 / 6 + sq * (1.0 / 120 + sq * (-1.0 / 5040 + sq * (1.0 / 362880))))
    )
    cosine = 1.0 + sq * (
        -0.5 + sq * (1.0 / 24 + sq * (-1.0 / 720 + sq * (1.0 / 40320 + sq * (-1.0 / 3628800))))
    )
    turn = quarter.astype(jnp.int32) & 3
    odd = (turn & 1) == 1
    cos_out = jnp.where(odd, sine, cosine)
    sin_out = jnp.where(odd, cosine, sine)
    cos_out = jnp.where((turn == 1) | (turn == 2), -cos_out, cos_out)
    sin_out = jnp.where(turn >= 2, -sin_out, sin_out)
    return cos_out, sin_out


def split_bf16(x):
    high = x.astype(jnp.bfloat16)
    low = (x - high.astype(jnp.float32)).astype(jnp.bfloat16)
    return high, low


def three_parts(x):
    parts = []
    for _ in range(3):
        part = x.astype(jnp.bfloat16)
        x = x - part.astype(jnp.float32)
        parts.append(part.astype(jnp.float32))
    return parts


def sort_kernel(sizes, *refs):
    groups, held, chans, cap, rows = sizes
    out_refs = refs[7 : 7 + groups]
    targets = refs[7 + groups : 14 + groups]
    plane_ref, group_ref, samples_b, place_b, offsets_ref, centre_ref, gain_ref = targets
    samples, place, sorted_, filled, sems = refs[14 + groups :]
    facet = lax.axis_index("facet")
    copies = [
        pltpu.make_async_copy(source, target, sems.at[n])
        for n, (source, target) in enumerate(zip(refs[:7], targets))
    ]
    for copy in copies:
        copy.start()
    sorted_[...] = jnp.zeros_like(sorted_)
    for g in range(groups):
        filled[g] = 0
    for copy in copies:
        copy.wait()
    samples[...] = samples_b[...].astype(jnp.float32)
    place[...] = place_b[...].astype(jnp.float32)
    lane = lax.broadcasted_iota(jnp.int32, (1, SU), 1)
    meta = 2 * cap * (chans + 1)
    centre = [
        part
        for axis in range(2)
        for part in three_parts(jnp.full((1, SU), centre_ref[axis, facet], jnp.float32))
    ]
    gains = three_parts(gain_ref[0])
    for g in range(groups):
        numbers = jnp.zeros((1, SU), jnp.float32)
        for axis in range(2):
            offset = offsets_ref[facet, axis, g].astype(jnp.float32)
            numbers = jnp.where(lane == axis, offset, numbers)
        for n, part in enumerate(centre):
            numbers = jnp.where(lane == 2 + n, part, numbers)
        sorted_[g, meta + 1 : meta + 2, :] = numbers
        for n, part in enumerate(gains):
            sorted_[g, meta + 2 + 2 * n : meta + 4 + 2 * n, :] = part
    for i in range(held):
        g = group_ref[0, i]
        k = filled[g]
        filled[g] = k + 1
        for part in range(2):
            at = part * cap * chans + k * chans
            sorted_[g, pl.ds(at, chans), :] = samples[pl.ds(2 * chans * i + part, chans, stride=2), :]
            at = 2 * cap * chans + part * cap + k
            sorted_[g, pl.ds(at, 1), :] = place[2 * i + part : 2 * i + part + 1, :]
        sorted_[g, meta : meta + 1, :] += jnp.where(
            lane == k, (plane_ref[0, i] + 1).astype(jnp.float32), 0.0
        )
    for shift, out_ref in enumerate(out_refs):
        g = lax.rem(lax.axis_index("bl") + shift, groups)
        out_ref[...] = sorted_[g].astype(jnp.bfloat16)


def grid_kernel(sizes, *refs):
    facets, groups, chans, cap, rows = sizes
    packed_refs = refs[:facets]
    grids = refs[facets]
    meta_v, meta_s, order, spots_u, spots_v, turns_real, turns_imag = refs[facets + 1 : facets + 8]
    lefts, rights = refs[facets + 8 : facets + 10], refs[facets + 10 : facets + 12]
    sem = refs[facets + 12]
    devices = facets * groups
    slots = 2 * facets
    lines = cap * chans
    meta_row = 2 * (lines + cap)
    tail = meta_row // 16 * 16
    facet = lax.axis_index("facet")
    group = lax.axis_index("bl")
    chan = lax.axis_index("chan")

    for f in range(facets):
        for g in range(groups):
            meta = packed_refs[f][g, tail : tail + 16, :].astype(jnp.float32)
            meta_v[f * groups + g : f * groups + g + 1, :] = meta[
                meta_row - tail : meta_row - tail + 1
            ].astype(jnp.int32)
            if f == 0 and g == 0:
                numbers = meta[meta_row - tail + 1 : meta_row - tail + 2]
    copy = pltpu.make_async_copy(meta_v, meta_s, sem)
    copy.start()
    for ref in (grids, lefts[1], rights[1]):
        ref[...] = jnp.zeros_like(ref)

    def number(n):
        return jnp.broadcast_to(numbers[:, n : n + 1], (lines, SU))

    offset_u = number(0)
    offset_v = number(1)
    along_l = number(2) + number(3) + number(4)
    along_m = number(5) + number(6) + number(7)
    line = lax.broadcasted_iota(jnp.int32, (lines, SU), 0)
    channel = (chan * chans + lax.rem(line, chans)).astype(jnp.float32)
    scale = 1.0 + 0.01 * (channel - 0.5 * (CH - 1))

    def spread_lines(place):
        return jnp.concatenate(
            [jnp.broadcast_to(place[k : k + 1], (chans, SU)) for k in range(cap)], axis=0
        )

    for f in range(facets):
        for g in range(groups):
            at = (f * groups + g) * lines
            wide = packed_refs[f][g].astype(jnp.float32)
            real = wide[:lines]
            imag = wide[lines : 2 * lines]
            along_u = spread_lines(wide[2 * lines : 2 * lines + cap])
            along_v = spread_lines(wide[2 * lines + cap : 2 * (lines + cap)])
            cosine, sine = cos_sin(
                (1.0 / SU) * (scale * (along_u * along_l + along_v * along_m))
            )
            spots_u[at : at + lines, :] = ALPHA * (scale * along_u - offset_u)
            spots_v[at : at + lines, :] = ALPHA * (scale * along_v - offset_v)
            turns_real[at : at + lines, :] = real * cosine - imag * sine
            turns_imag[at : at + lines, :] = real * sine + imag * cosine
    last = devices * lines
    for ref in (spots_u, spots_v, turns_real, turns_imag):
        ref[last : last + 8, :] = jnp.zeros((8, SU), jnp.float32)
    copy.wait()

    for i in range(UNROLL):
        order[i] = 0

    def pick(d, count):
        for k in range(cap):
            plane = meta_s[d, k] - 1
            set_id = jnp.where(lax.rem(plane, groups) == group, 0, 1)
            shift = lax.rem(facet - lax.div(plane, groups) + facets, facets)
            order[UNROLL + count] = (d * cap + k) * slots + 2 * shift + set_id
            count = count + jnp.where(plane >= 0, 1, 0)
        return count

    count = lax.fori_loop(0, devices, pick, 0)
    for i in range(3 * UNROLL):
        order[UNROLL + count + i] = devices * cap * slots

    cells = ALPHA * lax.broadcasted_iota(jnp.int32, (SU, SU), 0).astype(jnp.float32)

    def profile(spot):
        apart = spot - cells
        return jnp.exp2(-(apart * apart)).astype(jnp.bfloat16)

    def tiled(row):
        return jnp.broadcast_to(row, (16, SU)).astype(jnp.bfloat16)[None]

    def build(n, at, left_ref, right_ref):
        base = lax.div(order[at], slots) * chans
        for c in range(chans):
            here = pl.ds(base + c, 1)
            there = slice(c * SU, (c + 1) * SU)
            left = profile(spots_u[here, :]).reshape(SU // 16, 16, SU)
            left_ref[n, :SU, there] = (left * tiled(turns_real[here, :])).reshape(SU, SU)
            left_ref[n, SU:, there] = (left * tiled(turns_imag[here, :])).reshape(SU, SU)
            right_ref[n, :, there] = profile(spots_v[here, :])

    def multiply(n, at, left_ref, right_ref):
        slot = lax.rem(order[at], slots)
        grids[slot] += lax.dot_general(
            left_ref[n], right_ref[n], NT, preferred_element_type=jnp.float32
        )

    def step(k, carry):
        for half in range(2):
            at = (2 * k + half) * UNROLL
            for n in range(UNROLL):
                build(n, at + UNROLL + n, lefts[half], rights[half])
                multiply(n, at + n, lefts[1 - half], rights[1 - half])
        return carry

    lax.fori_loop(0, lax.div(count + 3 * UNROLL - 1, 2 * UNROLL), step, 0)


def regroup_kernel(groups, *refs):
    own, shifted, here, half = refs[groups:]
    chan = lax.axis_index("chan")
    for g in range(groups):
        here[g] = refs[g][...]
    half[0] = own[chan]
    half[1] = shifted[chan]


def table_kernel(sizes, norm, grids, packed, own, shifted, *refs):
    facets, meta_row = sizes
    slots = 2 * facets
    fetched = refs[: facets - 1]
    swapped = refs[facets - 1 : slots - 2]
    mine_ref, other_ref, table_f, total = refs[slots - 2 :]
    chan = lax.axis_index("chan")
    first = chan == 0

    def parts(table):
        table_f[...] = table
        return table_f[pl.ds(0, SU, stride=2), :], table_f[pl.ds(1, SU, stride=2), :]

    result = jnp.zeros((SU, 2 * SU), jnp.float32)
    for s in range(slots):
        shift, set_id = divmod(s, 2)
        if shift == 0:
            whole = (own, shifted)[set_id]
            u_table = whole[0].astype(jnp.float32)
            v_table = whole[1].astype(jnp.float32)
        else:
            ours = fetched[shift - 1][set_id].astype(jnp.float32)
            theirs = swapped[shift - 1][set_id].astype(jnp.float32)
            u_table = jnp.where(first, ours, theirs)
            v_table = jnp.where(first, theirs, ours)
        u_real, u_imag = parts(u_table)
        u_side = jnp.concatenate([u_real.T, u_imag.T], axis=1).astype(jnp.bfloat16)
        grid_real = grids[s, :SU, :]
        grid_imag = grids[s, SU:, :]
        inner = jnp.concatenate(
            [
                jnp.concatenate([grid_real, grid_imag], axis=1),
                jnp.concatenate([-grid_imag, grid_real], axis=1),
            ],
            axis=0,
        )
        high, low = split_bf16(inner)
        half = jnp.dot(u_side, high, preferred_element_type=jnp.float32) + jnp.dot(
            u_side, low, preferred_element_type=jnp.float32
        )
        v_real, v_imag = parts(v_table)
        v_side = jnp.concatenate(
            [
                jnp.concatenate([v_real, v_imag], axis=1),
                jnp.concatenate([-v_imag, v_real], axis=1),
            ],
            axis=0,
        ).astype(jnp.bfloat16)
        high, low = split_bf16(half)
        result = (
            result
            + jnp.dot(high, v_side, preferred_element_type=jnp.float32)
            + jnp.dot(low, v_side, preferred_element_type=jnp.float32)
        )
    tail = meta_row // 16 * 16
    wide = packed[0, tail : tail + 16, :].astype(jnp.float32)
    at = meta_row - tail + 2
    gain = (wide[at : at + 2] + wide[at + 2 : at + 4]) + wide[at + 4 : at + 6]
    gain_u = jnp.broadcast_to(gain[0:1], (SU, SU)).T
    gains = gain_u * gain[1:2] * norm
    total[...] = result * jnp.concatenate([gains, gains], axis=1)
    half_rows = mine_ref.shape[0]
    mine_ref[...] = total[pl.ds(pl.multiple_of(chan * half_rows, half_rows), half_rows), :]
    other_ref[...] = total[pl.ds(pl.multiple_of((1 - chan) * half_rows, half_rows), half_rows), :]


def ring(size, shift):
    return [(n, (n + shift) % size) for n in range(size)]


def body(
    visibilities, coords, plane_index, block_group, offsets, facet_centre, tables, antenna_gain
):
    facets = lax.axis_size("facet")
    groups = lax.axis_size("bl")
    chan_count = lax.axis_size("chan")
    held, chans = visibilities.shape[:2]
    devices = facets * groups
    slots = 2 * facets
    cap = max(2, 2 * held // groups)
    meta_row = 2 * cap * (chans + 1)
    rows = -(-(meta_row + 8) // 16) * 16
    half_rows = SU // chan_count
    norm = SU / math.sqrt(visibilities.shape[3] * held * facets * CH)

    pieces = pl.pallas_call(
        functools.partial(sort_kernel, (groups, held, chans, cap, rows)),
        out_shape=[jax.ShapeDtypeStruct((rows, SU), jnp.bfloat16)] * groups,
        in_specs=[HBM] * 7,
        out_specs=[VMEM] * groups,
        scratch_shapes=[
            pltpu.SMEM((1, held), jnp.int32),
            pltpu.SMEM((1, held), jnp.int32),
            pltpu.VMEM((held * 2 * chans, SU), jnp.bfloat16),
            pltpu.VMEM((held * 2, SU), jnp.bfloat16),
            pltpu.SMEM((facets, 2, groups), jnp.int32),
            pltpu.SMEM((2, facets), jnp.float32),
            pltpu.VMEM((1, 2, SU), jnp.float32),
            pltpu.VMEM((held * 2 * chans, SU), jnp.float32),
            pltpu.VMEM((held * 2, SU), jnp.float32),
            pltpu.VMEM((groups, rows, SU), jnp.float32),
            pltpu.SMEM((groups,), jnp.int32),
            pltpu.SemaphoreType.DMA((7,)),
        ],
        compiler_params=ALONE,
        cost_estimate=pl.CostEstimate(flops=100_000, bytes_accessed=100_000, transcendentals=0),
        name="sort_blocks",
    )(
        plane_index.reshape(1, held),
        block_group.T,
        visibilities.reshape(held * 2 * chans, SU),
        coords.reshape(held * 2, SU),
        offsets.transpose(0, 2, 1),
        facet_centre.T,
        antenna_gain,
    )
    own_table = tables.reshape(2, 2 * SU, SU)
    shifted = lax.ppermute(own_table, "bl", ring(groups, 1))
    pieces = [pieces[0]] + [
        lax.ppermute(pieces[shift], "bl", ring(groups, shift)) for shift in range(1, groups)
    ]
    here, half = pl.pallas_call(
        functools.partial(regroup_kernel, groups),
        out_shape=[
            jax.ShapeDtypeStruct((groups, rows, SU), jnp.bfloat16),
            jax.ShapeDtypeStruct((2, 2 * SU, SU), jnp.bfloat16),
        ],
        in_specs=[VMEM] * (groups + 2),
        out_specs=[VMEM] * 2,
        compiler_params=PARAMS,
        cost_estimate=pl.CostEstimate(flops=0, bytes_accessed=400_000, transcendentals=0),
        name="regroup",
    )(*pieces, own_table, shifted)
    shifts = range(1, facets)
    blocks = [here] + [lax.ppermute(here, "facet", ring(facets, shift)) for shift in shifts]
    swap = ring(chan_count, 1)
    fetched = [lax.ppermute(half, "facet", ring(facets, shift)) for shift in shifts]
    swapped = [lax.ppermute(table, "chan", swap) for table in fetched]

    grids = pl.pallas_call(
        functools.partial(grid_kernel, (facets, groups, chans, cap, rows)),
        out_shape=jax.ShapeDtypeStruct((slots, 2 * SU, SU), jnp.float32),
        in_specs=[VMEM] * facets,
        out_specs=VMEM,
        scratch_shapes=[
            pltpu.VMEM((devices, SU), jnp.int32),
            pltpu.SMEM((devices, SU), jnp.int32),
            pltpu.SMEM((devices * cap + 4 * UNROLL,), jnp.int32),
        ]
        + [pltpu.VMEM((devices * cap * chans + 8, SU), jnp.float32)] * 4
        + [pltpu.VMEM((UNROLL, 2 * SU, chans * SU), jnp.bfloat16)] * 2
        + [pltpu.VMEM((UNROLL, SU, chans * SU), jnp.bfloat16)] * 2
        + [pltpu.SemaphoreType.DMA],
        compiler_params=PARAMS,
        cost_estimate=pl.CostEstimate(
            flops=4_000_000_000, bytes_accessed=2_000_000, transcendentals=4_000_000
        ),
        name="grid",
    )(*blocks)
    mine, other = pl.pallas_call(
        functools.partial(table_kernel, (facets, meta_row), norm),
        out_shape=[jax.ShapeDtypeStruct((half_rows, 2 * SU), jnp.float32)] * 2,
        in_specs=[VMEM] * (4 + 2 * (facets - 1)),
        out_specs=[VMEM, VMEM],
        scratch_shapes=[
            pltpu.VMEM((2 * SU, SU), jnp.float32),
            pltpu.VMEM((SU, 2 * SU), jnp.float32),
        ],
        compiler_params=PARAMS,
        cost_estimate=pl.CostEstimate(
            flops=1_000_000_000, bytes_accessed=2_000_000, transcendentals=0
        ),
        name="apply_tables",
    )(grids, here, own_table, shifted, *fetched, *swapped)
    arrived = lax.ppermute(other, "chan", swap)
    return (mine + arrived).reshape(1, 1, half_rows, 2, SU)


def solution(mesh):
    in_specs = (
        P(("facet", "bl"), "chan", None, None),
        P(("facet", "bl"), None, None),
        P(("facet", "bl")),
        P(("facet", "bl"), None),
        P(),
        P(),
        P(("facet", "bl"), None, None, None, None),
        P("bl", None, None),
    )
    out_specs = P("facet", "bl", "chan", None, None)
    return jax.shard_map(body, mesh=mesh, in_specs=in_specs, out_specs=out_specs, check_vma=False)
```

```python
import functools
import math

import jax
import jax.numpy as jnp
from jax import lax
from jax.experimental import pallas as pl
from jax.experimental.pallas import tpu as pltpu
from jax.sharding import PartitionSpec as P

SU = 128
CH = 8
KERNEL_SPREAD = 1.5
ALPHA = math.sqrt(math.log2(math.e) / (2.0 * KERNEL_SPREAD * KERNEL_SPREAD))
UNROLL = 4
NT = (((1,), (1,)), ((), ()))
VMEM = pl.BlockSpec(memory_space=pltpu.VMEM)
HBM = pl.BlockSpec(memory_space=pltpu.HBM)
ANY = pl.BlockSpec(memory_space=pl.ANY)
PARAMS = pltpu.CompilerParams(vmem_limit_bytes=32 * 1024 * 1024)
ALONE = pltpu.CompilerParams(vmem_limit_bytes=60 * 1024 * 1024)


def cos_sin(turns):
    quarter = jnp.floor(4.0 * turns + 0.5)
    angle = (2.0 * math.pi) * (turns - 0.25 * quarter)
    sq = angle * angle
    sine = angle * (
        1.0 + sq * (-1.0 / 6 + sq * (1.0 / 120 + sq * (-1.0 / 5040 + sq * (1.0 / 362880))))
    )
    cosine = 1.0 + sq * (
        -0.5 + sq * (1.0 / 24 + sq * (-1.0 / 720 + sq * (1.0 / 40320 + sq * (-1.0 / 3628800))))
    )
    turn = quarter.astype(jnp.int32) & 3
    odd = (turn & 1) == 1
    cos_out = jnp.where(odd, sine, cosine)
    sin_out = jnp.where(odd, cosine, sine)
    cos_out = jnp.where((turn == 1) | (turn == 2), -cos_out, cos_out)
    sin_out = jnp.where(turn >= 2, -sin_out, sin_out)
    return cos_out, sin_out


def split_bf16(x):
    high = x.astype(jnp.bfloat16)
    low = (x - high.astype(jnp.float32)).astype(jnp.bfloat16)
    return high, low


def three_parts(x):
    parts = []
    for _ in range(3):
        part = x.astype(jnp.bfloat16)
        x = x - part.astype(jnp.float32)
        parts.append(part.astype(jnp.float32))
    return parts


def sort_kernel(sizes, *refs):
    groups, held, chans, cap, rows = sizes
    table_hbm, out_refs, half_hbm = refs[7], refs[8 : 8 + groups], refs[8 + groups]
    targets = refs[9 + groups : 16 + groups]
    plane_ref, group_ref, samples_b, place_b, offsets_ref, centre_ref, gain_ref = targets
    samples, place, sorted_, filled, sems = refs[16 + groups :]
    facet = lax.axis_index("facet")
    copies = [
        pltpu.make_async_copy(source, target, sems.at[n])
        for n, (source, target) in enumerate(zip(refs[:7], targets))
    ]
    half = pltpu.make_async_copy(table_hbm.at[lax.axis_index("chan")], half_hbm, sems.at[7])
    for copy in copies + [half]:
        copy.start()
    sorted_[...] = jnp.zeros_like(sorted_)
    for g in range(groups):
        filled[g] = 0
    for copy in copies:
        copy.wait()
    samples[...] = samples_b[...].astype(jnp.float32)
    place[...] = place_b[...].astype(jnp.float32)
    lane = lax.broadcasted_iota(jnp.int32, (1, SU), 1)
    meta = 2 * cap * (chans + 1)
    centre = [
        part
        for axis in range(2)
        for part in three_parts(jnp.full((1, SU), centre_ref[axis, facet], jnp.float32))
    ]
    gains = three_parts(gain_ref[0])
    for g in range(groups):
        numbers = jnp.zeros((1, SU), jnp.float32)
        for axis in range(2):
            offset = offsets_ref[facet, axis, g].astype(jnp.float32)
            numbers = jnp.where(lane == axis, offset, numbers)
        for n, part in enumerate(centre):
            numbers = jnp.where(lane == 2 + n, part, numbers)
        sorted_[g, meta + 1 : meta + 2, :] = numbers
        for n, part in enumerate(gains):
            sorted_[g, meta + 2 + 2 * n : meta + 4 + 2 * n, :] = part
    for i in range(held):
        g = group_ref[0, i]
        k = filled[g]
        filled[g] = k + 1
        for part in range(2):
            at = part * cap * chans + k * chans
            sorted_[g, pl.ds(at, chans), :] = samples[pl.ds(2 * chans * i + part, chans, stride=2), :]
            at = 2 * cap * chans + part * cap + k
            sorted_[g, pl.ds(at, 1), :] = place[2 * i + part : 2 * i + part + 1, :]
        sorted_[g, meta : meta + 1, :] += jnp.where(
            lane == k, (plane_ref[0, i] + 1).astype(jnp.float32), 0.0
        )
    for shift, out_ref in enumerate(out_refs):
        g = lax.rem(lax.axis_index("bl") + shift, groups)
        out_ref[...] = sorted_[g].astype(jnp.bfloat16)
    half.wait()


def grid_kernel(sizes, *refs):
    facets, groups, chans, cap, rows = sizes
    packed_refs = refs[:facets]
    grids = refs[facets]
    meta_v, meta_s, order, spots_u, spots_v, turns_real, turns_imag, sem = refs[facets + 1 :]
    devices = facets * groups
    slots = 2 * facets
    lines = cap * chans
    meta_row = 2 * (lines + cap)
    tail = meta_row // 16 * 16
    facet = lax.axis_index("facet")
    group = lax.axis_index("bl")
    chan = lax.axis_index("chan")

    lane = lax.broadcasted_iota(jnp.int32, (1, SU), 1)
    for f in range(facets):
        for g in range(groups):
            meta = packed_refs[f][g, tail : tail + 16, :].astype(jnp.float32)
            d = f * groups + g
            plane = meta[meta_row - tail : meta_row - tail + 1].astype(jnp.int32) - 1
            set_id = jnp.where(lax.rem(plane, groups) == group, 0, 1)
            shift = lax.rem(facet - lax.div(plane, groups) + facets, facets)
            code = (d * cap + lane) * slots + 2 * shift + set_id
            meta_v[d : d + 1, :] = jnp.where(plane >= 0, code, -1)
            if f == 0 and g == 0:
                numbers = meta[meta_row - tail + 1 : meta_row - tail + 2]
    copy = pltpu.make_async_copy(meta_v, meta_s, sem)
    copy.start()
    grids[...] = jnp.zeros_like(grids)

    def number(n):
        return jnp.broadcast_to(numbers[:, n : n + 1], (lines, SU))

    offset_u = number(0)
    offset_v = number(1)
    along_l = number(2) + number(3) + number(4)
    along_m = number(5) + number(6) + number(7)
    line = lax.broadcasted_iota(jnp.int32, (lines, SU), 0)
    channel = (chan * chans + lax.rem(line, chans)).astype(jnp.float32)
    scale = 1.0 + 0.01 * (channel - 0.5 * (CH - 1))

    def spread_lines(place):
        return jnp.concatenate(
            [jnp.broadcast_to(place[k : k + 1], (chans, SU)) for k in range(cap)], axis=0
        )

    for f in range(facets):
        for g in range(groups):
            at = (f * groups + g) * lines
            wide = packed_refs[f][g].astype(jnp.float32)
            real = wide[:lines]
            imag = wide[lines : 2 * lines]
            along_u = spread_lines(wide[2 * lines : 2 * lines + cap])
            along_v = spread_lines(wide[2 * lines + cap : 2 * (lines + cap)])
            cosine, sine = cos_sin(
                (1.0 / SU) * (scale * (along_u * along_l + along_v * along_m))
            )
            spots_u[at : at + lines, :] = ALPHA * (scale * along_u - offset_u)
            spots_v[at : at + lines, :] = ALPHA * (scale * along_v - offset_v)
            turns_real[at : at + lines, :] = real * cosine - imag * sine
            turns_imag[at : at + lines, :] = real * sine + imag * cosine
    last = devices * lines
    for ref in (spots_u, spots_v, turns_real, turns_imag):
        ref[last : last + 8, :] = jnp.zeros((8, SU), jnp.float32)
    copy.wait()

    count = jnp.int32(0)
    for d in range(devices):
        for k in range(cap):
            code = meta_s[d, k]
            order[count] = code
            count = count + jnp.where(code >= 0, 1, 0)
    for i in range(UNROLL):
        order[count + i] = devices * cap * slots

    cells = ALPHA * lax.broadcasted_iota(jnp.int32, (SU, SU), 0).astype(jnp.float32)

    def profile(spot):
        apart = spot - cells
        return jnp.exp2(-(apart * apart)).astype(jnp.bfloat16)

    def tiled(row):
        return jnp.broadcast_to(row, (16, SU)).astype(jnp.bfloat16)[None]

    def one_block(at):
        code = order[at]
        slot = lax.rem(code, slots)
        base = lax.div(code, slots) * chans
        lefts_real, lefts_imag, rights = [], [], []
        for c in range(chans):
            here = pl.ds(base + c, 1)
            left = profile(spots_u[here, :]).reshape(SU // 16, 16, SU)
            lefts_real.append((left * tiled(turns_real[here, :])).reshape(SU, SU))
            lefts_imag.append((left * tiled(turns_imag[here, :])).reshape(SU, SU))
            rights.append(profile(spots_v[here, :]))
        left = jnp.concatenate(
            [jnp.concatenate(lefts_real, axis=1), jnp.concatenate(lefts_imag, axis=1)], axis=0
        )
        right = jnp.concatenate(rights, axis=1)
        return slot, lax.dot_general(left, right, NT, preferred_element_type=jnp.float32)

    def step(k, carry):
        for slot, part in [one_block(k * UNROLL + i) for i in range(UNROLL)]:
            grids[slot] += part
        return carry

    lax.fori_loop(0, lax.div(count + UNROLL - 1, UNROLL), step, 0)


def copy_kernel(*refs):
    for source, target in zip(refs[: len(refs) // 2], refs[len(refs) // 2 :]):
        target[...] = source[...]


def stack_kernel(count, *refs):
    for n in range(count):
        refs[-1][n] = refs[n][...]


def local(kernel, operands, shapes, name, after=()):
    return pl.pallas_call(
        kernel,
        out_shape=[jax.ShapeDtypeStruct(shape, jnp.bfloat16) for shape in shapes],
        in_specs=[VMEM] * len(operands) + [ANY] * len(after),
        out_specs=[VMEM] * len(shapes),
        compiler_params=PARAMS,
        cost_estimate=pl.CostEstimate(flops=0, bytes_accessed=400_000, transcendentals=0),
        name=name,
    )(*operands, *after)


def table_kernel(sizes, norm, grids, packed, *refs):
    facets, meta_row = sizes
    slots = 2 * facets
    ours, theirs = refs[:facets], refs[facets:slots]
    mine_ref, other_ref, table_f, total = refs[slots:]
    chan = lax.axis_index("chan")
    first = chan == 0

    def parts(table):
        table_f[...] = table
        return table_f[pl.ds(0, SU, stride=2), :], table_f[pl.ds(1, SU, stride=2), :]

    result = jnp.zeros((SU, 2 * SU), jnp.float32)
    for s in range(slots):
        shift, set_id = divmod(s, 2)
        fetched = ours[shift][set_id].astype(jnp.float32)
        swapped = theirs[shift][set_id].astype(jnp.float32)
        u_table = jnp.where(first, fetched, swapped)
        v_table = jnp.where(first, swapped, fetched)
        u_real, u_imag = parts(u_table)
        u_side = jnp.concatenate([u_real.T, u_imag.T], axis=1).astype(jnp.bfloat16)
        grid_real = grids[s, :SU, :]
        grid_imag = grids[s, SU:, :]
        inner = jnp.concatenate(
            [
                jnp.concatenate([grid_real, grid_imag], axis=1),
                jnp.concatenate([-grid_imag, grid_real], axis=1),
            ],
            axis=0,
        )
        high, low = split_bf16(inner)
        half = jnp.dot(u_side, high, preferred_element_type=jnp.float32) + jnp.dot(
            u_side, low, preferred_element_type=jnp.float32
        )
        v_real, v_imag = parts(v_table)
        v_side = jnp.concatenate(
            [
                jnp.concatenate([v_real, v_imag], axis=1),
                jnp.concatenate([-v_imag, v_real], axis=1),
            ],
            axis=0,
        ).astype(jnp.bfloat16)
        high, low = split_bf16(half)
        result = (
            result
            + jnp.dot(high, v_side, preferred_element_type=jnp.float32)
            + jnp.dot(low, v_side, preferred_element_type=jnp.float32)
        )
    tail = meta_row // 16 * 16
    wide = packed[0, tail : tail + 16, :].astype(jnp.float32)
    at = meta_row - tail + 2
    gain = (wide[at : at + 2] + wide[at + 2 : at + 4]) + wide[at + 4 : at + 6]
    gain_u = jnp.broadcast_to(gain[0:1], (SU, SU)).T
    gains = gain_u * gain[1:2] * norm
    total[...] = result * jnp.concatenate([gains, gains], axis=1)
    half_rows = mine_ref.shape[0]
    mine_ref[...] = total[pl.ds(pl.multiple_of(chan * half_rows, half_rows), half_rows), :]
    other_ref[...] = total[pl.ds(pl.multiple_of((1 - chan) * half_rows, half_rows), half_rows), :]


def ring(size, shift):
    return [(n, (n + shift) % size) for n in range(size)]


def body(
    visibilities, coords, plane_index, block_group, offsets, facet_centre, tables, antenna_gain
):
    facets = lax.axis_size("facet")
    groups = lax.axis_size("bl")
    chan_count = lax.axis_size("chan")
    held, chans = visibilities.shape[:2]
    devices = facets * groups
    slots = 2 * facets
    cap = max(2, 2 * held // groups)
    meta_row = 2 * cap * (chans + 1)
    rows = -(-(meta_row + 8) // 16) * 16
    half_rows = SU // chan_count
    norm = SU / math.sqrt(visibilities.shape[3] * held * facets * CH)

    own_table = tables.reshape(2, 2 * SU, SU)
    *pieces, own_half = pl.pallas_call(
        functools.partial(sort_kernel, (groups, held, chans, cap, rows)),
        out_shape=[jax.ShapeDtypeStruct((rows, SU), jnp.bfloat16)] * groups
        + [jax.ShapeDtypeStruct((2 * SU, SU), jnp.bfloat16)],
        in_specs=[HBM] * 8,
        out_specs=[VMEM] * groups + [HBM],
        scratch_shapes=[
            pltpu.SMEM((1, held), jnp.int32),
            pltpu.SMEM((1, held), jnp.int32),
            pltpu.VMEM((held * 2 * chans, SU), jnp.bfloat16),
            pltpu.VMEM((held * 2, SU), jnp.bfloat16),
            pltpu.SMEM((facets, 2, groups), jnp.int32),
            pltpu.SMEM((2, facets), jnp.float32),
            pltpu.VMEM((1, 2, SU), jnp.float32),
            pltpu.VMEM((held * 2 * chans, SU), jnp.float32),
            pltpu.VMEM((held * 2, SU), jnp.float32),
            pltpu.VMEM((groups, rows, SU), jnp.float32),
            pltpu.SMEM((groups,), jnp.int32),
            pltpu.SemaphoreType.DMA((8,)),
        ],
        compiler_params=ALONE,
        cost_estimate=pl.CostEstimate(flops=100_000, bytes_accessed=100_000, transcendentals=0),
        name="sort_blocks",
    )(
        plane_index.reshape(1, held),
        block_group.T,
        visibilities.reshape(held * 2 * chans, SU),
        coords.reshape(held * 2, SU),
        offsets.transpose(0, 2, 1),
        facet_centre.T,
        antenna_gain,
        own_table,
    )
    arrived = [
        lax.ppermute(pieces[shift], "bl", ring(groups, shift)) for shift in range(1, groups)
    ]
    shifted_half = lax.ppermute(own_half, "bl", ring(groups, 1))
    kept, kept_half = local(
        copy_kernel, [pieces[0], own_half], [(rows, SU), (2 * SU, SU)], "keep_own"
    )
    (here,) = local(
        functools.partial(stack_kernel, groups), [kept, *arrived], [(groups, rows, SU)], "join"
    )
    shifts = range(1, facets)
    blocks = [here] + [lax.ppermute(here, "facet", ring(facets, shift)) for shift in shifts]
    (halves,) = local(
        functools.partial(stack_kernel, 2),
        [kept_half, shifted_half],
        [(2, 2 * SU, SU)],
        "stack_halves",
        after=blocks[1:2],
    )
    fetched = [lax.ppermute(halves, "facet", ring(facets, shift)) for shift in shifts]

    grids = pl.pallas_call(
        functools.partial(grid_kernel, (facets, groups, chans, cap, rows)),
        out_shape=jax.ShapeDtypeStruct((slots, 2 * SU, SU), jnp.float32),
        in_specs=[VMEM] * facets,
        out_specs=VMEM,
        scratch_shapes=[
            pltpu.VMEM((devices, SU), jnp.int32),
            pltpu.SMEM((devices, SU), jnp.int32),
            pltpu.SMEM((devices * cap + UNROLL,), jnp.int32),
        ]
        + [pltpu.VMEM((devices * cap * chans + 8, SU), jnp.float32)] * 4
        + [pltpu.SemaphoreType.DMA],
        compiler_params=PARAMS,
        cost_estimate=pl.CostEstimate(
            flops=4_000_000_000, bytes_accessed=2_000_000, transcendentals=4_000_000
        ),
        name="grid",
    )(*blocks)
    grids, halves, fetched = lax.optimization_barrier((grids, halves, fetched))
    swap = ring(chan_count, 1)
    ours = [halves, *fetched]
    theirs = [lax.ppermute(table, "chan", swap) for table in ours]
    mine, other = pl.pallas_call(
        functools.partial(table_kernel, (facets, meta_row), norm),
        out_shape=[jax.ShapeDtypeStruct((half_rows, 2 * SU), jnp.float32)] * 2,
        in_specs=[VMEM] * (2 + 2 * facets),
        out_specs=[VMEM, VMEM],
        scratch_shapes=[
            pltpu.VMEM((2 * SU, SU), jnp.float32),
            pltpu.VMEM((SU, 2 * SU), jnp.float32),
        ],
        compiler_params=PARAMS,
        cost_estimate=pl.CostEstimate(
            flops=1_000_000_000, bytes_accessed=2_000_000, transcendentals=0
        ),
        name="apply_tables",
    )(grids, here, *ours, *theirs)
    summand = lax.ppermute(other, "chan", swap)
    return (mine + summand).reshape(1, 1, half_rows, 2, SU)


def solution(mesh):
    in_specs = (
        P(("facet", "bl"), "chan", None, None),
        P(("facet", "bl"), None, None),
        P(("facet", "bl")),
        P(("facet", "bl"), None),
        P(),
        P(),
        P(("facet", "bl"), None, None, None, None),
        P("bl", None, None),
    )
    out_specs = P("facet", "bl", "chan", None, None)
    return jax.shard_map(body, mesh=mesh, in_specs=in_specs, out_specs=out_specs, check_vma=False)
```

```python
import functools
import math

import jax
import jax.numpy as jnp
from jax import lax
from jax.experimental import pallas as pl
from jax.experimental.pallas import tpu as pltpu
from jax.sharding import PartitionSpec as P

SU = 128
CH = 8
KERNEL_SPREAD = 1.5
ALPHA = math.sqrt(math.log2(math.e) / (2.0 * KERNEL_SPREAD * KERNEL_SPREAD))
UNROLL = 4
NT = (((1,), (1,)), ((), ()))
VMEM = pl.BlockSpec(memory_space=pltpu.VMEM)
HBM = pl.BlockSpec(memory_space=pltpu.HBM)
ANY = pl.BlockSpec(memory_space=pl.ANY)
PARAMS = pltpu.CompilerParams(vmem_limit_bytes=32 * 1024 * 1024)
ALONE = pltpu.CompilerParams(vmem_limit_bytes=60 * 1024 * 1024)


def partner(index, shift, size):
    if size & (size - 1) == 0:
        return index ^ shift
    return lax.rem(index + shift, size) if isinstance(index, jax.Array) else (index + shift) % size


def source(index, origin, size):
    if size & (size - 1) == 0:
        return index ^ origin
    return lax.rem(index - origin + size, size)


def cos_sin(turns):
    quarter = jnp.floor(4.0 * turns + 0.5)
    angle = (2.0 * math.pi) * (turns - 0.25 * quarter)
    sq = angle * angle
    sine = angle * (
        1.0 + sq * (-1.0 / 6 + sq * (1.0 / 120 + sq * (-1.0 / 5040 + sq * (1.0 / 362880))))
    )
    cosine = 1.0 + sq * (
        -0.5 + sq * (1.0 / 24 + sq * (-1.0 / 720 + sq * (1.0 / 40320 + sq * (-1.0 / 3628800))))
    )
    turn = quarter.astype(jnp.int32) & 3
    odd = (turn & 1) == 1
    cos_out = jnp.where(odd, sine, cosine)
    sin_out = jnp.where(odd, cosine, sine)
    cos_out = jnp.where((turn == 1) | (turn == 2), -cos_out, cos_out)
    sin_out = jnp.where(turn >= 2, -sin_out, sin_out)
    return cos_out, sin_out


def split_bf16(x):
    high = x.astype(jnp.bfloat16)
    low = (x - high.astype(jnp.float32)).astype(jnp.bfloat16)
    return high, low


def three_parts(x):
    parts = []
    for _ in range(3):
        part = x.astype(jnp.bfloat16)
        x = x - part.astype(jnp.float32)
        parts.append(part.astype(jnp.float32))
    return parts


def sort_kernel(sizes, *refs):
    groups, held, chans, cap, rows = sizes
    out_refs = refs[7 : 7 + groups]
    targets = refs[7 + groups : 14 + groups]
    plane_ref, group_ref, samples_b, place_b, offsets_ref, centre_ref, gain_ref = targets
    samples, place, sorted_, filled, sems = refs[14 + groups :]
    facet = lax.axis_index("facet")
    copies = [
        pltpu.make_async_copy(source, target, sems.at[n])
        for n, (source, target) in enumerate(zip(refs[:7], targets))
    ]
    for copy in copies:
        copy.start()
    sorted_[...] = jnp.zeros_like(sorted_)
    for g in range(groups):
        filled[g] = 0
    for copy in copies:
        copy.wait()
    samples[...] = samples_b[...].astype(jnp.float32)
    place[...] = place_b[...].astype(jnp.float32)
    lane = lax.broadcasted_iota(jnp.int32, (1, SU), 1)
    meta = 2 * cap * (chans + 1)
    centre = [
        part
        for axis in range(2)
        for part in three_parts(jnp.full((1, SU), centre_ref[axis, facet], jnp.float32))
    ]
    gains = three_parts(gain_ref[0])
    for g in range(groups):
        numbers = jnp.zeros((1, SU), jnp.float32)
        for axis in range(2):
            offset = offsets_ref[facet, axis, g].astype(jnp.float32)
            numbers = jnp.where(lane == axis, offset, numbers)
        for n, part in enumerate(centre):
            numbers = jnp.where(lane == 2 + n, part, numbers)
        sorted_[g, meta + 1 : meta + 2, :] = numbers
        for n, part in enumerate(gains):
            sorted_[g, meta + 2 + 2 * n : meta + 4 + 2 * n, :] = part
    for i in range(held):
        g = group_ref[0, i]
        k = filled[g]
        filled[g] = k + 1
        for part in range(2):
            at = part * cap * chans + k * chans
            sorted_[g, pl.ds(at, chans), :] = samples[pl.ds(2 * chans * i + part, chans, stride=2), :]
            at = 2 * cap * chans + part * cap + k
            sorted_[g, pl.ds(at, 1), :] = place[2 * i + part : 2 * i + part + 1, :]
        sorted_[g, meta : meta + 1, :] += jnp.where(
            lane == k, (plane_ref[0, i] + 1).astype(jnp.float32), 0.0
        )
    here = lax.axis_index("bl")
    for shift, out_ref in enumerate(out_refs):
        out_ref[...] = sorted_[partner(here, shift, groups)].astype(jnp.bfloat16)


def grid_kernel(sizes, *refs):
    facets, groups, chans, cap, rows = sizes
    packed_refs = refs[:facets]
    grids = refs[facets]
    meta_v, meta_s, order, spots_u, spots_v, turns_real, turns_imag, sem = refs[facets + 1 :]
    devices = facets * groups
    slots = 2 * facets
    lines = cap * chans
    meta_row = 2 * (lines + cap)
    tail = meta_row // 16 * 16
    facet = lax.axis_index("facet")
    group = lax.axis_index("bl")
    chan = lax.axis_index("chan")

    lane = lax.broadcasted_iota(jnp.int32, (1, SU), 1)
    for f in range(facets):
        for g in range(groups):
            meta = packed_refs[f][g, tail : tail + 16, :].astype(jnp.float32)
            d = f * groups + g
            plane = meta[meta_row - tail : meta_row - tail + 1].astype(jnp.int32) - 1
            set_id = jnp.where(lax.rem(plane, groups) == group, 0, 1)
            shift = source(facet, lax.div(plane, groups), facets)
            code = (d * cap + lane) * slots + 2 * shift + set_id
            meta_v[d : d + 1, :] = jnp.where(plane >= 0, code, -1)
            if f == 0 and g == 0:
                numbers = meta[meta_row - tail + 1 : meta_row - tail + 2]
    copy = pltpu.make_async_copy(meta_v, meta_s, sem)
    copy.start()
    grids[...] = jnp.zeros_like(grids)

    def number(n):
        return jnp.broadcast_to(numbers[:, n : n + 1], (lines, SU))

    offset_u = number(0)
    offset_v = number(1)
    along_l = number(2) + number(3) + number(4)
    along_m = number(5) + number(6) + number(7)
    line = lax.broadcasted_iota(jnp.int32, (lines, SU), 0)
    channel = (chan * chans + lax.rem(line, chans)).astype(jnp.float32)
    scale = 1.0 + 0.01 * (channel - 0.5 * (CH - 1))

    def spread_lines(place):
        return jnp.concatenate(
            [jnp.broadcast_to(place[k : k + 1], (chans, SU)) for k in range(cap)], axis=0
        )

    for f in range(facets):
        for g in range(groups):
            at = (f * groups + g) * lines
            wide = packed_refs[f][g].astype(jnp.float32)
            real = wide[:lines]
            imag = wide[lines : 2 * lines]
            along_u = spread_lines(wide[2 * lines : 2 * lines + cap])
            along_v = spread_lines(wide[2 * lines + cap : 2 * (lines + cap)])
            cosine, sine = cos_sin(
                (1.0 / SU) * (scale * (along_u * along_l + along_v * along_m))
            )
            spots_u[at : at + lines, :] = ALPHA * (scale * along_u - offset_u)
            spots_v[at : at + lines, :] = ALPHA * (scale * along_v - offset_v)
            turns_real[at : at + lines, :] = real * cosine - imag * sine
            turns_imag[at : at + lines, :] = real * sine + imag * cosine
    last = devices * lines
    for ref in (spots_u, spots_v, turns_real, turns_imag):
        ref[last : last + 8, :] = jnp.zeros((8, SU), jnp.float32)
    copy.wait()

    count = jnp.int32(0)
    for d in range(devices):
        for k in range(cap):
            code = meta_s[d, k]
            order[count] = code
            count = count + jnp.where(code >= 0, 1, 0)
    for i in range(UNROLL):
        order[count + i] = devices * cap * slots

    cells = ALPHA * lax.broadcasted_iota(jnp.int32, (SU, SU), 0).astype(jnp.float32)

    def profile(spot):
        apart = spot - cells
        return jnp.exp2(-(apart * apart)).astype(jnp.bfloat16)

    def tiled(row):
        return jnp.broadcast_to(row, (16, SU)).astype(jnp.bfloat16)[None]

    def one_block(at):
        code = order[at]
        slot = lax.rem(code, slots)
        base = lax.div(code, slots) * chans
        lefts_real, lefts_imag, rights = [], [], []
        for c in range(chans):
            here = pl.ds(base + c, 1)
            left = profile(spots_u[here, :]).reshape(SU // 16, 16, SU)
            lefts_real.append((left * tiled(turns_real[here, :])).reshape(SU, SU))
            lefts_imag.append((left * tiled(turns_imag[here, :])).reshape(SU, SU))
            rights.append(profile(spots_v[here, :]))
        left = jnp.concatenate(
            [jnp.concatenate(lefts_real, axis=1), jnp.concatenate(lefts_imag, axis=1)], axis=0
        )
        right = jnp.concatenate(rights, axis=1)
        return slot, lax.dot_general(left, right, NT, preferred_element_type=jnp.float32)

    def step(k, carry):
        for slot, part in [one_block(k * UNROLL + i) for i in range(UNROLL)]:
            grids[slot] += part
        return carry

    lax.fori_loop(0, lax.div(count + UNROLL - 1, UNROLL), step, 0)


def copy_kernel(*refs):
    for source, target in zip(refs[: len(refs) // 2], refs[len(refs) // 2 :]):
        target[...] = source[...]


def stack_kernel(count, *refs):
    for n in range(count):
        refs[-1][n] = refs[n][...]


def local(kernel, operands, shapes, name, after=()):
    return pl.pallas_call(
        kernel,
        out_shape=[jax.ShapeDtypeStruct(shape, jnp.bfloat16) for shape in shapes],
        in_specs=[VMEM] * len(operands) + [ANY] * len(after),
        out_specs=[VMEM] * len(shapes),
        compiler_params=PARAMS,
        cost_estimate=pl.CostEstimate(flops=0, bytes_accessed=400_000, transcendentals=0),
        name=name,
    )(*operands, *after)


def table_kernel(sizes, norm, grids, packed, *refs):
    facets, meta_row = sizes
    slots = 2 * facets
    own, ours, theirs = refs[0], refs[1 : 2 + facets - 1], refs[1 + facets : 1 + 2 * facets]
    mine_ref, other_ref, table_f, total = refs[1 + 2 * facets :]
    chan = lax.axis_index("chan")
    first = chan == 0

    def parts(table):
        table_f[...] = table
        return table_f[pl.ds(0, SU, stride=2), :], table_f[pl.ds(1, SU, stride=2), :]

    result = jnp.zeros((SU, 2 * SU), jnp.float32)
    for s in range(slots):
        shift, set_id = divmod(s, 2)

        def table(kind):
            if s == 0:
                return own[kind].astype(jnp.float32)
            if s == 1:
                fetched, given = ours[0][kind], theirs[0][kind]
            else:
                fetched, given = ours[shift][set_id, kind], theirs[shift][set_id, kind]
            return jnp.where(first, given.astype(jnp.float32), fetched.astype(jnp.float32))

        u_real, u_imag = parts(table(0))
        u_side = jnp.concatenate([u_real.T, u_imag.T], axis=1).astype(jnp.bfloat16)
        grid_real = grids[s, :SU, :]
        grid_imag = grids[s, SU:, :]
        inner = jnp.concatenate(
            [
                jnp.concatenate([grid_real, grid_imag], axis=1),
                jnp.concatenate([-grid_imag, grid_real], axis=1),
            ],
            axis=0,
        )
        high, low = split_bf16(inner)
        half = jnp.dot(u_side, high, preferred_element_type=jnp.float32) + jnp.dot(
            u_side, low, preferred_element_type=jnp.float32
        )
        v_real, v_imag = parts(table(1))
        v_side = jnp.concatenate(
            [
                jnp.concatenate([v_real, v_imag], axis=1),
                jnp.concatenate([-v_imag, v_real], axis=1),
            ],
            axis=0,
        ).astype(jnp.bfloat16)
        high, low = split_bf16(half)
        result = (
            result
            + jnp.dot(high, v_side, preferred_element_type=jnp.float32)
            + jnp.dot(low, v_side, preferred_element_type=jnp.float32)
        )
    tail = meta_row // 16 * 16
    wide = packed[0, tail : tail + 16, :].astype(jnp.float32)
    at = meta_row - tail + 2
    gain = (wide[at : at + 2] + wide[at + 2 : at + 4]) + wide[at + 4 : at + 6]
    gain_u = jnp.broadcast_to(gain[0:1], (SU, SU)).T
    gains = gain_u * gain[1:2] * norm
    total[...] = result * jnp.concatenate([gains, gains], axis=1)
    half_rows = mine_ref.shape[0]
    mine_ref[...] = total[pl.ds(pl.multiple_of(chan * half_rows, half_rows), half_rows), :]
    other_ref[...] = total[pl.ds(pl.multiple_of((1 - chan) * half_rows, half_rows), half_rows), :]


def pairs(size, shift):
    return [(n, partner(n, shift, size)) for n in range(size)]


def body(
    visibilities, coords, plane_index, block_group, offsets, facet_centre, tables, antenna_gain
):
    facets = lax.axis_size("facet")
    groups = lax.axis_size("bl")
    chan_count = lax.axis_size("chan")
    held, chans = visibilities.shape[:2]
    devices = facets * groups
    slots = 2 * facets
    cap = max(2, 2 * held // groups)
    meta_row = 2 * cap * (chans + 1)
    rows = -(-(meta_row + 8) // 16) * 16
    half_rows = SU // chan_count
    norm = SU / math.sqrt(visibilities.shape[3] * held * facets * CH)

    own_table = tables.reshape(2, 2 * SU, SU)
    pieces = pl.pallas_call(
        functools.partial(sort_kernel, (groups, held, chans, cap, rows)),
        out_shape=[jax.ShapeDtypeStruct((rows, SU), jnp.bfloat16)] * groups,
        in_specs=[HBM] * 7,
        out_specs=[VMEM] * groups,
        scratch_shapes=[
            pltpu.SMEM((1, held), jnp.int32),
            pltpu.SMEM((1, held), jnp.int32),
            pltpu.VMEM((held * 2 * chans, SU), jnp.bfloat16),
            pltpu.VMEM((held * 2, SU), jnp.bfloat16),
            pltpu.SMEM((facets, 2, groups), jnp.int32),
            pltpu.SMEM((2, facets), jnp.float32),
            pltpu.VMEM((1, 2, SU), jnp.float32),
            pltpu.VMEM((held * 2 * chans, SU), jnp.float32),
            pltpu.VMEM((held * 2, SU), jnp.float32),
            pltpu.VMEM((groups, rows, SU), jnp.float32),
            pltpu.SMEM((groups,), jnp.int32),
            pltpu.SemaphoreType.DMA((7,)),
        ],
        compiler_params=ALONE,
        cost_estimate=pl.CostEstimate(flops=100_000, bytes_accessed=100_000, transcendentals=0),
        name="sort_blocks",
    )(
        plane_index.reshape(1, held),
        block_group.T,
        visibilities.reshape(held * 2 * chans, SU),
        coords.reshape(held * 2, SU),
        offsets.transpose(0, 2, 1),
        facet_centre.T,
        antenna_gain,
    )
    last = chan_count - 1
    shifted = lax.ppermute(
        own_table,
        ("bl", "chan"),
        [(g * chan_count + last, (g + 1) % groups * chan_count + last) for g in range(groups)],
    )
    arrived = [
        lax.ppermute(pieces[shift], "bl", pairs(groups, shift)) for shift in range(1, groups)
    ]
    kept, kept_table = local(
        copy_kernel, [pieces[0], own_table], [(rows, SU), (2, 2 * SU, SU)], "keep_own"
    )
    (here,) = local(
        functools.partial(stack_kernel, groups), [kept, *arrived], [(groups, rows, SU)], "join"
    )
    shifts = range(1, facets)
    blocks = [here] + [lax.ppermute(here, "facet", pairs(facets, shift)) for shift in shifts]
    (both,) = local(
        functools.partial(stack_kernel, 2),
        [kept_table, shifted],
        [(2, 2, 2 * SU, SU)],
        "stack_tables",
        after=blocks[1:2],
    )
    fetched = [
        lax.ppermute(
            both,
            ("facet", "chan"),
            [(f * chan_count + last, t * chan_count + last) for f, t in pairs(facets, shift)],
        )
        for shift in shifts
    ]

    grids = pl.pallas_call(
        functools.partial(grid_kernel, (facets, groups, chans, cap, rows)),
        out_shape=jax.ShapeDtypeStruct((slots, 2 * SU, SU), jnp.float32),
        in_specs=[VMEM] * facets,
        out_specs=VMEM,
        scratch_shapes=[
            pltpu.VMEM((devices, SU), jnp.int32),
            pltpu.SMEM((devices, SU), jnp.int32),
            pltpu.SMEM((devices * cap + UNROLL,), jnp.int32),
        ]
        + [pltpu.VMEM((devices * cap * chans + 8, SU), jnp.float32)] * 4
        + [pltpu.SemaphoreType.DMA],
        compiler_params=PARAMS,
        cost_estimate=pl.CostEstimate(
            flops=4_000_000_000, bytes_accessed=2_000_000, transcendentals=4_000_000
        ),
        name="grid",
    )(*blocks)
    grids, fetched = lax.optimization_barrier((grids, fetched))
    ours = [kept_table, shifted, *fetched]
    theirs = [
        lax.ppermute(table, "chan", [(last, c) for c in range(last)][:1]) for table in ours[1:]
    ]
    mine, other = pl.pallas_call(
        functools.partial(table_kernel, (facets, meta_row), norm),
        out_shape=[jax.ShapeDtypeStruct((half_rows, 2 * SU), jnp.float32)] * 2,
        in_specs=[VMEM] * (3 + 2 * facets),
        out_specs=[VMEM, VMEM],
        scratch_shapes=[
            pltpu.VMEM((2 * SU, SU), jnp.float32),
            pltpu.VMEM((SU, 2 * SU), jnp.float32),
        ],
        compiler_params=PARAMS,
        cost_estimate=pl.CostEstimate(
            flops=1_000_000_000, bytes_accessed=2_000_000, transcendentals=0
        ),
        name="apply_tables",
    )(grids, here, *ours, *theirs)
    summand = lax.ppermute(other, "chan", pairs(chan_count, 1))
    return (mine + summand).reshape(1, 1, half_rows, 2, SU)


def solution(mesh):
    in_specs = (
        P(("facet", "bl"), "chan", None, None),
        P(("facet", "bl"), None, None),
        P(("facet", "bl")),
        P(("facet", "bl"), None),
        P(),
        P(),
        P(("facet", "bl"), None, None, None, None),
        P("bl", None, None),
    )
    out_specs = P("facet", "bl", "chan", None, None)
    return jax.shard_map(body, mesh=mesh, in_specs=in_specs, out_specs=out_specs, check_vma=False)
```

```python
import functools
import math

import jax
import jax.numpy as jnp
from jax import lax
from jax.experimental import pallas as pl
from jax.experimental.pallas import tpu as pltpu
from jax.sharding import PartitionSpec as P

SU = 128
CH = 8
KERNEL_SPREAD = 1.5
ALPHA = math.sqrt(math.log2(math.e) / (2.0 * KERNEL_SPREAD * KERNEL_SPREAD))
UNROLL = 4
NT = (((1,), (1,)), ((), ()))
VMEM = pl.BlockSpec(memory_space=pltpu.VMEM)
HBM = pl.BlockSpec(memory_space=pltpu.HBM)
ANY = pl.BlockSpec(memory_space=pl.ANY)
PARAMS = pltpu.CompilerParams(vmem_limit_bytes=32 * 1024 * 1024)
ALONE = pltpu.CompilerParams(vmem_limit_bytes=60 * 1024 * 1024)


def partner(index, shift, size):
    if size & (size - 1) == 0:
        return index ^ shift
    return lax.rem(index + shift, size) if isinstance(index, jax.Array) else (index + shift) % size


def source(index, origin, size):
    if size & (size - 1) == 0:
        return index ^ origin
    return lax.rem(index - origin + size, size)


def cos_sin(turns):
    quarter = jnp.floor(4.0 * turns + 0.5)
    angle = (2.0 * math.pi) * (turns - 0.25 * quarter)
    sq = angle * angle
    sine = angle * (
        1.0 + sq * (-1.0 / 6 + sq * (1.0 / 120 + sq * (-1.0 / 5040 + sq * (1.0 / 362880))))
    )
    cosine = 1.0 + sq * (
        -0.5 + sq * (1.0 / 24 + sq * (-1.0 / 720 + sq * (1.0 / 40320 + sq * (-1.0 / 3628800))))
    )
    turn = quarter.astype(jnp.int32) & 3
    odd = (turn & 1) == 1
    cos_out = jnp.where(odd, sine, cosine)
    sin_out = jnp.where(odd, cosine, sine)
    cos_out = jnp.where((turn == 1) | (turn == 2), -cos_out, cos_out)
    sin_out = jnp.where(turn >= 2, -sin_out, sin_out)
    return cos_out, sin_out


def split_bf16(x):
    high = x.astype(jnp.bfloat16)
    low = (x - high.astype(jnp.float32)).astype(jnp.bfloat16)
    return high, low


def three_parts(x):
    parts = []
    for _ in range(3):
        part = x.astype(jnp.bfloat16)
        x = x - part.astype(jnp.float32)
        parts.append(part.astype(jnp.float32))
    return parts


def sort_kernel(sizes, *refs):
    groups, held, chans, cap, rows = sizes
    out_refs = refs[7 : 7 + groups]
    targets = refs[7 + groups : 14 + groups]
    plane_ref, group_ref, samples_b, place_b, offsets_ref, centre_ref, gain_ref = targets
    samples, place, sorted_, filled, sems = refs[14 + groups :]
    facet = lax.axis_index("facet")
    copies = [
        pltpu.make_async_copy(source, target, sems.at[n])
        for n, (source, target) in enumerate(zip(refs[:7], targets))
    ]
    for copy in copies:
        copy.start()
    sorted_[...] = jnp.zeros_like(sorted_)
    for g in range(groups):
        filled[g] = 0
    for copy in copies:
        copy.wait()
    samples[...] = samples_b[...].astype(jnp.float32)
    place[...] = place_b[...].astype(jnp.float32)
    lane = lax.broadcasted_iota(jnp.int32, (1, SU), 1)
    meta = 2 * cap * (chans + 1)
    centre = [
        part
        for axis in range(2)
        for part in three_parts(jnp.full((1, SU), centre_ref[axis, facet], jnp.float32))
    ]
    gains = three_parts(gain_ref[0])
    for g in range(groups):
        numbers = jnp.zeros((1, SU), jnp.float32)
        for axis in range(2):
            offset = offsets_ref[facet, axis, g].astype(jnp.float32)
            numbers = jnp.where(lane == axis, offset, numbers)
        for n, part in enumerate(centre):
            numbers = jnp.where(lane == 2 + n, part, numbers)
        sorted_[g, meta + 1 : meta + 2, :] = numbers
        for n, part in enumerate(gains):
            sorted_[g, meta + 2 + 2 * n : meta + 4 + 2 * n, :] = part
    for i in range(held):
        g = group_ref[0, i]
        k = filled[g]
        filled[g] = k + 1
        for part in range(2):
            at = part * cap * chans + k * chans
            sorted_[g, pl.ds(at, chans), :] = samples[pl.ds(2 * chans * i + part, chans, stride=2), :]
            at = 2 * cap * chans + part * cap + k
            sorted_[g, pl.ds(at, 1), :] = place[2 * i + part : 2 * i + part + 1, :]
        sorted_[g, meta : meta + 1, :] += jnp.where(
            lane == k, (plane_ref[0, i] + 1).astype(jnp.float32), 0.0
        )
    here = lax.axis_index("bl")
    for shift, out_ref in enumerate(out_refs):
        out_ref[...] = sorted_[partner(here, shift, groups)].astype(jnp.bfloat16)


def grid_kernel(sizes, *refs):
    facets, groups, chans, cap, rows = sizes
    packed_refs = refs[:facets]
    grids = refs[facets]
    meta_v, meta_s, order, spots_u, spots_v, turns_real, turns_imag, sem = refs[facets + 1 :]
    devices = facets * groups
    slots = 2 * facets
    lines = cap * chans
    meta_row = 2 * (lines + cap)
    tail = meta_row // 16 * 16
    facet = lax.axis_index("facet")
    group = lax.axis_index("bl")
    chan = lax.axis_index("chan")

    lane = lax.broadcasted_iota(jnp.int32, (1, SU), 1)
    for f in range(facets):
        for g in range(groups):
            meta = packed_refs[f][g, tail : tail + 16, :].astype(jnp.float32)
            d = f * groups + g
            plane = meta[meta_row - tail : meta_row - tail + 1].astype(jnp.int32) - 1
            set_id = jnp.where(lax.rem(plane, groups) == group, 0, 1)
            shift = source(facet, lax.div(plane, groups), facets)
            code = (d * cap + lane) * slots + 2 * shift + set_id
            meta_v[d : d + 1, :] = jnp.where(plane >= 0, code, -1)
            if f == 0 and g == 0:
                numbers = meta[meta_row - tail + 1 : meta_row - tail + 2]
    copy = pltpu.make_async_copy(meta_v, meta_s, sem)
    copy.start()
    grids[...] = jnp.zeros_like(grids)

    def number(n):
        return jnp.broadcast_to(numbers[:, n : n + 1], (lines, SU))

    offset_u = number(0)
    offset_v = number(1)
    along_l = number(2) + number(3) + number(4)
    along_m = number(5) + number(6) + number(7)
    line = lax.broadcasted_iota(jnp.int32, (lines, SU), 0)
    channel = (chan * chans + lax.rem(line, chans)).astype(jnp.float32)
    scale = 1.0 + 0.01 * (channel - 0.5 * (CH - 1))

    def spread_lines(place):
        return jnp.concatenate(
            [jnp.broadcast_to(place[k : k + 1], (chans, SU)) for k in range(cap)], axis=0
        )

    for f in range(facets):
        for g in range(groups):
            at = (f * groups + g) * lines
            wide = packed_refs[f][g].astype(jnp.float32)
            real = wide[:lines]
            imag = wide[lines : 2 * lines]
            along_u = spread_lines(wide[2 * lines : 2 * lines + cap])
            along_v = spread_lines(wide[2 * lines + cap : 2 * (lines + cap)])
            cosine, sine = cos_sin(
                (1.0 / SU) * (scale * (along_u * along_l + along_v * along_m))
            )
            spots_u[at : at + lines, :] = ALPHA * (scale * along_u - offset_u)
            spots_v[at : at + lines, :] = ALPHA * (scale * along_v - offset_v)
            turns_real[at : at + lines, :] = real * cosine - imag * sine
            turns_imag[at : at + lines, :] = real * sine + imag * cosine
    last = devices * lines
    for ref in (spots_u, spots_v, turns_real, turns_imag):
        ref[last : last + 8, :] = jnp.zeros((8, SU), jnp.float32)
    copy.wait()

    count = jnp.int32(0)
    for d in range(devices):
        for k in range(cap):
            code = meta_s[d, k]
            order[count] = code
            count = count + jnp.where(code >= 0, 1, 0)
    for i in range(UNROLL):
        order[count + i] = devices * cap * slots

    cells = ALPHA * lax.broadcasted_iota(jnp.int32, (SU, SU), 0).astype(jnp.float32)

    def profile(spot):
        apart = spot - cells
        return jnp.exp2(-(apart * apart)).astype(jnp.bfloat16)

    def tiled(row):
        return jnp.broadcast_to(row, (16, SU)).astype(jnp.bfloat16)[None]

    def one_block(at):
        code = order[at]
        slot = lax.rem(code, slots)
        base = lax.div(code, slots) * chans
        lefts_real, lefts_imag, rights = [], [], []
        for c in range(chans):
            here = pl.ds(base + c, 1)
            left = profile(spots_u[here, :]).reshape(SU // 16, 16, SU)
            lefts_real.append((left * tiled(turns_real[here, :])).reshape(SU, SU))
            lefts_imag.append((left * tiled(turns_imag[here, :])).reshape(SU, SU))
            rights.append(profile(spots_v[here, :]))
        left = jnp.concatenate(
            [jnp.concatenate(lefts_real, axis=1), jnp.concatenate(lefts_imag, axis=1)], axis=0
        )
        right = jnp.concatenate(rights, axis=1)
        return slot, lax.dot_general(left, right, NT, preferred_element_type=jnp.float32)

    def step(k, carry):
        for slot, part in [one_block(k * UNROLL + i) for i in range(UNROLL)]:
            grids[slot] += part
        return carry

    lax.fori_loop(0, lax.div(count + UNROLL - 1, UNROLL), step, 0)


def keep_kernel(piece, table, kept, half):
    kept[...] = piece[...]
    half[...] = table[lax.axis_index("chan")]


def stack_kernel(count, *refs):
    for n in range(count):
        refs[-1][n] = refs[n][...]


def local(kernel, operands, shapes, name, after=()):
    return pl.pallas_call(
        kernel,
        out_shape=[jax.ShapeDtypeStruct(shape, jnp.bfloat16) for shape in shapes],
        in_specs=[VMEM] * len(operands) + [ANY] * len(after),
        out_specs=[VMEM] * len(shapes),
        compiler_params=PARAMS,
        cost_estimate=pl.CostEstimate(flops=0, bytes_accessed=400_000, transcendentals=0),
        name=name,
    )(*operands, *after)


def table_kernel(sizes, norm, grids, packed, *refs):
    facets, meta_row = sizes
    slots = 2 * facets
    ours, theirs = refs[:facets], refs[facets:slots]
    mine_ref, other_ref, table_f, total = refs[slots:]
    chan = lax.axis_index("chan")
    first = chan == 0

    def parts(table):
        table_f[...] = table
        return table_f[pl.ds(0, SU, stride=2), :], table_f[pl.ds(1, SU, stride=2), :]

    result = jnp.zeros((SU, 2 * SU), jnp.float32)
    for s in range(slots):
        shift, set_id = divmod(s, 2)
        fetched = ours[shift][set_id].astype(jnp.float32)
        swapped = theirs[shift][set_id].astype(jnp.float32)
        u_real, u_imag = parts(jnp.where(first, fetched, swapped))
        u_side = jnp.concatenate([u_real.T, u_imag.T], axis=1).astype(jnp.bfloat16)
        grid_real = grids[s, :SU, :]
        grid_imag = grids[s, SU:, :]
        inner = jnp.concatenate(
            [
                jnp.concatenate([grid_real, grid_imag], axis=1),
                jnp.concatenate([-grid_imag, grid_real], axis=1),
            ],
            axis=0,
        )
        high, low = split_bf16(inner)
        half = jnp.dot(u_side, high, preferred_element_type=jnp.float32) + jnp.dot(
            u_side, low, preferred_element_type=jnp.float32
        )
        v_real, v_imag = parts(jnp.where(first, swapped, fetched))
        v_side = jnp.concatenate(
            [
                jnp.concatenate([v_real, v_imag], axis=1),
                jnp.concatenate([-v_imag, v_real], axis=1),
            ],
            axis=0,
        ).astype(jnp.bfloat16)
        high, low = split_bf16(half)
        result = (
            result
            + jnp.dot(high, v_side, preferred_element_type=jnp.float32)
            + jnp.dot(low, v_side, preferred_element_type=jnp.float32)
        )
    tail = meta_row // 16 * 16
    wide = packed[0, tail : tail + 16, :].astype(jnp.float32)
    at = meta_row - tail + 2
    gain = (wide[at : at + 2] + wide[at + 2 : at + 4]) + wide[at + 4 : at + 6]
    gain_u = jnp.broadcast_to(gain[0:1], (SU, SU)).T
    gains = gain_u * gain[1:2] * norm
    total[...] = result * jnp.concatenate([gains, gains], axis=1)
    half_rows = mine_ref.shape[0]
    mine_ref[...] = total[pl.ds(pl.multiple_of(chan * half_rows, half_rows), half_rows), :]
    other_ref[...] = total[pl.ds(pl.multiple_of((1 - chan) * half_rows, half_rows), half_rows), :]


def pairs(size, shift):
    return [(n, partner(n, shift, size)) for n in range(size)]


def body(
    visibilities, coords, plane_index, block_group, offsets, facet_centre, tables, antenna_gain
):
    facets = lax.axis_size("facet")
    groups = lax.axis_size("bl")
    chan_count = lax.axis_size("chan")
    held, chans = visibilities.shape[:2]
    devices = facets * groups
    slots = 2 * facets
    cap = max(2, 2 * held // groups)
    meta_row = 2 * cap * (chans + 1)
    rows = -(-(meta_row + 8) // 16) * 16
    half_rows = SU // chan_count
    norm = SU / math.sqrt(visibilities.shape[3] * held * facets * CH)

    own_table = tables.reshape(2, 2 * SU, SU)
    pieces = pl.pallas_call(
        functools.partial(sort_kernel, (groups, held, chans, cap, rows)),
        out_shape=[jax.ShapeDtypeStruct((rows, SU), jnp.bfloat16)] * groups,
        in_specs=[HBM] * 7,
        out_specs=[VMEM] * groups,
        scratch_shapes=[
            pltpu.SMEM((1, held), jnp.int32),
            pltpu.SMEM((1, held), jnp.int32),
            pltpu.VMEM((held * 2 * chans, SU), jnp.bfloat16),
            pltpu.VMEM((held * 2, SU), jnp.bfloat16),
            pltpu.SMEM((facets, 2, groups), jnp.int32),
            pltpu.SMEM((2, facets), jnp.float32),
            pltpu.VMEM((1, 2, SU), jnp.float32),
            pltpu.VMEM((held * 2 * chans, SU), jnp.float32),
            pltpu.VMEM((held * 2, SU), jnp.float32),
            pltpu.VMEM((groups, rows, SU), jnp.float32),
            pltpu.SMEM((groups,), jnp.int32),
            pltpu.SemaphoreType.DMA((7,)),
        ],
        compiler_params=ALONE,
        cost_estimate=pl.CostEstimate(flops=100_000, bytes_accessed=100_000, transcendentals=0),
        name="sort_blocks",
    )(
        plane_index.reshape(1, held),
        block_group.T,
        visibilities.reshape(held * 2 * chans, SU),
        coords.reshape(held * 2, SU),
        offsets.transpose(0, 2, 1),
        facet_centre.T,
        antenna_gain,
    )
    arrived = [
        lax.ppermute(pieces[shift], "bl", pairs(groups, shift)) for shift in range(1, groups)
    ]
    kept, kept_half = local(
        keep_kernel, [pieces[0], own_table], [(rows, SU), (2 * SU, SU)], "keep_own"
    )
    shifted_half = lax.ppermute(kept_half, "bl", [(g, (g + 1) % groups) for g in range(groups)])
    (here,) = local(
        functools.partial(stack_kernel, groups), [kept, *arrived], [(groups, rows, SU)], "join"
    )
    shifts = range(1, facets)
    blocks = [here] + [lax.ppermute(here, "facet", pairs(facets, shift)) for shift in shifts]
    (halves,) = local(
        functools.partial(stack_kernel, 2),
        [kept_half, shifted_half],
        [(2, 2 * SU, SU)],
        "stack_halves",
        after=blocks[1:2],
    )
    fetched = [lax.ppermute(halves, "facet", pairs(facets, shift)) for shift in shifts]

    grids = pl.pallas_call(
        functools.partial(grid_kernel, (facets, groups, chans, cap, rows)),
        out_shape=jax.ShapeDtypeStruct((slots, 2 * SU, SU), jnp.float32),
        in_specs=[VMEM] * facets,
        out_specs=VMEM,
        scratch_shapes=[
            pltpu.VMEM((devices, SU), jnp.int32),
            pltpu.SMEM((devices, SU), jnp.int32),
            pltpu.SMEM((devices * cap + UNROLL,), jnp.int32),
        ]
        + [pltpu.VMEM((devices * cap * chans + 8, SU), jnp.float32)] * 4
        + [pltpu.SemaphoreType.DMA],
        compiler_params=PARAMS,
        cost_estimate=pl.CostEstimate(
            flops=4_000_000_000, bytes_accessed=2_000_000, transcendentals=4_000_000
        ),
        name="grid",
    )(*blocks)
    swap = pairs(chan_count, 1)
    grids, fetched = lax.optimization_barrier((grids, fetched))
    ours = [halves, *fetched]
    theirs = [lax.ppermute(table, "chan", swap) for table in ours]
    mine, other = pl.pallas_call(
        functools.partial(table_kernel, (facets, meta_row), norm),
        out_shape=[jax.ShapeDtypeStruct((half_rows, 2 * SU), jnp.float32)] * 2,
        in_specs=[VMEM] * (2 + 2 * facets),
        out_specs=[VMEM, VMEM],
        scratch_shapes=[
            pltpu.VMEM((2 * SU, SU), jnp.float32),
            pltpu.VMEM((SU, 2 * SU), jnp.float32),
        ],
        compiler_params=PARAMS,
        cost_estimate=pl.CostEstimate(
            flops=1_000_000_000, bytes_accessed=2_000_000, transcendentals=0
        ),
        name="apply_tables",
    )(grids, here, *ours, *theirs)
    summand = lax.ppermute(other, "chan", swap)
    return (mine + summand).reshape(1, 1, half_rows, 2, SU)


def solution(mesh):
    in_specs = (
        P(("facet", "bl"), "chan", None, None),
        P(("facet", "bl"), None, None),
        P(("facet", "bl")),
        P(("facet", "bl"), None),
        P(),
        P(),
        P(("facet", "bl"), None, None, None, None),
        P("bl", None, None),
    )
    out_specs = P("facet", "bl", "chan", None, None)
    return jax.shard_map(body, mesh=mesh, in_specs=in_specs, out_specs=out_specs, check_vma=False)
```

```python
import functools
import math

import jax
import jax.numpy as jnp
from jax import lax
from jax.experimental import pallas as pl
from jax.experimental.pallas import tpu as pltpu
from jax.sharding import PartitionSpec as P

SU = 128
CH = 8
KERNEL_SPREAD = 1.5
ALPHA = math.sqrt(math.log2(math.e) / (2.0 * KERNEL_SPREAD * KERNEL_SPREAD))
UNROLL = 4
NT = (((1,), (1,)), ((), ()))
VMEM = pl.BlockSpec(memory_space=pltpu.VMEM)
HBM = pl.BlockSpec(memory_space=pltpu.HBM)
PARAMS = pltpu.CompilerParams(vmem_limit_bytes=32 * 1024 * 1024)
ALONE = pltpu.CompilerParams(vmem_limit_bytes=60 * 1024 * 1024)


def cos_sin(turns):
    quarter = jnp.floor(4.0 * turns + 0.5)
    angle = (2.0 * math.pi) * (turns - 0.25 * quarter)
    sq = angle * angle
    sine = angle * (
        1.0 + sq * (-1.0 / 6 + sq * (1.0 / 120 + sq * (-1.0 / 5040 + sq * (1.0 / 362880))))
    )
    cosine = 1.0 + sq * (
        -0.5 + sq * (1.0 / 24 + sq * (-1.0 / 720 + sq * (1.0 / 40320 + sq * (-1.0 / 3628800))))
    )
    turn = quarter.astype(jnp.int32) & 3
    odd = (turn & 1) == 1
    cos_out = jnp.where(odd, sine, cosine)
    sin_out = jnp.where(odd, cosine, sine)
    cos_out = jnp.where((turn == 1) | (turn == 2), -cos_out, cos_out)
    sin_out = jnp.where(turn >= 2, -sin_out, sin_out)
    return cos_out, sin_out


def split_bf16(x):
    high = x.astype(jnp.bfloat16)
    low = (x - high.astype(jnp.float32)).astype(jnp.bfloat16)
    return high, low


def three_parts(x):
    parts = []
    for _ in range(3):
        part = x.astype(jnp.bfloat16)
        x = x - part.astype(jnp.float32)
        parts.append(part.astype(jnp.float32))
    return parts


def sort_kernel(sizes, *refs):
    facets, groups, held, chans, cap, rows = sizes
    out_ref = refs[7]
    targets = refs[8:15]
    plane_ref, group_ref, samples_b, place_b, offsets_ref, centre_ref, gain_ref = targets
    samples, place, sorted_, filled, sems = refs[15:]
    facet = lax.axis_index("facet")
    copies = [
        pltpu.make_async_copy(source, target, sems.at[n])
        for n, (source, target) in enumerate(zip(refs[:7], targets))
    ]
    for copy in copies:
        copy.start()
    sorted_[...] = jnp.zeros_like(sorted_)
    for g in range(groups):
        filled[g] = 0
    for copy in copies:
        copy.wait()
    samples[...] = samples_b[...].astype(jnp.float32)
    place[...] = place_b[...].astype(jnp.float32)
    lane = lax.broadcasted_iota(jnp.int32, (1, SU), 1)
    meta = 2 * cap * (chans + 1)
    centre = [
        part
        for axis in range(2)
        for part in three_parts(jnp.full((1, SU), centre_ref[axis, facet], jnp.float32))
    ]
    gains = three_parts(gain_ref[0])
    for g in range(groups):
        numbers = jnp.zeros((1, SU), jnp.float32)
        for axis in range(2):
            offset = offsets_ref[facet, axis, g].astype(jnp.float32)
            numbers = jnp.where(lane == axis, offset, numbers)
        for n, part in enumerate(centre):
            numbers = jnp.where(lane == 2 + n, part, numbers)
        sorted_[g, meta + 1 : meta + 2, :] = numbers
        for n, part in enumerate(gains):
            sorted_[g, meta + 2 + 2 * n : meta + 4 + 2 * n, :] = part
    for i in range(held):
        g = group_ref[0, i]
        k = filled[g]
        filled[g] = k + 1
        for part in range(2):
            at = part * cap * chans + k * chans
            sorted_[g, pl.ds(at, chans), :] = samples[pl.ds(2 * chans * i + part, chans, stride=2), :]
            at = 2 * cap * chans + part * cap + k
            sorted_[g, pl.ds(at, 1), :] = place[2 * i + part : 2 * i + part + 1, :]
        sorted_[g, meta : meta + 1, :] += jnp.where(
            lane == k, (plane_ref[0, i] + 1).astype(jnp.float32), 0.0
        )
    for g in range(groups):
        rows_of = sorted_[g].astype(jnp.bfloat16)
        for f in range(facets):
            out_ref[f * groups + g] = rows_of


def grid_kernel(sizes, *refs):
    facets, groups, chans, cap, rows = sizes
    packed, grids = refs[:2]
    meta_v, meta_s, order, spots_u, spots_v, turns_real, turns_imag, sem = refs[2:]
    devices = facets * groups
    slots = 2 * facets
    lines = cap * chans
    meta_row = 2 * (lines + cap)
    tail = meta_row // 16 * 16
    facet = lax.axis_index("facet")
    group = lax.axis_index("bl")
    chan = lax.axis_index("chan")

    lane = lax.broadcasted_iota(jnp.int32, (1, SU), 1)
    own = packed[facet * groups + group, tail : tail + 16, :].astype(jnp.float32)
    numbers = own[meta_row - tail + 1 : meta_row - tail + 2]
    for d in range(devices):
        meta = packed[d, tail : tail + 16, :].astype(jnp.float32)
        plane = meta[meta_row - tail : meta_row - tail + 1].astype(jnp.int32) - 1
        set_id = jnp.where(lax.rem(plane, groups) == group, 0, 1)
        code = (d * cap + lane) * slots + 2 * lax.div(plane, groups) + set_id
        meta_v[d : d + 1, :] = jnp.where(plane >= 0, code, -1)
    copy = pltpu.make_async_copy(meta_v, meta_s, sem)
    copy.start()
    grids[...] = jnp.zeros_like(grids)

    def number(n):
        return jnp.broadcast_to(numbers[:, n : n + 1], (lines, SU))

    offset_u = number(0)
    offset_v = number(1)
    along_l = number(2) + number(3) + number(4)
    along_m = number(5) + number(6) + number(7)
    line = lax.broadcasted_iota(jnp.int32, (lines, SU), 0)
    channel = (chan * chans + lax.rem(line, chans)).astype(jnp.float32)
    scale = 1.0 + 0.01 * (channel - 0.5 * (CH - 1))

    def spread_lines(place):
        return jnp.concatenate(
            [jnp.broadcast_to(place[k : k + 1], (chans, SU)) for k in range(cap)], axis=0
        )

    for d in range(devices):
        at = d * lines
        wide = packed[d].astype(jnp.float32)
        real = wide[:lines]
        imag = wide[lines : 2 * lines]
        along_u = spread_lines(wide[2 * lines : 2 * lines + cap])
        along_v = spread_lines(wide[2 * lines + cap : 2 * (lines + cap)])
        cosine, sine = cos_sin((1.0 / SU) * (scale * (along_u * along_l + along_v * along_m)))
        spots_u[at : at + lines, :] = ALPHA * (scale * along_u - offset_u)
        spots_v[at : at + lines, :] = ALPHA * (scale * along_v - offset_v)
        turns_real[at : at + lines, :] = real * cosine - imag * sine
        turns_imag[at : at + lines, :] = real * sine + imag * cosine
    last = devices * lines
    for ref in (spots_u, spots_v, turns_real, turns_imag):
        ref[last : last + 8, :] = jnp.zeros((8, SU), jnp.float32)
    copy.wait()

    count = jnp.int32(0)
    for d in range(devices):
        for k in range(cap):
            code = meta_s[d, k]
            order[count] = code
            count = count + jnp.where(code >= 0, 1, 0)
    for i in range(UNROLL):
        order[count + i] = devices * cap * slots

    cells = ALPHA * lax.broadcasted_iota(jnp.int32, (SU, SU), 0).astype(jnp.float32)

    def profile(spot):
        apart = spot - cells
        return jnp.exp2(-(apart * apart)).astype(jnp.bfloat16)

    def tiled(row):
        return jnp.broadcast_to(row, (16, SU)).astype(jnp.bfloat16)[None]

    def one_block(at):
        code = order[at]
        slot = lax.rem(code, slots)
        base = lax.div(code, slots) * chans
        lefts_real, lefts_imag, rights = [], [], []
        for c in range(chans):
            here = pl.ds(base + c, 1)
            left = profile(spots_u[here, :]).reshape(SU // 16, 16, SU)
            lefts_real.append((left * tiled(turns_real[here, :])).reshape(SU, SU))
            lefts_imag.append((left * tiled(turns_imag[here, :])).reshape(SU, SU))
            rights.append(profile(spots_v[here, :]))
        left = jnp.concatenate(
            [jnp.concatenate(lefts_real, axis=1), jnp.concatenate(lefts_imag, axis=1)], axis=0
        )
        right = jnp.concatenate(rights, axis=1)
        return slot, lax.dot_general(left, right, NT, preferred_element_type=jnp.float32)

    def step(k, carry):
        for slot, part in [one_block(k * UNROLL + i) for i in range(UNROLL)]:
            grids[slot] += part
        return carry

    lax.fori_loop(0, lax.div(count + UNROLL - 1, UNROLL), step, 0)


def spread_kernel(own, shifted, out_ref):
    chan = lax.axis_index("chan")
    for n, ref in enumerate((own, shifted)):
        table = ref[chan]
        for f in range(out_ref.shape[0]):
            out_ref[f, n] = table


def table_kernel(sizes, norm, grids, packed, ours, theirs, mine_ref, other_ref, table_f, total):
    slots, meta_row = sizes
    chan = lax.axis_index("chan")
    first = chan == 0
    own = lax.axis_index("facet") * lax.axis_size("bl") + lax.axis_index("bl")

    def parts(table):
        table_f[...] = table
        return table_f[pl.ds(0, SU, stride=2), :], table_f[pl.ds(1, SU, stride=2), :]

    result = jnp.zeros((SU, 2 * SU), jnp.float32)
    for s in range(slots):
        origin, set_id = divmod(s, 2)
        fetched = ours[origin, set_id].astype(jnp.float32)
        swapped = theirs[origin, set_id].astype(jnp.float32)
        u_real, u_imag = parts(jnp.where(first, fetched, swapped))
        u_side = jnp.concatenate([u_real.T, u_imag.T], axis=1).astype(jnp.bfloat16)
        grid_real = grids[s, :SU, :]
        grid_imag = grids[s, SU:, :]
        inner = jnp.concatenate(
            [
                jnp.concatenate([grid_real, grid_imag], axis=1),
                jnp.concatenate([-grid_imag, grid_real], axis=1),
            ],
            axis=0,
        )
        high, low = split_bf16(inner)
        half = jnp.dot(u_side, high, preferred_element_type=jnp.float32) + jnp.dot(
            u_side, low, preferred_element_type=jnp.float32
        )
        v_real, v_imag = parts(jnp.where(first, swapped, fetched))
        v_side = jnp.concatenate(
            [
                jnp.concatenate([v_real, v_imag], axis=1),
                jnp.concatenate([-v_imag, v_real], axis=1),
            ],
            axis=0,
        ).astype(jnp.bfloat16)
        high, low = split_bf16(half)
        result = (
            result
            + jnp.dot(high, v_side, preferred_element_type=jnp.float32)
            + jnp.dot(low, v_side, preferred_element_type=jnp.float32)
        )
    tail = meta_row // 16 * 16
    wide = packed[own, tail : tail + 16, :].astype(jnp.float32)
    at = meta_row - tail + 2
    gain = (wide[at : at + 2] + wide[at + 2 : at + 4]) + wide[at + 4 : at + 6]
    gain_u = jnp.broadcast_to(gain[0:1], (SU, SU)).T
    gains = gain_u * gain[1:2] * norm
    total[...] = result * jnp.concatenate([gains, gains], axis=1)
    half_rows = mine_ref.shape[0]
    mine_ref[...] = total[pl.ds(pl.multiple_of(chan * half_rows, half_rows), half_rows), :]
    other_ref[...] = total[pl.ds(pl.multiple_of((1 - chan) * half_rows, half_rows), half_rows), :]


def body(
    visibilities, coords, plane_index, block_group, offsets, facet_centre, tables, antenna_gain
):
    facets = lax.axis_size("facet")
    groups = lax.axis_size("bl")
    chan_count = lax.axis_size("chan")
    held, chans = visibilities.shape[:2]
    devices = facets * groups
    slots = 2 * facets
    cap = max(2, 2 * held // groups)
    meta_row = 2 * cap * (chans + 1)
    rows = -(-(meta_row + 8) // 16) * 16
    half_rows = SU // chan_count
    norm = SU / math.sqrt(visibilities.shape[3] * held * facets * CH)

    own_table = tables.reshape(2, 2 * SU, SU)
    packed = pl.pallas_call(
        functools.partial(sort_kernel, (facets, groups, held, chans, cap, rows)),
        out_shape=jax.ShapeDtypeStruct((devices, rows, SU), jnp.bfloat16),
        in_specs=[HBM] * 7,
        out_specs=VMEM,
        scratch_shapes=[
            pltpu.SMEM((1, held), jnp.int32),
            pltpu.SMEM((1, held), jnp.int32),
            pltpu.VMEM((held * 2 * chans, SU), jnp.bfloat16),
            pltpu.VMEM((held * 2, SU), jnp.bfloat16),
            pltpu.SMEM((facets, 2, groups), jnp.int32),
            pltpu.SMEM((2, facets), jnp.float32),
            pltpu.VMEM((1, 2, SU), jnp.float32),
            pltpu.VMEM((held * 2 * chans, SU), jnp.float32),
            pltpu.VMEM((held * 2, SU), jnp.float32),
            pltpu.VMEM((groups, rows, SU), jnp.float32),
            pltpu.SMEM((groups,), jnp.int32),
            pltpu.SemaphoreType.DMA((7,)),
        ],
        compiler_params=ALONE,
        cost_estimate=pl.CostEstimate(flops=100_000, bytes_accessed=100_000, transcendentals=0),
        name="sort_blocks",
    )(
        plane_index.reshape(1, held),
        block_group.T,
        visibilities.reshape(held * 2 * chans, SU),
        coords.reshape(held * 2, SU),
        offsets.transpose(0, 2, 1),
        facet_centre.T,
        antenna_gain,
    )
    blocks = lax.all_to_all(packed, ("facet", "bl"), split_axis=0, concat_axis=0, tiled=True)
    shifted = lax.ppermute(own_table, "bl", [(g, (g + 1) % groups) for g in range(groups)])
    own_table, packed = lax.optimization_barrier((own_table, packed))
    spread = pl.pallas_call(
        spread_kernel,
        out_shape=jax.ShapeDtypeStruct((facets, 2, 2 * SU, SU), jnp.bfloat16),
        in_specs=[VMEM, VMEM],
        out_specs=VMEM,
        compiler_params=PARAMS,
        cost_estimate=pl.CostEstimate(flops=0, bytes_accessed=800_000, transcendentals=0),
        name="spread_tables",
    )(own_table, shifted)
    fetched = lax.all_to_all(spread, "facet", split_axis=0, concat_axis=0, tiled=True)

    grids = pl.pallas_call(
        functools.partial(grid_kernel, (facets, groups, chans, cap, rows)),
        out_shape=jax.ShapeDtypeStruct((slots, 2 * SU, SU), jnp.float32),
        in_specs=[VMEM],
        out_specs=VMEM,
        scratch_shapes=[
            pltpu.VMEM((devices, SU), jnp.int32),
            pltpu.SMEM((devices, SU), jnp.int32),
            pltpu.SMEM((devices * cap + UNROLL,), jnp.int32),
        ]
        + [pltpu.VMEM((devices * cap * chans + 8, SU), jnp.float32)] * 4
        + [pltpu.SemaphoreType.DMA],
        compiler_params=PARAMS,
        cost_estimate=pl.CostEstimate(
            flops=4_000_000_000, bytes_accessed=2_000_000, transcendentals=4_000_000
        ),
        name="grid",
    )(blocks)
    swap = [(c, 1 - c) for c in range(chan_count)]
    grids, fetched = lax.optimization_barrier((grids, fetched))
    swapped = lax.ppermute(fetched, "chan", swap)
    mine, other = pl.pallas_call(
        functools.partial(table_kernel, (slots, meta_row), norm),
        out_shape=[jax.ShapeDtypeStruct((half_rows, 2 * SU), jnp.float32)] * 2,
        in_specs=[VMEM] * 4,
        out_specs=[VMEM, VMEM],
        scratch_shapes=[
            pltpu.VMEM((2 * SU, SU), jnp.float32),
            pltpu.VMEM((SU, 2 * SU), jnp.float32),
        ],
        compiler_params=PARAMS,
        cost_estimate=pl.CostEstimate(
            flops=1_000_000_000, bytes_accessed=2_000_000, transcendentals=0
        ),
        name="apply_tables",
    )(grids, blocks, fetched, swapped)
    summand = lax.ppermute(other, "chan", swap)
    return (mine + summand).reshape(1, 1, half_rows, 2, SU)


def solution(mesh):
    in_specs = (
        P(("facet", "bl"), "chan", None, None),
        P(("facet", "bl"), None, None),
        P(("facet", "bl")),
        P(("facet", "bl"), None),
        P(),
        P(),
        P(("facet", "bl"), None, None, None, None),
        P("bl", None, None),
    )
    out_specs = P("facet", "bl", "chan", None, None)
    return jax.shard_map(body, mesh=mesh, in_specs=in_specs, out_specs=out_specs, check_vma=False)
```

```python
import functools
import math

import jax
import jax.numpy as jnp
from jax import lax
from jax.experimental import pallas as pl
from jax.experimental.pallas import tpu as pltpu
from jax.sharding import PartitionSpec as P

SU = 128
CH = 8
KERNEL_SPREAD = 1.5
ALPHA = math.sqrt(math.log2(math.e) / (2.0 * KERNEL_SPREAD * KERNEL_SPREAD))
UNROLL = 8
REST = 2
NT = (((1,), (1,)), ((), ()))
VMEM = pl.BlockSpec(memory_space=pltpu.VMEM)
HBM = pl.BlockSpec(memory_space=pltpu.HBM)
PARAMS = pltpu.CompilerParams(vmem_limit_bytes=32 * 1024 * 1024)
ALONE = pltpu.CompilerParams(vmem_limit_bytes=60 * 1024 * 1024)


def cos_sin(turns):
    quarter = jnp.floor(4.0 * turns + 0.5)
    angle = (2.0 * math.pi) * (turns - 0.25 * quarter)
    sq = angle * angle
    sine = angle * (
        1.0 + sq * (-1.0 / 6 + sq * (1.0 / 120 + sq * (-1.0 / 5040 + sq * (1.0 / 362880))))
    )
    cosine = 1.0 + sq * (
        -0.5 + sq * (1.0 / 24 + sq * (-1.0 / 720 + sq * (1.0 / 40320 + sq * (-1.0 / 3628800))))
    )
    turn = quarter.astype(jnp.int32) & 3
    odd = (turn & 1) == 1
    cos_out = jnp.where(odd, sine, cosine)
    sin_out = jnp.where(odd, cosine, sine)
    cos_out = jnp.where((turn == 1) | (turn == 2), -cos_out, cos_out)
    sin_out = jnp.where(turn >= 2, -sin_out, sin_out)
    return cos_out, sin_out


def split_bf16(x):
    high = x.astype(jnp.bfloat16)
    low = (x - high.astype(jnp.float32)).astype(jnp.bfloat16)
    return high, low


def three_parts(x):
    parts = []
    for _ in range(3):
        part = x.astype(jnp.bfloat16)
        x = x - part.astype(jnp.float32)
        parts.append(part.astype(jnp.float32))
    return parts


def sort_kernel(sizes, *refs):
    facets, groups, held, chans, cap, rows = sizes
    out_ref = refs[7]
    targets = refs[8:15]
    plane_ref, group_ref, samples_b, place_b, offsets_ref, centre_ref, gain_ref = targets
    samples, place, sorted_, filled, sems = refs[15:]
    facet = lax.axis_index("facet")
    copies = [
        pltpu.make_async_copy(source, target, sems.at[n])
        for n, (source, target) in enumerate(zip(refs[:7], targets))
    ]
    for copy in copies:
        copy.start()
    sorted_[...] = jnp.zeros_like(sorted_)
    for g in range(groups):
        filled[g] = 0
    for copy in copies:
        copy.wait()
    samples[...] = samples_b[...].astype(jnp.float32)
    place[...] = place_b[...].astype(jnp.float32)
    lane = lax.broadcasted_iota(jnp.int32, (1, SU), 1)
    meta = 2 * cap * (chans + 1)
    centre = [
        part
        for axis in range(2)
        for part in three_parts(jnp.full((1, SU), centre_ref[axis, facet], jnp.float32))
    ]
    gains = three_parts(gain_ref[0])
    for g in range(groups):
        numbers = jnp.zeros((1, SU), jnp.float32)
        for axis in range(2):
            offset = offsets_ref[facet, axis, g].astype(jnp.float32)
            numbers = jnp.where(lane == axis, offset, numbers)
        for n, part in enumerate(centre):
            numbers = jnp.where(lane == 2 + n, part, numbers)
        sorted_[g, meta + 1 : meta + 2, :] = numbers
        for n, part in enumerate(gains):
            sorted_[g, meta + 2 + 2 * n : meta + 4 + 2 * n, :] = part
    for i in range(held):
        g = group_ref[0, i]
        k = filled[g]
        filled[g] = k + 1
        for part in range(2):
            at = part * cap * chans + k * chans
            sorted_[g, pl.ds(at, chans), :] = samples[pl.ds(2 * chans * i + part, chans, stride=2), :]
            at = 2 * cap * chans + part * cap + k
            sorted_[g, pl.ds(at, 1), :] = place[2 * i + part : 2 * i + part + 1, :]
        sorted_[g, meta : meta + 1, :] += jnp.where(
            lane == k, (plane_ref[0, i] + 1).astype(jnp.float32), 0.0
        )
    for g in range(groups):
        rows_of = sorted_[g].astype(jnp.bfloat16)
        for f in range(facets):
            out_ref[f * groups + g] = rows_of


def grid_kernel(sizes, *refs):
    facets, groups, chans, cap, rows = sizes
    packed, grids = refs[:2]
    meta_v, meta_s, order, spots_u, spots_v, turns_real, turns_imag, sem = refs[2:]
    devices = facets * groups
    slots = 2 * facets
    lines = cap * chans
    meta_row = 2 * (lines + cap)
    tail = meta_row // 16 * 16
    facet = lax.axis_index("facet")
    group = lax.axis_index("bl")
    chan = lax.axis_index("chan")

    lane = lax.broadcasted_iota(jnp.int32, (1, SU), 1)
    own = packed[facet * groups + group, tail : tail + 16, :].astype(jnp.float32)
    numbers = own[meta_row - tail + 1 : meta_row - tail + 2]
    for d in range(devices):
        meta = packed[d, tail : tail + 16, :].astype(jnp.float32)
        plane = meta[meta_row - tail : meta_row - tail + 1].astype(jnp.int32) - 1
        set_id = jnp.where(lax.rem(plane, groups) == group, 0, 1)
        code = (d * cap + lane) * slots + 2 * lax.div(plane, groups) + set_id
        meta_v[d : d + 1, :] = jnp.where(plane >= 0, code, -1)
    copy = pltpu.make_async_copy(meta_v, meta_s, sem)
    copy.start()
    grids[...] = jnp.zeros_like(grids)

    def number(n):
        return jnp.broadcast_to(numbers[:, n : n + 1], (lines, SU))

    offset_u = number(0)
    offset_v = number(1)
    along_l = number(2) + number(3) + number(4)
    along_m = number(5) + number(6) + number(7)
    line = lax.broadcasted_iota(jnp.int32, (lines, SU), 0)
    channel = (chan * chans + lax.rem(line, chans)).astype(jnp.float32)
    scale = 1.0 + 0.01 * (channel - 0.5 * (CH - 1))

    def spread_lines(place):
        return jnp.concatenate(
            [jnp.broadcast_to(place[k : k + 1], (chans, SU)) for k in range(cap)], axis=0
        )

    for d in range(devices):
        at = d * lines
        wide = packed[d].astype(jnp.float32)
        real = wide[:lines]
        imag = wide[lines : 2 * lines]
        along_u = spread_lines(wide[2 * lines : 2 * lines + cap])
        along_v = spread_lines(wide[2 * lines + cap : 2 * (lines + cap)])
        cosine, sine = cos_sin((1.0 / SU) * (scale * (along_u * along_l + along_v * along_m)))
        spots_u[at : at + lines, :] = ALPHA * (scale * along_u - offset_u)
        spots_v[at : at + lines, :] = ALPHA * (scale * along_v - offset_v)
        turns_real[at : at + lines, :] = real * cosine - imag * sine
        turns_imag[at : at + lines, :] = real * sine + imag * cosine
    last = devices * lines
    for ref in (spots_u, spots_v, turns_real, turns_imag):
        ref[last : last + 8, :] = jnp.zeros((8, SU), jnp.float32)
    copy.wait()

    count = jnp.int32(0)
    for d in range(devices):
        for k in range(cap):
            code = meta_s[d, k]
            order[count] = code
            count = count + jnp.where(code >= 0, 1, 0)
    for i in range(REST):
        order[count + i] = devices * cap * slots

    cells = ALPHA * lax.broadcasted_iota(jnp.int32, (SU, SU), 0).astype(jnp.float32)

    def profile(spot):
        apart = spot - cells
        return jnp.exp2(-(apart * apart)).astype(jnp.bfloat16)

    def tiled(row):
        return jnp.broadcast_to(row, (16, SU)).astype(jnp.bfloat16)[None]

    def one_block(at):
        code = order[at]
        slot = lax.rem(code, slots)
        base = lax.div(code, slots) * chans
        lefts_real, lefts_imag, rights = [], [], []
        for c in range(chans):
            here = pl.ds(base + c, 1)
            left = profile(spots_u[here, :]).reshape(SU // 16, 16, SU)
            lefts_real.append((left * tiled(turns_real[here, :])).reshape(SU, SU))
            lefts_imag.append((left * tiled(turns_imag[here, :])).reshape(SU, SU))
            rights.append(profile(spots_v[here, :]))
        left = jnp.concatenate(
            [jnp.concatenate(lefts_real, axis=1), jnp.concatenate(lefts_imag, axis=1)], axis=0
        )
        right = jnp.concatenate(rights, axis=1)
        return slot, lax.dot_general(left, right, NT, preferred_element_type=jnp.float32)

    def steps(first, blocks, number):
        def step(k, carry):
            for slot, part in [one_block(first + k * blocks + i) for i in range(blocks)]:
                grids[slot] += part
            return carry

        lax.fori_loop(0, number, step, 0)

    whole = lax.div(count, UNROLL)
    steps(0, UNROLL, whole)
    steps(whole * UNROLL, REST, lax.div(lax.rem(count, UNROLL) + REST - 1, REST))


def spread_kernel(own, out_ref):
    table = own[lax.axis_index("chan")]
    for f in range(out_ref.shape[0]):
        out_ref[f] = table


def table_kernel(sizes, norm, grids, packed, *refs):
    slots, meta_row = sizes
    ours, theirs = refs[:2], refs[2:4]
    mine_ref, other_ref, table_f, total = refs[4:]
    chan = lax.axis_index("chan")
    first = chan == 0
    own = lax.axis_index("facet") * lax.axis_size("bl") + lax.axis_index("bl")

    def parts(table):
        table_f[...] = table
        return table_f[pl.ds(0, SU, stride=2), :], table_f[pl.ds(1, SU, stride=2), :]

    result = jnp.zeros((SU, 2 * SU), jnp.float32)
    for s in range(slots):
        origin, set_id = divmod(s, 2)
        fetched = ours[set_id][origin].astype(jnp.float32)
        swapped = theirs[set_id][origin].astype(jnp.float32)
        u_real, u_imag = parts(jnp.where(first, fetched, swapped))
        u_side = jnp.concatenate([u_real.T, u_imag.T], axis=1).astype(jnp.bfloat16)
        grid_real = grids[s, :SU, :]
        grid_imag = grids[s, SU:, :]
        inner = jnp.concatenate(
            [
                jnp.concatenate([grid_real, grid_imag], axis=1),
                jnp.concatenate([-grid_imag, grid_real], axis=1),
            ],
            axis=0,
        )
        high, low = split_bf16(inner)
        half = jnp.dot(u_side, high, preferred_element_type=jnp.float32) + jnp.dot(
            u_side, low, preferred_element_type=jnp.float32
        )
        v_real, v_imag = parts(jnp.where(first, swapped, fetched))
        v_side = jnp.concatenate(
            [
                jnp.concatenate([v_real, v_imag], axis=1),
                jnp.concatenate([-v_imag, v_real], axis=1),
            ],
            axis=0,
        ).astype(jnp.bfloat16)
        high, low = split_bf16(half)
        result = (
            result
            + jnp.dot(high, v_side, preferred_element_type=jnp.float32)
            + jnp.dot(low, v_side, preferred_element_type=jnp.float32)
        )
    tail = meta_row // 16 * 16
    wide = packed[own, tail : tail + 16, :].astype(jnp.float32)
    at = meta_row - tail + 2
    gain = (wide[at : at + 2] + wide[at + 2 : at + 4]) + wide[at + 4 : at + 6]
    gain_u = jnp.broadcast_to(gain[0:1], (SU, SU)).T
    gains = gain_u * gain[1:2] * norm
    total[...] = result * jnp.concatenate([gains, gains], axis=1)
    half_rows = mine_ref.shape[0]
    mine_ref[...] = total[pl.ds(pl.multiple_of(chan * half_rows, half_rows), half_rows), :]
    other_ref[...] = total[pl.ds(pl.multiple_of((1 - chan) * half_rows, half_rows), half_rows), :]


def body(
    visibilities, coords, plane_index, block_group, offsets, facet_centre, tables, antenna_gain
):
    facets = lax.axis_size("facet")
    groups = lax.axis_size("bl")
    chan_count = lax.axis_size("chan")
    held, chans = visibilities.shape[:2]
    devices = facets * groups
    slots = 2 * facets
    cap = max(2, 2 * held // groups)
    meta_row = 2 * cap * (chans + 1)
    rows = -(-(meta_row + 8) // 16) * 16
    half_rows = SU // chan_count
    norm = SU / math.sqrt(visibilities.shape[3] * held * facets * CH)

    own_table = tables.reshape(2, 2 * SU, SU)
    packed = pl.pallas_call(
        functools.partial(sort_kernel, (facets, groups, held, chans, cap, rows)),
        out_shape=jax.ShapeDtypeStruct((devices, rows, SU), jnp.bfloat16),
        in_specs=[HBM] * 7,
        out_specs=VMEM,
        scratch_shapes=[
            pltpu.SMEM((1, held), jnp.int32),
            pltpu.SMEM((1, held), jnp.int32),
            pltpu.VMEM((held * 2 * chans, SU), jnp.bfloat16),
            pltpu.VMEM((held * 2, SU), jnp.bfloat16),
            pltpu.SMEM((facets, 2, groups), jnp.int32),
            pltpu.SMEM((2, facets), jnp.float32),
            pltpu.VMEM((1, 2, SU), jnp.float32),
            pltpu.VMEM((held * 2 * chans, SU), jnp.float32),
            pltpu.VMEM((held * 2, SU), jnp.float32),
            pltpu.VMEM((groups, rows, SU), jnp.float32),
            pltpu.SMEM((groups,), jnp.int32),
            pltpu.SemaphoreType.DMA((7,)),
        ],
        compiler_params=ALONE,
        cost_estimate=pl.CostEstimate(flops=100_000, bytes_accessed=100_000, transcendentals=0),
        name="sort_blocks",
    )(
        plane_index.reshape(1, held),
        block_group.T,
        visibilities.reshape(held * 2 * chans, SU),
        coords.reshape(held * 2, SU),
        offsets.transpose(0, 2, 1),
        facet_centre.T,
        antenna_gain,
    )
    blocks = lax.all_to_all(packed, ("facet", "bl"), split_axis=0, concat_axis=0, tiled=True)
    own_table, packed = lax.optimization_barrier((own_table, packed))
    spread = pl.pallas_call(
        spread_kernel,
        out_shape=jax.ShapeDtypeStruct((facets, 2 * SU, SU), jnp.bfloat16),
        in_specs=[VMEM],
        out_specs=VMEM,
        compiler_params=PARAMS,
        cost_estimate=pl.CostEstimate(flops=0, bytes_accessed=400_000, transcendentals=0),
        name="spread_tables",
    )(own_table)
    swap = [(c, 1 - c) for c in range(chan_count)]
    fetched = lax.all_to_all(spread, "facet", split_axis=0, concat_axis=0, tiled=True)
    fetched_swapped = lax.ppermute(fetched, "chan", swap)
    shifted = lax.ppermute(fetched, "bl", [(g, (g + 1) % groups) for g in range(groups)])

    grids = pl.pallas_call(
        functools.partial(grid_kernel, (facets, groups, chans, cap, rows)),
        out_shape=jax.ShapeDtypeStruct((slots, 2 * SU, SU), jnp.float32),
        in_specs=[VMEM],
        out_specs=VMEM,
        scratch_shapes=[
            pltpu.VMEM((devices, SU), jnp.int32),
            pltpu.SMEM((devices, SU), jnp.int32),
            pltpu.SMEM((devices * cap + REST,), jnp.int32),
        ]
        + [pltpu.VMEM((devices * cap * chans + 8, SU), jnp.float32)] * 4
        + [pltpu.SemaphoreType.DMA],
        compiler_params=PARAMS,
        cost_estimate=pl.CostEstimate(
            flops=4_000_000_000, bytes_accessed=2_000_000, transcendentals=4_000_000
        ),
        name="grid",
    )(blocks)
    grids, shifted = lax.optimization_barrier((grids, shifted))
    shifted_swapped = lax.ppermute(shifted, "chan", swap)
    mine, other = pl.pallas_call(
        functools.partial(table_kernel, (slots, meta_row), norm),
        out_shape=[jax.ShapeDtypeStruct((half_rows, 2 * SU), jnp.float32)] * 2,
        in_specs=[VMEM] * 6,
        out_specs=[VMEM, VMEM],
        scratch_shapes=[
            pltpu.VMEM((2 * SU, SU), jnp.float32),
            pltpu.VMEM((SU, 2 * SU), jnp.float32),
        ],
        compiler_params=PARAMS,
        cost_estimate=pl.CostEstimate(
            flops=1_000_000_000, bytes_accessed=2_000_000, transcendentals=0
        ),
        name="apply_tables",
    )(grids, blocks, fetched, shifted, fetched_swapped, shifted_swapped)
    summand = lax.ppermute(other, "chan", swap)
    return (mine + summand).reshape(1, 1, half_rows, 2, SU)


def solution(mesh):
    in_specs = (
        P(("facet", "bl"), "chan", None, None),
        P(("facet", "bl"), None, None),
        P(("facet", "bl")),
        P(("facet", "bl"), None),
        P(),
        P(),
        P(("facet", "bl"), None, None, None, None),
        P("bl", None, None),
    )
    out_specs = P("facet", "bl", "chan", None, None)
    return jax.shard_map(body, mesh=mesh, in_specs=in_specs, out_specs=out_specs, check_vma=False)
```

```python
import functools
import math

import jax
import jax.numpy as jnp
from jax import lax
from jax.experimental import pallas as pl
from jax.experimental.pallas import tpu as pltpu
from jax.sharding import PartitionSpec as P

SU = 128
CH = 8
KERNEL_SPREAD = 1.5
ALPHA = math.sqrt(math.log2(math.e) / (2.0 * KERNEL_SPREAD * KERNEL_SPREAD))
UNROLL = 8
REST = 2
NT = (((1,), (1,)), ((), ()))
VMEM = pl.BlockSpec(memory_space=pltpu.VMEM)
HBM = pl.BlockSpec(memory_space=pltpu.HBM)
PARAMS = pltpu.CompilerParams(vmem_limit_bytes=32 * 1024 * 1024)


def cos_sin(turns):
    quarter = jnp.floor(4.0 * turns + 0.5)
    angle = (2.0 * math.pi) * (turns - 0.25 * quarter)
    sq = angle * angle
    sine = angle * (
        1.0 + sq * (-1.0 / 6 + sq * (1.0 / 120 + sq * (-1.0 / 5040 + sq * (1.0 / 362880))))
    )
    cosine = 1.0 + sq * (
        -0.5 + sq * (1.0 / 24 + sq * (-1.0 / 720 + sq * (1.0 / 40320 + sq * (-1.0 / 3628800))))
    )
    turn = quarter.astype(jnp.int32) & 3
    odd = (turn & 1) == 1
    cos_out = jnp.where(odd, sine, cosine)
    sin_out = jnp.where(odd, cosine, sine)
    cos_out = jnp.where((turn == 1) | (turn == 2), -cos_out, cos_out)
    sin_out = jnp.where(turn >= 2, -sin_out, sin_out)
    return cos_out, sin_out


def split_bf16(x):
    high = x.astype(jnp.bfloat16)
    low = (x - high.astype(jnp.float32)).astype(jnp.bfloat16)
    return high, low


def three_parts(x):
    parts = []
    for _ in range(3):
        part = x.astype(jnp.bfloat16)
        x = x - part.astype(jnp.float32)
        parts.append(part.astype(jnp.float32))
    return parts


def sort_kernel(sizes, *refs):
    groups, held, chans, cap, rows = sizes
    table_hbm, send, keep, half = refs[7:11]
    targets = refs[11:18]
    plane_ref, group_ref, samples_b, place_b, offsets_ref, centre_ref, gain_ref = targets
    samples, place, sorted_, filled, sems = refs[18:]
    facet = lax.axis_index("facet")
    copies = [
        pltpu.make_async_copy(source, target, sems.at[n])
        for n, (source, target) in enumerate(zip(refs[:7], targets))
    ]
    table = pltpu.make_async_copy(table_hbm.at[lax.axis_index("chan")], half, sems.at[7])
    for copy in copies + [table]:
        copy.start()
    sorted_[...] = jnp.zeros_like(sorted_)
    for g in range(groups):
        filled[g] = 0
    for copy in copies:
        copy.wait()
    samples[...] = samples_b[...].astype(jnp.float32)
    place[...] = place_b[...].astype(jnp.float32)
    lane = lax.broadcasted_iota(jnp.int32, (1, SU), 1)
    meta = 2 * cap * (chans + 1)
    centre = [
        part
        for axis in range(2)
        for part in three_parts(jnp.full((1, SU), centre_ref[axis, facet], jnp.float32))
    ]
    gains = three_parts(gain_ref[0])
    for g in range(groups):
        numbers = jnp.zeros((1, SU), jnp.float32)
        for axis in range(2):
            offset = offsets_ref[facet, axis, g].astype(jnp.float32)
            numbers = jnp.where(lane == axis, offset, numbers)
        for n, part in enumerate(centre):
            numbers = jnp.where(lane == 2 + n, part, numbers)
        sorted_[g, meta + 1 : meta + 2, :] = numbers
        for n, part in enumerate(gains):
            sorted_[g, meta + 2 + 2 * n : meta + 4 + 2 * n, :] = part
    for i in range(held):
        g = group_ref[0, i]
        k = filled[g]
        filled[g] = k + 1
        for part in range(2):
            at = part * cap * chans + k * chans
            sorted_[g, pl.ds(at, chans), :] = samples[pl.ds(2 * chans * i + part, chans, stride=2), :]
            at = 2 * cap * chans + part * cap + k
            sorted_[g, pl.ds(at, 1), :] = place[2 * i + part : 2 * i + part + 1, :]
        sorted_[g, meta : meta + 1, :] += jnp.where(
            lane == k, (plane_ref[0, i] + 1).astype(jnp.float32), 0.0
        )
    here = lax.axis_index("bl")
    for step in range(groups):
        target = (keep, send)[step % 2]
        target[step // 2, 0] = sorted_[here ^ step].astype(jnp.bfloat16)
    table.wait()


def fold_kernel(keep, arrived, *refs):
    count = keep.shape[1]
    for n in range(keep.shape[0]):
        target = refs[n % 2]
        target[n // 2, :count] = keep[n]
        target[n // 2, count:] = arrived[n]


def grid_kernel(sizes, *refs):
    facets, groups, chans, cap, rows = sizes
    halves, grids = refs[:2], refs[2]
    meta_v, meta_s, order, spots_u, spots_v, turns_real, turns_imag, sem = refs[3:]
    pieces = [ref.at[n] for ref in halves for n in range(ref.shape[0])]
    devices = facets * groups
    slots = 2 * facets
    lines = cap * chans
    meta_row = 2 * (lines + cap)
    tail = meta_row // 16 * 16
    facet = lax.axis_index("facet")
    group = lax.axis_index("bl")
    chan = lax.axis_index("chan")

    lane = lax.broadcasted_iota(jnp.int32, (1, SU), 1)
    own = pieces[0][tail : tail + 16, :].astype(jnp.float32)
    numbers = own[meta_row - tail + 1 : meta_row - tail + 2]
    for d in range(devices):
        meta = pieces[d][tail : tail + 16, :].astype(jnp.float32)
        plane = meta[meta_row - tail : meta_row - tail + 1].astype(jnp.int32) - 1
        set_id = jnp.where(lax.rem(plane, groups) == group, 0, 1)
        code = (d * cap + lane) * slots + 2 * (lax.div(plane, groups) ^ facet) + set_id
        meta_v[d : d + 1, :] = jnp.where(plane >= 0, code, -1)
    copy = pltpu.make_async_copy(meta_v, meta_s, sem)
    copy.start()
    grids[...] = jnp.zeros_like(grids)

    def number(n):
        return jnp.broadcast_to(numbers[:, n : n + 1], (lines, SU))

    offset_u = number(0)
    offset_v = number(1)
    along_l = number(2) + number(3) + number(4)
    along_m = number(5) + number(6) + number(7)
    line = lax.broadcasted_iota(jnp.int32, (lines, SU), 0)
    channel = (chan * chans + lax.rem(line, chans)).astype(jnp.float32)
    scale = 1.0 + 0.01 * (channel - 0.5 * (CH - 1))

    def spread_lines(place):
        return jnp.concatenate(
            [jnp.broadcast_to(place[k : k + 1], (chans, SU)) for k in range(cap)], axis=0
        )

    for d in range(devices):
        at = d * lines
        wide = pieces[d][...].astype(jnp.float32)
        real = wide[:lines]
        imag = wide[lines : 2 * lines]
        along_u = spread_lines(wide[2 * lines : 2 * lines + cap])
        along_v = spread_lines(wide[2 * lines + cap : 2 * (lines + cap)])
        cosine, sine = cos_sin((1.0 / SU) * (scale * (along_u * along_l + along_v * along_m)))
        spots_u[at : at + lines, :] = ALPHA * (scale * along_u - offset_u)
        spots_v[at : at + lines, :] = ALPHA * (scale * along_v - offset_v)
        turns_real[at : at + lines, :] = real * cosine - imag * sine
        turns_imag[at : at + lines, :] = real * sine + imag * cosine
    last = devices * lines
    for ref in (spots_u, spots_v, turns_real, turns_imag):
        ref[last : last + 8, :] = jnp.zeros((8, SU), jnp.float32)
    copy.wait()

    count = jnp.int32(0)
    for d in range(devices):
        for k in range(cap):
            code = meta_s[d, k]
            order[count] = code
            count = count + jnp.where(code >= 0, 1, 0)
    for i in range(REST):
        order[count + i] = devices * cap * slots

    cells = ALPHA * lax.broadcasted_iota(jnp.int32, (SU, SU), 0).astype(jnp.float32)

    def profile(spot):
        apart = spot - cells
        return jnp.exp2(-(apart * apart)).astype(jnp.bfloat16)

    def tiled(row):
        return jnp.broadcast_to(row, (16, SU)).astype(jnp.bfloat16)[None]

    def one_block(at):
        code = order[at]
        slot = lax.rem(code, slots)
        base = lax.div(code, slots) * chans
        lefts_real, lefts_imag, rights = [], [], []
        for c in range(chans):
            here = pl.ds(base + c, 1)
            left = profile(spots_u[here, :]).reshape(SU // 16, 16, SU)
            lefts_real.append((left * tiled(turns_real[here, :])).reshape(SU, SU))
            lefts_imag.append((left * tiled(turns_imag[here, :])).reshape(SU, SU))
            rights.append(profile(spots_v[here, :]))
        left = jnp.concatenate(
            [jnp.concatenate(lefts_real, axis=1), jnp.concatenate(lefts_imag, axis=1)], axis=0
        )
        right = jnp.concatenate(rights, axis=1)
        return slot, lax.dot_general(left, right, NT, preferred_element_type=jnp.float32)

    def steps(first, blocks, number):
        def step(k, carry):
            for slot, part in [one_block(first + k * blocks + i) for i in range(blocks)]:
                grids[slot] += part
            return carry

        lax.fori_loop(0, number, step, 0)

    whole = lax.div(count, UNROLL)
    steps(0, UNROLL, whole)
    steps(whole * UNROLL, REST, lax.div(lax.rem(count, UNROLL) + REST - 1, REST))


def fold(keep, arrived):
    parts, count = keep.shape[:2]
    shape = (max(parts // 2, 1), 2 * count) + keep.shape[2:]
    outs = min(parts, 2)
    return pl.pallas_call(
        fold_kernel,
        out_shape=[jax.ShapeDtypeStruct(shape, keep.dtype)] * outs,
        in_specs=[VMEM] * 2,
        out_specs=[VMEM] * outs,
        compiler_params=PARAMS,
        cost_estimate=pl.CostEstimate(flops=0, bytes_accessed=200_000, transcendentals=0),
        name="fold",
    )(keep, arrived)


def exchange(value, axis, bit):
    return lax.ppermute(value, axis, [(n, n ^ bit) for n in range(lax.axis_size(axis))])


def gather(value, axis, whole=False):
    bit = 1
    while True:
        arrived = exchange(value, axis, bit)
        bit *= 2
        if bit == lax.axis_size(axis) and not whole:
            return [value, arrived]
        (value,) = fold(value[None], arrived[None])
        value = value[0]
        if bit == lax.axis_size(axis):
            return value


def table_kernel(sizes, norm, grids, packed, *refs):
    slots, meta_row = sizes
    ours, theirs = refs[:2], refs[2:4]
    mine_ref, other_ref, table_f, total = refs[4:]
    chan = lax.axis_index("chan")
    first = chan == 0

    def parts(table):
        table_f[...] = table
        return table_f[pl.ds(0, SU, stride=2), :], table_f[pl.ds(1, SU, stride=2), :]

    result = jnp.zeros((SU, 2 * SU), jnp.float32)
    for s in range(slots):
        origin, set_id = divmod(s, 2)
        fetched = ours[set_id][origin].astype(jnp.float32)
        swapped = theirs[set_id][origin].astype(jnp.float32)
        u_real, u_imag = parts(jnp.where(first, fetched, swapped))
        u_side = jnp.concatenate([u_real.T, u_imag.T], axis=1).astype(jnp.bfloat16)
        grid_real = grids[s, :SU, :]
        grid_imag = grids[s, SU:, :]
        inner = jnp.concatenate(
            [
                jnp.concatenate([grid_real, grid_imag], axis=1),
                jnp.concatenate([-grid_imag, grid_real], axis=1),
            ],
            axis=0,
        )
        high, low = split_bf16(inner)
        half = jnp.dot(u_side, high, preferred_element_type=jnp.float32) + jnp.dot(
            u_side, low, preferred_element_type=jnp.float32
        )
        v_real, v_imag = parts(jnp.where(first, swapped, fetched))
        v_side = jnp.concatenate(
            [
                jnp.concatenate([v_real, v_imag], axis=1),
                jnp.concatenate([-v_imag, v_real], axis=1),
            ],
            axis=0,
        ).astype(jnp.bfloat16)
        high, low = split_bf16(half)
        result = (
            result
            + jnp.dot(high, v_side, preferred_element_type=jnp.float32)
            + jnp.dot(low, v_side, preferred_element_type=jnp.float32)
        )
    tail = meta_row // 16 * 16
    wide = packed[0, tail : tail + 16, :].astype(jnp.float32)
    at = meta_row - tail + 2
    gain = (wide[at : at + 2] + wide[at + 2 : at + 4]) + wide[at + 4 : at + 6]
    gain_u = jnp.broadcast_to(gain[0:1], (SU, SU)).T
    gains = gain_u * gain[1:2] * norm
    total[...] = result * jnp.concatenate([gains, gains], axis=1)
    half_rows = mine_ref.shape[0]
    mine_ref[...] = total[pl.ds(pl.multiple_of(chan * half_rows, half_rows), half_rows), :]
    other_ref[...] = total[pl.ds(pl.multiple_of((1 - chan) * half_rows, half_rows), half_rows), :]


def body(
    visibilities, coords, plane_index, block_group, offsets, facet_centre, tables, antenna_gain
):
    facets = lax.axis_size("facet")
    groups = lax.axis_size("bl")
    chan_count = lax.axis_size("chan")
    held, chans = visibilities.shape[:2]
    devices = facets * groups
    slots = 2 * facets
    cap = max(2, 2 * held // groups)
    meta_row = 2 * cap * (chans + 1)
    rows = -(-(meta_row + 8) // 16) * 16
    half_rows = SU // chan_count
    norm = SU / math.sqrt(visibilities.shape[3] * held * facets * CH)

    own_table = tables.reshape(2, 2 * SU, SU)
    send, keep, half = pl.pallas_call(
        functools.partial(sort_kernel, (groups, held, chans, cap, rows)),
        out_shape=[jax.ShapeDtypeStruct((groups // 2, 1, rows, SU), jnp.bfloat16)] * 2
        + [jax.ShapeDtypeStruct((2 * SU, SU), jnp.bfloat16)],
        in_specs=[HBM] * 8,
        out_specs=[VMEM] * 3,
        scratch_shapes=[
            pltpu.SMEM((1, held), jnp.int32),
            pltpu.SMEM((1, held), jnp.int32),
            pltpu.VMEM((held * 2 * chans, SU), jnp.bfloat16),
            pltpu.VMEM((held * 2, SU), jnp.bfloat16),
            pltpu.SMEM((facets, 2, groups), jnp.int32),
            pltpu.SMEM((2, facets), jnp.float32),
            pltpu.VMEM((1, 2, SU), jnp.float32),
            pltpu.VMEM((held * 2 * chans, SU), jnp.float32),
            pltpu.VMEM((held * 2, SU), jnp.float32),
            pltpu.VMEM((groups, rows, SU), jnp.float32),
            pltpu.SMEM((groups,), jnp.int32),
            pltpu.SemaphoreType.DMA((8,)),
        ],
        compiler_params=PARAMS,
        cost_estimate=pl.CostEstimate(flops=100_000, bytes_accessed=100_000, transcendentals=0),
        name="sort_blocks",
    )(
        *(
            pltpu.with_memory_space_constraint(operand, pltpu.HBM)
            for operand in (
                plane_index.reshape(1, held),
                block_group.T,
                visibilities.reshape(held * 2 * chans, SU),
                coords.reshape(held * 2, SU),
                offsets.transpose(0, 2, 1),
                facet_centre.T,
                antenna_gain,
                own_table,
            )
        )
    )
    bit = 1
    while bit < groups:
        arrived = exchange(send, "bl", bit)
        keep, *send = fold(keep, arrived)
        send = send[0] if send else None
        bit *= 2
    blocks = gather(keep[0], "facet")
    fetched = gather(half[None], "facet", True)
    swap = [(c, 1 - c) for c in range(chan_count)]
    fetched_swapped = lax.ppermute(fetched, "chan", swap)
    shifted = lax.ppermute(fetched, "bl", [(g, (g + 1) % groups) for g in range(groups)])

    grids = pl.pallas_call(
        functools.partial(grid_kernel, (facets, groups, chans, cap, rows)),
        out_shape=jax.ShapeDtypeStruct((slots, 2 * SU, SU), jnp.float32),
        in_specs=[VMEM] * 2,
        out_specs=VMEM,
        scratch_shapes=[
            pltpu.VMEM((devices, SU), jnp.int32),
            pltpu.SMEM((devices, SU), jnp.int32),
            pltpu.SMEM((devices * cap + REST,), jnp.int32),
        ]
        + [pltpu.VMEM((devices * cap * chans + 8, SU), jnp.float32)] * 4
        + [pltpu.SemaphoreType.DMA],
        compiler_params=PARAMS,
        cost_estimate=pl.CostEstimate(
            flops=4_000_000_000, bytes_accessed=2_000_000, transcendentals=4_000_000
        ),
        name="grid",
    )(*blocks)
    grids, shifted = lax.optimization_barrier((grids, shifted))
    shifted_swapped = lax.ppermute(shifted, "chan", swap)
    mine, other = pl.pallas_call(
        functools.partial(table_kernel, (slots, meta_row), norm),
        out_shape=[jax.ShapeDtypeStruct((half_rows, 2 * SU), jnp.float32)] * 2,
        in_specs=[VMEM] * 6,
        out_specs=[VMEM, VMEM],
        scratch_shapes=[
            pltpu.VMEM((2 * SU, SU), jnp.float32),
            pltpu.VMEM((SU, 2 * SU), jnp.float32),
        ],
        compiler_params=PARAMS,
        cost_estimate=pl.CostEstimate(
            flops=1_000_000_000, bytes_accessed=2_000_000, transcendentals=0
        ),
        name="apply_tables",
    )(grids, blocks[0], fetched, shifted, fetched_swapped, shifted_swapped)
    summand = lax.ppermute(other, "chan", swap)
    return (mine + summand).reshape(1, 1, half_rows, 2, SU)


def solution(mesh):
    in_specs = (
        P(("facet", "bl"), "chan", None, None),
        P(("facet", "bl"), None, None),
        P(("facet", "bl")),
        P(("facet", "bl"), None),
        P(),
        P(),
        P(("facet", "bl"), None, None, None, None),
        P("bl", None, None),
    )
    out_specs = P("facet", "bl", "chan", None, None)
    return jax.shard_map(body, mesh=mesh, in_specs=in_specs, out_specs=out_specs, check_vma=False)
```

```python
import functools
import math

import jax
import jax.numpy as jnp
from jax import lax
from jax.experimental import pallas as pl
from jax.experimental.pallas import tpu as pltpu
from jax.sharding import PartitionSpec as P

SU = 128
CH = 8
KERNEL_SPREAD = 1.5
ALPHA = math.sqrt(math.log2(math.e) / (2.0 * KERNEL_SPREAD * KERNEL_SPREAD))
UNROLL = 8
REST = 2
NT = (((1,), (1,)), ((), ()))
VMEM = pl.BlockSpec(memory_space=pltpu.VMEM)
HBM = pl.BlockSpec(memory_space=pltpu.HBM)
PARAMS = pltpu.CompilerParams(vmem_limit_bytes=32 * 1024 * 1024)


def cos_sin(turns):
    quarter = jnp.floor(4.0 * turns + 0.5)
    angle = (2.0 * math.pi) * (turns - 0.25 * quarter)
    sq = angle * angle
    sine = angle * (
        1.0 + sq * (-1.0 / 6 + sq * (1.0 / 120 + sq * (-1.0 / 5040 + sq * (1.0 / 362880))))
    )
    cosine = 1.0 + sq * (
        -0.5 + sq * (1.0 / 24 + sq * (-1.0 / 720 + sq * (1.0 / 40320 + sq * (-1.0 / 3628800))))
    )
    turn = quarter.astype(jnp.int32) & 3
    odd = (turn & 1) == 1
    cos_out = jnp.where(odd, sine, cosine)
    sin_out = jnp.where(odd, cosine, sine)
    cos_out = jnp.where((turn == 1) | (turn == 2), -cos_out, cos_out)
    sin_out = jnp.where(turn >= 2, -sin_out, sin_out)
    return cos_out, sin_out


def split_bf16(x):
    high = x.astype(jnp.bfloat16)
    low = (x - high.astype(jnp.float32)).astype(jnp.bfloat16)
    return high, low


def three_parts(x):
    parts = []
    for _ in range(3):
        part = x.astype(jnp.bfloat16)
        x = x - part.astype(jnp.float32)
        parts.append(part.astype(jnp.float32))
    return parts


def sort_kernel(sizes, *refs):
    groups, held, chans, cap, rows = sizes
    table_hbm, outs, half = refs[7], refs[8 : 8 + groups], refs[8 + groups]
    targets = refs[9 + groups : 16 + groups]
    plane_ref, group_ref, samples_b, place_b, offsets_ref, centre_ref, gain_ref = targets
    samples, place, sorted_, filled, sems = refs[16 + groups :]
    facet = lax.axis_index("facet")
    copies = [
        pltpu.make_async_copy(source, target, sems.at[n])
        for n, (source, target) in enumerate(zip(refs[:7], targets))
    ]
    table = pltpu.make_async_copy(table_hbm.at[lax.axis_index("chan")], half, sems.at[7])
    for copy in copies + [table]:
        copy.start()
    sorted_[...] = jnp.zeros_like(sorted_)
    for g in range(groups):
        filled[g] = 0
    for copy in copies:
        copy.wait()
    samples[...] = samples_b[...].astype(jnp.float32)
    place[...] = place_b[...].astype(jnp.float32)
    lane = lax.broadcasted_iota(jnp.int32, (1, SU), 1)
    meta = 2 * cap * (chans + 1)
    centre = [
        part
        for axis in range(2)
        for part in three_parts(jnp.full((1, SU), centre_ref[axis, facet], jnp.float32))
    ]
    gains = three_parts(gain_ref[0])
    for g in range(groups):
        numbers = jnp.zeros((1, SU), jnp.float32)
        for axis in range(2):
            offset = offsets_ref[facet, axis, g].astype(jnp.float32)
            numbers = jnp.where(lane == axis, offset, numbers)
        for n, part in enumerate(centre):
            numbers = jnp.where(lane == 2 + n, part, numbers)
        sorted_[g, meta + 1 : meta + 2, :] = numbers
        for n, part in enumerate(gains):
            sorted_[g, meta + 2 + 2 * n : meta + 4 + 2 * n, :] = part
    for i in range(held):
        g = group_ref[0, i]
        k = filled[g]
        filled[g] = k + 1
        for part in range(2):
            at = part * cap * chans + k * chans
            sorted_[g, pl.ds(at, chans), :] = samples[pl.ds(2 * chans * i + part, chans, stride=2), :]
            at = 2 * cap * chans + part * cap + k
            sorted_[g, pl.ds(at, 1), :] = place[2 * i + part : 2 * i + part + 1, :]
        sorted_[g, meta : meta + 1, :] += jnp.where(
            lane == k, (plane_ref[0, i] + 1).astype(jnp.float32), 0.0
        )
    for shift, out_ref in enumerate(outs):
        g = lax.rem(lax.axis_index("bl") + shift, groups)
        out_ref[:rows, :] = sorted_[g].astype(jnp.bfloat16)
    table.wait()
    outs[1][rows:, :] = half[...]


def join_kernel(rows, half, *refs):
    *pieces, here, joined = refs
    for n, ref in enumerate(pieces):
        piece = ref[:rows, :]
        here[n * rows : (n + 1) * rows, :] = piece
        joined[n * rows : (n + 1) * rows, :] = piece
    at = len(pieces) * rows
    joined[at : at + 2 * SU, :] = half[...]
    joined[at + 2 * SU :, :] = pieces[1][rows:, :]


def stack_kernel(skip, own, arrived, out_ref):
    count = own.shape[0] - skip
    out_ref[:count, :] = own[skip:, :]
    out_ref[count:, :] = arrived[skip:, :]


def grid_kernel(sizes, *refs):
    facets, groups, chans, cap, rows = sizes
    grids = refs[facets]
    meta_v, meta_s, order, spots_u, spots_v, turns_real, turns_imag, sem = refs[facets + 1 :]
    pieces = [ref.at[pl.ds(n * rows, rows)] for ref in refs[:facets] for n in range(groups)]
    devices = facets * groups
    slots = 2 * facets
    lines = cap * chans
    meta_row = 2 * (lines + cap)
    tail = meta_row // 16 * 16
    facet = lax.axis_index("facet")
    group = lax.axis_index("bl")
    chan = lax.axis_index("chan")

    lane = lax.broadcasted_iota(jnp.int32, (1, SU), 1)
    own = pieces[0][tail : tail + 16, :].astype(jnp.float32)
    numbers = own[meta_row - tail + 1 : meta_row - tail + 2]
    for d in range(devices):
        meta = pieces[d][tail : tail + 16, :].astype(jnp.float32)
        plane = meta[meta_row - tail : meta_row - tail + 1].astype(jnp.int32) - 1
        set_id = jnp.where(lax.rem(plane, groups) == group, 0, 1)
        code = (d * cap + lane) * slots + 2 * (lax.div(plane, groups) ^ facet) + set_id
        meta_v[d : d + 1, :] = jnp.where(plane >= 0, code, -1)
    copy = pltpu.make_async_copy(meta_v, meta_s, sem)
    copy.start()
    grids[...] = jnp.zeros_like(grids)

    def number(n):
        return jnp.broadcast_to(numbers[:, n : n + 1], (lines, SU))

    offset_u = number(0)
    offset_v = number(1)
    along_l = number(2) + number(3) + number(4)
    along_m = number(5) + number(6) + number(7)
    line = lax.broadcasted_iota(jnp.int32, (lines, SU), 0)
    channel = (chan * chans + lax.rem(line, chans)).astype(jnp.float32)
    scale = 1.0 + 0.01 * (channel - 0.5 * (CH - 1))

    def spread_lines(place):
        return jnp.concatenate(
            [jnp.broadcast_to(place[k : k + 1], (chans, SU)) for k in range(cap)], axis=0
        )

    for d in range(devices):
        at = d * lines
        wide = pieces[d][...].astype(jnp.float32)
        real = wide[:lines]
        imag = wide[lines : 2 * lines]
        along_u = spread_lines(wide[2 * lines : 2 * lines + cap])
        along_v = spread_lines(wide[2 * lines + cap : 2 * (lines + cap)])
        cosine, sine = cos_sin((1.0 / SU) * (scale * (along_u * along_l + along_v * along_m)))
        spots_u[at : at + lines, :] = ALPHA * (scale * along_u - offset_u)
        spots_v[at : at + lines, :] = ALPHA * (scale * along_v - offset_v)
        turns_real[at : at + lines, :] = real * cosine - imag * sine
        turns_imag[at : at + lines, :] = real * sine + imag * cosine
    last = devices * lines
    for ref in (spots_u, spots_v, turns_real, turns_imag):
        ref[last : last + 8, :] = jnp.zeros((8, SU), jnp.float32)
    copy.wait()

    count = jnp.int32(0)
    for d in range(devices):
        for k in range(cap):
            code = meta_s[d, k]
            order[count] = code
            count = count + jnp.where(code >= 0, 1, 0)
    for i in range(REST):
        order[count + i] = devices * cap * slots

    cells = ALPHA * lax.broadcasted_iota(jnp.int32, (SU, SU), 0).astype(jnp.float32)

    def profile(spot):
        apart = spot - cells
        return jnp.exp2(-(apart * apart)).astype(jnp.bfloat16)

    def tiled(row):
        return jnp.broadcast_to(row, (16, SU)).astype(jnp.bfloat16)[None]

    def one_block(at):
        code = order[at]
        slot = lax.rem(code, slots)
        base = lax.div(code, slots) * chans
        lefts_real, lefts_imag, rights = [], [], []
        for c in range(chans):
            here = pl.ds(base + c, 1)
            left = profile(spots_u[here, :]).reshape(SU // 16, 16, SU)
            lefts_real.append((left * tiled(turns_real[here, :])).reshape(SU, SU))
            lefts_imag.append((left * tiled(turns_imag[here, :])).reshape(SU, SU))
            rights.append(profile(spots_v[here, :]))
        left = jnp.concatenate(
            [jnp.concatenate(lefts_real, axis=1), jnp.concatenate(lefts_imag, axis=1)], axis=0
        )
        right = jnp.concatenate(rights, axis=1)
        return slot, lax.dot_general(left, right, NT, preferred_element_type=jnp.float32)

    def steps(first, blocks, number):
        def step(k, carry):
            for slot, part in [one_block(first + k * blocks + i) for i in range(blocks)]:
                grids[slot] += part
            return carry

        lax.fori_loop(0, number, step, 0)

    whole = lax.div(count, UNROLL)
    steps(0, UNROLL, whole)
    steps(whole * UNROLL, REST, lax.div(lax.rem(count, UNROLL) + REST - 1, REST))


def local(kernel, operands, shapes, name):
    return pl.pallas_call(
        kernel,
        out_shape=[jax.ShapeDtypeStruct(shape, jnp.bfloat16) for shape in shapes],
        in_specs=[VMEM] * len(operands),
        out_specs=[VMEM] * len(shapes),
        compiler_params=PARAMS,
        cost_estimate=pl.CostEstimate(flops=0, bytes_accessed=400_000, transcendentals=0),
        name=name,
    )(*operands)


def exchange(value, axis, shift):
    return lax.ppermute(value, axis, [(n, n ^ shift) for n in range(lax.axis_size(axis))])


def table_kernel(sizes, norm, grids, packed, *refs):
    slots, meta_row = sizes
    ours, theirs = refs[:2], refs[2:4]
    mine_ref, other_ref, table_f, total = refs[4:]
    chan = lax.axis_index("chan")
    first = chan == 0

    def parts(table):
        table_f[...] = table
        return table_f[pl.ds(0, SU, stride=2), :], table_f[pl.ds(1, SU, stride=2), :]

    result = jnp.zeros((SU, 2 * SU), jnp.float32)
    for s in range(slots):
        half, at = divmod(2 * SU * s, ours[0].shape[0])
        fetched = ours[half][at : at + 2 * SU, :].astype(jnp.float32)
        swapped = theirs[half][at : at + 2 * SU, :].astype(jnp.float32)
        u_real, u_imag = parts(jnp.where(first, fetched, swapped))
        u_side = jnp.concatenate([u_real.T, u_imag.T], axis=1).astype(jnp.bfloat16)
        grid_real = grids[s, :SU, :]
        grid_imag = grids[s, SU:, :]
        inner = jnp.concatenate(
            [
                jnp.concatenate([grid_real, grid_imag], axis=1),
                jnp.concatenate([-grid_imag, grid_real], axis=1),
            ],
            axis=0,
        )
        high, low = split_bf16(inner)
        half = jnp.dot(u_side, high, preferred_element_type=jnp.float32) + jnp.dot(
            u_side, low, preferred_element_type=jnp.float32
        )
        v_real, v_imag = parts(jnp.where(first, swapped, fetched))
        v_side = jnp.concatenate(
            [
                jnp.concatenate([v_real, v_imag], axis=1),
                jnp.concatenate([-v_imag, v_real], axis=1),
            ],
            axis=0,
        ).astype(jnp.bfloat16)
        high, low = split_bf16(half)
        result = (
            result
            + jnp.dot(high, v_side, preferred_element_type=jnp.float32)
            + jnp.dot(low, v_side, preferred_element_type=jnp.float32)
        )
    tail = meta_row // 16 * 16
    wide = packed[tail : tail + 16, :].astype(jnp.float32)
    at = meta_row - tail + 2
    gain = (wide[at : at + 2] + wide[at + 2 : at + 4]) + wide[at + 4 : at + 6]
    gain_u = jnp.broadcast_to(gain[0:1], (SU, SU)).T
    gains = gain_u * gain[1:2] * norm
    total[...] = result * jnp.concatenate([gains, gains], axis=1)
    half_rows = mine_ref.shape[0]
    mine_ref[...] = total[pl.ds(pl.multiple_of(chan * half_rows, half_rows), half_rows), :]
    other_ref[...] = total[pl.ds(pl.multiple_of((1 - chan) * half_rows, half_rows), half_rows), :]


def body(
    visibilities, coords, plane_index, block_group, offsets, facet_centre, tables, antenna_gain
):
    facets = lax.axis_size("facet")
    groups = lax.axis_size("bl")
    chan_count = lax.axis_size("chan")
    held, chans = visibilities.shape[:2]
    devices = facets * groups
    slots = 2 * facets
    cap = max(2, 2 * held // groups)
    meta_row = 2 * cap * (chans + 1)
    rows = -(-(meta_row + 8) // 16) * 16
    half_rows = SU // chan_count
    norm = SU / math.sqrt(visibilities.shape[3] * held * facets * CH)

    own_table = tables.reshape(2, 2 * SU, SU)
    *pieces, half = pl.pallas_call(
        functools.partial(sort_kernel, (groups, held, chans, cap, rows)),
        out_shape=[
            jax.ShapeDtypeStruct((rows + (2 * SU if shift == 1 else 0), SU), jnp.bfloat16)
            for shift in range(groups)
        ]
        + [jax.ShapeDtypeStruct((2 * SU, SU), jnp.bfloat16)],
        in_specs=[HBM] * 8,
        out_specs=[VMEM] * (groups + 1),
        scratch_shapes=[
            pltpu.SMEM((1, held), jnp.int32),
            pltpu.SMEM((1, held), jnp.int32),
            pltpu.VMEM((held * 2 * chans, SU), jnp.bfloat16),
            pltpu.VMEM((held * 2, SU), jnp.bfloat16),
            pltpu.SMEM((facets, 2, groups), jnp.int32),
            pltpu.SMEM((2, facets), jnp.float32),
            pltpu.VMEM((1, 2, SU), jnp.float32),
            pltpu.VMEM((held * 2 * chans, SU), jnp.float32),
            pltpu.VMEM((held * 2, SU), jnp.float32),
            pltpu.VMEM((groups, rows, SU), jnp.float32),
            pltpu.SMEM((groups,), jnp.int32),
            pltpu.SemaphoreType.DMA((8,)),
        ],
        compiler_params=PARAMS,
        cost_estimate=pl.CostEstimate(flops=100_000, bytes_accessed=100_000, transcendentals=0),
        name="sort_blocks",
    )(
        *(
            pltpu.with_memory_space_constraint(operand, pltpu.HBM)
            for operand in (
                plane_index.reshape(1, held),
                block_group.T,
                visibilities.reshape(held * 2 * chans, SU),
                coords.reshape(held * 2, SU),
                offsets.transpose(0, 2, 1),
                facet_centre.T,
                antenna_gain,
                own_table,
            )
        )
    )
    arrived = [
        lax.ppermute(pieces[shift], "bl", [(g, (g + shift) % groups) for g in range(groups)])
        for shift in range(1, groups)
    ]
    vis_rows = groups * rows
    here, joined = local(
        functools.partial(join_kernel, rows),
        [half, pieces[0], *arrived],
        [(vis_rows, SU), (vis_rows + 4 * SU, SU)],
        "join",
    )
    blocks = [here] + [
        exchange(joined if shift == 1 else here, "facet", shift) for shift in range(1, facets)
    ]
    (near,) = local(
        functools.partial(stack_kernel, vis_rows), [joined, blocks[1]], [(8 * SU, SU)], "stack"
    )
    bit = 2
    while True:
        far = exchange(near, "facet", bit)
        bit *= 2
        if bit == facets:
            break
        (near,) = local(
            functools.partial(stack_kernel, 0), [near, far], [(2 * near.shape[0], SU)], "stack"
        )
    swap = [(c, 1 - c) for c in range(chan_count)]
    near_swapped = lax.ppermute(near, "chan", swap)

    grids = pl.pallas_call(
        functools.partial(grid_kernel, (facets, groups, chans, cap, rows)),
        out_shape=jax.ShapeDtypeStruct((slots, 2 * SU, SU), jnp.float32),
        in_specs=[VMEM] * facets,
        out_specs=VMEM,
        scratch_shapes=[
            pltpu.VMEM((devices, SU), jnp.int32),
            pltpu.SMEM((devices, SU), jnp.int32),
            pltpu.SMEM((devices * cap + REST,), jnp.int32),
        ]
        + [pltpu.VMEM((devices * cap * chans + 8, SU), jnp.float32)] * 4
        + [pltpu.SemaphoreType.DMA],
        compiler_params=PARAMS,
        cost_estimate=pl.CostEstimate(
            flops=4_000_000_000, bytes_accessed=2_000_000, transcendentals=4_000_000
        ),
        name="grid",
    )(*blocks)
    grids, far = lax.optimization_barrier((grids, far))
    far_swapped = lax.ppermute(far, "chan", swap)
    mine, other = pl.pallas_call(
        functools.partial(table_kernel, (slots, meta_row), norm),
        out_shape=[jax.ShapeDtypeStruct((half_rows, 2 * SU), jnp.float32)] * 2,
        in_specs=[VMEM] * 6,
        out_specs=[VMEM, VMEM],
        scratch_shapes=[
            pltpu.VMEM((2 * SU, SU), jnp.float32),
            pltpu.VMEM((SU, 2 * SU), jnp.float32),
        ],
        compiler_params=PARAMS,
        cost_estimate=pl.CostEstimate(
            flops=1_000_000_000, bytes_accessed=2_000_000, transcendentals=0
        ),
        name="apply_tables",
    )(grids, here, near, far, near_swapped, far_swapped)
    summand = lax.ppermute(other, "chan", swap)
    return (mine + summand).reshape(1, 1, half_rows, 2, SU)


def solution(mesh):
    in_specs = (
        P(("facet", "bl"), "chan", None, None),
        P(("facet", "bl"), None, None),
        P(("facet", "bl")),
        P(("facet", "bl"), None),
        P(),
        P(),
        P(("facet", "bl"), None, None, None, None),
        P("bl", None, None),
    )
    out_specs = P("facet", "bl", "chan", None, None)
    return jax.shard_map(body, mesh=mesh, in_specs=in_specs, out_specs=out_specs, check_vma=False)
```

```python
import functools
import math

import jax
import jax.numpy as jnp
from jax import lax
from jax.experimental import pallas as pl
from jax.experimental.pallas import tpu as pltpu
from jax.sharding import PartitionSpec as P

SU = 128
CH = 8
KERNEL_SPREAD = 1.5
ALPHA = math.sqrt(math.log2(math.e) / (2.0 * KERNEL_SPREAD * KERNEL_SPREAD))
UNROLL = 8
REST = 2
NT = (((1,), (1,)), ((), ()))
VMEM = pl.BlockSpec(memory_space=pltpu.VMEM)
HBM = pl.BlockSpec(memory_space=pltpu.HBM)
PARAMS = pltpu.CompilerParams(vmem_limit_bytes=32 * 1024 * 1024)


def cos_sin(turns):
    quarter = jnp.floor(4.0 * turns + 0.5)
    angle = (2.0 * math.pi) * (turns - 0.25 * quarter)
    sq = angle * angle
    sine = angle * (
        1.0 + sq * (-1.0 / 6 + sq * (1.0 / 120 + sq * (-1.0 / 5040 + sq * (1.0 / 362880))))
    )
    cosine = 1.0 + sq * (
        -0.5 + sq * (1.0 / 24 + sq * (-1.0 / 720 + sq * (1.0 / 40320 + sq * (-1.0 / 3628800))))
    )
    turn = quarter.astype(jnp.int32) & 3
    odd = (turn & 1) == 1
    cos_out = jnp.where(odd, sine, cosine)
    sin_out = jnp.where(odd, cosine, sine)
    cos_out = jnp.where((turn == 1) | (turn == 2), -cos_out, cos_out)
    sin_out = jnp.where(turn >= 2, -sin_out, sin_out)
    return cos_out, sin_out


def split_bf16(x):
    high = x.astype(jnp.bfloat16)
    low = (x - high.astype(jnp.float32)).astype(jnp.bfloat16)
    return high, low


def three_parts(x):
    parts = []
    for _ in range(3):
        part = x.astype(jnp.bfloat16)
        x = x - part.astype(jnp.float32)
        parts.append(part.astype(jnp.float32))
    return parts


def sort_kernel(sizes, *refs):
    groups, held, chans, cap, rows = sizes
    table_hbm, outs, half = refs[7], refs[8 : 8 + groups], refs[8 + groups]
    targets = refs[9 + groups : 16 + groups]
    plane_ref, group_ref, samples_b, place_b, offsets_ref, centre_ref, gain_ref = targets
    samples, place, sorted_, filled, sems = refs[16 + groups :]
    facet = lax.axis_index("facet")
    copies = [
        pltpu.make_async_copy(source, target, sems.at[n])
        for n, (source, target) in enumerate(zip(refs[:7], targets))
    ]
    table = pltpu.make_async_copy(table_hbm.at[lax.axis_index("chan")], half, sems.at[7])
    for copy in copies + [table]:
        copy.start()
    sorted_[...] = jnp.zeros_like(sorted_)
    for g in range(groups):
        filled[g] = 0
    for copy in copies:
        copy.wait()
    samples[...] = samples_b[...].astype(jnp.float32)
    place[...] = place_b[...].astype(jnp.float32)
    lane = lax.broadcasted_iota(jnp.int32, (1, SU), 1)
    meta = 2 * cap * (chans + 1)
    centre = [
        part
        for axis in range(2)
        for part in three_parts(jnp.full((1, SU), centre_ref[axis, facet], jnp.float32))
    ]
    gains = three_parts(gain_ref[0])
    for g in range(groups):
        numbers = jnp.zeros((1, SU), jnp.float32)
        for axis in range(2):
            offset = offsets_ref[facet, axis, g].astype(jnp.float32)
            numbers = jnp.where(lane == axis, offset, numbers)
        for n, part in enumerate(centre):
            numbers = jnp.where(lane == 2 + n, part, numbers)
        sorted_[g, meta + 1 : meta + 2, :] = numbers
        for n, part in enumerate(gains):
            sorted_[g, meta + 2 + 2 * n : meta + 4 + 2 * n, :] = part
    for i in range(held):
        g = group_ref[0, i]
        k = filled[g]
        filled[g] = k + 1
        for part in range(2):
            at = part * cap * chans + k * chans
            sorted_[g, pl.ds(at, chans), :] = samples[pl.ds(2 * chans * i + part, chans, stride=2), :]
            at = 2 * cap * chans + part * cap + k
            sorted_[g, pl.ds(at, 1), :] = place[2 * i + part : 2 * i + part + 1, :]
        sorted_[g, meta : meta + 1, :] += jnp.where(
            lane == k, (plane_ref[0, i] + 1).astype(jnp.float32), 0.0
        )
    for shift, out_ref in enumerate(outs):
        g = lax.rem(lax.axis_index("bl") + shift, groups)
        out_ref[:rows, :] = sorted_[g].astype(jnp.bfloat16)
    table.wait()
    outs[1][rows:, :] = half[...]


def join_kernel(rows, half, *refs):
    *pieces, joined = refs
    for n, ref in enumerate(pieces):
        joined[n * rows : (n + 1) * rows, :] = ref[:rows, :]
    at = len(pieces) * rows
    joined[at : at + 2 * SU, :] = half[...]
    joined[at + 2 * SU :, :] = pieces[1][rows:, :]


def collect_kernel(skip, *refs):
    for n, ref in enumerate(refs[:-1]):
        refs[-1][n * 4 * SU : (n + 1) * 4 * SU, :] = ref[skip:, :]


def grid_kernel(sizes, *refs):
    facets, groups, chans, cap, rows = sizes
    grids = refs[facets]
    meta_v, meta_s, order, spots_u, spots_v, turns_real, turns_imag, sem = refs[facets + 1 :]
    pieces = [ref.at[pl.ds(n * rows, rows)] for ref in refs[:facets] for n in range(groups)]
    devices = facets * groups
    slots = 2 * facets
    lines = cap * chans
    meta_row = 2 * (lines + cap)
    tail = meta_row // 16 * 16
    facet = lax.axis_index("facet")
    group = lax.axis_index("bl")
    chan = lax.axis_index("chan")

    lane = lax.broadcasted_iota(jnp.int32, (1, SU), 1)
    own = pieces[0][tail : tail + 16, :].astype(jnp.float32)
    numbers = own[meta_row - tail + 1 : meta_row - tail + 2]
    for d in range(devices):
        meta = pieces[d][tail : tail + 16, :].astype(jnp.float32)
        plane = meta[meta_row - tail : meta_row - tail + 1].astype(jnp.int32) - 1
        set_id = jnp.where(lax.rem(plane, groups) == group, 0, 1)
        code = (d * cap + lane) * slots + 2 * (lax.div(plane, groups) ^ facet) + set_id
        meta_v[d : d + 1, :] = jnp.where(plane >= 0, code, -1)
    copy = pltpu.make_async_copy(meta_v, meta_s, sem)
    copy.start()
    grids[...] = jnp.zeros_like(grids)

    def number(n):
        return jnp.broadcast_to(numbers[:, n : n + 1], (lines, SU))

    offset_u = number(0)
    offset_v = number(1)
    along_l = number(2) + number(3) + number(4)
    along_m = number(5) + number(6) + number(7)
    line = lax.broadcasted_iota(jnp.int32, (lines, SU), 0)
    channel = (chan * chans + lax.rem(line, chans)).astype(jnp.float32)
    scale = 1.0 + 0.01 * (channel - 0.5 * (CH - 1))

    def spread_lines(place):
        return jnp.concatenate(
            [jnp.broadcast_to(place[k : k + 1], (chans, SU)) for k in range(cap)], axis=0
        )

    for d in range(devices):
        at = d * lines
        wide = pieces[d][...].astype(jnp.float32)
        real = wide[:lines]
        imag = wide[lines : 2 * lines]
        along_u = spread_lines(wide[2 * lines : 2 * lines + cap])
        along_v = spread_lines(wide[2 * lines + cap : 2 * (lines + cap)])
        cosine, sine = cos_sin((1.0 / SU) * (scale * (along_u * along_l + along_v * along_m)))
        spots_u[at : at + lines, :] = ALPHA * (scale * along_u - offset_u)
        spots_v[at : at + lines, :] = ALPHA * (scale * along_v - offset_v)
        turns_real[at : at + lines, :] = real * cosine - imag * sine
        turns_imag[at : at + lines, :] = real * sine + imag * cosine
    last = devices * lines
    for ref in (spots_u, spots_v, turns_real, turns_imag):
        ref[last : last + 8, :] = jnp.zeros((8, SU), jnp.float32)
    copy.wait()

    count = jnp.int32(0)
    for d in range(devices):
        for k in range(cap):
            code = meta_s[d, k]
            order[count] = code
            count = count + jnp.where(code >= 0, 1, 0)
    for i in range(REST):
        order[count + i] = devices * cap * slots

    cells = ALPHA * lax.broadcasted_iota(jnp.int32, (SU, SU), 0).astype(jnp.float32)

    def profile(spot):
        apart = spot - cells
        return jnp.exp2(-(apart * apart)).astype(jnp.bfloat16)

    def tiled(row):
        return jnp.broadcast_to(row, (16, SU)).astype(jnp.bfloat16)[None]

    def one_block(at):
        code = order[at]
        slot = lax.rem(code, slots)
        base = lax.div(code, slots) * chans
        lefts_real, lefts_imag, rights = [], [], []
        for c in range(chans):
            here = pl.ds(base + c, 1)
            left = profile(spots_u[here, :]).reshape(SU // 16, 16, SU)
            lefts_real.append((left * tiled(turns_real[here, :])).reshape(SU, SU))
            lefts_imag.append((left * tiled(turns_imag[here, :])).reshape(SU, SU))
            rights.append(profile(spots_v[here, :]))
        left = jnp.concatenate(
            [jnp.concatenate(lefts_real, axis=1), jnp.concatenate(lefts_imag, axis=1)], axis=0
        )
        right = jnp.concatenate(rights, axis=1)
        return slot, lax.dot_general(left, right, NT, preferred_element_type=jnp.float32)

    def steps(first, blocks, number):
        def step(k, carry):
            for slot, part in [one_block(first + k * blocks + i) for i in range(blocks)]:
                grids[slot] += part
            return carry

        lax.fori_loop(0, number, step, 0)

    whole = lax.div(count, UNROLL)
    steps(0, UNROLL, whole)
    steps(whole * UNROLL, REST, lax.div(lax.rem(count, UNROLL) + REST - 1, REST))


def local(kernel, operands, shape, name):
    return pl.pallas_call(
        kernel,
        out_shape=jax.ShapeDtypeStruct(shape, jnp.bfloat16),
        in_specs=[VMEM] * len(operands),
        out_specs=VMEM,
        compiler_params=PARAMS,
        cost_estimate=pl.CostEstimate(flops=0, bytes_accessed=400_000, transcendentals=0),
        name=name,
    )(*operands)


def exchange(value, axis, shift):
    return lax.ppermute(value, axis, [(n, n ^ shift) for n in range(lax.axis_size(axis))])


def table_kernel(sizes, norm, grids, packed, ours, theirs, mine_ref, other_ref, table_f, total):
    slots, meta_row = sizes
    chan = lax.axis_index("chan")
    first = chan == 0

    def parts(table):
        table_f[...] = table
        return table_f[pl.ds(0, SU, stride=2), :], table_f[pl.ds(1, SU, stride=2), :]

    result = jnp.zeros((SU, 2 * SU), jnp.float32)
    for s in range(slots):
        at = slice(2 * SU * s, 2 * SU * (s + 1))
        fetched = ours[at, :].astype(jnp.float32)
        swapped = theirs[at, :].astype(jnp.float32)
        u_real, u_imag = parts(jnp.where(first, fetched, swapped))
        u_side = jnp.concatenate([u_real.T, u_imag.T], axis=1).astype(jnp.bfloat16)
        grid_real = grids[s, :SU, :]
        grid_imag = grids[s, SU:, :]
        inner = jnp.concatenate(
            [
                jnp.concatenate([grid_real, grid_imag], axis=1),
                jnp.concatenate([-grid_imag, grid_real], axis=1),
            ],
            axis=0,
        )
        high, low = split_bf16(inner)
        half = jnp.dot(u_side, high, preferred_element_type=jnp.float32) + jnp.dot(
            u_side, low, preferred_element_type=jnp.float32
        )
        v_real, v_imag = parts(jnp.where(first, swapped, fetched))
        v_side = jnp.concatenate(
            [
                jnp.concatenate([v_real, v_imag], axis=1),
                jnp.concatenate([-v_imag, v_real], axis=1),
            ],
            axis=0,
        ).astype(jnp.bfloat16)
        high, low = split_bf16(half)
        result = (
            result
            + jnp.dot(high, v_side, preferred_element_type=jnp.float32)
            + jnp.dot(low, v_side, preferred_element_type=jnp.float32)
        )
    tail = meta_row // 16 * 16
    wide = packed[tail : tail + 16, :].astype(jnp.float32)
    at = meta_row - tail + 2
    gain = (wide[at : at + 2] + wide[at + 2 : at + 4]) + wide[at + 4 : at + 6]
    gain_u = jnp.broadcast_to(gain[0:1], (SU, SU)).T
    gains = gain_u * gain[1:2] * norm
    total[...] = result * jnp.concatenate([gains, gains], axis=1)
    half_rows = mine_ref.shape[0]
    mine_ref[...] = total[pl.ds(pl.multiple_of(chan * half_rows, half_rows), half_rows), :]
    other_ref[...] = total[pl.ds(pl.multiple_of((1 - chan) * half_rows, half_rows), half_rows), :]


def body(
    visibilities, coords, plane_index, block_group, offsets, facet_centre, tables, antenna_gain
):
    facets = lax.axis_size("facet")
    groups = lax.axis_size("bl")
    chan_count = lax.axis_size("chan")
    held, chans = visibilities.shape[:2]
    devices = facets * groups
    slots = 2 * facets
    cap = max(2, 2 * held // groups)
    meta_row = 2 * cap * (chans + 1)
    rows = -(-(meta_row + 8) // 16) * 16
    half_rows = SU // chan_count
    norm = SU / math.sqrt(visibilities.shape[3] * held * facets * CH)

    own_table = tables.reshape(2, 2 * SU, SU)
    *pieces, half = pl.pallas_call(
        functools.partial(sort_kernel, (groups, held, chans, cap, rows)),
        out_shape=[
            jax.ShapeDtypeStruct((rows + (2 * SU if shift == 1 else 0), SU), jnp.bfloat16)
            for shift in range(groups)
        ]
        + [jax.ShapeDtypeStruct((2 * SU, SU), jnp.bfloat16)],
        in_specs=[HBM] * 8,
        out_specs=[VMEM] * (groups + 1),
        scratch_shapes=[
            pltpu.SMEM((1, held), jnp.int32),
            pltpu.SMEM((1, held), jnp.int32),
            pltpu.VMEM((held * 2 * chans, SU), jnp.bfloat16),
            pltpu.VMEM((held * 2, SU), jnp.bfloat16),
            pltpu.SMEM((facets, 2, groups), jnp.int32),
            pltpu.SMEM((2, facets), jnp.float32),
            pltpu.VMEM((1, 2, SU), jnp.float32),
            pltpu.VMEM((held * 2 * chans, SU), jnp.float32),
            pltpu.VMEM((held * 2, SU), jnp.float32),
            pltpu.VMEM((groups, rows, SU), jnp.float32),
            pltpu.SMEM((groups,), jnp.int32),
            pltpu.SemaphoreType.DMA((8,)),
        ],
        compiler_params=PARAMS,
        cost_estimate=pl.CostEstimate(flops=100_000, bytes_accessed=100_000, transcendentals=0),
        name="sort_blocks",
    )(
        *(
            pltpu.with_memory_space_constraint(operand, pltpu.HBM)
            for operand in (
                plane_index.reshape(1, held),
                block_group.T,
                visibilities.reshape(held * 2 * chans, SU),
                coords.reshape(held * 2, SU),
                offsets.transpose(0, 2, 1),
                facet_centre.T,
                antenna_gain,
                own_table,
            )
        )
    )
    arrived = [
        lax.ppermute(pieces[shift], "bl", [(g, (g + shift) % groups) for g in range(groups)])
        for shift in range(1, groups)
    ]
    vis_rows = groups * rows
    joined = local(
        functools.partial(join_kernel, rows),
        [half, pieces[0], *arrived],
        (vis_rows + 4 * SU, SU),
        "join",
    )
    blocks = [joined] + [exchange(joined, "facet", shift) for shift in range(1, facets)]
    fetched = local(
        functools.partial(collect_kernel, vis_rows), blocks, (facets * 4 * SU, SU), "collect"
    )
    swapped = lax.ppermute(fetched, "chan", [(c, 1 - c) for c in range(chan_count)])

    grids = pl.pallas_call(
        functools.partial(grid_kernel, (facets, groups, chans, cap, rows)),
        out_shape=jax.ShapeDtypeStruct((slots, 2 * SU, SU), jnp.float32),
        in_specs=[VMEM] * facets,
        out_specs=VMEM,
        scratch_shapes=[
            pltpu.VMEM((devices, SU), jnp.int32),
            pltpu.SMEM((devices, SU), jnp.int32),
            pltpu.SMEM((devices * cap + REST,), jnp.int32),
        ]
        + [pltpu.VMEM((devices * cap * chans + 8, SU), jnp.float32)] * 4
        + [pltpu.SemaphoreType.DMA],
        compiler_params=PARAMS,
        cost_estimate=pl.CostEstimate(
            flops=4_000_000_000, bytes_accessed=2_000_000, transcendentals=4_000_000
        ),
        name="grid",
    )(*blocks)
    mine, other = pl.pallas_call(
        functools.partial(table_kernel, (slots, meta_row), norm),
        out_shape=[jax.ShapeDtypeStruct((half_rows, 2 * SU), jnp.float32)] * 2,
        in_specs=[VMEM] * 4,
        out_specs=[VMEM, VMEM],
        scratch_shapes=[
            pltpu.VMEM((2 * SU, SU), jnp.float32),
            pltpu.VMEM((SU, 2 * SU), jnp.float32),
        ],
        compiler_params=PARAMS,
        cost_estimate=pl.CostEstimate(
            flops=1_000_000_000, bytes_accessed=2_000_000, transcendentals=0
        ),
        name="apply_tables",
    )(grids, joined, fetched, swapped)
    summand = lax.ppermute(other, "chan", [(c, 1 - c) for c in range(chan_count)])
    return (mine + summand).reshape(1, 1, half_rows, 2, SU)


def solution(mesh):
    in_specs = (
        P(("facet", "bl"), "chan", None, None),
        P(("facet", "bl"), None, None),
        P(("facet", "bl")),
        P(("facet", "bl"), None),
        P(),
        P(),
        P(("facet", "bl"), None, None, None, None),
        P("bl", None, None),
    )
    out_specs = P("facet", "bl", "chan", None, None)
    return jax.shard_map(body, mesh=mesh, in_specs=in_specs, out_specs=out_specs, check_vma=False)
```

```python
import functools
import math

import jax
import jax.numpy as jnp
from jax import lax
from jax.experimental import pallas as pl
from jax.experimental.pallas import tpu as pltpu
from jax.sharding import PartitionSpec as P

SU = 128
CH = 8
KERNEL_SPREAD = 1.5
ALPHA = math.sqrt(math.log2(math.e) / (2.0 * KERNEL_SPREAD * KERNEL_SPREAD))
UNROLL = 8
REST = 2
NT = (((1,), (1,)), ((), ()))
VMEM = pl.BlockSpec(memory_space=pltpu.VMEM)
HBM = pl.BlockSpec(memory_space=pltpu.HBM)
PARAMS = pltpu.CompilerParams(vmem_limit_bytes=32 * 1024 * 1024)


def cos_sin(turns):
    quarter = jnp.floor(4.0 * turns + 0.5)
    angle = (2.0 * math.pi) * (turns - 0.25 * quarter)
    sq = angle * angle
    sine = angle * (
        1.0 + sq * (-1.0 / 6 + sq * (1.0 / 120 + sq * (-1.0 / 5040 + sq * (1.0 / 362880))))
    )
    cosine = 1.0 + sq * (
        -0.5 + sq * (1.0 / 24 + sq * (-1.0 / 720 + sq * (1.0 / 40320 + sq * (-1.0 / 3628800))))
    )
    turn = quarter.astype(jnp.int32) & 3
    odd = (turn & 1) == 1
    cos_out = jnp.where(odd, sine, cosine)
    sin_out = jnp.where(odd, cosine, sine)
    cos_out = jnp.where((turn == 1) | (turn == 2), -cos_out, cos_out)
    sin_out = jnp.where(turn >= 2, -sin_out, sin_out)
    return cos_out, sin_out


def split_bf16(x):
    high = x.astype(jnp.bfloat16)
    low = (x - high.astype(jnp.float32)).astype(jnp.bfloat16)
    return high, low


def three_parts(x):
    parts = []
    for _ in range(3):
        part = x.astype(jnp.bfloat16)
        x = x - part.astype(jnp.float32)
        parts.append(part.astype(jnp.float32))
    return parts


def sort_kernel(sizes, *refs):
    groups, held, chans, cap, rows = sizes
    table_hbm, outs, half = refs[7], refs[8 : 8 + groups], refs[8 + groups]
    targets = refs[9 + groups : 16 + groups]
    plane_ref, group_ref, samples_b, place_b, offsets_ref, centre_ref, gain_ref = targets
    samples, place, sorted_, filled, sems = refs[16 + groups :]
    facet = lax.axis_index("facet")
    copies = [
        pltpu.make_async_copy(source, target, sems.at[n])
        for n, (source, target) in enumerate(zip(refs[:7], targets))
    ]
    table = pltpu.make_async_copy(table_hbm.at[lax.axis_index("chan")], half, sems.at[7])
    for copy in copies + [table]:
        copy.start()
    sorted_[...] = jnp.zeros_like(sorted_)
    for g in range(groups):
        filled[g] = 0
    for copy in copies:
        copy.wait()
    samples[...] = samples_b[...].astype(jnp.float32)
    place[...] = place_b[...].astype(jnp.float32)
    lane = lax.broadcasted_iota(jnp.int32, (1, SU), 1)
    meta = 2 * cap * (chans + 1)
    centre = [
        part
        for axis in range(2)
        for part in three_parts(jnp.full((1, SU), centre_ref[axis, facet], jnp.float32))
    ]
    gains = three_parts(gain_ref[0])
    for g in range(groups):
        numbers = jnp.zeros((1, SU), jnp.float32)
        for axis in range(2):
            offset = offsets_ref[facet, axis, g].astype(jnp.float32)
            numbers = jnp.where(lane == axis, offset, numbers)
        for n, part in enumerate(centre):
            numbers = jnp.where(lane == 2 + n, part, numbers)
        sorted_[g, meta + 1 : meta + 2, :] = numbers
        for n, part in enumerate(gains):
            sorted_[g, meta + 2 + 2 * n : meta + 4 + 2 * n, :] = part
    for i in range(held):
        g = group_ref[0, i]
        k = filled[g]
        filled[g] = k + 1
        for part in range(2):
            at = part * cap * chans + k * chans
            sorted_[g, pl.ds(at, chans), :] = samples[pl.ds(2 * chans * i + part, chans, stride=2), :]
            at = 2 * cap * chans + part * cap + k
            sorted_[g, pl.ds(at, 1), :] = place[2 * i + part : 2 * i + part + 1, :]
        sorted_[g, meta : meta + 1, :] += jnp.where(
            lane == k, (plane_ref[0, i] + 1).astype(jnp.float32), 0.0
        )
    for shift, out_ref in enumerate(outs):
        g = lax.rem(lax.axis_index("bl") + shift, groups)
        out_ref[:rows, :] = sorted_[g].astype(jnp.bfloat16)
    table.wait()
    outs[1][rows:, :] = half[...]


def join_kernel(rows, half, *refs):
    *pieces, joined = refs
    for n, ref in enumerate(pieces):
        joined[n * rows : (n + 1) * rows, :] = ref[:rows, :]
    at = len(pieces) * rows
    joined[at : at + 2 * SU, :] = half[...]
    joined[at + 2 * SU :, :] = pieces[1][rows:, :]


def collect_kernel(skip, *refs):
    for n, ref in enumerate(refs[:-1]):
        refs[-1][n * 4 * SU : (n + 1) * 4 * SU, :] = ref[skip:, :]


def grid_kernel(sizes, *refs):
    facets, groups, chans, cap, rows, count_here = sizes
    own_ref, grids = refs[0], refs[1 + count_here]
    meta_v, meta_s, order, spots_u, spots_v, turns_real, turns_imag, sem = refs[2 + count_here :]
    pieces = [
        ref.at[pl.ds(n * rows, rows)] for ref in refs[1 : 1 + count_here] for n in range(groups)
    ]
    devices = len(pieces)
    slots = 2 * facets
    lines = cap * chans
    meta_row = 2 * (lines + cap)
    tail = meta_row // 16 * 16
    facet = lax.axis_index("facet")
    group = lax.axis_index("bl")
    chan = lax.axis_index("chan")

    lane = lax.broadcasted_iota(jnp.int32, (1, SU), 1)
    own = own_ref[tail : tail + 16, :].astype(jnp.float32)
    numbers = own[meta_row - tail + 1 : meta_row - tail + 2]
    for d in range(devices):
        meta = pieces[d][tail : tail + 16, :].astype(jnp.float32)
        plane = meta[meta_row - tail : meta_row - tail + 1].astype(jnp.int32) - 1
        set_id = jnp.where(lax.rem(plane, groups) == group, 0, 1)
        code = (d * cap + lane) * slots + 2 * (lax.div(plane, groups) ^ facet) + set_id
        meta_v[d : d + 1, :] = jnp.where(plane >= 0, code, -1)
    copy = pltpu.make_async_copy(meta_v, meta_s, sem)
    copy.start()
    grids[...] = jnp.zeros_like(grids)

    def number(n):
        return jnp.broadcast_to(numbers[:, n : n + 1], (lines, SU))

    offset_u = number(0)
    offset_v = number(1)
    along_l = number(2) + number(3) + number(4)
    along_m = number(5) + number(6) + number(7)
    line = lax.broadcasted_iota(jnp.int32, (lines, SU), 0)
    channel = (chan * chans + lax.rem(line, chans)).astype(jnp.float32)
    scale = 1.0 + 0.01 * (channel - 0.5 * (CH - 1))

    def spread_lines(place):
        return jnp.concatenate(
            [jnp.broadcast_to(place[k : k + 1], (chans, SU)) for k in range(cap)], axis=0
        )

    for d in range(devices):
        at = d * lines
        wide = pieces[d][...].astype(jnp.float32)
        real = wide[:lines]
        imag = wide[lines : 2 * lines]
        along_u = spread_lines(wide[2 * lines : 2 * lines + cap])
        along_v = spread_lines(wide[2 * lines + cap : 2 * (lines + cap)])
        cosine, sine = cos_sin((1.0 / SU) * (scale * (along_u * along_l + along_v * along_m)))
        spots_u[at : at + lines, :] = ALPHA * (scale * along_u - offset_u)
        spots_v[at : at + lines, :] = ALPHA * (scale * along_v - offset_v)
        turns_real[at : at + lines, :] = real * cosine - imag * sine
        turns_imag[at : at + lines, :] = real * sine + imag * cosine
    last = devices * lines
    for ref in (spots_u, spots_v, turns_real, turns_imag):
        ref[last : last + 8, :] = jnp.zeros((8, SU), jnp.float32)
    copy.wait()

    count = jnp.int32(0)
    for d in range(devices):
        for k in range(cap):
            code = meta_s[d, k]
            order[count] = code
            count = count + jnp.where(code >= 0, 1, 0)
    for i in range(REST):
        order[count + i] = devices * cap * slots

    cells = ALPHA * lax.broadcasted_iota(jnp.int32, (SU, SU), 0).astype(jnp.float32)

    def profile(spot):
        apart = spot - cells
        return jnp.exp2(-(apart * apart)).astype(jnp.bfloat16)

    def tiled(row):
        return jnp.broadcast_to(row, (16, SU)).astype(jnp.bfloat16)[None]

    def one_block(at):
        code = order[at]
        slot = lax.rem(code, slots)
        base = lax.div(code, slots) * chans
        lefts_real, lefts_imag, rights = [], [], []
        for c in range(chans):
            here = pl.ds(base + c, 1)
            left = profile(spots_u[here, :]).reshape(SU // 16, 16, SU)
            lefts_real.append((left * tiled(turns_real[here, :])).reshape(SU, SU))
            lefts_imag.append((left * tiled(turns_imag[here, :])).reshape(SU, SU))
            rights.append(profile(spots_v[here, :]))
        left = jnp.concatenate(
            [jnp.concatenate(lefts_real, axis=1), jnp.concatenate(lefts_imag, axis=1)], axis=0
        )
        right = jnp.concatenate(rights, axis=1)
        return slot, lax.dot_general(left, right, NT, preferred_element_type=jnp.float32)

    def steps(first, blocks, number):
        def step(k, carry):
            for slot, part in [one_block(first + k * blocks + i) for i in range(blocks)]:
                grids[slot] += part
            return carry

        lax.fori_loop(0, number, step, 0)

    whole = lax.div(count, UNROLL)
    steps(0, UNROLL, whole)
    steps(whole * UNROLL, REST, lax.div(lax.rem(count, UNROLL) + REST - 1, REST))


def local(kernel, operands, shape, name):
    return pl.pallas_call(
        kernel,
        out_shape=jax.ShapeDtypeStruct(shape, jnp.bfloat16),
        in_specs=[VMEM] * len(operands),
        out_specs=VMEM,
        compiler_params=PARAMS,
        cost_estimate=pl.CostEstimate(flops=0, bytes_accessed=400_000, transcendentals=0),
        name=name,
    )(*operands)


def exchange(value, axis, shift):
    return lax.ppermute(value, axis, [(n, n ^ shift) for n in range(lax.axis_size(axis))])


def table_kernel(sizes, norm, packed, ours, theirs, *refs):
    slots, meta_row = sizes
    grids, (mine_ref, other_ref, table_f, total) = refs[:-4], refs[-4:]
    chan = lax.axis_index("chan")
    first = chan == 0

    def parts(table):
        table_f[...] = table
        return table_f[pl.ds(0, SU, stride=2), :], table_f[pl.ds(1, SU, stride=2), :]

    result = jnp.zeros((SU, 2 * SU), jnp.float32)
    for s in range(slots):
        at = slice(2 * SU * s, 2 * SU * (s + 1))
        fetched = ours[at, :].astype(jnp.float32)
        swapped = theirs[at, :].astype(jnp.float32)
        u_real, u_imag = parts(jnp.where(first, fetched, swapped))
        u_side = jnp.concatenate([u_real.T, u_imag.T], axis=1).astype(jnp.bfloat16)
        grid_real, grid_imag = (
            sum(ref[s, part * SU : (part + 1) * SU, :] for ref in grids) for part in range(2)
        )
        inner = jnp.concatenate(
            [
                jnp.concatenate([grid_real, grid_imag], axis=1),
                jnp.concatenate([-grid_imag, grid_real], axis=1),
            ],
            axis=0,
        )
        high, low = split_bf16(inner)
        half = jnp.dot(u_side, high, preferred_element_type=jnp.float32) + jnp.dot(
            u_side, low, preferred_element_type=jnp.float32
        )
        v_real, v_imag = parts(jnp.where(first, swapped, fetched))
        v_side = jnp.concatenate(
            [
                jnp.concatenate([v_real, v_imag], axis=1),
                jnp.concatenate([-v_imag, v_real], axis=1),
            ],
            axis=0,
        ).astype(jnp.bfloat16)
        high, low = split_bf16(half)
        result = (
            result
            + jnp.dot(high, v_side, preferred_element_type=jnp.float32)
            + jnp.dot(low, v_side, preferred_element_type=jnp.float32)
        )
    tail = meta_row // 16 * 16
    wide = packed[tail : tail + 16, :].astype(jnp.float32)
    at = meta_row - tail + 2
    gain = (wide[at : at + 2] + wide[at + 2 : at + 4]) + wide[at + 4 : at + 6]
    gain_u = jnp.broadcast_to(gain[0:1], (SU, SU)).T
    gains = gain_u * gain[1:2] * norm
    total[...] = result * jnp.concatenate([gains, gains], axis=1)
    half_rows = mine_ref.shape[0]
    mine_ref[...] = total[pl.ds(pl.multiple_of(chan * half_rows, half_rows), half_rows), :]
    other_ref[...] = total[pl.ds(pl.multiple_of((1 - chan) * half_rows, half_rows), half_rows), :]


def body(
    visibilities, coords, plane_index, block_group, offsets, facet_centre, tables, antenna_gain
):
    facets = lax.axis_size("facet")
    groups = lax.axis_size("bl")
    chan_count = lax.axis_size("chan")
    held, chans = visibilities.shape[:2]
    devices = facets * groups
    slots = 2 * facets
    cap = max(2, 2 * held // groups)
    meta_row = 2 * cap * (chans + 1)
    rows = -(-(meta_row + 8) // 16) * 16
    half_rows = SU // chan_count
    norm = SU / math.sqrt(visibilities.shape[3] * held * facets * CH)

    own_table = tables.reshape(2, 2 * SU, SU)
    *pieces, half = pl.pallas_call(
        functools.partial(sort_kernel, (groups, held, chans, cap, rows)),
        out_shape=[
            jax.ShapeDtypeStruct((rows + (2 * SU if shift == 1 else 0), SU), jnp.bfloat16)
            for shift in range(groups)
        ]
        + [jax.ShapeDtypeStruct((2 * SU, SU), jnp.bfloat16)],
        in_specs=[HBM] * 8,
        out_specs=[VMEM] * (groups + 1),
        scratch_shapes=[
            pltpu.SMEM((1, held), jnp.int32),
            pltpu.SMEM((1, held), jnp.int32),
            pltpu.VMEM((held * 2 * chans, SU), jnp.bfloat16),
            pltpu.VMEM((held * 2, SU), jnp.bfloat16),
            pltpu.SMEM((facets, 2, groups), jnp.int32),
            pltpu.SMEM((2, facets), jnp.float32),
            pltpu.VMEM((1, 2, SU), jnp.float32),
            pltpu.VMEM((held * 2 * chans, SU), jnp.float32),
            pltpu.VMEM((held * 2, SU), jnp.float32),
            pltpu.VMEM((groups, rows, SU), jnp.float32),
            pltpu.SMEM((groups,), jnp.int32),
            pltpu.SemaphoreType.DMA((8,)),
        ],
        compiler_params=PARAMS,
        cost_estimate=pl.CostEstimate(flops=100_000, bytes_accessed=100_000, transcendentals=0),
        name="sort_blocks",
    )(
        *(
            pltpu.with_memory_space_constraint(operand, pltpu.HBM)
            for operand in (
                plane_index.reshape(1, held),
                block_group.T,
                visibilities.reshape(held * 2 * chans, SU),
                coords.reshape(held * 2, SU),
                offsets.transpose(0, 2, 1),
                facet_centre.T,
                antenna_gain,
                own_table,
            )
        )
    )
    arrived = [
        lax.ppermute(pieces[shift], "bl", [(g, (g + shift) % groups) for g in range(groups)])
        for shift in [1, *range(groups - 1, 1, -1)]
    ]
    vis_rows = groups * rows
    joined = local(
        functools.partial(join_kernel, rows),
        [half, pieces[0], *arrived],
        (vis_rows + 4 * SU, SU),
        "join",
    )
    blocks = [joined] + [exchange(joined, "facet", shift) for shift in range(1, facets)]
    def grid(some):
        lines = len(some) * groups * cap
        return pl.pallas_call(
            functools.partial(grid_kernel, (facets, groups, chans, cap, rows, len(some))),
            out_shape=jax.ShapeDtypeStruct((slots, 2 * SU, SU), jnp.float32),
            in_specs=[VMEM] * (1 + len(some)),
            out_specs=VMEM,
            scratch_shapes=[
                pltpu.VMEM((len(some) * groups, SU), jnp.int32),
                pltpu.SMEM((len(some) * groups, SU), jnp.int32),
                pltpu.SMEM((lines + REST,), jnp.int32),
            ]
            + [pltpu.VMEM((lines * chans + 8, SU), jnp.float32)] * 4
            + [pltpu.SemaphoreType.DMA],
            compiler_params=PARAMS,
            cost_estimate=pl.CostEstimate(
                flops=len(some) * 1_000_000_000,
                bytes_accessed=1_000_000,
                transcendentals=len(some) * 1_000_000,
            ),
            name="grid",
        )(joined, *some)

    grids = [grid(blocks[:1]), grid(blocks[-1:])]
    blocks, grids = lax.optimization_barrier((blocks, grids))
    fetched = local(
        functools.partial(collect_kernel, vis_rows), blocks, (facets * 4 * SU, SU), "collect"
    )
    swapped = lax.ppermute(fetched, "chan", [(c, 1 - c) for c in range(chan_count)])
    grids.append(grid(blocks[1:-1]))
    mine, other = pl.pallas_call(
        functools.partial(table_kernel, (slots, meta_row), norm),
        out_shape=[jax.ShapeDtypeStruct((half_rows, 2 * SU), jnp.float32)] * 2,
        in_specs=[VMEM] * (3 + len(grids)),
        out_specs=[VMEM, VMEM],
        scratch_shapes=[
            pltpu.VMEM((2 * SU, SU), jnp.float32),
            pltpu.VMEM((SU, 2 * SU), jnp.float32),
        ],
        compiler_params=PARAMS,
        cost_estimate=pl.CostEstimate(
            flops=1_000_000_000, bytes_accessed=2_000_000, transcendentals=0
        ),
        name="apply_tables",
    )(joined, fetched, swapped, *grids)
    summand = lax.ppermute(other, "chan", [(c, 1 - c) for c in range(chan_count)])
    return (mine + summand).reshape(1, 1, half_rows, 2, SU)


def solution(mesh):
    in_specs = (
        P(("facet", "bl"), "chan", None, None),
        P(("facet", "bl"), None, None),
        P(("facet", "bl")),
        P(("facet", "bl"), None),
        P(),
        P(),
        P(("facet", "bl"), None, None, None, None),
        P("bl", None, None),
    )
    out_specs = P("facet", "bl", "chan", None, None)
    return jax.shard_map(body, mesh=mesh, in_specs=in_specs, out_specs=out_specs, check_vma=False)
```

```python
import functools
import math

import jax
import jax.numpy as jnp
from jax import lax
from jax.experimental import pallas as pl
from jax.experimental.pallas import tpu as pltpu
from jax.sharding import PartitionSpec as P

SU = 128
CH = 8
KERNEL_SPREAD = 1.5
ALPHA = math.sqrt(math.log2(math.e) / (2.0 * KERNEL_SPREAD * KERNEL_SPREAD))
UNROLL = 4
NT = (((1,), (1,)), ((), ()))
VMEM = pl.BlockSpec(memory_space=pltpu.VMEM)
HBM = pl.BlockSpec(memory_space=pltpu.HBM)
PARAMS = pltpu.CompilerParams(vmem_limit_bytes=32 * 1024 * 1024)


def cos_sin(turns):
    quarter = jnp.floor(4.0 * turns + 0.5)
    angle = (2.0 * math.pi) * (turns - 0.25 * quarter)
    sq = angle * angle
    sine = angle * (
        1.0 + sq * (-1.0 / 6 + sq * (1.0 / 120 + sq * (-1.0 / 5040 + sq * (1.0 / 362880))))
    )
    cosine = 1.0 + sq * (
        -0.5 + sq * (1.0 / 24 + sq * (-1.0 / 720 + sq * (1.0 / 40320 + sq * (-1.0 / 3628800))))
    )
    turn = quarter.astype(jnp.int32) & 3
    odd = (turn & 1) == 1
    cos_out = jnp.where(odd, sine, cosine)
    sin_out = jnp.where(odd, cosine, sine)
    cos_out = jnp.where((turn == 1) | (turn == 2), -cos_out, cos_out)
    sin_out = jnp.where(turn >= 2, -sin_out, sin_out)
    return cos_out, sin_out


def split_bf16(x):
    high = x.astype(jnp.bfloat16)
    low = (x - high.astype(jnp.float32)).astype(jnp.bfloat16)
    return high, low


def three_parts(x):
    parts = []
    for _ in range(3):
        part = x.astype(jnp.bfloat16)
        x = x - part.astype(jnp.float32)
        parts.append(part.astype(jnp.float32))
    return parts


def sort_kernel(sizes, *refs):
    groups, held, chans, cap, rows = sizes
    table_hbm, outs, half = refs[7], refs[8 : 8 + groups], refs[8 + groups]
    targets = refs[9 + groups : 16 + groups]
    plane_ref, group_ref, samples_b, place_b, offsets_ref, centre_ref, gain_ref = targets
    samples, place, sorted_, filled, sems = refs[16 + groups :]
    facet = lax.axis_index("facet")
    copies = [
        pltpu.make_async_copy(source, target, sems.at[n])
        for n, (source, target) in enumerate(zip(refs[:7], targets))
    ]
    table = pltpu.make_async_copy(table_hbm.at[lax.axis_index("chan")], half, sems.at[7])
    for copy in copies + [table]:
        copy.start()
    sorted_[...] = jnp.zeros_like(sorted_)
    for g in range(groups):
        filled[g] = 0
    for copy in copies:
        copy.wait()
    samples[...] = samples_b[...].astype(jnp.float32)
    place[...] = place_b[...].astype(jnp.float32)
    lane = lax.broadcasted_iota(jnp.int32, (1, SU), 1)
    meta = 2 * cap * (chans + 1)
    centre = [
        part
        for axis in range(2)
        for part in three_parts(jnp.full((1, SU), centre_ref[axis, facet], jnp.float32))
    ]
    gains = three_parts(gain_ref[0])
    for g in range(groups):
        numbers = jnp.zeros((1, SU), jnp.float32)
        for axis in range(2):
            offset = offsets_ref[facet, axis, g].astype(jnp.float32)
            numbers = jnp.where(lane == axis, offset, numbers)
        for n, part in enumerate(centre):
            numbers = jnp.where(lane == 2 + n, part, numbers)
        sorted_[g, meta + 1 : meta + 2, :] = numbers
        for n, part in enumerate(gains):
            sorted_[g, meta + 2 + 2 * n : meta + 4 + 2 * n, :] = part
    for i in range(held):
        g = group_ref[0, i]
        k = filled[g]
        filled[g] = k + 1
        for part in range(2):
            at = part * cap * chans + k * chans
            sorted_[g, pl.ds(at, chans), :] = samples[pl.ds(2 * chans * i + part, chans, stride=2), :]
            at = 2 * cap * chans + part * cap + k
            sorted_[g, pl.ds(at, 1), :] = place[2 * i + part : 2 * i + part + 1, :]
        sorted_[g, meta : meta + 1, :] += jnp.where(
            lane == k, (plane_ref[0, i] + 1).astype(jnp.float32), 0.0
        )
    for shift, out_ref in enumerate(outs):
        g = lax.rem(lax.axis_index("bl") + shift, groups)
        out_ref[:rows, :] = sorted_[g].astype(jnp.bfloat16)
    table.wait()
    outs[1][rows:, :] = half[...]


def join_kernel(rows, half, *refs):
    *pieces, joined = refs
    for n, ref in enumerate(pieces):
        joined[n * rows : (n + 1) * rows, :] = ref[:rows, :]
    at = len(pieces) * rows
    joined[at : at + 2 * SU, :] = half[...]
    joined[at + 2 * SU :, :] = pieces[1][rows:, :]


def collect_kernel(skip, *refs):
    for n, ref in enumerate(refs[:-1]):
        refs[-1][n * 4 * SU : (n + 1) * 4 * SU, :] = ref[skip:, :]


def grid_kernel(sizes, *refs):
    facets, groups, chans, cap, rows, count_here = sizes
    own_ref, grids = refs[0], refs[1 + count_here]
    meta_v, meta_s, order, spots_u, spots_v, turns_real, turns_imag, sem = refs[2 + count_here :]
    pieces = [
        ref.at[pl.ds(n * rows, rows)] for ref in refs[1 : 1 + count_here] for n in range(groups)
    ]
    devices = len(pieces)
    slots = 2 * facets
    lines = cap * chans
    meta_row = 2 * (lines + cap)
    tail = meta_row // 16 * 16
    facet = lax.axis_index("facet")
    group = lax.axis_index("bl")
    chan = lax.axis_index("chan")

    lane = lax.broadcasted_iota(jnp.int32, (1, SU), 1)
    own = own_ref[tail : tail + 16, :].astype(jnp.float32)
    numbers = own[meta_row - tail + 1 : meta_row - tail + 2]
    for d in range(devices):
        meta = pieces[d][tail : tail + 16, :].astype(jnp.float32)
        plane = meta[meta_row - tail : meta_row - tail + 1].astype(jnp.int32) - 1
        set_id = jnp.where(lax.rem(plane, groups) == group, 0, 1)
        code = (d * cap + lane) * slots + 2 * (lax.div(plane, groups) ^ facet) + set_id
        meta_v[d : d + 1, :] = jnp.where(plane >= 0, code, -1)
    copy = pltpu.make_async_copy(meta_v, meta_s, sem)
    copy.start()
    grids[...] = jnp.zeros_like(grids)

    def number(n):
        return jnp.broadcast_to(numbers[:, n : n + 1], (lines, SU))

    offset_u = number(0)
    offset_v = number(1)
    along_l = number(2) + number(3) + number(4)
    along_m = number(5) + number(6) + number(7)
    line = lax.broadcasted_iota(jnp.int32, (lines, SU), 0)
    channel = (chan * chans + lax.rem(line, chans)).astype(jnp.float32)
    scale = 1.0 + 0.01 * (channel - 0.5 * (CH - 1))

    def spread_lines(place):
        return jnp.concatenate(
            [jnp.broadcast_to(place[k : k + 1], (chans, SU)) for k in range(cap)], axis=0
        )

    for d in range(devices):
        at = d * lines
        wide = pieces[d][...].astype(jnp.float32)
        real = wide[:lines]
        imag = wide[lines : 2 * lines]
        along_u = spread_lines(wide[2 * lines : 2 * lines + cap])
        along_v = spread_lines(wide[2 * lines + cap : 2 * (lines + cap)])
        cosine, sine = cos_sin((1.0 / SU) * (scale * (along_u * along_l + along_v * along_m)))
        spots_u[at : at + lines, :] = ALPHA * (scale * along_u - offset_u)
        spots_v[at : at + lines, :] = ALPHA * (scale * along_v - offset_v)
        turns_real[at : at + lines, :] = real * cosine - imag * sine
        turns_imag[at : at + lines, :] = real * sine + imag * cosine
    last = devices * lines
    for ref in (spots_u, spots_v, turns_real, turns_imag):
        ref[last : last + 8, :] = jnp.zeros((8, SU), jnp.float32)
    copy.wait()

    count = jnp.int32(0)
    for d in range(devices):
        for k in range(cap):
            code = meta_s[d, k]
            order[count] = code
            count = count + jnp.where(code >= 0, 1, 0)
    for i in range(UNROLL):
        order[count + i] = devices * cap * slots

    cells = ALPHA * lax.broadcasted_iota(jnp.int32, (SU, SU), 0).astype(jnp.float32)

    def profile(spot):
        apart = spot - cells
        return jnp.exp2(-(apart * apart)).astype(jnp.bfloat16)

    def tiled(row):
        return jnp.broadcast_to(row, (16, SU)).astype(jnp.bfloat16)[None]

    def one_block(at):
        code = order[at]
        slot = lax.rem(code, slots)
        base = lax.div(code, slots) * chans
        lefts_real, lefts_imag, rights = [], [], []
        for c in range(chans):
            here = pl.ds(base + c, 1)
            left = profile(spots_u[here, :]).reshape(SU // 16, 16, SU)
            lefts_real.append((left * tiled(turns_real[here, :])).reshape(SU, SU))
            lefts_imag.append((left * tiled(turns_imag[here, :])).reshape(SU, SU))
            rights.append(profile(spots_v[here, :]))
        left = jnp.concatenate(
            [jnp.concatenate(lefts_real, axis=1), jnp.concatenate(lefts_imag, axis=1)], axis=0
        )
        right = jnp.concatenate(rights, axis=1)
        return slot, lax.dot_general(left, right, NT, preferred_element_type=jnp.float32)

    def step(k, carry):
        for slot, part in [one_block(k * UNROLL + i) for i in range(UNROLL)]:
            grids[slot] += part
        return carry

    lax.fori_loop(0, lax.div(count + UNROLL - 1, UNROLL), step, 0)


def local(kernel, operands, shape, name):
    return pl.pallas_call(
        kernel,
        out_shape=jax.ShapeDtypeStruct(shape, jnp.bfloat16),
        in_specs=[VMEM] * len(operands),
        out_specs=VMEM,
        compiler_params=PARAMS,
        cost_estimate=pl.CostEstimate(flops=0, bytes_accessed=400_000, transcendentals=0),
        name=name,
    )(*operands)


def exchange(value, axis, shift):
    return lax.ppermute(value, axis, [(n, n ^ shift) for n in range(lax.axis_size(axis))])


def table_kernel(sizes, norm, packed, ours, theirs, *refs):
    slots, meta_row = sizes
    grids, (mine_ref, other_ref, table_f, total) = refs[:-4], refs[-4:]
    chan = lax.axis_index("chan")
    first = chan == 0

    def parts(table):
        table_f[...] = table
        return table_f[pl.ds(0, SU, stride=2), :], table_f[pl.ds(1, SU, stride=2), :]

    result = jnp.zeros((SU, 2 * SU), jnp.float32)
    for s in range(slots):
        at = slice(2 * SU * s, 2 * SU * (s + 1))
        fetched = ours[at, :].astype(jnp.float32)
        swapped = theirs[at, :].astype(jnp.float32)
        u_real, u_imag = parts(jnp.where(first, fetched, swapped))
        u_side = jnp.concatenate([u_real.T, u_imag.T], axis=1).astype(jnp.bfloat16)
        grid_real, grid_imag = (
            sum(ref[s, part * SU : (part + 1) * SU, :] for ref in grids) for part in range(2)
        )
        high, low = (
            jnp.concatenate(
                [
                    jnp.concatenate([real, imag], axis=1),
                    jnp.concatenate([-imag, real], axis=1),
                ],
                axis=0,
            )
            for real, imag in zip(split_bf16(grid_real), split_bf16(grid_imag))
        )
        half = jnp.dot(u_side, high, preferred_element_type=jnp.float32) + jnp.dot(
            u_side, low, preferred_element_type=jnp.float32
        )
        v_real, v_imag = parts(jnp.where(first, swapped, fetched))
        v_side = jnp.concatenate(
            [
                jnp.concatenate([v_real, v_imag], axis=1),
                jnp.concatenate([-v_imag, v_real], axis=1),
            ],
            axis=0,
        ).astype(jnp.bfloat16)
        high, low = split_bf16(half)
        result = (
            result
            + jnp.dot(high, v_side, preferred_element_type=jnp.float32)
            + jnp.dot(low, v_side, preferred_element_type=jnp.float32)
        )
    tail = meta_row // 16 * 16
    wide = packed[tail : tail + 16, :].astype(jnp.float32)
    at = meta_row - tail + 2
    gain = (wide[at : at + 2] + wide[at + 2 : at + 4]) + wide[at + 4 : at + 6]
    gain_u = jnp.broadcast_to(gain[0:1], (SU, SU)).T
    gains = gain_u * gain[1:2] * norm
    total[...] = result * jnp.concatenate([gains, gains], axis=1)
    half_rows = mine_ref.shape[0]
    mine_ref[...] = total[pl.ds(pl.multiple_of(chan * half_rows, half_rows), half_rows), :]
    other_ref[...] = total[pl.ds(pl.multiple_of((1 - chan) * half_rows, half_rows), half_rows), :]


def body(
    visibilities, coords, plane_index, block_group, offsets, facet_centre, tables, antenna_gain
):
    facets = lax.axis_size("facet")
    groups = lax.axis_size("bl")
    chan_count = lax.axis_size("chan")
    held, chans = visibilities.shape[:2]
    devices = facets * groups
    slots = 2 * facets
    cap = max(2, 2 * held // groups)
    meta_row = 2 * cap * (chans + 1)
    rows = -(-(meta_row + 8) // 16) * 16
    half_rows = SU // chan_count
    norm = SU / math.sqrt(visibilities.shape[3] * held * facets * CH)

    own_table = tables.reshape(2, 2 * SU, SU)
    *pieces, half = pl.pallas_call(
        functools.partial(sort_kernel, (groups, held, chans, cap, rows)),
        out_shape=[
            jax.ShapeDtypeStruct((rows + (2 * SU if shift == 1 else 0), SU), jnp.bfloat16)
            for shift in range(groups)
        ]
        + [jax.ShapeDtypeStruct((2 * SU, SU), jnp.bfloat16)],
        in_specs=[HBM] * 8,
        out_specs=[VMEM] * (groups + 1),
        scratch_shapes=[
            pltpu.SMEM((1, held), jnp.int32),
            pltpu.SMEM((1, held), jnp.int32),
            pltpu.VMEM((held * 2 * chans, SU), jnp.bfloat16),
            pltpu.VMEM((held * 2, SU), jnp.bfloat16),
            pltpu.SMEM((facets, 2, groups), jnp.int32),
            pltpu.SMEM((2, facets), jnp.float32),
            pltpu.VMEM((1, 2, SU), jnp.float32),
            pltpu.VMEM((held * 2 * chans, SU), jnp.float32),
            pltpu.VMEM((held * 2, SU), jnp.float32),
            pltpu.VMEM((groups, rows, SU), jnp.float32),
            pltpu.SMEM((groups,), jnp.int32),
            pltpu.SemaphoreType.DMA((8,)),
        ],
        compiler_params=PARAMS,
        cost_estimate=pl.CostEstimate(flops=100_000, bytes_accessed=100_000, transcendentals=0),
        name="sort_blocks",
    )(
        *(
            pltpu.with_memory_space_constraint(operand, pltpu.HBM)
            for operand in (
                plane_index.reshape(1, held),
                block_group.T,
                visibilities.reshape(held * 2 * chans, SU),
                coords.reshape(held * 2, SU),
                offsets.transpose(0, 2, 1),
                facet_centre.T,
                antenna_gain,
                own_table,
            )
        )
    )
    arrived = [
        lax.ppermute(pieces[shift], "bl", [(g, (g + shift) % groups) for g in range(groups)])
        for shift in [1, *range(groups - 1, 1, -1)]
    ]
    vis_rows = groups * rows
    joined = local(
        functools.partial(join_kernel, rows),
        [half, pieces[0], *arrived],
        (vis_rows + 4 * SU, SU),
        "join",
    )
    blocks = [joined] + [exchange(joined, "facet", shift) for shift in range(1, facets)]
    def grid(some):
        lines = len(some) * groups * cap
        return pl.pallas_call(
            functools.partial(grid_kernel, (facets, groups, chans, cap, rows, len(some))),
            out_shape=jax.ShapeDtypeStruct((slots, 2 * SU, SU), jnp.float32),
            in_specs=[VMEM] * (1 + len(some)),
            out_specs=VMEM,
            scratch_shapes=[
                pltpu.VMEM((len(some) * groups, SU), jnp.int32),
                pltpu.SMEM((len(some) * groups, SU), jnp.int32),
                pltpu.SMEM((lines + UNROLL,), jnp.int32),
            ]
            + [pltpu.VMEM((lines * chans + 8, SU), jnp.float32)] * 4
            + [pltpu.SemaphoreType.DMA],
            compiler_params=PARAMS,
            cost_estimate=pl.CostEstimate(
                flops=len(some) * 1_000_000_000,
                bytes_accessed=1_000_000,
                transcendentals=len(some) * 1_000_000,
            ),
            name="grid",
        )(joined, *some)

    grids = [grid(blocks[:1]), grid(blocks[-1:])]
    blocks, grids = lax.optimization_barrier((blocks, grids))
    fetched = local(
        functools.partial(collect_kernel, vis_rows), blocks, (facets * 4 * SU, SU), "collect"
    )
    swapped = lax.ppermute(fetched, "chan", [(c, 1 - c) for c in range(chan_count)])
    grids.append(grid(blocks[1:-1]))
    mine, other = pl.pallas_call(
        functools.partial(table_kernel, (slots, meta_row), norm),
        out_shape=[jax.ShapeDtypeStruct((half_rows, 2 * SU), jnp.float32)] * 2,
        in_specs=[VMEM] * (3 + len(grids)),
        out_specs=[VMEM, VMEM],
        scratch_shapes=[
            pltpu.VMEM((2 * SU, SU), jnp.float32),
            pltpu.VMEM((SU, 2 * SU), jnp.float32),
        ],
        compiler_params=PARAMS,
        cost_estimate=pl.CostEstimate(
            flops=1_000_000_000, bytes_accessed=2_000_000, transcendentals=0
        ),
        name="apply_tables",
    )(joined, fetched, swapped, *grids)
    summand = lax.ppermute(other, "chan", [(c, 1 - c) for c in range(chan_count)])
    return (mine + summand).reshape(1, 1, half_rows, 2, SU)


def solution(mesh):
    in_specs = (
        P(("facet", "bl"), "chan", None, None),
        P(("facet", "bl"), None, None),
        P(("facet", "bl")),
        P(("facet", "bl"), None),
        P(),
        P(),
        P(("facet", "bl"), None, None, None, None),
        P("bl", None, None),
    )
    out_specs = P("facet", "bl", "chan", None, None)
    return jax.shard_map(body, mesh=mesh, in_specs=in_specs, out_specs=out_specs, check_vma=False)
```

```python
import functools
import math

import jax
import jax.numpy as jnp
from jax import lax
from jax.experimental import pallas as pl
from jax.experimental.pallas import tpu as pltpu
from jax.sharding import PartitionSpec as P

SU = 128
CH = 8
KERNEL_SPREAD = 1.5
ALPHA = math.sqrt(math.log2(math.e) / (2.0 * KERNEL_SPREAD * KERNEL_SPREAD))
UNROLL = 4
NT = (((1,), (1,)), ((), ()))
VMEM = pl.BlockSpec(memory_space=pltpu.VMEM)
HBM = pl.BlockSpec(memory_space=pltpu.HBM)
PARAMS = pltpu.CompilerParams(vmem_limit_bytes=32 * 1024 * 1024)


def cos_sin(turns):
    quarter = jnp.floor(4.0 * turns + 0.5)
    angle = (2.0 * math.pi) * (turns - 0.25 * quarter)
    sq = angle * angle
    sine = angle * (
        1.0 + sq * (-1.0 / 6 + sq * (1.0 / 120 + sq * (-1.0 / 5040 + sq * (1.0 / 362880))))
    )
    cosine = 1.0 + sq * (
        -0.5 + sq * (1.0 / 24 + sq * (-1.0 / 720 + sq * (1.0 / 40320 + sq * (-1.0 / 3628800))))
    )
    turn = quarter.astype(jnp.int32) & 3
    odd = (turn & 1) == 1
    cos_out = jnp.where(odd, sine, cosine)
    sin_out = jnp.where(odd, cosine, sine)
    cos_out = jnp.where((turn == 1) | (turn == 2), -cos_out, cos_out)
    sin_out = jnp.where(turn >= 2, -sin_out, sin_out)
    return cos_out, sin_out


def split_bf16(x):
    high = x.astype(jnp.bfloat16)
    low = (x - high.astype(jnp.float32)).astype(jnp.bfloat16)
    return high, low


def three_parts(x):
    parts = []
    for _ in range(3):
        part = x.astype(jnp.bfloat16)
        x = x - part.astype(jnp.float32)
        parts.append(part.astype(jnp.float32))
    return parts


def sort_kernel(sizes, *refs):
    groups, held, chans, cap, rows = sizes
    table_hbm, outs, half = refs[7], refs[8 : 8 + groups], refs[8 + groups]
    targets = refs[9 + groups : 16 + groups]
    plane_ref, group_ref, samples_b, place_b, offsets_ref, centre_ref, gain_ref = targets
    samples, place, sorted_, filled, sems = refs[16 + groups :]
    facet = lax.axis_index("facet")
    copies = [
        pltpu.make_async_copy(source, target, sems.at[n])
        for n, (source, target) in enumerate(zip(refs[:7], targets))
    ]
    table = pltpu.make_async_copy(table_hbm.at[lax.axis_index("chan")], half, sems.at[7])
    for copy in copies + [table]:
        copy.start()
    sorted_[...] = jnp.zeros_like(sorted_)
    for g in range(groups):
        filled[g] = 0
    for copy in copies:
        copy.wait()
    samples[...] = samples_b[...].astype(jnp.float32)
    place[...] = place_b[...].astype(jnp.float32)
    lane = lax.broadcasted_iota(jnp.int32, (1, SU), 1)
    meta = 2 * cap * (chans + 1)
    centre = [
        part
        for axis in range(2)
        for part in three_parts(jnp.full((1, SU), centre_ref[axis, facet], jnp.float32))
    ]
    gains = three_parts(gain_ref[0])
    for g in range(groups):
        numbers = jnp.zeros((1, SU), jnp.float32)
        for axis in range(2):
            offset = offsets_ref[facet, axis, g].astype(jnp.float32)
            numbers = jnp.where(lane == axis, offset, numbers)
        for n, part in enumerate(centre):
            numbers = jnp.where(lane == 2 + n, part, numbers)
        sorted_[g, meta + 1 : meta + 2, :] = numbers
        for n, part in enumerate(gains):
            sorted_[g, meta + 2 + 2 * n : meta + 4 + 2 * n, :] = part
    for i in range(held):
        g = group_ref[0, i]
        k = filled[g]
        filled[g] = k + 1
        for part in range(2):
            at = part * cap * chans + k * chans
            sorted_[g, pl.ds(at, chans), :] = samples[pl.ds(2 * chans * i + part, chans, stride=2), :]
            at = 2 * cap * chans + part * cap + k
            sorted_[g, pl.ds(at, 1), :] = place[2 * i + part : 2 * i + part + 1, :]
        sorted_[g, meta : meta + 1, :] += jnp.where(
            lane == k, (plane_ref[0, i] + 1).astype(jnp.float32), 0.0
        )
    for shift, out_ref in enumerate(outs):
        g = lax.rem(lax.axis_index("bl") + shift, groups)
        out_ref[:rows, :] = sorted_[g].astype(jnp.bfloat16)
    table.wait()
    outs[1][rows:, :] = half[...]


def join_kernel(rows, half, *refs):
    *pieces, joined = refs
    for n, ref in enumerate(pieces):
        joined[n * rows : (n + 1) * rows, :] = ref[:rows, :]
    at = len(pieces) * rows
    joined[at : at + 2 * SU, :] = half[...]
    joined[at + 2 * SU :, :] = pieces[1][rows:, :]


def collect_kernel(skip, *refs):
    for n, ref in enumerate(refs[:-1]):
        refs[-1][n * 4 * SU : (n + 1) * 4 * SU, :] = ref[skip:, :]


def grid_kernel(sizes, *refs):
    facets, groups, chans, cap, rows, count_here = sizes
    own_ref, grids = refs[0], refs[1 + count_here]
    order, spots_u, spots_v, turns_real, turns_imag = refs[2 + count_here :]
    pieces = [
        ref.at[pl.ds(n * rows, rows)] for ref in refs[1 : 1 + count_here] for n in range(groups)
    ]
    devices = len(pieces)
    slots = 2 * facets
    lines = cap * chans
    meta_row = 2 * (lines + cap)
    tail = meta_row // 16 * 16
    facet = lax.axis_index("facet")
    group = lax.axis_index("bl")
    chan = lax.axis_index("chan")

    lane = lax.broadcasted_iota(jnp.int32, (1, SU), 1)
    own = own_ref[tail : tail + 16, :].astype(jnp.float32)
    numbers = own[meta_row - tail + 1 : meta_row - tail + 2]
    codes = []
    for d in range(devices):
        meta = pieces[d][tail : tail + 16, :].astype(jnp.float32)
        plane = meta[meta_row - tail : meta_row - tail + 1].astype(jnp.int32) - 1
        set_id = jnp.where(lax.rem(plane, groups) == group, 0, 1)
        code = (d * cap + lane) * slots + 2 * (lax.div(plane, groups) ^ facet) + set_id
        codes.append(jnp.where(plane >= 0, code, -1))
    grids[...] = jnp.zeros_like(grids)

    def number(n):
        return jnp.broadcast_to(numbers[:, n : n + 1], (lines, SU))

    offset_u = number(0)
    offset_v = number(1)
    along_l = number(2) + number(3) + number(4)
    along_m = number(5) + number(6) + number(7)
    line = lax.broadcasted_iota(jnp.int32, (lines, SU), 0)
    channel = (chan * chans + lax.rem(line, chans)).astype(jnp.float32)
    scale = 1.0 + 0.01 * (channel - 0.5 * (CH - 1))

    def spread_lines(place):
        return jnp.concatenate(
            [jnp.broadcast_to(place[k : k + 1], (chans, SU)) for k in range(cap)], axis=0
        )

    for d in range(devices):
        at = d * lines
        wide = pieces[d][...].astype(jnp.float32)
        real = wide[:lines]
        imag = wide[lines : 2 * lines]
        along_u = spread_lines(wide[2 * lines : 2 * lines + cap])
        along_v = spread_lines(wide[2 * lines + cap : 2 * (lines + cap)])
        cosine, sine = cos_sin((1.0 / SU) * (scale * (along_u * along_l + along_v * along_m)))
        spots_u[at : at + lines, :] = ALPHA * (scale * along_u - offset_u)
        spots_v[at : at + lines, :] = ALPHA * (scale * along_v - offset_v)
        turns_real[at : at + lines, :] = real * cosine - imag * sine
        turns_imag[at : at + lines, :] = real * sine + imag * cosine
    last = devices * lines
    for ref in (spots_u, spots_v, turns_real, turns_imag):
        ref[last : last + 8, :] = jnp.zeros((8, SU), jnp.float32)

    count = jnp.int32(0)
    for d in range(devices):
        for k in range(cap):
            code = codes[d][0, k]
            order[count] = code
            count = count + jnp.where(code >= 0, 1, 0)
    for i in range(UNROLL):
        order[count + i] = devices * cap * slots

    cells = ALPHA * lax.broadcasted_iota(jnp.int32, (SU, SU), 0).astype(jnp.float32)

    def profile(spot):
        apart = spot - cells
        return jnp.exp2(-((apart * apart).astype(jnp.bfloat16)))

    def tiled(row):
        return jnp.broadcast_to(row, (16, SU)).astype(jnp.bfloat16)[None]

    def one_block(at):
        code = order[at]
        slot = lax.rem(code, slots)
        base = lax.div(code, slots) * chans
        lefts_real, lefts_imag, rights = [], [], []
        for c in range(chans):
            here = pl.ds(base + c, 1)
            left = profile(spots_u[here, :]).reshape(SU // 16, 16, SU)
            lefts_real.append((left * tiled(turns_real[here, :])).reshape(SU, SU))
            lefts_imag.append((left * tiled(turns_imag[here, :])).reshape(SU, SU))
            rights.append(profile(spots_v[here, :]))
        left = jnp.concatenate(
            [jnp.concatenate(lefts_real, axis=1), jnp.concatenate(lefts_imag, axis=1)], axis=0
        )
        right = jnp.concatenate(rights, axis=1)
        return slot, lax.dot_general(left, right, NT, preferred_element_type=jnp.float32)

    def step(k, carry):
        for slot, part in [one_block(k * UNROLL + i) for i in range(UNROLL)]:
            grids[slot] += part
        return carry

    lax.fori_loop(0, lax.div(count + UNROLL - 1, UNROLL), step, 0)


def local(kernel, operands, shape, name):
    return pl.pallas_call(
        kernel,
        out_shape=jax.ShapeDtypeStruct(shape, jnp.bfloat16),
        in_specs=[VMEM] * len(operands),
        out_specs=VMEM,
        compiler_params=PARAMS,
        cost_estimate=pl.CostEstimate(flops=0, bytes_accessed=400_000, transcendentals=0),
        name=name,
    )(*operands)


def exchange(value, axis, shift):
    return lax.ppermute(value, axis, [(n, n ^ shift) for n in range(lax.axis_size(axis))])


def table_kernel(sizes, norm, packed, ours, theirs, *refs):
    slots, meta_row = sizes
    grids, (mine_ref, other_ref, table_f, total) = refs[:-4], refs[-4:]
    chan = lax.axis_index("chan")
    first = chan == 0

    def parts(table):
        table_f[...] = table
        return table_f[pl.ds(0, SU, stride=2), :], table_f[pl.ds(1, SU, stride=2), :]

    result = jnp.zeros((SU, 2 * SU), jnp.float32)
    for s in range(slots):
        at = slice(2 * SU * s, 2 * SU * (s + 1))
        fetched = ours[at, :].astype(jnp.float32)
        swapped = theirs[at, :].astype(jnp.float32)
        u_real, u_imag = parts(jnp.where(first, fetched, swapped))
        u_side = jnp.concatenate([u_real.T, u_imag.T], axis=1).astype(jnp.bfloat16)
        grid_real, grid_imag = (
            sum(ref[s, part * SU : (part + 1) * SU, :] for ref in grids) for part in range(2)
        )
        high, low = (
            jnp.concatenate(
                [
                    jnp.concatenate([real, imag], axis=1),
                    jnp.concatenate([-imag, real], axis=1),
                ],
                axis=0,
            )
            for real, imag in zip(split_bf16(grid_real), split_bf16(grid_imag))
        )
        half = jnp.dot(u_side, high, preferred_element_type=jnp.float32) + jnp.dot(
            u_side, low, preferred_element_type=jnp.float32
        )
        v_real, v_imag = parts(jnp.where(first, swapped, fetched))
        v_side = jnp.concatenate(
            [
                jnp.concatenate([v_real, v_imag], axis=1),
                jnp.concatenate([-v_imag, v_real], axis=1),
            ],
            axis=0,
        ).astype(jnp.bfloat16)
        high, low = split_bf16(half)
        result = (
            result
            + jnp.dot(high, v_side, preferred_element_type=jnp.float32)
            + jnp.dot(low, v_side, preferred_element_type=jnp.float32)
        )
    tail = meta_row // 16 * 16
    wide = packed[tail : tail + 16, :].astype(jnp.float32)
    at = meta_row - tail + 2
    gain = (wide[at : at + 2] + wide[at + 2 : at + 4]) + wide[at + 4 : at + 6]
    gain_u = jnp.broadcast_to(gain[0:1], (SU, SU)).T
    gains = gain_u * gain[1:2] * norm
    total[...] = result * jnp.concatenate([gains, gains], axis=1)
    half_rows = mine_ref.shape[0]
    mine_ref[...] = total[pl.ds(pl.multiple_of(chan * half_rows, half_rows), half_rows), :]
    other_ref[...] = total[pl.ds(pl.multiple_of((1 - chan) * half_rows, half_rows), half_rows), :]


def body(
    visibilities, coords, plane_index, block_group, offsets, facet_centre, tables, antenna_gain
):
    facets = lax.axis_size("facet")
    groups = lax.axis_size("bl")
    chan_count = lax.axis_size("chan")
    held, chans = visibilities.shape[:2]
    devices = facets * groups
    slots = 2 * facets
    cap = max(2, 2 * held // groups)
    meta_row = 2 * cap * (chans + 1)
    rows = -(-(meta_row + 8) // 16) * 16
    half_rows = SU // chan_count
    norm = SU / math.sqrt(visibilities.shape[3] * held * facets * CH)

    own_table = tables.reshape(2, 2 * SU, SU)
    *pieces, half = pl.pallas_call(
        functools.partial(sort_kernel, (groups, held, chans, cap, rows)),
        out_shape=[
            jax.ShapeDtypeStruct((rows + (2 * SU if shift == 1 else 0), SU), jnp.bfloat16)
            for shift in range(groups)
        ]
        + [jax.ShapeDtypeStruct((2 * SU, SU), jnp.bfloat16)],
        in_specs=[HBM] * 8,
        out_specs=[VMEM] * (groups + 1),
        scratch_shapes=[
            pltpu.SMEM((1, held), jnp.int32),
            pltpu.SMEM((1, held), jnp.int32),
            pltpu.VMEM((held * 2 * chans, SU), jnp.bfloat16),
            pltpu.VMEM((held * 2, SU), jnp.bfloat16),
            pltpu.SMEM((facets, 2, groups), jnp.int32),
            pltpu.SMEM((2, facets), jnp.float32),
            pltpu.VMEM((1, 2, SU), jnp.float32),
            pltpu.VMEM((held * 2 * chans, SU), jnp.float32),
            pltpu.VMEM((held * 2, SU), jnp.float32),
            pltpu.VMEM((groups, rows, SU), jnp.float32),
            pltpu.SMEM((groups,), jnp.int32),
            pltpu.SemaphoreType.DMA((8,)),
        ],
        compiler_params=PARAMS,
        cost_estimate=pl.CostEstimate(flops=100_000, bytes_accessed=100_000, transcendentals=0),
        name="sort_blocks",
    )(
        *(
            pltpu.with_memory_space_constraint(operand, pltpu.HBM)
            for operand in (
                plane_index.reshape(1, held),
                block_group.T,
                visibilities.reshape(held * 2 * chans, SU),
                coords.reshape(held * 2, SU),
                offsets.transpose(0, 2, 1),
                facet_centre.T,
                antenna_gain,
                own_table,
            )
        )
    )
    arrived = [
        lax.ppermute(pieces[shift], "bl", [(g, (g + shift) % groups) for g in range(groups)])
        for shift in [1, *range(groups - 1, 1, -1)]
    ]
    vis_rows = groups * rows
    joined = local(
        functools.partial(join_kernel, rows),
        [half, pieces[0], *arrived],
        (vis_rows + 4 * SU, SU),
        "join",
    )
    blocks = [joined] + [exchange(joined, "facet", shift) for shift in range(1, facets)]
    def grid(some):
        lines = len(some) * groups * cap
        return pl.pallas_call(
            functools.partial(grid_kernel, (facets, groups, chans, cap, rows, len(some))),
            out_shape=jax.ShapeDtypeStruct((slots, 2 * SU, SU), jnp.float32),
            in_specs=[VMEM] * (1 + len(some)),
            out_specs=VMEM,
            scratch_shapes=[
                pltpu.SMEM((lines + UNROLL,), jnp.int32),
            ]
            + [pltpu.VMEM((lines * chans + 8, SU), jnp.float32)] * 4,
            compiler_params=PARAMS,
            cost_estimate=pl.CostEstimate(
                flops=len(some) * 1_000_000_000,
                bytes_accessed=1_000_000,
                transcendentals=len(some) * 1_000_000,
            ),
            name="grid",
        )(joined, *some)

    grids = [grid(blocks[:1]), grid(blocks[-1:])]
    blocks, grids = lax.optimization_barrier((blocks, grids))
    fetched = local(
        functools.partial(collect_kernel, vis_rows), blocks, (facets * 4 * SU, SU), "collect"
    )
    swapped = lax.ppermute(fetched, "chan", [(c, 1 - c) for c in range(chan_count)])
    grids.append(grid(blocks[1:-1]))
    mine, other = pl.pallas_call(
        functools.partial(table_kernel, (slots, meta_row), norm),
        out_shape=[jax.ShapeDtypeStruct((half_rows, 2 * SU), jnp.float32)] * 2,
        in_specs=[VMEM] * (3 + len(grids)),
        out_specs=[VMEM, VMEM],
        scratch_shapes=[
            pltpu.VMEM((2 * SU, SU), jnp.float32),
            pltpu.VMEM((SU, 2 * SU), jnp.float32),
        ],
        compiler_params=PARAMS,
        cost_estimate=pl.CostEstimate(
            flops=1_000_000_000, bytes_accessed=2_000_000, transcendentals=0
        ),
        name="apply_tables",
    )(joined, fetched, swapped, *grids)
    summand = lax.ppermute(other, "chan", [(c, 1 - c) for c in range(chan_count)])
    return (mine + summand).reshape(1, 1, half_rows, 2, SU)


def solution(mesh):
    in_specs = (
        P(("facet", "bl"), "chan", None, None),
        P(("facet", "bl"), None, None),
        P(("facet", "bl")),
        P(("facet", "bl"), None),
        P(),
        P(),
        P(("facet", "bl"), None, None, None, None),
        P("bl", None, None),
    )
    out_specs = P("facet", "bl", "chan", None, None)
    return jax.shard_map(body, mesh=mesh, in_specs=in_specs, out_specs=out_specs, check_vma=False)
```

```python
import functools
import math

import jax
import jax.numpy as jnp
from jax import lax
from jax.experimental import pallas as pl
from jax.experimental.pallas import tpu as pltpu
from jax.sharding import PartitionSpec as P

SU = 128
CH = 8
KERNEL_SPREAD = 1.5
ALPHA = math.sqrt(math.log2(math.e) / (2.0 * KERNEL_SPREAD * KERNEL_SPREAD))
UNROLL = 4
NT = (((1,), (1,)), ((), ()))
VMEM = pl.BlockSpec(memory_space=pltpu.VMEM)
HBM = pl.BlockSpec(memory_space=pltpu.HBM)
PARAMS = pltpu.CompilerParams(vmem_limit_bytes=32 * 1024 * 1024)


def cos_sin(turns):
    quarter = jnp.floor(4.0 * turns + 0.5)
    angle = (2.0 * math.pi) * (turns - 0.25 * quarter)
    sq = angle * angle
    sine = angle * (
        1.0 + sq * (-1.0 / 6 + sq * (1.0 / 120 + sq * (-1.0 / 5040 + sq * (1.0 / 362880))))
    )
    cosine = 1.0 + sq * (
        -0.5 + sq * (1.0 / 24 + sq * (-1.0 / 720 + sq * (1.0 / 40320 + sq * (-1.0 / 3628800))))
    )
    turn = quarter.astype(jnp.int32) & 3
    odd = (turn & 1) == 1
    cos_out = jnp.where(odd, sine, cosine)
    sin_out = jnp.where(odd, cosine, sine)
    cos_out = jnp.where((turn == 1) | (turn == 2), -cos_out, cos_out)
    sin_out = jnp.where(turn >= 2, -sin_out, sin_out)
    return cos_out, sin_out


def split_bf16(x):
    high = x.astype(jnp.bfloat16)
    low = (x - high.astype(jnp.float32)).astype(jnp.bfloat16)
    return high, low


def three_parts(x):
    parts = []
    for _ in range(3):
        part = x.astype(jnp.bfloat16)
        x = x - part.astype(jnp.float32)
        parts.append(part.astype(jnp.float32))
    return parts


def sort_kernel(sizes, *refs):
    groups, held, chans, cap, rows = sizes
    table_hbm, outs, half = refs[7], refs[8 : 8 + groups], refs[8 + groups]
    targets = refs[9 + groups : 16 + groups]
    plane_ref, group_ref, samples_b, place_b, offsets_ref, centre_ref, gain_ref = targets
    samples, place, sorted_, filled, sems = refs[16 + groups :]
    facet = lax.axis_index("facet")
    copies = [
        pltpu.make_async_copy(source, target, sems.at[n])
        for n, (source, target) in enumerate(zip(refs[:7], targets))
    ]
    table = pltpu.make_async_copy(table_hbm.at[lax.axis_index("chan")], half, sems.at[7])
    for copy in copies + [table]:
        copy.start()
    sorted_[...] = jnp.zeros_like(sorted_)
    for g in range(groups):
        filled[g] = 0
    for copy in copies:
        copy.wait()
    samples[...] = samples_b[...].astype(jnp.float32)
    place[...] = place_b[...].astype(jnp.float32)
    lane = lax.broadcasted_iota(jnp.int32, (1, SU), 1)
    meta = 2 * cap * (chans + 1)
    centre = [
        part
        for axis in range(2)
        for part in three_parts(jnp.full((1, SU), centre_ref[axis, facet], jnp.float32))
    ]
    gains = three_parts(gain_ref[0])
    for g in range(groups):
        numbers = jnp.zeros((1, SU), jnp.float32)
        for axis in range(2):
            offset = offsets_ref[facet, axis, g].astype(jnp.float32)
            numbers = jnp.where(lane == axis, offset, numbers)
        for n, part in enumerate(centre):
            numbers = jnp.where(lane == 2 + n, part, numbers)
        sorted_[g, meta + 1 : meta + 2, :] = numbers
        for n, part in enumerate(gains):
            sorted_[g, meta + 2 + 2 * n : meta + 4 + 2 * n, :] = part
    for i in range(held):
        g = group_ref[0, i]
        k = filled[g]
        filled[g] = k + 1
        for part in range(2):
            at = part * cap * chans + k * chans
            sorted_[g, pl.ds(at, chans), :] = samples[pl.ds(2 * chans * i + part, chans, stride=2), :]
            at = 2 * cap * chans + part * cap + k
            sorted_[g, pl.ds(at, 1), :] = place[2 * i + part : 2 * i + part + 1, :]
        sorted_[g, meta : meta + 1, :] += jnp.where(
            lane == k, (plane_ref[0, i] + 1).astype(jnp.float32), 0.0
        )
    for shift, out_ref in enumerate(outs):
        g = lax.rem(lax.axis_index("bl") + shift, groups)
        out_ref[:rows, :] = sorted_[g].astype(jnp.bfloat16)
    table.wait()
    outs[1][rows:, :] = half[...]


def join_kernel(rows, half, *refs):
    *pieces, joined = refs
    for n, ref in enumerate(pieces):
        joined[n * rows : (n + 1) * rows, :] = ref[:rows, :]
    at = len(pieces) * rows
    joined[at : at + 2 * SU, :] = half[...]
    joined[at + 2 * SU :, :] = pieces[1][rows:, :]


def collect_kernel(skip, *refs):
    for n, ref in enumerate(refs[:-1]):
        refs[-1][n * 4 * SU : (n + 1) * 4 * SU, :] = ref[skip:, :]


def grid_kernel(sizes, *refs):
    facets, groups, chans, cap, rows, count_here = sizes
    own_ref, grids = refs[0], refs[1 + count_here]
    order, spots_u, spots_v, turns_real, turns_imag = refs[2 + count_here :]
    pieces = [
        ref.at[pl.ds(n * rows, rows)] for ref in refs[1 : 1 + count_here] for n in range(groups)
    ]
    devices = len(pieces)
    slots = 2 * facets
    lines = cap * chans
    meta_row = 2 * (lines + cap)
    tail = meta_row // 16 * 16
    facet = lax.axis_index("facet")
    group = lax.axis_index("bl")
    chan = lax.axis_index("chan")

    lane = lax.broadcasted_iota(jnp.int32, (1, SU), 1)
    own = own_ref[tail : tail + 16, :].astype(jnp.float32)
    numbers = own[meta_row - tail + 1 : meta_row - tail + 2]
    codes = []
    for d in range(devices):
        meta = pieces[d][tail : tail + 16, :].astype(jnp.float32)
        plane = meta[meta_row - tail : meta_row - tail + 1].astype(jnp.int32) - 1
        set_id = jnp.where(lax.rem(plane, groups) == group, 0, 1)
        code = (d * cap + lane) * slots + 2 * (lax.div(plane, groups) ^ facet) + set_id
        codes.append(jnp.where(plane >= 0, code, -1))
    grids[...] = jnp.zeros_like(grids)

    def number(n):
        return jnp.broadcast_to(numbers[:, n : n + 1], (lines, SU))

    offset_u = number(0)
    offset_v = number(1)
    along_l = number(2) + number(3) + number(4)
    along_m = number(5) + number(6) + number(7)
    line = lax.broadcasted_iota(jnp.int32, (lines, SU), 0)
    channel = (chan * chans + lax.rem(line, chans)).astype(jnp.float32)
    scale = 1.0 + 0.01 * (channel - 0.5 * (CH - 1))

    def spread_lines(place):
        return jnp.concatenate(
            [jnp.broadcast_to(place[k : k + 1], (chans, SU)) for k in range(cap)], axis=0
        )

    for d in range(devices):
        at = d * lines
        wide = pieces[d][...].astype(jnp.float32)
        real = wide[:lines]
        imag = wide[lines : 2 * lines]
        along_u = spread_lines(wide[2 * lines : 2 * lines + cap])
        along_v = spread_lines(wide[2 * lines + cap : 2 * (lines + cap)])
        cosine, sine = cos_sin((1.0 / SU) * (scale * (along_u * along_l + along_v * along_m)))
        spots_u[at : at + lines, :] = ALPHA * (scale * along_u - offset_u)
        spots_v[at : at + lines, :] = ALPHA * (scale * along_v - offset_v)
        turns_real[at : at + lines, :] = real * cosine - imag * sine
        turns_imag[at : at + lines, :] = real * sine + imag * cosine
    last = devices * lines
    for ref in (spots_u, spots_v, turns_real, turns_imag):
        ref[last : last + 8, :] = jnp.zeros((8, SU), jnp.float32)

    count = jnp.int32(0)
    for d in range(devices):
        for k in range(cap):
            code = codes[d][0, k]
            order[count] = code
            count = count + jnp.where(code >= 0, 1, 0)
    for i in range(UNROLL):
        order[count + i] = devices * cap * slots

    cells = ALPHA * lax.broadcasted_iota(jnp.int32, (SU, SU), 0).astype(jnp.float32)

    def profile(spot):
        apart = spot - cells
        return jnp.exp2(-((apart * apart).astype(jnp.bfloat16)))

    def tiled(row):
        return jnp.broadcast_to(row, (16, SU)).astype(jnp.bfloat16)[None]

    def one_block(at):
        code = order[at]
        slot = lax.rem(code, slots)
        base = lax.div(code, slots) * chans
        part = jnp.zeros((2 * SU, SU), jnp.float32)
        for pair in range(0, chans, 2):
            lefts_real, lefts_imag, rights = [], [], []
            for c in range(pair, pair + 2):
                here = pl.ds(base + c, 1)
                left = profile(spots_u[here, :]).reshape(SU // 16, 16, SU)
                lefts_real.append((left * tiled(turns_real[here, :])).reshape(SU, SU))
                lefts_imag.append((left * tiled(turns_imag[here, :])).reshape(SU, SU))
                rights.append(profile(spots_v[here, :]))
            left = jnp.concatenate(
                [jnp.concatenate(lefts_real, axis=1), jnp.concatenate(lefts_imag, axis=1)], axis=0
            )
            right = jnp.concatenate(rights, axis=1)
            part = part + lax.dot_general(left, right, NT, preferred_element_type=jnp.float32)
        grids[slot] += part

    def step(k, carry):
        for i in range(UNROLL):
            one_block(k * UNROLL + i)
        return carry

    lax.fori_loop(0, lax.div(count + UNROLL - 1, UNROLL), step, 0)


def local(kernel, operands, shape, name):
    return pl.pallas_call(
        kernel,
        out_shape=jax.ShapeDtypeStruct(shape, jnp.bfloat16),
        in_specs=[VMEM] * len(operands),
        out_specs=VMEM,
        compiler_params=PARAMS,
        cost_estimate=pl.CostEstimate(flops=0, bytes_accessed=400_000, transcendentals=0),
        name=name,
    )(*operands)


def exchange(value, axis, shift):
    return lax.ppermute(value, axis, [(n, n ^ shift) for n in range(lax.axis_size(axis))])


def table_kernel(sizes, norm, packed, ours, theirs, *refs):
    slots, meta_row = sizes
    grids, (mine_ref, other_ref, table_f, total) = refs[:-4], refs[-4:]
    chan = lax.axis_index("chan")
    first = chan == 0

    def parts(table):
        table_f[...] = table
        return table_f[pl.ds(0, SU, stride=2), :], table_f[pl.ds(1, SU, stride=2), :]

    result = jnp.zeros((SU, 2 * SU), jnp.float32)
    for s in range(slots):
        at = slice(2 * SU * s, 2 * SU * (s + 1))
        fetched = ours[at, :].astype(jnp.float32)
        swapped = theirs[at, :].astype(jnp.float32)
        u_real, u_imag = parts(jnp.where(first, fetched, swapped))
        u_side = jnp.concatenate([u_real.T, u_imag.T], axis=1).astype(jnp.bfloat16)
        grid_real, grid_imag = (
            sum(ref[s, part * SU : (part + 1) * SU, :] for ref in grids) for part in range(2)
        )
        high, low = (
            jnp.concatenate(
                [
                    jnp.concatenate([real, imag], axis=1),
                    jnp.concatenate([-imag, real], axis=1),
                ],
                axis=0,
            )
            for real, imag in zip(split_bf16(grid_real), split_bf16(grid_imag))
        )
        half = jnp.dot(u_side, high, preferred_element_type=jnp.float32) + jnp.dot(
            u_side, low, preferred_element_type=jnp.float32
        )
        v_real, v_imag = parts(jnp.where(first, swapped, fetched))
        v_side = jnp.concatenate(
            [
                jnp.concatenate([v_real, v_imag], axis=1),
                jnp.concatenate([-v_imag, v_real], axis=1),
            ],
            axis=0,
        ).astype(jnp.bfloat16)
        high, low = split_bf16(half)
        result = (
            result
            + jnp.dot(high, v_side, preferred_element_type=jnp.float32)
            + jnp.dot(low, v_side, preferred_element_type=jnp.float32)
        )
    tail = meta_row // 16 * 16
    wide = packed[tail : tail + 16, :].astype(jnp.float32)
    at = meta_row - tail + 2
    gain = (wide[at : at + 2] + wide[at + 2 : at + 4]) + wide[at + 4 : at + 6]
    gain_u = jnp.broadcast_to(gain[0:1], (SU, SU)).T
    gains = gain_u * gain[1:2] * norm
    total[...] = result * jnp.concatenate([gains, gains], axis=1)
    half_rows = mine_ref.shape[0]
    mine_ref[...] = total[pl.ds(pl.multiple_of(chan * half_rows, half_rows), half_rows), :]
    other_ref[...] = total[pl.ds(pl.multiple_of((1 - chan) * half_rows, half_rows), half_rows), :]


def body(
    visibilities, coords, plane_index, block_group, offsets, facet_centre, tables, antenna_gain
):
    facets = lax.axis_size("facet")
    groups = lax.axis_size("bl")
    chan_count = lax.axis_size("chan")
    held, chans = visibilities.shape[:2]
    devices = facets * groups
    slots = 2 * facets
    cap = max(2, 2 * held // groups)
    meta_row = 2 * cap * (chans + 1)
    rows = -(-(meta_row + 8) // 16) * 16
    half_rows = SU // chan_count
    norm = SU / math.sqrt(visibilities.shape[3] * held * facets * CH)

    own_table = tables.reshape(2, 2 * SU, SU)
    *pieces, half = pl.pallas_call(
        functools.partial(sort_kernel, (groups, held, chans, cap, rows)),
        out_shape=[
            jax.ShapeDtypeStruct((rows + (2 * SU if shift == 1 else 0), SU), jnp.bfloat16)
            for shift in range(groups)
        ]
        + [jax.ShapeDtypeStruct((2 * SU, SU), jnp.bfloat16)],
        in_specs=[HBM] * 8,
        out_specs=[VMEM] * (groups + 1),
        scratch_shapes=[
            pltpu.SMEM((1, held), jnp.int32),
            pltpu.SMEM((1, held), jnp.int32),
            pltpu.VMEM((held * 2 * chans, SU), jnp.bfloat16),
            pltpu.VMEM((held * 2, SU), jnp.bfloat16),
            pltpu.SMEM((facets, 2, groups), jnp.int32),
            pltpu.SMEM((2, facets), jnp.float32),
            pltpu.VMEM((1, 2, SU), jnp.float32),
            pltpu.VMEM((held * 2 * chans, SU), jnp.float32),
            pltpu.VMEM((held * 2, SU), jnp.float32),
            pltpu.VMEM((groups, rows, SU), jnp.float32),
            pltpu.SMEM((groups,), jnp.int32),
            pltpu.SemaphoreType.DMA((8,)),
        ],
        compiler_params=PARAMS,
        cost_estimate=pl.CostEstimate(flops=100_000, bytes_accessed=100_000, transcendentals=0),
        name="sort_blocks",
    )(
        *(
            pltpu.with_memory_space_constraint(operand, pltpu.HBM)
            for operand in (
                plane_index.reshape(1, held),
                block_group.T,
                visibilities.reshape(held * 2 * chans, SU),
                coords.reshape(held * 2, SU),
                offsets.transpose(0, 2, 1),
                facet_centre.T,
                antenna_gain,
                own_table,
            )
        )
    )
    arrived = [
        lax.ppermute(pieces[shift], "bl", [(g, (g + shift) % groups) for g in range(groups)])
        for shift in [1, *range(groups - 1, 1, -1)]
    ]
    vis_rows = groups * rows
    joined = local(
        functools.partial(join_kernel, rows),
        [half, pieces[0], *arrived],
        (vis_rows + 4 * SU, SU),
        "join",
    )
    blocks = [joined] + [exchange(joined, "facet", shift) for shift in range(1, facets)]
    def grid(some):
        lines = len(some) * groups * cap
        return pl.pallas_call(
            functools.partial(grid_kernel, (facets, groups, chans, cap, rows, len(some))),
            out_shape=jax.ShapeDtypeStruct((slots, 2 * SU, SU), jnp.float32),
            in_specs=[VMEM] * (1 + len(some)),
            out_specs=VMEM,
            scratch_shapes=[
                pltpu.SMEM((lines + UNROLL,), jnp.int32),
            ]
            + [pltpu.VMEM((lines * chans + 8, SU), jnp.float32)] * 4,
            compiler_params=PARAMS,
            cost_estimate=pl.CostEstimate(
                flops=len(some) * 1_000_000_000,
                bytes_accessed=1_000_000,
                transcendentals=len(some) * 1_000_000,
            ),
            name="grid",
        )(joined, *some)

    grids = [grid([block]) for block in (blocks[0], blocks[-1], *blocks[1:-2])]
    blocks, grids = lax.optimization_barrier((blocks, grids))
    fetched = local(
        functools.partial(collect_kernel, vis_rows), blocks, (facets * 4 * SU, SU), "collect"
    )
    swapped = lax.ppermute(fetched, "chan", [(c, 1 - c) for c in range(chan_count)])
    grids.append(grid(blocks[-2:-1]))
    mine, other = pl.pallas_call(
        functools.partial(table_kernel, (slots, meta_row), norm),
        out_shape=[jax.ShapeDtypeStruct((half_rows, 2 * SU), jnp.float32)] * 2,
        in_specs=[VMEM] * (3 + len(grids)),
        out_specs=[VMEM, VMEM],
        scratch_shapes=[
            pltpu.VMEM((2 * SU, SU), jnp.float32),
            pltpu.VMEM((SU, 2 * SU), jnp.float32),
        ],
        compiler_params=PARAMS,
        cost_estimate=pl.CostEstimate(
            flops=1_000_000_000, bytes_accessed=2_000_000, transcendentals=0
        ),
        name="apply_tables",
    )(joined, fetched, swapped, *grids)
    summand = lax.ppermute(other, "chan", [(c, 1 - c) for c in range(chan_count)])
    return (mine + summand).reshape(1, 1, half_rows, 2, SU)


def solution(mesh):
    in_specs = (
        P(("facet", "bl"), "chan", None, None),
        P(("facet", "bl"), None, None),
        P(("facet", "bl")),
        P(("facet", "bl"), None),
        P(),
        P(),
        P(("facet", "bl"), None, None, None, None),
        P("bl", None, None),
    )
    out_specs = P("facet", "bl", "chan", None, None)
    return jax.shard_map(body, mesh=mesh, in_specs=in_specs, out_specs=out_specs, check_vma=False)
```

```python
import functools
import math

import jax
import jax.numpy as jnp
from jax import lax
from jax.experimental import pallas as pl
from jax.experimental.pallas import tpu as pltpu
from jax.sharding import PartitionSpec as P

SU = 128
CH = 8
KERNEL_SPREAD = 1.5
ALPHA = math.sqrt(math.log2(math.e) / (2.0 * KERNEL_SPREAD * KERNEL_SPREAD))
UNROLL = 4
NT = (((1,), (1,)), ((), ()))
VMEM = pl.BlockSpec(memory_space=pltpu.VMEM)
HBM = pl.BlockSpec(memory_space=pltpu.HBM)
PARAMS = pltpu.CompilerParams(vmem_limit_bytes=32 * 1024 * 1024)


def cos_sin(turns):
    quarter = jnp.floor(4.0 * turns + 0.5)
    angle = (2.0 * math.pi) * (turns - 0.25 * quarter)
    sq = angle * angle
    sine = angle * (
        1.0 + sq * (-1.0 / 6 + sq * (1.0 / 120 + sq * (-1.0 / 5040 + sq * (1.0 / 362880))))
    )
    cosine = 1.0 + sq * (
        -0.5 + sq * (1.0 / 24 + sq * (-1.0 / 720 + sq * (1.0 / 40320 + sq * (-1.0 / 3628800))))
    )
    turn = quarter.astype(jnp.int32) & 3
    odd = (turn & 1) == 1
    cos_out = jnp.where(odd, sine, cosine)
    sin_out = jnp.where(odd, cosine, sine)
    cos_out = jnp.where((turn == 1) | (turn == 2), -cos_out, cos_out)
    sin_out = jnp.where(turn >= 2, -sin_out, sin_out)
    return cos_out, sin_out


def split_bf16(x):
    high = x.astype(jnp.bfloat16)
    low = (x - high.astype(jnp.float32)).astype(jnp.bfloat16)
    return high, low


def three_parts(x):
    parts = []
    for _ in range(3):
        part = x.astype(jnp.bfloat16)
        x = x - part.astype(jnp.float32)
        parts.append(part.astype(jnp.float32))
    return parts


def sort_kernel(sizes, *refs):
    groups, held, chans, cap, rows = sizes
    table_hbm, outs, half = refs[7], refs[8 : 8 + groups], refs[8 + groups]
    targets = refs[9 + groups : 16 + groups]
    plane_ref, group_ref, samples_b, place_b, offsets_ref, centre_ref, gain_ref = targets
    samples, place, sorted_, filled, sems = refs[16 + groups :]
    facet = lax.axis_index("facet")
    copies = [
        pltpu.make_async_copy(source, target, sems.at[n])
        for n, (source, target) in enumerate(zip(refs[:7], targets))
    ]
    table = pltpu.make_async_copy(table_hbm.at[lax.axis_index("chan")], half, sems.at[7])
    for copy in copies + [table]:
        copy.start()
    sorted_[...] = jnp.zeros_like(sorted_)
    for g in range(groups):
        filled[g] = 0
    for copy in copies:
        copy.wait()
    samples[...] = samples_b[...].astype(jnp.float32)
    place[...] = place_b[...].astype(jnp.float32)
    lane = lax.broadcasted_iota(jnp.int32, (1, SU), 1)
    meta = 2 * cap * (chans + 1)
    centre = [
        part
        for axis in range(2)
        for part in three_parts(jnp.full((1, SU), centre_ref[axis, facet], jnp.float32))
    ]
    gains = three_parts(gain_ref[0])
    for g in range(groups):
        numbers = jnp.zeros((1, SU), jnp.float32)
        for axis in range(2):
            offset = offsets_ref[facet, axis, g].astype(jnp.float32)
            numbers = jnp.where(lane == axis, offset, numbers)
        for n, part in enumerate(centre):
            numbers = jnp.where(lane == 2 + n, part, numbers)
        sorted_[g, meta + 1 : meta + 2, :] = numbers
        for n, part in enumerate(gains):
            sorted_[g, meta + 2 + 2 * n : meta + 4 + 2 * n, :] = part
    for i in range(held):
        g = group_ref[0, i]
        k = filled[g]
        filled[g] = k + 1
        for part in range(2):
            at = part * cap * chans + k * chans
            sorted_[g, pl.ds(at, chans), :] = samples[pl.ds(2 * chans * i + part, chans, stride=2), :]
            at = 2 * cap * chans + part * cap + k
            sorted_[g, pl.ds(at, 1), :] = place[2 * i + part : 2 * i + part + 1, :]
        sorted_[g, meta : meta + 1, :] += jnp.where(
            lane == k, (plane_ref[0, i] + 1).astype(jnp.float32), 0.0
        )
    for shift, out_ref in enumerate(outs):
        g = lax.rem(lax.axis_index("bl") + shift, groups)
        out_ref[:rows, :] = sorted_[g].astype(jnp.bfloat16)
    table.wait()
    outs[1][rows:, :] = half[...]


def join_kernel(rows, half, *refs):
    *pieces, joined = refs
    for n, ref in enumerate(pieces):
        joined[n * rows : (n + 1) * rows, :] = ref[:rows, :]
    at = len(pieces) * rows
    joined[at : at + 2 * SU, :] = half[...]
    joined[at + 2 * SU :, :] = pieces[1][rows:, :]


def collect_kernel(skip, *refs):
    for n, ref in enumerate(refs[:-1]):
        refs[-1][n * 4 * SU : (n + 1) * 4 * SU, :] = ref[skip:, :]


def grid_kernel(sizes, *refs):
    facets, groups, chans, cap, rows, count_here = sizes
    own_ref, grids = refs[0], refs[1 + count_here]
    order, spots_u, spots_v, turns_real, turns_imag = refs[2 + count_here :]
    pieces = [
        ref.at[pl.ds(n * rows, rows)] for ref in refs[1 : 1 + count_here] for n in range(groups)
    ]
    devices = len(pieces)
    slots = 2 * facets
    lines = cap * chans
    meta_row = 2 * (lines + cap)
    tail = meta_row // 16 * 16
    facet = lax.axis_index("facet")
    group = lax.axis_index("bl")
    chan = lax.axis_index("chan")

    lane = lax.broadcasted_iota(jnp.int32, (1, SU), 1)
    own = own_ref[tail : tail + 16, :].astype(jnp.float32)
    numbers = own[meta_row - tail + 1 : meta_row - tail + 2]
    codes = []
    for d in range(devices):
        meta = pieces[d][tail : tail + 16, :].astype(jnp.float32)
        plane = meta[meta_row - tail : meta_row - tail + 1].astype(jnp.int32) - 1
        set_id = jnp.where(lax.rem(plane, groups) == group, 0, 1)
        code = (d * cap + lane) * slots + 2 * (lax.div(plane, groups) ^ facet) + set_id
        codes.append(jnp.where(plane >= 0, code, -1))
    grids[...] = jnp.zeros_like(grids)

    def number(n):
        return jnp.broadcast_to(numbers[:, n : n + 1], (lines, SU))

    offset_u = number(0)
    offset_v = number(1)
    along_l = number(2) + number(3) + number(4)
    along_m = number(5) + number(6) + number(7)
    line = lax.broadcasted_iota(jnp.int32, (lines, SU), 0)
    channel = (chan * chans + lax.rem(line, chans)).astype(jnp.float32)
    scale = 1.0 + 0.01 * (channel - 0.5 * (CH - 1))

    def spread_lines(place):
        return jnp.concatenate(
            [jnp.broadcast_to(place[k : k + 1], (chans, SU)) for k in range(cap)], axis=0
        )

    for d in range(devices):
        at = d * lines
        wide = pieces[d][...].astype(jnp.float32)
        real = wide[:lines]
        imag = wide[lines : 2 * lines]
        along_u = spread_lines(wide[2 * lines : 2 * lines + cap])
        along_v = spread_lines(wide[2 * lines + cap : 2 * (lines + cap)])
        cosine, sine = cos_sin((1.0 / SU) * (scale * (along_u * along_l + along_v * along_m)))
        spots_u[at : at + lines, :] = ALPHA * (scale * along_u - offset_u)
        spots_v[at : at + lines, :] = ALPHA * (scale * along_v - offset_v)
        turns_real[at : at + lines, :] = real * cosine - imag * sine
        turns_imag[at : at + lines, :] = real * sine + imag * cosine
    last = devices * lines
    for ref in (spots_u, spots_v, turns_real, turns_imag):
        ref[last : last + 8, :] = jnp.zeros((8, SU), jnp.float32)

    count = jnp.int32(0)
    for d in range(devices):
        for k in range(cap):
            code = codes[d][0, k]
            order[count] = code
            count = count + jnp.where(code >= 0, 1, 0)
    for i in range(UNROLL):
        order[count + i] = devices * cap * slots

    cells = ALPHA * lax.broadcasted_iota(jnp.int32, (SU, SU), 0).astype(jnp.float32)

    def profile(spot):
        apart = spot - cells
        return jnp.exp2(-((apart * apart).astype(jnp.bfloat16)))

    def tiled(row):
        return jnp.broadcast_to(row, (16, SU)).astype(jnp.bfloat16)[None]

    def one_block(at):
        code = order[at]
        slot = lax.rem(code, slots)
        base = lax.div(code, slots) * chans
        lefts_real, lefts_imag, rights = [], [], []
        for c in range(chans):
            here = pl.ds(base + c, 1)
            left = profile(spots_u[here, :]).reshape(SU // 16, 16, SU)
            lefts_real.append((left * tiled(turns_real[here, :])).reshape(SU, SU))
            lefts_imag.append((left * tiled(turns_imag[here, :])).reshape(SU, SU))
            rights.append(profile(spots_v[here, :]))
        left = jnp.concatenate(
            [jnp.concatenate(lefts_real, axis=1), jnp.concatenate(lefts_imag, axis=1)], axis=0
        )
        right = jnp.concatenate(rights, axis=1)
        return slot, lax.dot_general(right, left, NT, preferred_element_type=jnp.float32)

    def step(k, carry):
        for slot, part in [one_block(k * UNROLL + i) for i in range(UNROLL)]:
            grids[slot] += part
        return carry

    lax.fori_loop(0, lax.div(count + UNROLL - 1, UNROLL), step, 0)


def local(kernel, operands, shape, name):
    return pl.pallas_call(
        kernel,
        out_shape=jax.ShapeDtypeStruct(shape, jnp.bfloat16),
        in_specs=[VMEM] * len(operands),
        out_specs=VMEM,
        compiler_params=PARAMS,
        cost_estimate=pl.CostEstimate(flops=0, bytes_accessed=400_000, transcendentals=0),
        name=name,
    )(*operands)


def exchange(value, axis, shift):
    return lax.ppermute(value, axis, [(n, n ^ shift) for n in range(lax.axis_size(axis))])


def table_kernel(sizes, norm, packed, ours, theirs, *refs):
    slots, meta_row = sizes
    grids, (mine_ref, other_ref, table_f, total) = refs[:-4], refs[-4:]
    chan = lax.axis_index("chan")
    first = chan == 0

    def parts(table):
        table_f[...] = table
        return table_f[pl.ds(0, SU, stride=2), :], table_f[pl.ds(1, SU, stride=2), :]

    result = jnp.zeros((SU, 2 * SU), jnp.float32)
    for s in range(slots):
        at = slice(2 * SU * s, 2 * SU * (s + 1))
        fetched = ours[at, :].astype(jnp.float32)
        swapped = theirs[at, :].astype(jnp.float32)
        v_real, v_imag = parts(jnp.where(first, swapped, fetched))
        v_side = jnp.concatenate([v_real.T, v_imag.T], axis=1).astype(jnp.bfloat16)
        grid = sum(ref[s] for ref in grids)
        high, low = (
            jnp.concatenate(
                [
                    part,
                    jnp.concatenate([-part[:, SU:], part[:, :SU]], axis=1),
                ],
                axis=0,
            )
            for part in split_bf16(grid)
        )
        half = jnp.dot(v_side, high, preferred_element_type=jnp.float32) + jnp.dot(
            v_side, low, preferred_element_type=jnp.float32
        )
        u_real, u_imag = parts(jnp.where(first, fetched, swapped))
        u_side = jnp.concatenate(
            [
                jnp.concatenate([u_real, u_imag], axis=1),
                jnp.concatenate([-u_imag, u_real], axis=1),
            ],
            axis=0,
        ).astype(jnp.bfloat16)
        high, low = split_bf16(half)
        result = (
            result
            + jnp.dot(high, u_side, preferred_element_type=jnp.float32)
            + jnp.dot(low, u_side, preferred_element_type=jnp.float32)
        )
    result = jnp.concatenate([result[:, :SU].T, result[:, SU:].T], axis=1)
    tail = meta_row // 16 * 16
    wide = packed[tail : tail + 16, :].astype(jnp.float32)
    at = meta_row - tail + 2
    gain = (wide[at : at + 2] + wide[at + 2 : at + 4]) + wide[at + 4 : at + 6]
    gain_u = jnp.broadcast_to(gain[0:1], (SU, SU)).T
    gains = gain_u * gain[1:2] * norm
    total[...] = result * jnp.concatenate([gains, gains], axis=1)
    half_rows = mine_ref.shape[0]
    mine_ref[...] = total[pl.ds(pl.multiple_of(chan * half_rows, half_rows), half_rows), :]
    other_ref[...] = total[pl.ds(pl.multiple_of((1 - chan) * half_rows, half_rows), half_rows), :]


def body(
    visibilities, coords, plane_index, block_group, offsets, facet_centre, tables, antenna_gain
):
    facets = lax.axis_size("facet")
    groups = lax.axis_size("bl")
    chan_count = lax.axis_size("chan")
    held, chans = visibilities.shape[:2]
    devices = facets * groups
    slots = 2 * facets
    cap = max(2, 2 * held // groups)
    meta_row = 2 * cap * (chans + 1)
    rows = -(-(meta_row + 8) // 16) * 16
    half_rows = SU // chan_count
    norm = SU / math.sqrt(visibilities.shape[3] * held * facets * CH)

    own_table = tables.reshape(2, 2 * SU, SU)
    *pieces, half = pl.pallas_call(
        functools.partial(sort_kernel, (groups, held, chans, cap, rows)),
        out_shape=[
            jax.ShapeDtypeStruct((rows + (2 * SU if shift == 1 else 0), SU), jnp.bfloat16)
            for shift in range(groups)
        ]
        + [jax.ShapeDtypeStruct((2 * SU, SU), jnp.bfloat16)],
        in_specs=[HBM] * 8,
        out_specs=[VMEM] * (groups + 1),
        scratch_shapes=[
            pltpu.SMEM((1, held), jnp.int32),
            pltpu.SMEM((1, held), jnp.int32),
            pltpu.VMEM((held * 2 * chans, SU), jnp.bfloat16),
            pltpu.VMEM((held * 2, SU), jnp.bfloat16),
            pltpu.SMEM((facets, 2, groups), jnp.int32),
            pltpu.SMEM((2, facets), jnp.float32),
            pltpu.VMEM((1, 2, SU), jnp.float32),
            pltpu.VMEM((held * 2 * chans, SU), jnp.float32),
            pltpu.VMEM((held * 2, SU), jnp.float32),
            pltpu.VMEM((groups, rows, SU), jnp.float32),
            pltpu.SMEM((groups,), jnp.int32),
            pltpu.SemaphoreType.DMA((8,)),
        ],
        compiler_params=PARAMS,
        cost_estimate=pl.CostEstimate(flops=100_000, bytes_accessed=100_000, transcendentals=0),
        name="sort_blocks",
    )(
        *(
            pltpu.with_memory_space_constraint(operand, pltpu.HBM)
            for operand in (
                plane_index.reshape(1, held),
                block_group.T,
                visibilities.reshape(held * 2 * chans, SU),
                coords.reshape(held * 2, SU),
                offsets.transpose(0, 2, 1),
                facet_centre.T,
                antenna_gain,
                own_table,
            )
        )
    )
    arrived = [
        lax.ppermute(pieces[shift], "bl", [(g, (g + shift) % groups) for g in range(groups)])
        for shift in [1, *range(groups - 1, 1, -1)]
    ]
    vis_rows = groups * rows
    joined = local(
        functools.partial(join_kernel, rows),
        [half, pieces[0], *arrived],
        (vis_rows + 4 * SU, SU),
        "join",
    )
    blocks = [joined] + [exchange(joined, "facet", shift) for shift in range(1, facets)]
    def grid(some):
        lines = len(some) * groups * cap
        return pl.pallas_call(
            functools.partial(grid_kernel, (facets, groups, chans, cap, rows, len(some))),
            out_shape=jax.ShapeDtypeStruct((slots, SU, 2 * SU), jnp.float32),
            in_specs=[VMEM] * (1 + len(some)),
            out_specs=VMEM,
            scratch_shapes=[
                pltpu.SMEM((lines + UNROLL,), jnp.int32),
            ]
            + [pltpu.VMEM((lines * chans + 8, SU), jnp.float32)] * 4,
            compiler_params=PARAMS,
            cost_estimate=pl.CostEstimate(
                flops=len(some) * 1_000_000_000,
                bytes_accessed=1_000_000,
                transcendentals=len(some) * 1_000_000,
            ),
            name="grid",
        )(joined, *some)

    grids = [grid(blocks[:1]), grid(blocks[-1:])]
    blocks, grids = lax.optimization_barrier((blocks, grids))
    fetched = local(
        functools.partial(collect_kernel, vis_rows), blocks, (facets * 4 * SU, SU), "collect"
    )
    swapped = lax.ppermute(fetched, "chan", [(c, 1 - c) for c in range(chan_count)])
    grids.append(grid(blocks[1:-1]))
    mine, other = pl.pallas_call(
        functools.partial(table_kernel, (slots, meta_row), norm),
        out_shape=[jax.ShapeDtypeStruct((half_rows, 2 * SU), jnp.float32)] * 2,
        in_specs=[VMEM] * (3 + len(grids)),
        out_specs=[VMEM, VMEM],
        scratch_shapes=[
            pltpu.VMEM((2 * SU, SU), jnp.float32),
            pltpu.VMEM((SU, 2 * SU), jnp.float32),
        ],
        compiler_params=PARAMS,
        cost_estimate=pl.CostEstimate(
            flops=1_000_000_000, bytes_accessed=2_000_000, transcendentals=0
        ),
        name="apply_tables",
    )(joined, fetched, swapped, *grids)
    summand = lax.ppermute(other, "chan", [(c, 1 - c) for c in range(chan_count)])
    return (mine + summand).reshape(1, 1, half_rows, 2, SU)


def solution(mesh):
    in_specs = (
        P(("facet", "bl"), "chan", None, None),
        P(("facet", "bl"), None, None),
        P(("facet", "bl")),
        P(("facet", "bl"), None),
        P(),
        P(),
        P(("facet", "bl"), None, None, None, None),
        P("bl", None, None),
    )
    out_specs = P("facet", "bl", "chan", None, None)
    return jax.shard_map(body, mesh=mesh, in_specs=in_specs, out_specs=out_specs, check_vma=False)
```

```python
import functools
import math

import jax
import jax.numpy as jnp
from jax import lax
from jax.experimental import pallas as pl
from jax.experimental.pallas import tpu as pltpu
from jax.sharding import PartitionSpec as P

SU = 128
CH = 8
KERNEL_SPREAD = 1.5
ALPHA = math.sqrt(math.log2(math.e) / (2.0 * KERNEL_SPREAD * KERNEL_SPREAD))
UNROLL = 4
NT = (((1,), (1,)), ((), ()))
VMEM = pl.BlockSpec(memory_space=pltpu.VMEM)
HBM = pl.BlockSpec(memory_space=pltpu.HBM)
PARAMS = pltpu.CompilerParams(vmem_limit_bytes=32 * 1024 * 1024)


def cos_sin(turns):
    quarter = jnp.floor(4.0 * turns + 0.5)
    angle = (2.0 * math.pi) * (turns - 0.25 * quarter)
    sq = angle * angle
    sine = angle * (
        1.0 + sq * (-1.0 / 6 + sq * (1.0 / 120 + sq * (-1.0 / 5040 + sq * (1.0 / 362880))))
    )
    cosine = 1.0 + sq * (
        -0.5 + sq * (1.0 / 24 + sq * (-1.0 / 720 + sq * (1.0 / 40320 + sq * (-1.0 / 3628800))))
    )
    turn = quarter.astype(jnp.int32) & 3
    odd = (turn & 1) == 1
    cos_out = jnp.where(odd, sine, cosine)
    sin_out = jnp.where(odd, cosine, sine)
    cos_out = jnp.where((turn == 1) | (turn == 2), -cos_out, cos_out)
    sin_out = jnp.where(turn >= 2, -sin_out, sin_out)
    return cos_out, sin_out


def split_bf16(x):
    high = x.astype(jnp.bfloat16)
    low = (x - high.astype(jnp.float32)).astype(jnp.bfloat16)
    return high, low


def three_parts(x):
    parts = []
    for _ in range(3):
        part = x.astype(jnp.bfloat16)
        x = x - part.astype(jnp.float32)
        parts.append(part.astype(jnp.float32))
    return parts


def sort_kernel(sizes, *refs):
    groups, held, chans, cap, rows = sizes
    table_hbm, outs, half = refs[7], refs[8 : 8 + groups], refs[8 + groups]
    targets = refs[9 + groups : 16 + groups]
    plane_ref, group_ref, samples_b, place_b, offsets_ref, centre_ref, gain_ref = targets
    samples, place, sorted_, filled, sems = refs[16 + groups :]
    facet = lax.axis_index("facet")
    copies = [
        pltpu.make_async_copy(source, target, sems.at[n])
        for n, (source, target) in enumerate(zip(refs[:7], targets))
    ]
    table = pltpu.make_async_copy(table_hbm.at[lax.axis_index("chan")], half, sems.at[7])
    for copy in copies + [table]:
        copy.start()
    sorted_[...] = jnp.zeros_like(sorted_)
    for g in range(groups):
        filled[g] = 0
    for copy in copies:
        copy.wait()
    samples[...] = samples_b[...].astype(jnp.float32)
    place[...] = place_b[...].astype(jnp.float32)
    lane = lax.broadcasted_iota(jnp.int32, (1, SU), 1)
    meta = 2 * cap * (chans + 1)
    centre = [
        part
        for axis in range(2)
        for part in three_parts(jnp.full((1, SU), centre_ref[axis, facet], jnp.float32))
    ]
    gains = three_parts(gain_ref[0])
    for g in range(groups):
        numbers = jnp.zeros((1, SU), jnp.float32)
        for axis in range(2):
            offset = offsets_ref[facet, axis, g].astype(jnp.float32)
            numbers = jnp.where(lane == axis, offset, numbers)
        for n, part in enumerate(centre):
            numbers = jnp.where(lane == 2 + n, part, numbers)
        sorted_[g, meta + 1 : meta + 2, :] = numbers
        for n, part in enumerate(gains):
            sorted_[g, meta + 2 + 2 * n : meta + 4 + 2 * n, :] = part
    for i in range(held):
        g = group_ref[0, i]
        k = filled[g]
        filled[g] = k + 1
        for part in range(2):
            at = part * cap * chans + k * chans
            sorted_[g, pl.ds(at, chans), :] = samples[pl.ds(2 * chans * i + part, chans, stride=2), :]
            at = 2 * cap * chans + part * cap + k
            sorted_[g, pl.ds(at, 1), :] = place[2 * i + part : 2 * i + part + 1, :]
        sorted_[g, meta : meta + 1, :] += jnp.where(
            lane == k, (plane_ref[0, i] + 1).astype(jnp.float32), 0.0
        )
    for shift, out_ref in enumerate(outs):
        g = lax.rem(lax.axis_index("bl") + shift, groups)
        out_ref[:rows, :] = sorted_[g].astype(jnp.bfloat16)
    table.wait()
    outs[1][rows:, :] = half[...]


def join_kernel(rows, half, *refs):
    *pieces, here, tables, joined = refs
    at = len(pieces) * rows
    for n, ref in enumerate(pieces):
        piece = ref[:rows, :]
        here[n * rows : (n + 1) * rows, :] = piece
        joined[n * rows : (n + 1) * rows, :] = piece
    for n, ref in enumerate((half, pieces[1].at[pl.ds(rows, 2 * SU)])):
        table = ref[...]
        tables[n * 2 * SU : (n + 1) * 2 * SU, :] = table
        joined[at + n * 2 * SU : at + (n + 1) * 2 * SU, :] = table


def collect_kernel(tables, *refs):
    *joined, diagonal, out_ref = refs
    for n, ref in enumerate((tables, *joined, diagonal)):
        start = ref.shape[0] - 4 * SU
        out_ref[n * 4 * SU : (n + 1) * 4 * SU, :] = ref[start:, :]


def grid_kernel(sizes, *refs):
    facets, groups, chans, cap, rows, count_here = sizes
    own_ref, grids = refs[0], refs[1 + count_here]
    order, spots_u, spots_v, turns_real, turns_imag = refs[2 + count_here :]
    pieces = [
        ref.at[pl.ds(n * rows, rows)] for ref in refs[1 : 1 + count_here] for n in range(groups)
    ]
    devices = len(pieces)
    slots = 2 * facets
    lines = cap * chans
    meta_row = 2 * (lines + cap)
    tail = meta_row // 16 * 16
    facet = lax.axis_index("facet")
    group = lax.axis_index("bl")
    chan = lax.axis_index("chan")

    lane = lax.broadcasted_iota(jnp.int32, (1, SU), 1)
    own = own_ref[tail : tail + 16, :].astype(jnp.float32)
    numbers = own[meta_row - tail + 1 : meta_row - tail + 2]
    codes = []
    for d in range(devices):
        meta = pieces[d][tail : tail + 16, :].astype(jnp.float32)
        plane = meta[meta_row - tail : meta_row - tail + 1].astype(jnp.int32) - 1
        set_id = jnp.where(lax.rem(plane, groups) == group, 0, 1)
        code = (d * cap + lane) * slots + 2 * (lax.div(plane, groups) ^ facet) + set_id
        codes.append(jnp.where(plane >= 0, code, -1))
    grids[...] = jnp.zeros_like(grids)

    def number(n):
        return jnp.broadcast_to(numbers[:, n : n + 1], (lines, SU))

    offset_u = number(0)
    offset_v = number(1)
    along_l = number(2) + number(3) + number(4)
    along_m = number(5) + number(6) + number(7)
    line = lax.broadcasted_iota(jnp.int32, (lines, SU), 0)
    channel = (chan * chans + lax.rem(line, chans)).astype(jnp.float32)
    scale = 1.0 + 0.01 * (channel - 0.5 * (CH - 1))

    def spread_lines(place):
        return jnp.concatenate(
            [jnp.broadcast_to(place[k : k + 1], (chans, SU)) for k in range(cap)], axis=0
        )

    for d in range(devices):
        at = d * lines
        wide = pieces[d][...].astype(jnp.float32)
        real = wide[:lines]
        imag = wide[lines : 2 * lines]
        along_u = spread_lines(wide[2 * lines : 2 * lines + cap])
        along_v = spread_lines(wide[2 * lines + cap : 2 * (lines + cap)])
        cosine, sine = cos_sin((1.0 / SU) * (scale * (along_u * along_l + along_v * along_m)))
        spots_u[at : at + lines, :] = ALPHA * (scale * along_u - offset_u)
        spots_v[at : at + lines, :] = ALPHA * (scale * along_v - offset_v)
        turns_real[at : at + lines, :] = real * cosine - imag * sine
        turns_imag[at : at + lines, :] = real * sine + imag * cosine
    last = devices * lines
    for ref in (spots_u, spots_v, turns_real, turns_imag):
        ref[last : last + 8, :] = jnp.zeros((8, SU), jnp.float32)

    count = jnp.int32(0)
    for d in range(devices):
        for k in range(cap):
            code = codes[d][0, k]
            order[count] = code
            count = count + jnp.where(code >= 0, 1, 0)
    for i in range(UNROLL):
        order[count + i] = devices * cap * slots

    cells = ALPHA * lax.broadcasted_iota(jnp.int32, (SU, SU), 0).astype(jnp.float32)

    def profile(spot):
        apart = spot - cells
        return jnp.exp2(-((apart * apart).astype(jnp.bfloat16)))

    def tiled(row):
        return jnp.broadcast_to(row, (16, SU)).astype(jnp.bfloat16)[None]

    def one_block(at):
        code = order[at]
        slot = lax.rem(code, slots)
        base = lax.div(code, slots) * chans
        lefts_real, lefts_imag, rights = [], [], []
        for c in range(chans):
            here = pl.ds(base + c, 1)
            left = profile(spots_u[here, :]).reshape(SU // 16, 16, SU)
            lefts_real.append((left * tiled(turns_real[here, :])).reshape(SU, SU))
            lefts_imag.append((left * tiled(turns_imag[here, :])).reshape(SU, SU))
            rights.append(profile(spots_v[here, :]))
        left = jnp.concatenate(
            [jnp.concatenate(lefts_real, axis=1), jnp.concatenate(lefts_imag, axis=1)], axis=0
        )
        right = jnp.concatenate(rights, axis=1)
        return slot, lax.dot_general(right, left, NT, preferred_element_type=jnp.float32)

    def step(k, carry):
        for slot, part in [one_block(k * UNROLL + i) for i in range(UNROLL)]:
            grids[slot] += part
        return carry

    lax.fori_loop(0, lax.div(count + UNROLL - 1, UNROLL), step, 0)


def local(kernel, operands, shapes, name):
    return pl.pallas_call(
        kernel,
        out_shape=[jax.ShapeDtypeStruct(shape, jnp.bfloat16) for shape in shapes],
        in_specs=[VMEM] * len(operands),
        out_specs=[VMEM] * len(shapes),
        compiler_params=PARAMS,
        cost_estimate=pl.CostEstimate(flops=0, bytes_accessed=400_000, transcendentals=0),
        name=name,
    )(*operands)


def exchange(value, axis, shift):
    return lax.ppermute(value, axis, [(n, n ^ shift) for n in range(lax.axis_size(axis))])


def table_kernel(sizes, norm, packed, ours, theirs, *refs):
    slots, meta_row = sizes
    grids, (mine_ref, other_ref, table_f, total) = refs[:-4], refs[-4:]
    chan = lax.axis_index("chan")
    first = chan == 0

    def parts(table):
        table_f[...] = table
        return table_f[pl.ds(0, SU, stride=2), :], table_f[pl.ds(1, SU, stride=2), :]

    result = jnp.zeros((SU, 2 * SU), jnp.float32)
    for s in range(slots):
        at = slice(2 * SU * s, 2 * SU * (s + 1))
        fetched = ours[at, :].astype(jnp.float32)
        swapped = theirs[at, :].astype(jnp.float32)
        v_real, v_imag = parts(jnp.where(first, swapped, fetched))
        v_side = jnp.concatenate([v_real.T, v_imag.T], axis=1).astype(jnp.bfloat16)
        grid = sum(ref[s] for ref in grids)
        high, low = (
            jnp.concatenate(
                [
                    part,
                    jnp.concatenate([-part[:, SU:], part[:, :SU]], axis=1),
                ],
                axis=0,
            )
            for part in split_bf16(grid)
        )
        half = jnp.dot(v_side, high, preferred_element_type=jnp.float32) + jnp.dot(
            v_side, low, preferred_element_type=jnp.float32
        )
        u_real, u_imag = parts(jnp.where(first, fetched, swapped))
        u_side = jnp.concatenate(
            [
                jnp.concatenate([u_real, u_imag], axis=1),
                jnp.concatenate([-u_imag, u_real], axis=1),
            ],
            axis=0,
        ).astype(jnp.bfloat16)
        high, low = split_bf16(half)
        result = (
            result
            + jnp.dot(high, u_side, preferred_element_type=jnp.float32)
            + jnp.dot(low, u_side, preferred_element_type=jnp.float32)
        )
    result = jnp.concatenate([result[:, :SU].T, result[:, SU:].T], axis=1)
    tail = meta_row // 16 * 16
    wide = packed[tail : tail + 16, :].astype(jnp.float32)
    at = meta_row - tail + 2
    gain = (wide[at : at + 2] + wide[at + 2 : at + 4]) + wide[at + 4 : at + 6]
    gain_u = jnp.broadcast_to(gain[0:1], (SU, SU)).T
    gains = gain_u * gain[1:2] * norm
    total[...] = result * jnp.concatenate([gains, gains], axis=1)
    half_rows = mine_ref.shape[0]
    mine_ref[...] = total[pl.ds(pl.multiple_of(chan * half_rows, half_rows), half_rows), :]
    other_ref[...] = total[pl.ds(pl.multiple_of((1 - chan) * half_rows, half_rows), half_rows), :]


def body(
    visibilities, coords, plane_index, block_group, offsets, facet_centre, tables, antenna_gain
):
    facets = lax.axis_size("facet")
    groups = lax.axis_size("bl")
    chan_count = lax.axis_size("chan")
    held, chans = visibilities.shape[:2]
    devices = facets * groups
    slots = 2 * facets
    cap = max(2, 2 * held // groups)
    meta_row = 2 * cap * (chans + 1)
    rows = -(-(meta_row + 8) // 16) * 16
    half_rows = SU // chan_count
    norm = SU / math.sqrt(visibilities.shape[3] * held * facets * CH)

    own_table = tables.reshape(2, 2 * SU, SU)
    *pieces, half = pl.pallas_call(
        functools.partial(sort_kernel, (groups, held, chans, cap, rows)),
        out_shape=[
            jax.ShapeDtypeStruct((rows + (2 * SU if shift == 1 else 0), SU), jnp.bfloat16)
            for shift in range(groups)
        ]
        + [jax.ShapeDtypeStruct((2 * SU, SU), jnp.bfloat16)],
        in_specs=[HBM] * 8,
        out_specs=[VMEM] * (groups + 1),
        scratch_shapes=[
            pltpu.SMEM((1, held), jnp.int32),
            pltpu.SMEM((1, held), jnp.int32),
            pltpu.VMEM((held * 2 * chans, SU), jnp.bfloat16),
            pltpu.VMEM((held * 2, SU), jnp.bfloat16),
            pltpu.SMEM((facets, 2, groups), jnp.int32),
            pltpu.SMEM((2, facets), jnp.float32),
            pltpu.VMEM((1, 2, SU), jnp.float32),
            pltpu.VMEM((held * 2 * chans, SU), jnp.float32),
            pltpu.VMEM((held * 2, SU), jnp.float32),
            pltpu.VMEM((groups, rows, SU), jnp.float32),
            pltpu.SMEM((groups,), jnp.int32),
            pltpu.SemaphoreType.DMA((8,)),
        ],
        compiler_params=PARAMS,
        cost_estimate=pl.CostEstimate(flops=100_000, bytes_accessed=100_000, transcendentals=0),
        name="sort_blocks",
    )(
        *(
            pltpu.with_memory_space_constraint(operand, pltpu.HBM)
            for operand in (
                plane_index.reshape(1, held),
                block_group.T,
                visibilities.reshape(held * 2 * chans, SU),
                coords.reshape(held * 2, SU),
                offsets.transpose(0, 2, 1),
                facet_centre.T,
                antenna_gain,
                own_table,
            )
        )
    )
    arrived = [
        lax.ppermute(pieces[shift], "bl", [(g, (g + shift) % groups) for g in range(groups)])
        for shift in [1, *range(groups - 1, 1, -1)]
    ]
    vis_rows = groups * rows
    here, both, joined = local(
        functools.partial(join_kernel, rows),
        [half, pieces[0], *arrived],
        [(vis_rows, SU), (4 * SU, SU), (vis_rows + 4 * SU, SU)],
        "join",
    )
    blocks = (
        [here]
        + [exchange(joined, "facet", shift) for shift in range(1, facets - 1)]
        + [exchange(here, "facet", facets - 1)]
    )
    last_tables = exchange(both, "facet", facets - 1)

    def grid(some):
        lines = len(some) * groups * cap
        return pl.pallas_call(
            functools.partial(grid_kernel, (facets, groups, chans, cap, rows, len(some))),
            out_shape=jax.ShapeDtypeStruct((slots, SU, 2 * SU), jnp.float32),
            in_specs=[VMEM] * (1 + len(some)),
            out_specs=VMEM,
            scratch_shapes=[
                pltpu.SMEM((lines + UNROLL,), jnp.int32),
            ]
            + [pltpu.VMEM((lines * chans + 8, SU), jnp.float32)] * 4,
            compiler_params=PARAMS,
            cost_estimate=pl.CostEstimate(
                flops=len(some) * 1_000_000_000,
                bytes_accessed=1_000_000,
                transcendentals=len(some) * 1_000_000,
            ),
            name="grid",
        )(here, *some)

    grids = [grid(blocks[:1]), grid([blocks[-1], *blocks[1:-2]])]
    blocks, last_tables, grids = lax.optimization_barrier((blocks, last_tables, grids))
    (fetched,) = local(
        collect_kernel,
        [both, *blocks[1:-1], last_tables],
        [(facets * 4 * SU, SU)],
        "collect",
    )
    swapped = lax.ppermute(fetched, "chan", [(c, 1 - c) for c in range(chan_count)])
    grids.append(grid(blocks[-2:-1]))
    mine, other = pl.pallas_call(
        functools.partial(table_kernel, (slots, meta_row), norm),
        out_shape=[jax.ShapeDtypeStruct((half_rows, 2 * SU), jnp.float32)] * 2,
        in_specs=[VMEM] * (3 + len(grids)),
        out_specs=[VMEM, VMEM],
        scratch_shapes=[
            pltpu.VMEM((2 * SU, SU), jnp.float32),
            pltpu.VMEM((SU, 2 * SU), jnp.float32),
        ],
        compiler_params=PARAMS,
        cost_estimate=pl.CostEstimate(
            flops=1_000_000_000, bytes_accessed=2_000_000, transcendentals=0
        ),
        name="apply_tables",
    )(here, fetched, swapped, *grids)
    summand = lax.ppermute(other, "chan", [(c, 1 - c) for c in range(chan_count)])
    return (mine + summand).reshape(1, 1, half_rows, 2, SU)


def solution(mesh):
    in_specs = (
        P(("facet", "bl"), "chan", None, None),
        P(("facet", "bl"), None, None),
        P(("facet", "bl")),
        P(("facet", "bl"), None),
        P(),
        P(),
        P(("facet", "bl"), None, None, None, None),
        P("bl", None, None),
    )
    out_specs = P("facet", "bl", "chan", None, None)
    return jax.shard_map(body, mesh=mesh, in_specs=in_specs, out_specs=out_specs, check_vma=False)
```

```python
import functools
import math

import jax
import jax.numpy as jnp
from jax import lax
from jax.experimental import pallas as pl
from jax.experimental.pallas import tpu as pltpu
from jax.sharding import PartitionSpec as P

SU = 128
CH = 8
KERNEL_SPREAD = 1.5
ALPHA = math.sqrt(math.log2(math.e) / (2.0 * KERNEL_SPREAD * KERNEL_SPREAD))
UNROLL = 4
REST = 2
NT = (((1,), (1,)), ((), ()))
VMEM = pl.BlockSpec(memory_space=pltpu.VMEM)
HBM = pl.BlockSpec(memory_space=pltpu.HBM)
PARAMS = pltpu.CompilerParams(vmem_limit_bytes=32 * 1024 * 1024)


def cos_sin(turns):
    quarter = jnp.floor(4.0 * turns + 0.5)
    angle = (2.0 * math.pi) * (turns - 0.25 * quarter)
    sq = angle * angle
    sine = angle * (
        1.0 + sq * (-1.0 / 6 + sq * (1.0 / 120 + sq * (-1.0 / 5040 + sq * (1.0 / 362880))))
    )
    cosine = 1.0 + sq * (
        -0.5 + sq * (1.0 / 24 + sq * (-1.0 / 720 + sq * (1.0 / 40320 + sq * (-1.0 / 3628800))))
    )
    turn = quarter.astype(jnp.int32) & 3
    odd = (turn & 1) == 1
    cos_out = jnp.where(odd, sine, cosine)
    sin_out = jnp.where(odd, cosine, sine)
    cos_out = jnp.where((turn == 1) | (turn == 2), -cos_out, cos_out)
    sin_out = jnp.where(turn >= 2, -sin_out, sin_out)
    return cos_out, sin_out


def split_bf16(x):
    high = x.astype(jnp.bfloat16)
    low = (x - high.astype(jnp.float32)).astype(jnp.bfloat16)
    return high, low


def three_parts(x):
    parts = []
    for _ in range(3):
        part = x.astype(jnp.bfloat16)
        x = x - part.astype(jnp.float32)
        parts.append(part.astype(jnp.float32))
    return parts


def sort_kernel(sizes, *refs):
    groups, held, chans, cap, rows = sizes
    table_hbm, outs, half = refs[7], refs[8 : 8 + groups], refs[8 + groups]
    targets = refs[9 + groups : 16 + groups]
    plane_ref, group_ref, samples_b, place_b, offsets_ref, centre_ref, gain_ref = targets
    samples, place, sorted_, filled, sems = refs[16 + groups :]
    facet = lax.axis_index("facet")
    copies = [
        pltpu.make_async_copy(source, target, sems.at[n])
        for n, (source, target) in enumerate(zip(refs[:7], targets))
    ]
    table = pltpu.make_async_copy(table_hbm.at[lax.axis_index("chan")], half, sems.at[7])
    for copy in copies + [table]:
        copy.start()
    sorted_[...] = jnp.zeros_like(sorted_)
    for g in range(groups):
        filled[g] = 0
    for copy in copies:
        copy.wait()
    samples[...] = samples_b[...].astype(jnp.float32)
    place[...] = place_b[...].astype(jnp.float32)
    lane = lax.broadcasted_iota(jnp.int32, (1, SU), 1)
    meta = 2 * cap * (chans + 1)
    centre = [
        part
        for axis in range(2)
        for part in three_parts(jnp.full((1, SU), centre_ref[axis, facet], jnp.float32))
    ]
    gains = three_parts(gain_ref[0])
    for g in range(groups):
        numbers = jnp.zeros((1, SU), jnp.float32)
        for axis in range(2):
            offset = offsets_ref[facet, axis, g].astype(jnp.float32)
            numbers = jnp.where(lane == axis, offset, numbers)
        for n, part in enumerate(centre):
            numbers = jnp.where(lane == 2 + n, part, numbers)
        sorted_[g, meta + 1 : meta + 2, :] = numbers
        for n, part in enumerate(gains):
            sorted_[g, meta + 2 + 2 * n : meta + 4 + 2 * n, :] = part
    for i in range(held):
        g = group_ref[0, i]
        k = filled[g]
        filled[g] = k + 1
        for part in range(2):
            at = part * cap * chans + k * chans
            sorted_[g, pl.ds(at, chans), :] = samples[pl.ds(2 * chans * i + part, chans, stride=2), :]
            at = 2 * cap * chans + part * cap + k
            sorted_[g, pl.ds(at, 1), :] = place[2 * i + part : 2 * i + part + 1, :]
        sorted_[g, meta : meta + 1, :] += jnp.where(
            lane == k, (plane_ref[0, i] + 1).astype(jnp.float32), 0.0
        )
    for shift, out_ref in enumerate(outs):
        g = lax.rem(lax.axis_index("bl") + shift, groups)
        out_ref[:rows, :] = sorted_[g].astype(jnp.bfloat16)
    table.wait()
    outs[1][rows:, :] = half[...]


def join_kernel(rows, half, *refs):
    *pieces, joined = refs
    for n, ref in enumerate(pieces):
        joined[n * rows : (n + 1) * rows, :] = ref[:rows, :]
    at = len(pieces) * rows
    joined[at : at + 2 * SU, :] = half[...]
    joined[at + 2 * SU :, :] = pieces[1][rows:, :]


def collect_kernel(skip, *refs):
    for n, ref in enumerate(refs[:-1]):
        refs[-1][n * 4 * SU : (n + 1) * 4 * SU, :] = ref[skip:, :]


def grid_kernel(sizes, *refs):
    facets, groups, chans, cap, rows, count_here = sizes
    own_ref, grids = refs[0], refs[1 + count_here]
    order, spots_u, spots_v, turns_real, turns_imag, cells = refs[2 + count_here :]
    pieces = [
        ref.at[pl.ds(n * rows, rows)] for ref in refs[1 : 1 + count_here] for n in range(groups)
    ]
    devices = len(pieces)
    slots = 2 * facets
    lines = cap * chans
    meta_row = 2 * (lines + cap)
    tail = meta_row // 16 * 16
    facet = lax.axis_index("facet")
    group = lax.axis_index("bl")
    chan = lax.axis_index("chan")

    lane = lax.broadcasted_iota(jnp.int32, (1, SU), 1)
    own = own_ref[tail : tail + 16, :].astype(jnp.float32)
    numbers = own[meta_row - tail + 1 : meta_row - tail + 2]
    codes = []
    for d in range(devices):
        meta = pieces[d][tail : tail + 16, :].astype(jnp.float32)
        plane = meta[meta_row - tail : meta_row - tail + 1].astype(jnp.int32) - 1
        set_id = jnp.where(lax.rem(plane, groups) == group, 0, 1)
        code = (d * cap + lane) * slots + 2 * (lax.div(plane, groups) ^ facet) + set_id
        codes.append(jnp.where(plane >= 0, code, -1))
    grids[...] = jnp.zeros_like(grids)

    def number(n):
        return jnp.broadcast_to(numbers[:, n : n + 1], (lines, SU))

    offset_u = number(0)
    offset_v = number(1)
    along_l = number(2) + number(3) + number(4)
    along_m = number(5) + number(6) + number(7)
    line = lax.broadcasted_iota(jnp.int32, (lines, SU), 0)
    channel = (chan * chans + lax.rem(line, chans)).astype(jnp.float32)
    scale = 1.0 + 0.01 * (channel - 0.5 * (CH - 1))

    def spread_lines(place):
        return jnp.concatenate(
            [jnp.broadcast_to(place[k : k + 1], (chans, SU)) for k in range(cap)], axis=0
        )

    for d in range(devices):
        at = d * lines
        wide = pieces[d][...].astype(jnp.float32)
        real = wide[:lines]
        imag = wide[lines : 2 * lines]
        along_u = spread_lines(wide[2 * lines : 2 * lines + cap])
        along_v = spread_lines(wide[2 * lines + cap : 2 * (lines + cap)])
        cosine, sine = cos_sin((1.0 / SU) * (scale * (along_u * along_l + along_v * along_m)))
        spots_u[at : at + lines, :] = ALPHA * (scale * along_u - offset_u)
        spots_v[at : at + lines, :] = ALPHA * (scale * along_v - offset_v)
        turns_real[at : at + lines, :] = real * cosine - imag * sine
        turns_imag[at : at + lines, :] = real * sine + imag * cosine
    last = devices * lines
    for ref in (spots_u, spots_v, turns_real, turns_imag):
        ref[last : last + 8, :] = jnp.zeros((8, SU), jnp.float32)

    count = jnp.int32(0)
    for d in range(devices):
        for k in range(cap):
            code = codes[d][0, k]
            order[count] = code
            count = count + jnp.where(code >= 0, 1, 0)
    for i in range(UNROLL):
        order[count + i] = devices * cap * slots

    cells[...] = ALPHA * lax.broadcasted_iota(jnp.int32, (SU, SU), 0).astype(jnp.float32)

    def profile(spot):
        apart = spot - cells[...]
        return jnp.exp2(-((apart * apart).astype(jnp.bfloat16)))

    def tiled(row):
        return jnp.broadcast_to(row, (16, SU)).astype(jnp.bfloat16)[None]

    def one_block(at):
        code = order[at]
        slot = lax.rem(code, slots)
        base = lax.div(code, slots) * chans
        lefts_real, lefts_imag, rights = [], [], []
        for c in range(chans):
            here = pl.ds(base + c, 1)
            left = profile(spots_u[here, :]).reshape(SU // 16, 16, SU)
            lefts_real.append((left * tiled(turns_real[here, :])).reshape(SU, SU))
            lefts_imag.append((left * tiled(turns_imag[here, :])).reshape(SU, SU))
            rights.append(profile(spots_v[here, :]))
        left = jnp.concatenate(
            [jnp.concatenate(lefts_real, axis=1), jnp.concatenate(lefts_imag, axis=1)], axis=0
        )
        right = jnp.concatenate(rights, axis=1)
        return slot, lax.dot_general(right, left, NT, preferred_element_type=jnp.float32)

    def steps(first, blocks, number):
        def step(k, carry):
            for slot, part in [one_block(first + k * blocks + i) for i in range(blocks)]:
                grids[slot] += part
            return carry

        lax.fori_loop(0, number, step, 0)

    whole = lax.div(count, UNROLL)
    steps(0, UNROLL, whole)
    steps(whole * UNROLL, REST, lax.div(lax.rem(count, UNROLL) + REST - 1, REST))


def local(kernel, operands, shape, name):
    return pl.pallas_call(
        kernel,
        out_shape=jax.ShapeDtypeStruct(shape, jnp.bfloat16),
        in_specs=[VMEM] * len(operands),
        out_specs=VMEM,
        compiler_params=PARAMS,
        cost_estimate=pl.CostEstimate(flops=0, bytes_accessed=400_000, transcendentals=0),
        name=name,
    )(*operands)


def exchange(value, axis, shift):
    return lax.ppermute(value, axis, [(n, n ^ shift) for n in range(lax.axis_size(axis))])


def table_kernel(sizes, norm, packed, ours, theirs, *refs):
    slots, meta_row = sizes
    grids, (mine_ref, other_ref, table_f, total) = refs[:-4], refs[-4:]
    chan = lax.axis_index("chan")
    first = chan == 0

    def parts(table):
        table_f[...] = table
        return table_f[pl.ds(0, SU, stride=2), :], table_f[pl.ds(1, SU, stride=2), :]

    result = jnp.zeros((SU, 2 * SU), jnp.float32)
    for s in range(slots):
        at = slice(2 * SU * s, 2 * SU * (s + 1))
        fetched = ours[at, :].astype(jnp.float32)
        swapped = theirs[at, :].astype(jnp.float32)
        v_real, v_imag = parts(jnp.where(first, swapped, fetched))
        v_side = jnp.concatenate([v_real.T, v_imag.T], axis=1).astype(jnp.bfloat16)
        grid = sum(ref[s] for ref in grids)
        high, low = (
            jnp.concatenate(
                [
                    part,
                    jnp.concatenate([-part[:, SU:], part[:, :SU]], axis=1),
                ],
                axis=0,
            )
            for part in split_bf16(grid)
        )
        half = jnp.dot(v_side, high, preferred_element_type=jnp.float32) + jnp.dot(
            v_side, low, preferred_element_type=jnp.float32
        )
        u_real, u_imag = parts(jnp.where(first, fetched, swapped))
        u_side = jnp.concatenate(
            [
                jnp.concatenate([u_real, u_imag], axis=1),
                jnp.concatenate([-u_imag, u_real], axis=1),
            ],
            axis=0,
        ).astype(jnp.bfloat16)
        high, low = split_bf16(half)
        result = (
            result
            + jnp.dot(high, u_side, preferred_element_type=jnp.float32)
            + jnp.dot(low, u_side, preferred_element_type=jnp.float32)
        )
    result = jnp.concatenate([result[:, :SU].T, result[:, SU:].T], axis=1)
    tail = meta_row // 16 * 16
    wide = packed[tail : tail + 16, :].astype(jnp.float32)
    at = meta_row - tail + 2
    gain = (wide[at : at + 2] + wide[at + 2 : at + 4]) + wide[at + 4 : at + 6]
    gain_u = jnp.broadcast_to(gain[0:1], (SU, SU)).T
    gains = gain_u * gain[1:2] * norm
    total[...] = result * jnp.concatenate([gains, gains], axis=1)
    half_rows = mine_ref.shape[0]
    mine_ref[...] = total[pl.ds(pl.multiple_of(chan * half_rows, half_rows), half_rows), :]
    other_ref[...] = total[pl.ds(pl.multiple_of((1 - chan) * half_rows, half_rows), half_rows), :]


def body(
    visibilities, coords, plane_index, block_group, offsets, facet_centre, tables, antenna_gain
):
    facets = lax.axis_size("facet")
    groups = lax.axis_size("bl")
    chan_count = lax.axis_size("chan")
    held, chans = visibilities.shape[:2]
    devices = facets * groups
    slots = 2 * facets
    cap = max(2, 2 * held // groups)
    meta_row = 2 * cap * (chans + 1)
    rows = -(-(meta_row + 8) // 16) * 16
    half_rows = SU // chan_count
    norm = SU / math.sqrt(visibilities.shape[3] * held * facets * CH)

    own_table = tables.reshape(2, 2 * SU, SU)
    *pieces, half = pl.pallas_call(
        functools.partial(sort_kernel, (groups, held, chans, cap, rows)),
        out_shape=[
            jax.ShapeDtypeStruct((rows + (2 * SU if shift == 1 else 0), SU), jnp.bfloat16)
            for shift in range(groups)
        ]
        + [jax.ShapeDtypeStruct((2 * SU, SU), jnp.bfloat16)],
        in_specs=[HBM] * 8,
        out_specs=[VMEM] * (groups + 1),
        scratch_shapes=[
            pltpu.SMEM((1, held), jnp.int32),
            pltpu.SMEM((1, held), jnp.int32),
            pltpu.VMEM((held * 2 * chans, SU), jnp.bfloat16),
            pltpu.VMEM((held * 2, SU), jnp.bfloat16),
            pltpu.SMEM((facets, 2, groups), jnp.int32),
            pltpu.SMEM((2, facets), jnp.float32),
            pltpu.VMEM((1, 2, SU), jnp.float32),
            pltpu.VMEM((held * 2 * chans, SU), jnp.float32),
            pltpu.VMEM((held * 2, SU), jnp.float32),
            pltpu.VMEM((groups, rows, SU), jnp.float32),
            pltpu.SMEM((groups,), jnp.int32),
            pltpu.SemaphoreType.DMA((8,)),
        ],
        compiler_params=PARAMS,
        cost_estimate=pl.CostEstimate(flops=100_000, bytes_accessed=100_000, transcendentals=0),
        name="sort_blocks",
    )(
        *(
            pltpu.with_memory_space_constraint(operand, pltpu.HBM)
            for operand in (
                plane_index.reshape(1, held),
                block_group.T,
                visibilities.reshape(held * 2 * chans, SU),
                coords.reshape(held * 2, SU),
                offsets.transpose(0, 2, 1),
                facet_centre.T,
                antenna_gain,
                own_table,
            )
        )
    )
    arrived = [
        lax.ppermute(pieces[shift], "bl", [(g, (g + shift) % groups) for g in range(groups)])
        for shift in [1, *range(groups - 1, 1, -1)]
    ]
    vis_rows = groups * rows
    joined = local(
        functools.partial(join_kernel, rows),
        [half, pieces[0], *arrived],
        (vis_rows + 4 * SU, SU),
        "join",
    )
    blocks = [joined] + [exchange(joined, "facet", shift) for shift in range(1, facets)]
    def grid(some):
        lines = len(some) * groups * cap
        return pl.pallas_call(
            functools.partial(grid_kernel, (facets, groups, chans, cap, rows, len(some))),
            out_shape=jax.ShapeDtypeStruct((slots, SU, 2 * SU), jnp.float32),
            in_specs=[VMEM] * (1 + len(some)),
            out_specs=VMEM,
            scratch_shapes=[
                pltpu.SMEM((lines + UNROLL,), jnp.int32),
            ]
            + [pltpu.VMEM((lines * chans + 8, SU), jnp.float32)] * 4
            + [pltpu.VMEM((SU, SU), jnp.float32)],
            compiler_params=PARAMS,
            cost_estimate=pl.CostEstimate(
                flops=len(some) * 1_000_000_000,
                bytes_accessed=1_000_000,
                transcendentals=len(some) * 1_000_000,
            ),
            name="grid",
        )(joined, *some)

    grids = [grid(blocks[:1]), grid(blocks[-1:])]
    blocks, grids = lax.optimization_barrier((blocks, grids))
    fetched = local(
        functools.partial(collect_kernel, vis_rows), blocks, (facets * 4 * SU, SU), "collect"
    )
    swapped = lax.ppermute(fetched, "chan", [(c, 1 - c) for c in range(chan_count)])
    grids.append(grid(blocks[1:-1]))
    mine, other = pl.pallas_call(
        functools.partial(table_kernel, (slots, meta_row), norm),
        out_shape=[jax.ShapeDtypeStruct((half_rows, 2 * SU), jnp.float32)] * 2,
        in_specs=[VMEM] * (3 + len(grids)),
        out_specs=[VMEM, VMEM],
        scratch_shapes=[
            pltpu.VMEM((2 * SU, SU), jnp.float32),
            pltpu.VMEM((SU, 2 * SU), jnp.float32),
        ],
        compiler_params=PARAMS,
        cost_estimate=pl.CostEstimate(
            flops=1_000_000_000, bytes_accessed=2_000_000, transcendentals=0
        ),
        name="apply_tables",
    )(joined, fetched, swapped, *grids)
    summand = lax.ppermute(other, "chan", [(c, 1 - c) for c in range(chan_count)])
    return (mine + summand).reshape(1, 1, half_rows, 2, SU)


def solution(mesh):
    in_specs = (
        P(("facet", "bl"), "chan", None, None),
        P(("facet", "bl"), None, None),
        P(("facet", "bl")),
        P(("facet", "bl"), None),
        P(),
        P(),
        P(("facet", "bl"), None, None, None, None),
        P("bl", None, None),
    )
    out_specs = P("facet", "bl", "chan", None, None)
    return jax.shard_map(body, mesh=mesh, in_specs=in_specs, out_specs=out_specs, check_vma=False)
```

```python
import functools
import math

import jax
import jax.numpy as jnp
from jax import lax
from jax.experimental import pallas as pl
from jax.experimental.pallas import tpu as pltpu
from jax.sharding import PartitionSpec as P

SU = 128
CH = 8
KERNEL_SPREAD = 1.5
ALPHA = math.sqrt(math.log2(math.e) / (2.0 * KERNEL_SPREAD * KERNEL_SPREAD))
UNROLL = 4
REST = 2
NT = (((1,), (1,)), ((), ()))
VMEM = pl.BlockSpec(memory_space=pltpu.VMEM)
HBM = pl.BlockSpec(memory_space=pltpu.HBM)
PARAMS = pltpu.CompilerParams(vmem_limit_bytes=32 * 1024 * 1024)


def cos_sin(turns):
    quarter = jnp.floor(4.0 * turns + 0.5)
    angle = (2.0 * math.pi) * (turns - 0.25 * quarter)
    sq = angle * angle
    sine = angle * (
        1.0 + sq * (-1.0 / 6 + sq * (1.0 / 120 + sq * (-1.0 / 5040 + sq * (1.0 / 362880))))
    )
    cosine = 1.0 + sq * (
        -0.5 + sq * (1.0 / 24 + sq * (-1.0 / 720 + sq * (1.0 / 40320 + sq * (-1.0 / 3628800))))
    )
    turn = quarter.astype(jnp.int32) & 3
    odd = (turn & 1) == 1
    cos_out = jnp.where(odd, sine, cosine)
    sin_out = jnp.where(odd, cosine, sine)
    cos_out = jnp.where((turn == 1) | (turn == 2), -cos_out, cos_out)
    sin_out = jnp.where(turn >= 2, -sin_out, sin_out)
    return cos_out, sin_out


def split_bf16(x):
    high = x.astype(jnp.bfloat16)
    low = (x - high.astype(jnp.float32)).astype(jnp.bfloat16)
    return high, low


def three_parts(x):
    parts = []
    for _ in range(3):
        part = x.astype(jnp.bfloat16)
        x = x - part.astype(jnp.float32)
        parts.append(part.astype(jnp.float32))
    return parts


def sort_kernel(sizes, *refs):
    groups, held, chans, cap, rows = sizes
    table_hbm, outs, half = refs[7], refs[8 : 8 + groups], refs[8 + groups]
    targets = refs[9 + groups : 16 + groups]
    plane_ref, group_ref, samples_b, place_b, offsets_ref, centre_ref, gain_ref = targets
    samples, place, sorted_, filled, sems = refs[16 + groups :]
    facet = lax.axis_index("facet")
    copies = [
        pltpu.make_async_copy(source, target, sems.at[n])
        for n, (source, target) in enumerate(zip(refs[:7], targets))
    ]
    table = pltpu.make_async_copy(table_hbm.at[lax.axis_index("chan")], half, sems.at[7])
    for copy in copies + [table]:
        copy.start()
    sorted_[...] = jnp.zeros_like(sorted_)
    for g in range(groups):
        filled[g] = 0
    for copy in copies:
        copy.wait()
    samples[...] = samples_b[...].astype(jnp.float32)
    place[...] = place_b[...].astype(jnp.float32)
    lane = lax.broadcasted_iota(jnp.int32, (1, SU), 1)
    meta = 2 * cap * (chans + 1)
    centre = [
        part
        for axis in range(2)
        for part in three_parts(jnp.full((1, SU), centre_ref[axis, facet], jnp.float32))
    ]
    gains = three_parts(gain_ref[0])
    for g in range(groups):
        numbers = jnp.zeros((1, SU), jnp.float32)
        for axis in range(2):
            offset = offsets_ref[facet, axis, g].astype(jnp.float32)
            numbers = jnp.where(lane == axis, offset, numbers)
        for n, part in enumerate(centre):
            numbers = jnp.where(lane == 2 + n, part, numbers)
        sorted_[g, meta + 1 : meta + 2, :] = numbers
        for n, part in enumerate(gains):
            sorted_[g, meta + 2 + 2 * n : meta + 4 + 2 * n, :] = part
    for i in range(held):
        g = group_ref[0, i]
        k = filled[g]
        filled[g] = k + 1
        for part in range(2):
            at = part * cap * chans + k * chans
            sorted_[g, pl.ds(at, chans), :] = samples[pl.ds(2 * chans * i + part, chans, stride=2), :]
            at = 2 * cap * chans + part * cap + k
            sorted_[g, pl.ds(at, 1), :] = place[2 * i + part : 2 * i + part + 1, :]
        sorted_[g, meta : meta + 1, :] += jnp.where(
            lane == k, (plane_ref[0, i] + 1).astype(jnp.float32), 0.0
        )
    for shift, out_ref in enumerate(outs):
        g = lax.rem(lax.axis_index("bl") + shift, groups)
        out_ref[:rows, :] = sorted_[g].astype(jnp.bfloat16)
    table.wait()
    outs[1][rows:, :] = half[...]


def join_kernel(rows, half, *refs):
    *pieces, joined = refs
    for n, ref in enumerate(pieces):
        joined[n * rows : (n + 1) * rows, :] = ref[:rows, :]
    at = len(pieces) * rows
    joined[at : at + 2 * SU, :] = half[...]
    joined[at + 2 * SU :, :] = pieces[1][rows:, :]


def collect_kernel(skip, *refs):
    for n, ref in enumerate(refs[:-1]):
        refs[-1][n * 4 * SU : (n + 1) * 4 * SU, :] = ref[skip:, :]


def grid_kernel(sizes, *refs):
    facets, groups, chans, cap, rows, count_here = sizes
    own_ref, grids = refs[0], refs[1 + count_here]
    order, spots_u, spots_v, turns_real, turns_imag, cells = refs[2 + count_here :]
    pieces = [
        ref.at[pl.ds(n * rows, rows)] for ref in refs[1 : 1 + count_here] for n in range(groups)
    ]
    devices = len(pieces)
    slots = 2 * facets
    lines = cap * chans
    meta_row = 2 * (lines + cap)
    tail = meta_row // 16 * 16
    facet = lax.axis_index("facet")
    group = lax.axis_index("bl")
    chan = lax.axis_index("chan")

    lane = lax.broadcasted_iota(jnp.int32, (1, SU), 1)
    own = own_ref[tail : tail + 16, :].astype(jnp.float32)
    numbers = own[meta_row - tail + 1 : meta_row - tail + 2]
    codes = []
    for d in range(devices):
        meta = pieces[d][tail : tail + 16, :].astype(jnp.float32)
        plane = meta[meta_row - tail : meta_row - tail + 1].astype(jnp.int32) - 1
        set_id = jnp.where(lax.rem(plane, groups) == group, 0, 1)
        code = (d * cap + lane) * slots + 2 * (lax.div(plane, groups) ^ facet) + set_id
        codes.append(jnp.where(plane >= 0, code, -1))
    grids[...] = jnp.zeros_like(grids)

    def number(n):
        return jnp.broadcast_to(numbers[:, n : n + 1], (lines, SU))

    offset_u = number(0)
    offset_v = number(1)
    along_l = number(2) + number(3) + number(4)
    along_m = number(5) + number(6) + number(7)
    line = lax.broadcasted_iota(jnp.int32, (lines, SU), 0)
    channel = (chan * chans + lax.rem(line, chans)).astype(jnp.float32)
    scale = 1.0 + 0.01 * (channel - 0.5 * (CH - 1))

    def spread_lines(place):
        return jnp.concatenate(
            [jnp.broadcast_to(place[k : k + 1], (chans, SU)) for k in range(cap)], axis=0
        )

    for d in range(devices):
        at = d * lines
        wide = pieces[d][...].astype(jnp.float32)
        real = wide[:lines]
        imag = wide[lines : 2 * lines]
        along_u = spread_lines(wide[2 * lines : 2 * lines + cap])
        along_v = spread_lines(wide[2 * lines + cap : 2 * (lines + cap)])
        cosine, sine = cos_sin((1.0 / SU) * (scale * (along_u * along_l + along_v * along_m)))
        spots_u[at : at + lines, :] = ALPHA * (scale * along_u - offset_u)
        spots_v[at : at + lines, :] = ALPHA * (scale * along_v - offset_v)
        turns_real[at : at + lines, :] = real * cosine - imag * sine
        turns_imag[at : at + lines, :] = real * sine + imag * cosine
    last = devices * lines
    for ref in (spots_u, spots_v, turns_real, turns_imag):
        ref[last : last + 8, :] = jnp.zeros((8, SU), jnp.float32)

    count = jnp.int32(0)
    for d in range(devices):
        for k in range(cap):
            code = codes[d][0, k]
            order[count] = code
            count = count + jnp.where(code >= 0, 1, 0)
    for i in range(UNROLL):
        order[count + i] = devices * cap * slots

    cells[...] = ALPHA * lax.broadcasted_iota(jnp.int32, (SU, SU), 0).astype(jnp.float32)

    def profile(spot):
        apart = spot - cells[...]
        return jnp.exp2(-((apart * apart).astype(jnp.bfloat16)))

    def tiled(row):
        return jnp.broadcast_to(row, (16, SU)).astype(jnp.bfloat16)[None]

    def one_block(at):
        code = order[at]
        slot = lax.rem(code, slots)
        base = lax.div(code, slots) * chans
        lefts_real, lefts_imag, rights = [], [], []
        for c in range(chans):
            here = pl.ds(base + c, 1)
            left = profile(spots_u[here, :]).reshape(SU // 16, 16, SU)
            lefts_real.append((left * tiled(turns_real[here, :])).reshape(SU, SU))
            lefts_imag.append((left * tiled(turns_imag[here, :])).reshape(SU, SU))
            rights.append(profile(spots_v[here, :]))
        left = jnp.concatenate(
            [jnp.concatenate(lefts_real, axis=1), jnp.concatenate(lefts_imag, axis=1)], axis=0
        )
        right = jnp.concatenate(rights, axis=1)
        return slot, lax.dot_general(right, left, NT, preferred_element_type=jnp.float32)

    def steps(first, blocks, number):
        def step(k, carry):
            for slot, part in [one_block(first + k * blocks + i) for i in range(blocks)]:
                grids[slot] += part
            return carry

        lax.fori_loop(0, number, step, 0)

    whole = lax.div(count, UNROLL)
    steps(0, UNROLL, whole)
    steps(whole * UNROLL, REST, lax.div(lax.rem(count, UNROLL) + REST - 1, REST))


def local(kernel, operands, shape, name):
    return pl.pallas_call(
        kernel,
        out_shape=jax.ShapeDtypeStruct(shape, jnp.bfloat16),
        in_specs=[VMEM] * len(operands),
        out_specs=VMEM,
        compiler_params=PARAMS,
        cost_estimate=pl.CostEstimate(flops=0, bytes_accessed=400_000, transcendentals=0),
        name=name,
    )(*operands)


def exchange(value, axis, shift):
    return lax.ppermute(value, axis, [(n, n ^ shift) for n in range(lax.axis_size(axis))])


def table_kernel(sizes, norm, packed, ours, theirs, *refs):
    slots, meta_row = sizes
    grids, (mine_ref, other_ref, table_f, total) = refs[:-4], refs[-4:]
    chan = lax.axis_index("chan")
    first = chan == 0

    def parts(table):
        table_f[...] = table
        return table_f[pl.ds(0, SU, stride=2), :], table_f[pl.ds(1, SU, stride=2), :]

    result = jnp.zeros((SU, 2 * SU), jnp.float32)
    for s in range(slots):
        at = slice(2 * SU * s, 2 * SU * (s + 1))
        fetched = ours[at, :].astype(jnp.float32)
        swapped = theirs[at, :].astype(jnp.float32)
        v_real, v_imag = parts(jnp.where(first, swapped, fetched))
        v_side = jnp.concatenate([v_real.T, v_imag.T], axis=1).astype(jnp.bfloat16)
        grid = sum(ref[s] for ref in grids)
        high, low = (
            jnp.concatenate(
                [
                    part,
                    jnp.concatenate([-part[:, SU:], part[:, :SU]], axis=1),
                ],
                axis=0,
            )
            for part in split_bf16(grid)
        )
        half = jnp.dot(v_side, high, preferred_element_type=jnp.float32) + jnp.dot(
            v_side, low, preferred_element_type=jnp.float32
        )
        u_real, u_imag = parts(jnp.where(first, fetched, swapped))
        u_side = jnp.concatenate(
            [
                jnp.concatenate([u_real, u_imag], axis=1),
                jnp.concatenate([-u_imag, u_real], axis=1),
            ],
            axis=0,
        ).astype(jnp.bfloat16)
        high, low = split_bf16(half)
        result = (
            result
            + jnp.dot(high, u_side, preferred_element_type=jnp.float32)
            + jnp.dot(low, u_side, preferred_element_type=jnp.float32)
        )
    result = jnp.concatenate([result[:, :SU].T, result[:, SU:].T], axis=1)
    tail = meta_row // 16 * 16
    wide = packed[tail : tail + 16, :].astype(jnp.float32)
    at = meta_row - tail + 2
    gain = (wide[at : at + 2] + wide[at + 2 : at + 4]) + wide[at + 4 : at + 6]
    gain_u = jnp.broadcast_to(gain[0:1], (SU, SU)).T
    gains = gain_u * gain[1:2] * norm
    total[...] = result * jnp.concatenate([gains, gains], axis=1)
    half_rows = mine_ref.shape[0]
    mine_ref[...] = total[pl.ds(pl.multiple_of(chan * half_rows, half_rows), half_rows), :]
    other_ref[...] = total[pl.ds(pl.multiple_of((1 - chan) * half_rows, half_rows), half_rows), :]


def body(
    visibilities, coords, plane_index, block_group, offsets, facet_centre, tables, antenna_gain
):
    facets = lax.axis_size("facet")
    groups = lax.axis_size("bl")
    chan_count = lax.axis_size("chan")
    held, chans = visibilities.shape[:2]
    devices = facets * groups
    slots = 2 * facets
    cap = max(2, 2 * held // groups)
    meta_row = 2 * cap * (chans + 1)
    rows = -(-(meta_row + 8) // 16) * 16
    half_rows = SU // chan_count
    norm = SU / math.sqrt(visibilities.shape[3] * held * facets * CH)

    own_table = tables.reshape(2, 2 * SU, SU)
    *pieces, half = pl.pallas_call(
        functools.partial(sort_kernel, (groups, held, chans, cap, rows)),
        out_shape=[
            jax.ShapeDtypeStruct((rows + (2 * SU if shift == 1 else 0), SU), jnp.bfloat16)
            for shift in range(groups)
        ]
        + [jax.ShapeDtypeStruct((2 * SU, SU), jnp.bfloat16)],
        in_specs=[HBM] * 8,
        out_specs=[VMEM] * (groups + 1),
        scratch_shapes=[
            pltpu.SMEM((1, held), jnp.int32),
            pltpu.SMEM((1, held), jnp.int32),
            pltpu.VMEM((held * 2 * chans, SU), jnp.bfloat16),
            pltpu.VMEM((held * 2, SU), jnp.bfloat16),
            pltpu.SMEM((facets, 2, groups), jnp.int32),
            pltpu.SMEM((2, facets), jnp.float32),
            pltpu.VMEM((1, 2, SU), jnp.float32),
            pltpu.VMEM((held * 2 * chans, SU), jnp.float32),
            pltpu.VMEM((held * 2, SU), jnp.float32),
            pltpu.VMEM((groups, rows, SU), jnp.float32),
            pltpu.SMEM((groups,), jnp.int32),
            pltpu.SemaphoreType.DMA((8,)),
        ],
        compiler_params=PARAMS,
        cost_estimate=pl.CostEstimate(flops=100_000, bytes_accessed=100_000, transcendentals=0),
        name="sort_blocks",
    )(
        *(
            pltpu.with_memory_space_constraint(operand, pltpu.HBM)
            for operand in (
                plane_index.reshape(1, held),
                block_group.T,
                visibilities.reshape(held * 2 * chans, SU),
                coords.reshape(held * 2, SU),
                offsets.transpose(0, 2, 1),
                facet_centre.T,
                antenna_gain,
                own_table,
            )
        )
    )
    arrived = [
        lax.ppermute(pieces[shift], "bl", [(g, (g + shift) % groups) for g in range(groups)])
        for shift in [1, *range(groups - 1, 1, -1)]
    ]
    vis_rows = groups * rows
    joined = local(
        functools.partial(join_kernel, rows),
        [half, pieces[0], *arrived],
        (vis_rows + 4 * SU, SU),
        "join",
    )
    blocks = [joined] + [exchange(joined, "facet", shift) for shift in range(1, facets)]
    def grid(some):
        lines = len(some) * groups * cap
        return pl.pallas_call(
            functools.partial(grid_kernel, (facets, groups, chans, cap, rows, len(some))),
            out_shape=jax.ShapeDtypeStruct((slots, SU, 2 * SU), jnp.float32),
            in_specs=[VMEM] * (1 + len(some)),
            out_specs=VMEM,
            scratch_shapes=[
                pltpu.SMEM((lines + UNROLL,), jnp.int32),
            ]
            + [pltpu.VMEM((lines * chans + 8, SU), jnp.float32)] * 4
            + [pltpu.VMEM((SU, SU), jnp.float32)],
            compiler_params=PARAMS,
            cost_estimate=pl.CostEstimate(
                flops=len(some) * 1_000_000_000,
                bytes_accessed=1_000_000,
                transcendentals=len(some) * 1_000_000,
            ),
            name="grid",
        )(joined, *some)

    grids = [grid(blocks[:1]), grid(blocks[1:-1])]
    blocks, grids = lax.optimization_barrier((blocks, grids))
    fetched = local(
        functools.partial(collect_kernel, vis_rows), blocks, (facets * 4 * SU, SU), "collect"
    )
    swapped = lax.ppermute(fetched, "chan", [(c, 1 - c) for c in range(chan_count)])
    grids.append(grid(blocks[-1:]))
    mine, other = pl.pallas_call(
        functools.partial(table_kernel, (slots, meta_row), norm),
        out_shape=[jax.ShapeDtypeStruct((half_rows, 2 * SU), jnp.float32)] * 2,
        in_specs=[VMEM] * (3 + len(grids)),
        out_specs=[VMEM, VMEM],
        scratch_shapes=[
            pltpu.VMEM((2 * SU, SU), jnp.float32),
            pltpu.VMEM((SU, 2 * SU), jnp.float32),
        ],
        compiler_params=PARAMS,
        cost_estimate=pl.CostEstimate(
            flops=1_000_000_000, bytes_accessed=2_000_000, transcendentals=0
        ),
        name="apply_tables",
    )(joined, fetched, swapped, *grids)
    summand = lax.ppermute(other, "chan", [(c, 1 - c) for c in range(chan_count)])
    return (mine + summand).reshape(1, 1, half_rows, 2, SU)


def solution(mesh):
    in_specs = (
        P(("facet", "bl"), "chan", None, None),
        P(("facet", "bl"), None, None),
        P(("facet", "bl")),
        P(("facet", "bl"), None),
        P(),
        P(),
        P(("facet", "bl"), None, None, None, None),
        P("bl", None, None),
    )
    out_specs = P("facet", "bl", "chan", None, None)
    return jax.shard_map(body, mesh=mesh, in_specs=in_specs, out_specs=out_specs, check_vma=False)
```

```python
import functools
import math

import jax
import jax.numpy as jnp
from jax import lax
from jax.experimental import pallas as pl
from jax.experimental.pallas import tpu as pltpu
from jax.sharding import PartitionSpec as P

SU = 128
CH = 8
KERNEL_SPREAD = 1.5
ALPHA = math.sqrt(math.log2(math.e) / (2.0 * KERNEL_SPREAD * KERNEL_SPREAD))
UNROLL = 4
REST = 2
NT = (((1,), (1,)), ((), ()))
VMEM = pl.BlockSpec(memory_space=pltpu.VMEM)
HBM = pl.BlockSpec(memory_space=pltpu.HBM)
PARAMS = pltpu.CompilerParams(vmem_limit_bytes=32 * 1024 * 1024)


def cos_sin(turns):
    quarter = jnp.floor(4.0 * turns + 0.5)
    angle = (2.0 * math.pi) * (turns - 0.25 * quarter)
    sq = angle * angle
    sine = angle * (
        1.0 + sq * (-1.0 / 6 + sq * (1.0 / 120 + sq * (-1.0 / 5040 + sq * (1.0 / 362880))))
    )
    cosine = 1.0 + sq * (
        -0.5 + sq * (1.0 / 24 + sq * (-1.0 / 720 + sq * (1.0 / 40320 + sq * (-1.0 / 3628800))))
    )
    turn = quarter.astype(jnp.int32) & 3
    odd = (turn & 1) == 1
    cos_out = jnp.where(odd, sine, cosine)
    sin_out = jnp.where(odd, cosine, sine)
    cos_out = jnp.where((turn == 1) | (turn == 2), -cos_out, cos_out)
    sin_out = jnp.where(turn >= 2, -sin_out, sin_out)
    return cos_out, sin_out


def split_bf16(x):
    high = x.astype(jnp.bfloat16)
    low = (x - high.astype(jnp.float32)).astype(jnp.bfloat16)
    return high, low


def three_parts(x):
    parts = []
    for _ in range(3):
        part = x.astype(jnp.bfloat16)
        x = x - part.astype(jnp.float32)
        parts.append(part.astype(jnp.float32))
    return parts


def sort_kernel(sizes, *refs):
    groups, held, chans, cap, rows = sizes
    table_hbm, outs, half = refs[7], refs[8 : 8 + groups], refs[8 + groups]
    targets = refs[9 + groups : 16 + groups]
    plane_ref, group_ref, samples_b, place_b, offsets_ref, centre_ref, gain_ref = targets
    samples, place, sorted_, filled, sems = refs[16 + groups :]
    facet = lax.axis_index("facet")
    copies = [
        pltpu.make_async_copy(source, target, sems.at[n])
        for n, (source, target) in enumerate(zip(refs[:7], targets))
    ]
    table = pltpu.make_async_copy(table_hbm.at[lax.axis_index("chan")], half, sems.at[7])
    for copy in copies + [table]:
        copy.start()
    sorted_[...] = jnp.zeros_like(sorted_)
    for g in range(groups):
        filled[g] = 0
    for copy in copies:
        copy.wait()
    samples[...] = samples_b[...].astype(jnp.float32)
    place[...] = place_b[...].astype(jnp.float32)
    lane = lax.broadcasted_iota(jnp.int32, (1, SU), 1)
    meta = 2 * cap * (chans + 1)
    centre = [
        part
        for axis in range(2)
        for part in three_parts(jnp.full((1, SU), centre_ref[axis, facet], jnp.float32))
    ]
    gains = three_parts(gain_ref[0])
    for g in range(groups):
        numbers = jnp.zeros((1, SU), jnp.float32)
        for axis in range(2):
            offset = offsets_ref[facet, axis, g].astype(jnp.float32)
            numbers = jnp.where(lane == axis, offset, numbers)
        for n, part in enumerate(centre):
            numbers = jnp.where(lane == 2 + n, part, numbers)
        sorted_[g, meta + 1 : meta + 2, :] = numbers
        for n, part in enumerate(gains):
            sorted_[g, meta + 2 + 2 * n : meta + 4 + 2 * n, :] = part
    for i in range(held):
        g = group_ref[0, i]
        k = filled[g]
        filled[g] = k + 1
        for part in range(2):
            at = part * cap * chans + k * chans
            sorted_[g, pl.ds(at, chans), :] = samples[pl.ds(2 * chans * i + part, chans, stride=2), :]
            at = 2 * cap * chans + part * cap + k
            sorted_[g, pl.ds(at, 1), :] = place[2 * i + part : 2 * i + part + 1, :]
        sorted_[g, meta : meta + 1, :] += jnp.where(
            lane == k, (plane_ref[0, i] + 1).astype(jnp.float32), 0.0
        )
    for shift, out_ref in enumerate(outs):
        g = lax.rem(lax.axis_index("bl") + shift, groups)
        out_ref[:rows, :] = sorted_[g].astype(jnp.bfloat16)
    table.wait()
    outs[1][rows:, :] = half[...]


def join_kernel(rows, half, *refs):
    *pieces, here, tables, joined = refs
    at = len(pieces) * rows
    for n, ref in enumerate(pieces):
        piece = ref[:rows, :]
        here[n * rows : (n + 1) * rows, :] = piece
        joined[n * rows : (n + 1) * rows, :] = piece
    for n, ref in enumerate((half, pieces[1].at[pl.ds(rows, 2 * SU)])):
        table = ref[...]
        tables[n * 2 * SU : (n + 1) * 2 * SU, :] = table
        joined[at + n * 2 * SU : at + (n + 1) * 2 * SU, :] = table


def collect_kernel(tables, *refs):
    *joined, diagonal, out_ref = refs
    for n, ref in enumerate((tables, *joined, diagonal)):
        start = ref.shape[0] - 4 * SU
        out_ref[n * 4 * SU : (n + 1) * 4 * SU, :] = ref[start:, :]


def grid_kernel(sizes, *refs):
    facets, groups, chans, cap, rows, count_here = sizes
    own_ref, grids = refs[0], refs[1 + count_here]
    order, spots_u, spots_v, turns_real, turns_imag, cells = refs[2 + count_here :]
    pieces = [
        ref.at[pl.ds(n * rows, rows)] for ref in refs[1 : 1 + count_here] for n in range(groups)
    ]
    devices = len(pieces)
    slots = 2 * facets
    lines = cap * chans
    meta_row = 2 * (lines + cap)
    tail = meta_row // 16 * 16
    facet = lax.axis_index("facet")
    group = lax.axis_index("bl")
    chan = lax.axis_index("chan")

    lane = lax.broadcasted_iota(jnp.int32, (1, SU), 1)
    own = own_ref[tail : tail + 16, :].astype(jnp.float32)
    numbers = own[meta_row - tail + 1 : meta_row - tail + 2]
    codes = []
    for d in range(devices):
        meta = pieces[d][tail : tail + 16, :].astype(jnp.float32)
        plane = meta[meta_row - tail : meta_row - tail + 1].astype(jnp.int32) - 1
        set_id = jnp.where(lax.rem(plane, groups) == group, 0, 1)
        code = (d * cap + lane) * slots + 2 * (lax.div(plane, groups) ^ facet) + set_id
        codes.append(jnp.where(plane >= 0, code, -1))
    grids[...] = jnp.zeros_like(grids)

    def number(n):
        return jnp.broadcast_to(numbers[:, n : n + 1], (lines, SU))

    offset_u = number(0)
    offset_v = number(1)
    along_l = number(2) + number(3) + number(4)
    along_m = number(5) + number(6) + number(7)
    line = lax.broadcasted_iota(jnp.int32, (lines, SU), 0)
    channel = (chan * chans + lax.rem(line, chans)).astype(jnp.float32)
    scale = 1.0 + 0.01 * (channel - 0.5 * (CH - 1))

    def spread_lines(place):
        return jnp.concatenate(
            [jnp.broadcast_to(place[k : k + 1], (chans, SU)) for k in range(cap)], axis=0
        )

    for d in range(devices):
        at = d * lines
        wide = pieces[d][...].astype(jnp.float32)
        real = wide[:lines]
        imag = wide[lines : 2 * lines]
        along_u = spread_lines(wide[2 * lines : 2 * lines + cap])
        along_v = spread_lines(wide[2 * lines + cap : 2 * (lines + cap)])
        cosine, sine = cos_sin((1.0 / SU) * (scale * (along_u * along_l + along_v * along_m)))
        spots_u[at : at + lines, :] = ALPHA * (scale * along_u - offset_u)
        spots_v[at : at + lines, :] = ALPHA * (scale * along_v - offset_v)
        turns_real[at : at + lines, :] = real * cosine - imag * sine
        turns_imag[at : at + lines, :] = real * sine + imag * cosine
    last = devices * lines
    for ref in (spots_u, spots_v, turns_real, turns_imag):
        ref[last : last + 8, :] = jnp.zeros((8, SU), jnp.float32)

    count = jnp.int32(0)
    for d in range(devices):
        for k in range(cap):
            code = codes[d][0, k]
            order[count] = code
            count = count + jnp.where(code >= 0, 1, 0)
    for i in range(UNROLL):
        order[count + i] = devices * cap * slots

    cells[...] = ALPHA * lax.broadcasted_iota(jnp.int32, (SU, SU), 0).astype(jnp.float32)

    def profile(spot):
        apart = spot - cells[...]
        return jnp.exp2(-((apart * apart).astype(jnp.bfloat16)))

    def tiled(row):
        return jnp.broadcast_to(row, (16, SU)).astype(jnp.bfloat16)[None]

    def one_block(at):
        code = order[at]
        slot = lax.rem(code, slots)
        base = lax.div(code, slots) * chans
        lefts_real, lefts_imag, rights = [], [], []
        for c in range(chans):
            here = pl.ds(base + c, 1)
            left = profile(spots_u[here, :]).reshape(SU // 16, 16, SU)
            lefts_real.append((left * tiled(turns_real[here, :])).reshape(SU, SU))
            lefts_imag.append((left * tiled(turns_imag[here, :])).reshape(SU, SU))
            rights.append(profile(spots_v[here, :]))
        left = jnp.concatenate(
            [jnp.concatenate(lefts_real, axis=1), jnp.concatenate(lefts_imag, axis=1)], axis=0
        )
        right = jnp.concatenate(rights, axis=1)
        return slot, lax.dot_general(right, left, NT, preferred_element_type=jnp.float32)

    def steps(first, blocks, number):
        def step(k, carry):
            for slot, part in [one_block(first + k * blocks + i) for i in range(blocks)]:
                grids[slot] += part
            return carry

        lax.fori_loop(0, number, step, 0)

    whole = lax.div(count, UNROLL)
    steps(0, UNROLL, whole)
    steps(whole * UNROLL, REST, lax.div(lax.rem(count, UNROLL) + REST - 1, REST))


def local(kernel, operands, shapes, name):
    return pl.pallas_call(
        kernel,
        out_shape=[jax.ShapeDtypeStruct(shape, jnp.bfloat16) for shape in shapes],
        in_specs=[VMEM] * len(operands),
        out_specs=[VMEM] * len(shapes),
        compiler_params=PARAMS,
        cost_estimate=pl.CostEstimate(flops=0, bytes_accessed=400_000, transcendentals=0),
        name=name,
    )(*operands)


def exchange(value, axis, shift):
    return lax.ppermute(value, axis, [(n, n ^ shift) for n in range(lax.axis_size(axis))])


def table_kernel(sizes, norm, packed, ours, theirs, *refs):
    slots, meta_row = sizes
    grids, (mine_ref, other_ref, table_f, total) = refs[:-4], refs[-4:]
    chan = lax.axis_index("chan")
    first = chan == 0

    def parts(table):
        table_f[...] = table
        return table_f[pl.ds(0, SU, stride=2), :], table_f[pl.ds(1, SU, stride=2), :]

    result = jnp.zeros((SU, 2 * SU), jnp.float32)
    for s in range(slots):
        at = slice(2 * SU * s, 2 * SU * (s + 1))
        fetched = ours[at, :].astype(jnp.float32)
        swapped = theirs[at, :].astype(jnp.float32)
        v_real, v_imag = parts(jnp.where(first, swapped, fetched))
        v_side = jnp.concatenate([v_real.T, v_imag.T], axis=1).astype(jnp.bfloat16)
        grid = sum(ref[s] for ref in grids)
        high, low = (
            jnp.concatenate(
                [
                    part,
                    jnp.concatenate([-part[:, SU:], part[:, :SU]], axis=1),
                ],
                axis=0,
            )
            for part in split_bf16(grid)
        )
        half = jnp.dot(v_side, high, preferred_element_type=jnp.float32) + jnp.dot(
            v_side, low, preferred_element_type=jnp.float32
        )
        u_real, u_imag = parts(jnp.where(first, fetched, swapped))
        u_side = jnp.concatenate(
            [
                jnp.concatenate([u_real, u_imag], axis=1),
                jnp.concatenate([-u_imag, u_real], axis=1),
            ],
            axis=0,
        ).astype(jnp.bfloat16)
        high, low = split_bf16(half)
        result = (
            result
            + jnp.dot(high, u_side, preferred_element_type=jnp.float32)
            + jnp.dot(low, u_side, preferred_element_type=jnp.float32)
        )
    result = jnp.concatenate([result[:, :SU].T, result[:, SU:].T], axis=1)
    tail = meta_row // 16 * 16
    wide = packed[tail : tail + 16, :].astype(jnp.float32)
    at = meta_row - tail + 2
    gain = (wide[at : at + 2] + wide[at + 2 : at + 4]) + wide[at + 4 : at + 6]
    gain_u = jnp.broadcast_to(gain[0:1], (SU, SU)).T
    gains = gain_u * gain[1:2] * norm
    total[...] = result * jnp.concatenate([gains, gains], axis=1)
    half_rows = mine_ref.shape[0]
    mine_ref[...] = total[pl.ds(pl.multiple_of(chan * half_rows, half_rows), half_rows), :]
    other_ref[...] = total[pl.ds(pl.multiple_of((1 - chan) * half_rows, half_rows), half_rows), :]


def body(
    visibilities, coords, plane_index, block_group, offsets, facet_centre, tables, antenna_gain
):
    facets = lax.axis_size("facet")
    groups = lax.axis_size("bl")
    chan_count = lax.axis_size("chan")
    held, chans = visibilities.shape[:2]
    devices = facets * groups
    slots = 2 * facets
    cap = max(2, 2 * held // groups)
    meta_row = 2 * cap * (chans + 1)
    rows = -(-(meta_row + 8) // 16) * 16
    half_rows = SU // chan_count
    norm = SU / math.sqrt(visibilities.shape[3] * held * facets * CH)

    own_table = tables.reshape(2, 2 * SU, SU)
    *pieces, half = pl.pallas_call(
        functools.partial(sort_kernel, (groups, held, chans, cap, rows)),
        out_shape=[
            jax.ShapeDtypeStruct((rows + (2 * SU if shift == 1 else 0), SU), jnp.bfloat16)
            for shift in range(groups)
        ]
        + [jax.ShapeDtypeStruct((2 * SU, SU), jnp.bfloat16)],
        in_specs=[HBM] * 8,
        out_specs=[VMEM] * (groups + 1),
        scratch_shapes=[
            pltpu.SMEM((1, held), jnp.int32),
            pltpu.SMEM((1, held), jnp.int32),
            pltpu.VMEM((held * 2 * chans, SU), jnp.bfloat16),
            pltpu.VMEM((held * 2, SU), jnp.bfloat16),
            pltpu.SMEM((facets, 2, groups), jnp.int32),
            pltpu.SMEM((2, facets), jnp.float32),
            pltpu.VMEM((1, 2, SU), jnp.float32),
            pltpu.VMEM((held * 2 * chans, SU), jnp.float32),
            pltpu.VMEM((held * 2, SU), jnp.float32),
            pltpu.VMEM((groups, rows, SU), jnp.float32),
            pltpu.SMEM((groups,), jnp.int32),
            pltpu.SemaphoreType.DMA((8,)),
        ],
        compiler_params=PARAMS,
        cost_estimate=pl.CostEstimate(flops=100_000, bytes_accessed=100_000, transcendentals=0),
        name="sort_blocks",
    )(
        *(
            pltpu.with_memory_space_constraint(operand, pltpu.HBM)
            for operand in (
                plane_index.reshape(1, held),
                block_group.T,
                visibilities.reshape(held * 2 * chans, SU),
                coords.reshape(held * 2, SU),
                offsets.transpose(0, 2, 1),
                facet_centre.T,
                antenna_gain,
                own_table,
            )
        )
    )
    arrived = [
        lax.ppermute(pieces[shift], "bl", [(g, (g + shift) % groups) for g in range(groups)])
        for shift in [1, *range(groups - 1, 1, -1)]
    ]
    vis_rows = groups * rows
    here, both, joined = local(
        functools.partial(join_kernel, rows),
        [half, pieces[0], *arrived],
        [(vis_rows, SU), (4 * SU, SU), (vis_rows + 4 * SU, SU)],
        "join",
    )
    blocks = (
        [here]
        + [exchange(joined, "facet", shift) for shift in range(1, facets - 1)]
        + [exchange(here, "facet", facets - 1)]
    )
    last_tables = exchange(both, "facet", facets - 1)

    def grid(some):
        lines = len(some) * groups * cap
        return pl.pallas_call(
            functools.partial(grid_kernel, (facets, groups, chans, cap, rows, len(some))),
            out_shape=jax.ShapeDtypeStruct((slots, SU, 2 * SU), jnp.float32),
            in_specs=[VMEM] * (1 + len(some)),
            out_specs=VMEM,
            scratch_shapes=[
                pltpu.SMEM((lines + UNROLL,), jnp.int32),
            ]
            + [pltpu.VMEM((lines * chans + 8, SU), jnp.float32)] * 4
            + [pltpu.VMEM((SU, SU), jnp.float32)],
            compiler_params=PARAMS,
            cost_estimate=pl.CostEstimate(
                flops=len(some) * 1_000_000_000,
                bytes_accessed=1_000_000,
                transcendentals=len(some) * 1_000_000,
            ),
            name="grid",
        )(here, *some)

    grids = [grid(blocks[:1]), grid([blocks[-1], *blocks[1:-2]])]
    blocks, last_tables, grids = lax.optimization_barrier((blocks, last_tables, grids))
    (fetched,) = local(
        collect_kernel,
        [both, *blocks[1:-1], last_tables],
        [(facets * 4 * SU, SU)],
        "collect",
    )
    swapped = lax.ppermute(fetched, "chan", [(c, 1 - c) for c in range(chan_count)])
    grids.append(grid(blocks[-2:-1]))
    mine, other = pl.pallas_call(
        functools.partial(table_kernel, (slots, meta_row), norm),
        out_shape=[jax.ShapeDtypeStruct((half_rows, 2 * SU), jnp.float32)] * 2,
        in_specs=[VMEM] * (3 + len(grids)),
        out_specs=[VMEM, VMEM],
        scratch_shapes=[
            pltpu.VMEM((2 * SU, SU), jnp.float32),
            pltpu.VMEM((SU, 2 * SU), jnp.float32),
        ],
        compiler_params=PARAMS,
        cost_estimate=pl.CostEstimate(
            flops=1_000_000_000, bytes_accessed=2_000_000, transcendentals=0
        ),
        name="apply_tables",
    )(here, fetched, swapped, *grids)
    summand = lax.ppermute(other, "chan", [(c, 1 - c) for c in range(chan_count)])
    return (mine + summand).reshape(1, 1, half_rows, 2, SU)


def solution(mesh):
    in_specs = (
        P(("facet", "bl"), "chan", None, None),
        P(("facet", "bl"), None, None),
        P(("facet", "bl")),
        P(("facet", "bl"), None),
        P(),
        P(),
        P(("facet", "bl"), None, None, None, None),
        P("bl", None, None),
    )
    out_specs = P("facet", "bl", "chan", None, None)
    return jax.shard_map(body, mesh=mesh, in_specs=in_specs, out_specs=out_specs, check_vma=False)
```

```python
import functools
import math

import jax
import jax.numpy as jnp
from jax import lax
from jax.experimental import pallas as pl
from jax.experimental.pallas import tpu as pltpu
from jax.sharding import PartitionSpec as P

SU = 128
CH = 8
KERNEL_SPREAD = 1.5
ALPHA = math.sqrt(math.log2(math.e) / (2.0 * KERNEL_SPREAD * KERNEL_SPREAD))
UNROLL = 4
REST = 2
NT = (((1,), (1,)), ((), ()))
VMEM = pl.BlockSpec(memory_space=pltpu.VMEM)
HBM = pl.BlockSpec(memory_space=pltpu.HBM)
PARAMS = pltpu.CompilerParams(vmem_limit_bytes=32 * 1024 * 1024)


def cos_sin(turns):
    quarter = jnp.floor(4.0 * turns + 0.5)
    angle = (2.0 * math.pi) * (turns - 0.25 * quarter)
    sq = angle * angle
    sine = angle * (
        1.0 + sq * (-1.0 / 6 + sq * (1.0 / 120 + sq * (-1.0 / 5040 + sq * (1.0 / 362880))))
    )
    cosine = 1.0 + sq * (
        -0.5 + sq * (1.0 / 24 + sq * (-1.0 / 720 + sq * (1.0 / 40320 + sq * (-1.0 / 3628800))))
    )
    turn = quarter.astype(jnp.int32) & 3
    odd = (turn & 1) == 1
    cos_out = jnp.where(odd, sine, cosine)
    sin_out = jnp.where(odd, cosine, sine)
    cos_out = jnp.where((turn == 1) | (turn == 2), -cos_out, cos_out)
    sin_out = jnp.where(turn >= 2, -sin_out, sin_out)
    return cos_out, sin_out


def split_bf16(x):
    high = x.astype(jnp.bfloat16)
    low = (x - high.astype(jnp.float32)).astype(jnp.bfloat16)
    return high, low


def three_parts(x):
    parts = []
    for _ in range(3):
        part = x.astype(jnp.bfloat16)
        x = x - part.astype(jnp.float32)
        parts.append(part.astype(jnp.float32))
    return parts


def sort_kernel(sizes, *refs):
    groups, held, chans, cap, rows = sizes
    table_hbm, outs, half = refs[7], refs[8 : 8 + groups], refs[8 + groups]
    targets = refs[9 + groups : 16 + groups]
    plane_ref, group_ref, samples_b, place_b, offsets_ref, centre_ref, gain_ref = targets
    samples, place, sorted_, filled, sems = refs[16 + groups :]
    facet = lax.axis_index("facet")
    copies = [
        pltpu.make_async_copy(source, target, sems.at[n])
        for n, (source, target) in enumerate(zip(refs[:7], targets))
    ]
    table = pltpu.make_async_copy(table_hbm.at[lax.axis_index("chan")], half, sems.at[7])
    for copy in copies + [table]:
        copy.start()
    sorted_[...] = jnp.zeros_like(sorted_)
    for g in range(groups):
        filled[g] = 0
    for copy in copies:
        copy.wait()
    samples[...] = samples_b[...].astype(jnp.float32)
    place[...] = place_b[...].astype(jnp.float32)
    lane = lax.broadcasted_iota(jnp.int32, (1, SU), 1)
    meta = 2 * cap * (chans + 1)
    centre = [
        part
        for axis in range(2)
        for part in three_parts(jnp.full((1, SU), centre_ref[axis, facet], jnp.float32))
    ]
    gains = three_parts(gain_ref[0])
    for g in range(groups):
        numbers = jnp.zeros((1, SU), jnp.float32)
        for axis in range(2):
            offset = offsets_ref[facet, axis, g].astype(jnp.float32)
            numbers = jnp.where(lane == axis, offset, numbers)
        for n, part in enumerate(centre):
            numbers = jnp.where(lane == 2 + n, part, numbers)
        sorted_[g, meta + 1 : meta + 2, :] = numbers
        for n, part in enumerate(gains):
            sorted_[g, meta + 2 + 2 * n : meta + 4 + 2 * n, :] = part
    for i in range(held):
        g = group_ref[0, i]
        k = filled[g]
        filled[g] = k + 1
        for part in range(2):
            at = part * cap * chans + k * chans
            sorted_[g, pl.ds(at, chans), :] = samples[pl.ds(2 * chans * i + part, chans, stride=2), :]
            at = 2 * cap * chans + part * cap + k
            sorted_[g, pl.ds(at, 1), :] = place[2 * i + part : 2 * i + part + 1, :]
        sorted_[g, meta : meta + 1, :] += jnp.where(
            lane == k, (plane_ref[0, i] + 1).astype(jnp.float32), 0.0
        )
    for shift, out_ref in enumerate(outs):
        g = lax.rem(lax.axis_index("bl") + shift, groups)
        out_ref[:rows, :] = sorted_[g].astype(jnp.bfloat16)
    table.wait()
    outs[1][rows:, :] = half[...]


def join_kernel(rows, half, *refs):
    *pieces, joined, short = refs
    at = len(pieces) * rows
    for n, ref in enumerate(pieces):
        piece = ref[:rows, :]
        joined[n * rows : (n + 1) * rows, :] = piece
        short[n * rows : (n + 1) * rows, :] = piece
    table = pieces[1][rows:, :]
    joined[at : at + 2 * SU, :] = table
    short[at:, :] = table
    joined[at + 2 * SU :, :] = half[...]


def collect_kernel(skip, *refs):
    *joined, last_own, out_ref = refs
    for n, ref in enumerate(joined):
        count = ref.shape[0] - skip
        out_ref[n * 4 * SU : n * 4 * SU + count, :] = ref[skip:, :]
    out_ref[out_ref.shape[0] - 2 * SU :, :] = last_own[lax.axis_index("chan")]


def grid_kernel(sizes, *refs):
    facets, groups, chans, cap, rows, count_here = sizes
    own_ref, grids = refs[0], refs[1 + count_here]
    order, spots_u, spots_v, turns_real, turns_imag, cells = refs[2 + count_here :]
    pieces = [
        ref.at[pl.ds(n * rows, rows)] for ref in refs[1 : 1 + count_here] for n in range(groups)
    ]
    devices = len(pieces)
    slots = 2 * facets
    lines = cap * chans
    meta_row = 2 * (lines + cap)
    tail = meta_row // 16 * 16
    facet = lax.axis_index("facet")
    group = lax.axis_index("bl")
    chan = lax.axis_index("chan")

    lane = lax.broadcasted_iota(jnp.int32, (1, SU), 1)
    own = own_ref[tail : tail + 16, :].astype(jnp.float32)
    numbers = own[meta_row - tail + 1 : meta_row - tail + 2]
    codes = []
    for d in range(devices):
        meta = pieces[d][tail : tail + 16, :].astype(jnp.float32)
        plane = meta[meta_row - tail : meta_row - tail + 1].astype(jnp.int32) - 1
        set_id = jnp.where(lax.rem(plane, groups) == group, 1, 0)
        code = (d * cap + lane) * slots + 2 * (lax.div(plane, groups) ^ facet) + set_id
        codes.append(jnp.where(plane >= 0, code, -1))
    grids[...] = jnp.zeros_like(grids)

    def number(n):
        return jnp.broadcast_to(numbers[:, n : n + 1], (lines, SU))

    offset_u = number(0)
    offset_v = number(1)
    along_l = number(2) + number(3) + number(4)
    along_m = number(5) + number(6) + number(7)
    line = lax.broadcasted_iota(jnp.int32, (lines, SU), 0)
    channel = (chan * chans + lax.rem(line, chans)).astype(jnp.float32)
    scale = 1.0 + 0.01 * (channel - 0.5 * (CH - 1))

    def spread_lines(place):
        return jnp.concatenate(
            [jnp.broadcast_to(place[k : k + 1], (chans, SU)) for k in range(cap)], axis=0
        )

    for d in range(devices):
        at = d * lines
        wide = pieces[d][...].astype(jnp.float32)
        real = wide[:lines]
        imag = wide[lines : 2 * lines]
        along_u = spread_lines(wide[2 * lines : 2 * lines + cap])
        along_v = spread_lines(wide[2 * lines + cap : 2 * (lines + cap)])
        cosine, sine = cos_sin((1.0 / SU) * (scale * (along_u * along_l + along_v * along_m)))
        spots_u[at : at + lines, :] = ALPHA * (scale * along_u - offset_u)
        spots_v[at : at + lines, :] = ALPHA * (scale * along_v - offset_v)
        turns_real[at : at + lines, :] = real * cosine - imag * sine
        turns_imag[at : at + lines, :] = real * sine + imag * cosine
    last = devices * lines
    for ref in (spots_u, spots_v, turns_real, turns_imag):
        ref[last : last + 8, :] = jnp.zeros((8, SU), jnp.float32)

    count = jnp.int32(0)
    for d in range(devices):
        for k in range(cap):
            code = codes[d][0, k]
            order[count] = code
            count = count + jnp.where(code >= 0, 1, 0)
    for i in range(UNROLL):
        order[count + i] = devices * cap * slots

    cells[...] = ALPHA * lax.broadcasted_iota(jnp.int32, (SU, SU), 0).astype(jnp.float32)

    def profile(spot):
        apart = spot - cells[...]
        return jnp.exp2(-((apart * apart).astype(jnp.bfloat16)))

    def tiled(row):
        return jnp.broadcast_to(row, (16, SU)).astype(jnp.bfloat16)[None]

    def one_block(at):
        code = order[at]
        slot = lax.rem(code, slots)
        base = lax.div(code, slots) * chans
        lefts_real, lefts_imag, rights = [], [], []
        for c in range(chans):
            here = pl.ds(base + c, 1)
            left = profile(spots_u[here, :]).reshape(SU // 16, 16, SU)
            lefts_real.append((left * tiled(turns_real[here, :])).reshape(SU, SU))
            lefts_imag.append((left * tiled(turns_imag[here, :])).reshape(SU, SU))
            rights.append(profile(spots_v[here, :]))
        left = jnp.concatenate(
            [jnp.concatenate(lefts_real, axis=1), jnp.concatenate(lefts_imag, axis=1)], axis=0
        )
        right = jnp.concatenate(rights, axis=1)
        return slot, lax.dot_general(right, left, NT, preferred_element_type=jnp.float32)

    def steps(first, blocks, number):
        def step(k, carry):
            for slot, part in [one_block(first + k * blocks + i) for i in range(blocks)]:
                grids[slot] += part
            return carry

        lax.fori_loop(0, number, step, 0)

    whole = lax.div(count, UNROLL)
    steps(0, UNROLL, whole)
    steps(whole * UNROLL, REST, lax.div(lax.rem(count, UNROLL) + REST - 1, REST))


def local(kernel, operands, shapes, name):
    return pl.pallas_call(
        kernel,
        out_shape=[jax.ShapeDtypeStruct(shape, jnp.bfloat16) for shape in shapes],
        in_specs=[VMEM] * len(operands),
        out_specs=[VMEM] * len(shapes),
        compiler_params=PARAMS,
        cost_estimate=pl.CostEstimate(flops=0, bytes_accessed=400_000, transcendentals=0),
        name=name,
    )(*operands)


def exchange(value, axis, shift):
    return lax.ppermute(value, axis, [(n, n ^ shift) for n in range(lax.axis_size(axis))])


def table_kernel(sizes, norm, packed, ours, theirs, *refs):
    slots, meta_row = sizes
    grids, (mine_ref, other_ref, table_f, total) = refs[:-4], refs[-4:]
    chan = lax.axis_index("chan")
    first = chan == 0

    def parts(table):
        table_f[...] = table
        return table_f[pl.ds(0, SU, stride=2), :], table_f[pl.ds(1, SU, stride=2), :]

    result = jnp.zeros((SU, 2 * SU), jnp.float32)
    for s in range(slots):
        at = slice(2 * SU * s, 2 * SU * (s + 1))
        fetched = ours[at, :].astype(jnp.float32)
        swapped = theirs[at, :].astype(jnp.float32)
        v_real, v_imag = parts(jnp.where(first, swapped, fetched))
        v_side = jnp.concatenate([v_real.T, v_imag.T], axis=1).astype(jnp.bfloat16)
        grid = sum(ref[s] for ref in grids)
        high, low = (
            jnp.concatenate(
                [
                    part,
                    jnp.concatenate([-part[:, SU:], part[:, :SU]], axis=1),
                ],
                axis=0,
            )
            for part in split_bf16(grid)
        )
        half = jnp.dot(v_side, high, preferred_element_type=jnp.float32) + jnp.dot(
            v_side, low, preferred_element_type=jnp.float32
        )
        u_real, u_imag = parts(jnp.where(first, fetched, swapped))
        u_side = jnp.concatenate(
            [
                jnp.concatenate([u_real, u_imag], axis=1),
                jnp.concatenate([-u_imag, u_real], axis=1),
            ],
            axis=0,
        ).astype(jnp.bfloat16)
        high, low = split_bf16(half)
        result = (
            result
            + jnp.dot(high, u_side, preferred_element_type=jnp.float32)
            + jnp.dot(low, u_side, preferred_element_type=jnp.float32)
        )
    result = jnp.concatenate([result[:, :SU].T, result[:, SU:].T], axis=1)
    tail = meta_row // 16 * 16
    wide = packed[tail : tail + 16, :].astype(jnp.float32)
    at = meta_row - tail + 2
    gain = (wide[at : at + 2] + wide[at + 2 : at + 4]) + wide[at + 4 : at + 6]
    gain_u = jnp.broadcast_to(gain[0:1], (SU, SU)).T
    gains = gain_u * gain[1:2] * norm
    total[...] = result * jnp.concatenate([gains, gains], axis=1)
    half_rows = mine_ref.shape[0]
    mine_ref[...] = total[pl.ds(pl.multiple_of(chan * half_rows, half_rows), half_rows), :]
    other_ref[...] = total[pl.ds(pl.multiple_of((1 - chan) * half_rows, half_rows), half_rows), :]


def body(
    visibilities, coords, plane_index, block_group, offsets, facet_centre, tables, antenna_gain
):
    facets = lax.axis_size("facet")
    groups = lax.axis_size("bl")
    chan_count = lax.axis_size("chan")
    held, chans = visibilities.shape[:2]
    devices = facets * groups
    slots = 2 * facets
    cap = max(2, 2 * held // groups)
    meta_row = 2 * cap * (chans + 1)
    rows = -(-(meta_row + 8) // 16) * 16
    half_rows = SU // chan_count
    norm = SU / math.sqrt(visibilities.shape[3] * held * facets * CH)

    own_table = tables.reshape(2, 2 * SU, SU)
    *pieces, half = pl.pallas_call(
        functools.partial(sort_kernel, (groups, held, chans, cap, rows)),
        out_shape=[
            jax.ShapeDtypeStruct((rows + (2 * SU if shift == 1 else 0), SU), jnp.bfloat16)
            for shift in range(groups)
        ]
        + [jax.ShapeDtypeStruct((2 * SU, SU), jnp.bfloat16)],
        in_specs=[HBM] * 8,
        out_specs=[VMEM] * (groups + 1),
        scratch_shapes=[
            pltpu.SMEM((1, held), jnp.int32),
            pltpu.SMEM((1, held), jnp.int32),
            pltpu.VMEM((held * 2 * chans, SU), jnp.bfloat16),
            pltpu.VMEM((held * 2, SU), jnp.bfloat16),
            pltpu.SMEM((facets, 2, groups), jnp.int32),
            pltpu.SMEM((2, facets), jnp.float32),
            pltpu.VMEM((1, 2, SU), jnp.float32),
            pltpu.VMEM((held * 2 * chans, SU), jnp.float32),
            pltpu.VMEM((held * 2, SU), jnp.float32),
            pltpu.VMEM((groups, rows, SU), jnp.float32),
            pltpu.SMEM((groups,), jnp.int32),
            pltpu.SemaphoreType.DMA((8,)),
        ],
        compiler_params=PARAMS,
        cost_estimate=pl.CostEstimate(flops=100_000, bytes_accessed=100_000, transcendentals=0),
        name="sort_blocks",
    )(
        *(
            pltpu.with_memory_space_constraint(operand, pltpu.HBM)
            for operand in (
                plane_index.reshape(1, held),
                block_group.T,
                visibilities.reshape(held * 2 * chans, SU),
                coords.reshape(held * 2, SU),
                offsets.transpose(0, 2, 1),
                facet_centre.T,
                antenna_gain,
                own_table,
            )
        )
    )
    arrived = [
        lax.ppermute(pieces[shift], "bl", [(g, (g + shift) % groups) for g in range(groups)])
        for shift in [1, *range(groups - 1, 1, -1)]
    ]
    vis_rows = groups * rows
    last_own = exchange(own_table, "facet", facets - 1)
    arrived, last_own = lax.optimization_barrier((arrived, last_own))
    joined, short = local(
        functools.partial(join_kernel, rows),
        [half, pieces[0], *arrived],
        [(vis_rows + 4 * SU, SU), (vis_rows + 2 * SU, SU)],
        "join",
    )
    blocks = (
        [joined]
        + [exchange(joined, "facet", shift) for shift in range(1, facets - 1)]
        + [exchange(short, "facet", facets - 1)]
    )

    def grid(some):
        lines = len(some) * groups * cap
        return pl.pallas_call(
            functools.partial(grid_kernel, (facets, groups, chans, cap, rows, len(some))),
            out_shape=jax.ShapeDtypeStruct((slots, SU, 2 * SU), jnp.float32),
            in_specs=[VMEM] * (1 + len(some)),
            out_specs=VMEM,
            scratch_shapes=[
                pltpu.SMEM((lines + UNROLL,), jnp.int32),
            ]
            + [pltpu.VMEM((lines * chans + 8, SU), jnp.float32)] * 4
            + [pltpu.VMEM((SU, SU), jnp.float32)],
            compiler_params=PARAMS,
            cost_estimate=pl.CostEstimate(
                flops=len(some) * 1_000_000_000,
                bytes_accessed=1_000_000,
                transcendentals=len(some) * 1_000_000,
            ),
            name="grid",
        )(joined, *some)

    grids = [grid(blocks[:1]), grid(blocks[-1:])]
    blocks, grids = lax.optimization_barrier((blocks, grids))
    (fetched,) = local(
        functools.partial(collect_kernel, vis_rows),
        [*blocks, last_own],
        [(facets * 4 * SU, SU)],
        "collect",
    )
    swapped = lax.ppermute(fetched, "chan", [(c, 1 - c) for c in range(chan_count)])
    grids.append(grid(blocks[1:-1]))
    mine, other = pl.pallas_call(
        functools.partial(table_kernel, (slots, meta_row), norm),
        out_shape=[jax.ShapeDtypeStruct((half_rows, 2 * SU), jnp.float32)] * 2,
        in_specs=[VMEM] * (3 + len(grids)),
        out_specs=[VMEM, VMEM],
        scratch_shapes=[
            pltpu.VMEM((2 * SU, SU), jnp.float32),
            pltpu.VMEM((SU, 2 * SU), jnp.float32),
        ],
        compiler_params=PARAMS,
        cost_estimate=pl.CostEstimate(
            flops=1_000_000_000, bytes_accessed=2_000_000, transcendentals=0
        ),
        name="apply_tables",
    )(joined, fetched, swapped, *grids)
    summand = lax.ppermute(other, "chan", [(c, 1 - c) for c in range(chan_count)])
    return (mine + summand).reshape(1, 1, half_rows, 2, SU)


def solution(mesh):
    in_specs = (
        P(("facet", "bl"), "chan", None, None),
        P(("facet", "bl"), None, None),
        P(("facet", "bl")),
        P(("facet", "bl"), None),
        P(),
        P(),
        P(("facet", "bl"), None, None, None, None),
        P("bl", None, None),
    )
    out_specs = P("facet", "bl", "chan", None, None)
    return jax.shard_map(body, mesh=mesh, in_specs=in_specs, out_specs=out_specs, check_vma=False)
```

```python
import functools
import math

import jax
import jax.numpy as jnp
from jax import lax
from jax.experimental import pallas as pl
from jax.experimental.pallas import tpu as pltpu
from jax.sharding import PartitionSpec as P

SU = 128
CH = 8
KERNEL_SPREAD = 1.5
ALPHA = math.sqrt(math.log2(math.e) / (2.0 * KERNEL_SPREAD * KERNEL_SPREAD))
UNROLL = 4
REST = 2
NT = (((1,), (1,)), ((), ()))
VMEM = pl.BlockSpec(memory_space=pltpu.VMEM)
HBM = pl.BlockSpec(memory_space=pltpu.HBM)
PARAMS = pltpu.CompilerParams(vmem_limit_bytes=32 * 1024 * 1024)


def cos_sin(turns):
    quarter = jnp.floor(4.0 * turns + 0.5)
    angle = (2.0 * math.pi) * (turns - 0.25 * quarter)
    sq = angle * angle
    sine = angle * (
        1.0 + sq * (-1.0 / 6 + sq * (1.0 / 120 + sq * (-1.0 / 5040 + sq * (1.0 / 362880))))
    )
    cosine = 1.0 + sq * (
        -0.5 + sq * (1.0 / 24 + sq * (-1.0 / 720 + sq * (1.0 / 40320 + sq * (-1.0 / 3628800))))
    )
    turn = quarter.astype(jnp.int32) & 3
    odd = (turn & 1) == 1
    cos_out = jnp.where(odd, sine, cosine)
    sin_out = jnp.where(odd, cosine, sine)
    cos_out = jnp.where((turn == 1) | (turn == 2), -cos_out, cos_out)
    sin_out = jnp.where(turn >= 2, -sin_out, sin_out)
    return cos_out, sin_out


def split_bf16(x):
    high = x.astype(jnp.bfloat16)
    low = (x - high.astype(jnp.float32)).astype(jnp.bfloat16)
    return high, low


def three_parts(x):
    parts = []
    for _ in range(3):
        part = x.astype(jnp.bfloat16)
        x = x - part.astype(jnp.float32)
        parts.append(part.astype(jnp.float32))
    return parts


def sort_kernel(sizes, *refs):
    groups, held, chans, cap, rows = sizes
    table_hbm, outs, half = refs[7], refs[8 : 8 + groups], refs[8 + groups]
    targets = refs[9 + groups : 16 + groups]
    plane_ref, group_ref, samples_b, place_b, offsets_ref, centre_ref, gain_ref = targets
    samples, place, sorted_, filled, table_b, table_f, sems = refs[16 + groups :]
    facet = lax.axis_index("facet")
    copies = [
        pltpu.make_async_copy(source, target, sems.at[n])
        for n, (source, target) in enumerate(zip(refs[:7], targets))
    ]
    table = pltpu.make_async_copy(table_hbm.at[lax.axis_index("chan")], table_b, sems.at[7])
    for copy in copies + [table]:
        copy.start()
    sorted_[...] = jnp.zeros_like(sorted_)
    for g in range(groups):
        filled[g] = 0
    for copy in copies:
        copy.wait()
    samples[...] = samples_b[...].astype(jnp.float32)
    place[...] = place_b[...].astype(jnp.float32)
    lane = lax.broadcasted_iota(jnp.int32, (1, SU), 1)
    meta = 2 * cap * (chans + 1)
    centre = [
        part
        for axis in range(2)
        for part in three_parts(jnp.full((1, SU), centre_ref[axis, facet], jnp.float32))
    ]
    gains = three_parts(gain_ref[0])
    for g in range(groups):
        numbers = jnp.zeros((1, SU), jnp.float32)
        for axis in range(2):
            offset = offsets_ref[facet, axis, g].astype(jnp.float32)
            numbers = jnp.where(lane == axis, offset, numbers)
        for n, part in enumerate(centre):
            numbers = jnp.where(lane == 2 + n, part, numbers)
        sorted_[g, meta + 1 : meta + 2, :] = numbers
        for n, part in enumerate(gains):
            sorted_[g, meta + 2 + 2 * n : meta + 4 + 2 * n, :] = part
    for i in range(held):
        g = group_ref[0, i]
        k = filled[g]
        filled[g] = k + 1
        for part in range(2):
            at = part * cap * chans + k * chans
            sorted_[g, pl.ds(at, chans), :] = samples[pl.ds(2 * chans * i + part, chans, stride=2), :]
            at = 2 * cap * chans + part * cap + k
            sorted_[g, pl.ds(at, 1), :] = place[2 * i + part : 2 * i + part + 1, :]
        sorted_[g, meta : meta + 1, :] += jnp.where(
            lane == k, (plane_ref[0, i] + 1).astype(jnp.float32), 0.0
        )
    for shift, out_ref in enumerate(outs):
        g = lax.rem(lax.axis_index("bl") + shift, groups)
        out_ref[:rows, :] = sorted_[g].astype(jnp.bfloat16)
    table.wait()
    table_f[...] = table_b[...].astype(jnp.float32)
    for part in range(2):
        matrix = table_f[pl.ds(part, SU, stride=2), :]
        matrix = jnp.where(lax.axis_index("chan") == 0, matrix, matrix.T).astype(jnp.bfloat16)
        half[part * SU : (part + 1) * SU, :] = matrix
        outs[1][rows + part * SU : rows + (part + 1) * SU, :] = matrix


def join_kernel(rows, half, *refs):
    *pieces, joined = refs
    for n, ref in enumerate(pieces):
        joined[n * rows : (n + 1) * rows, :] = ref[:rows, :]
    at = len(pieces) * rows
    joined[at : at + 2 * SU, :] = half[...]
    joined[at + 2 * SU :, :] = pieces[1][rows:, :]


def collect_kernel(skip, *refs):
    for n, ref in enumerate(refs[:-1]):
        refs[-1][n * 4 * SU : (n + 1) * 4 * SU, :] = ref[skip:, :]


def grid_kernel(sizes, *refs):
    facets, groups, chans, cap, rows, count_here = sizes
    own_ref, grids = refs[0], refs[1 + count_here]
    order, spots_u, spots_v, turns_real, turns_imag, cells = refs[2 + count_here :]
    pieces = [
        ref.at[pl.ds(n * rows, rows)] for ref in refs[1 : 1 + count_here] for n in range(groups)
    ]
    devices = len(pieces)
    slots = 2 * facets
    lines = cap * chans
    meta_row = 2 * (lines + cap)
    tail = meta_row // 16 * 16
    facet = lax.axis_index("facet")
    group = lax.axis_index("bl")
    chan = lax.axis_index("chan")

    lane = lax.broadcasted_iota(jnp.int32, (1, SU), 1)
    own = own_ref[tail : tail + 16, :].astype(jnp.float32)
    numbers = own[meta_row - tail + 1 : meta_row - tail + 2]
    codes = []
    for d in range(devices):
        meta = pieces[d][tail : tail + 16, :].astype(jnp.float32)
        plane = meta[meta_row - tail : meta_row - tail + 1].astype(jnp.int32) - 1
        set_id = jnp.where(lax.rem(plane, groups) == group, 0, 1)
        code = (d * cap + lane) * slots + 2 * (lax.div(plane, groups) ^ facet) + set_id
        codes.append(jnp.where(plane >= 0, code, -1))
    grids[...] = jnp.zeros_like(grids)

    def number(n):
        return jnp.broadcast_to(numbers[:, n : n + 1], (lines, SU))

    offset_u = number(0)
    offset_v = number(1)
    along_l = number(2) + number(3) + number(4)
    along_m = number(5) + number(6) + number(7)
    line = lax.broadcasted_iota(jnp.int32, (lines, SU), 0)
    channel = (chan * chans + lax.rem(line, chans)).astype(jnp.float32)
    scale = 1.0 + 0.01 * (channel - 0.5 * (CH - 1))

    def spread_lines(place):
        return jnp.concatenate(
            [jnp.broadcast_to(place[k : k + 1], (chans, SU)) for k in range(cap)], axis=0
        )

    for d in range(devices):
        at = d * lines
        wide = pieces[d][...].astype(jnp.float32)
        real = wide[:lines]
        imag = wide[lines : 2 * lines]
        along_u = spread_lines(wide[2 * lines : 2 * lines + cap])
        along_v = spread_lines(wide[2 * lines + cap : 2 * (lines + cap)])
        cosine, sine = cos_sin((1.0 / SU) * (scale * (along_u * along_l + along_v * along_m)))
        spots_u[at : at + lines, :] = ALPHA * (scale * along_u - offset_u)
        spots_v[at : at + lines, :] = ALPHA * (scale * along_v - offset_v)
        turns_real[at : at + lines, :] = real * cosine - imag * sine
        turns_imag[at : at + lines, :] = real * sine + imag * cosine
    last = devices * lines
    for ref in (spots_u, spots_v, turns_real, turns_imag):
        ref[last : last + 8, :] = jnp.zeros((8, SU), jnp.float32)

    count = jnp.int32(0)
    for d in range(devices):
        for k in range(cap):
            code = codes[d][0, k]
            order[count] = code
            count = count + jnp.where(code >= 0, 1, 0)
    for i in range(UNROLL):
        order[count + i] = devices * cap * slots

    cells[...] = ALPHA * lax.broadcasted_iota(jnp.int32, (SU, SU), 0).astype(jnp.float32)

    def profile(spot):
        apart = spot - cells[...]
        return jnp.exp2(-((apart * apart).astype(jnp.bfloat16)))

    def tiled(row):
        return jnp.broadcast_to(row, (16, SU)).astype(jnp.bfloat16)[None]

    def one_block(at):
        code = order[at]
        slot = lax.rem(code, slots)
        base = lax.div(code, slots) * chans
        lefts_real, lefts_imag, rights = [], [], []
        for c in range(chans):
            here = pl.ds(base + c, 1)
            left = profile(spots_u[here, :]).reshape(SU // 16, 16, SU)
            lefts_real.append((left * tiled(turns_real[here, :])).reshape(SU, SU))
            lefts_imag.append((left * tiled(turns_imag[here, :])).reshape(SU, SU))
            rights.append(profile(spots_v[here, :]))
        left = jnp.concatenate(
            [jnp.concatenate(lefts_real, axis=1), jnp.concatenate(lefts_imag, axis=1)], axis=0
        )
        right = jnp.concatenate(rights, axis=1)
        return slot, lax.dot_general(right, left, NT, preferred_element_type=jnp.float32)

    def steps(first, blocks, number):
        def step(k, carry):
            for slot, part in [one_block(first + k * blocks + i) for i in range(blocks)]:
                grids[slot] += part
            return carry

        lax.fori_loop(0, number, step, 0)

    whole = lax.div(count, UNROLL)
    steps(0, UNROLL, whole)
    steps(whole * UNROLL, REST, lax.div(lax.rem(count, UNROLL) + REST - 1, REST))


def local(kernel, operands, shape, name):
    return pl.pallas_call(
        kernel,
        out_shape=jax.ShapeDtypeStruct(shape, jnp.bfloat16),
        in_specs=[VMEM] * len(operands),
        out_specs=VMEM,
        compiler_params=PARAMS,
        cost_estimate=pl.CostEstimate(flops=0, bytes_accessed=400_000, transcendentals=0),
        name=name,
    )(*operands)


def exchange(value, axis, shift):
    return lax.ppermute(value, axis, [(n, n ^ shift) for n in range(lax.axis_size(axis))])


def table_kernel(sizes, norm, packed, ours, theirs, *refs):
    slots, meta_row = sizes
    grids, (mine_ref, other_ref, total) = refs[:-3], refs[-3:]
    chan = lax.axis_index("chan")
    first = chan == 0

    result = jnp.zeros((SU, 2 * SU), jnp.float32)
    for s in range(slots):
        at = slice(2 * SU * s, 2 * SU * (s + 1))
        fetched = ours[at, :]
        swapped = theirs[at, :]
        v_table = jnp.where(first, swapped, fetched)
        v_side = jnp.concatenate([v_table[:SU], v_table[SU:]], axis=1)
        grid = sum(ref[s] for ref in grids)
        high, low = (
            jnp.concatenate(
                [
                    part,
                    jnp.concatenate([-part[:, SU:], part[:, :SU]], axis=1),
                ],
                axis=0,
            )
            for part in split_bf16(grid)
        )
        half = jnp.dot(v_side, high, preferred_element_type=jnp.float32) + jnp.dot(
            v_side, low, preferred_element_type=jnp.float32
        )
        u_table = jnp.where(first, fetched, swapped)
        u_side = jnp.concatenate(
            [
                jnp.concatenate([u_table[:SU], u_table[SU:]], axis=1),
                jnp.concatenate([-u_table[SU:], u_table[:SU]], axis=1),
            ],
            axis=0,
        )
        high, low = split_bf16(half)
        result = (
            result
            + jnp.dot(high, u_side, preferred_element_type=jnp.float32)
            + jnp.dot(low, u_side, preferred_element_type=jnp.float32)
        )
    result = jnp.concatenate([result[:, :SU].T, result[:, SU:].T], axis=1)
    tail = meta_row // 16 * 16
    wide = packed[tail : tail + 16, :].astype(jnp.float32)
    at = meta_row - tail + 2
    gain = (wide[at : at + 2] + wide[at + 2 : at + 4]) + wide[at + 4 : at + 6]
    gain_u = jnp.broadcast_to(gain[0:1], (SU, SU)).T
    gains = gain_u * gain[1:2] * norm
    total[...] = result * jnp.concatenate([gains, gains], axis=1)
    half_rows = mine_ref.shape[0]
    mine_ref[...] = total[pl.ds(pl.multiple_of(chan * half_rows, half_rows), half_rows), :]
    other_ref[...] = total[pl.ds(pl.multiple_of((1 - chan) * half_rows, half_rows), half_rows), :]


def body(
    visibilities, coords, plane_index, block_group, offsets, facet_centre, tables, antenna_gain
):
    facets = lax.axis_size("facet")
    groups = lax.axis_size("bl")
    chan_count = lax.axis_size("chan")
    held, chans = visibilities.shape[:2]
    devices = facets * groups
    slots = 2 * facets
    cap = max(2, 2 * held // groups)
    meta_row = 2 * cap * (chans + 1)
    rows = -(-(meta_row + 8) // 16) * 16
    half_rows = SU // chan_count
    norm = SU / math.sqrt(visibilities.shape[3] * held * facets * CH)

    own_table = tables.reshape(2, 2 * SU, SU)
    *pieces, half = pl.pallas_call(
        functools.partial(sort_kernel, (groups, held, chans, cap, rows)),
        out_shape=[
            jax.ShapeDtypeStruct((rows + (2 * SU if shift == 1 else 0), SU), jnp.bfloat16)
            for shift in range(groups)
        ]
        + [jax.ShapeDtypeStruct((2 * SU, SU), jnp.bfloat16)],
        in_specs=[HBM] * 8,
        out_specs=[VMEM] * (groups + 1),
        scratch_shapes=[
            pltpu.SMEM((1, held), jnp.int32),
            pltpu.SMEM((1, held), jnp.int32),
            pltpu.VMEM((held * 2 * chans, SU), jnp.bfloat16),
            pltpu.VMEM((held * 2, SU), jnp.bfloat16),
            pltpu.SMEM((facets, 2, groups), jnp.int32),
            pltpu.SMEM((2, facets), jnp.float32),
            pltpu.VMEM((1, 2, SU), jnp.float32),
            pltpu.VMEM((held * 2 * chans, SU), jnp.float32),
            pltpu.VMEM((held * 2, SU), jnp.float32),
            pltpu.VMEM((groups, rows, SU), jnp.float32),
            pltpu.SMEM((groups,), jnp.int32),
            pltpu.VMEM((2 * SU, SU), jnp.bfloat16),
            pltpu.VMEM((2 * SU, SU), jnp.float32),
            pltpu.SemaphoreType.DMA((8,)),
        ],
        compiler_params=PARAMS,
        cost_estimate=pl.CostEstimate(flops=100_000, bytes_accessed=100_000, transcendentals=0),
        name="sort_blocks",
    )(
        *(
            pltpu.with_memory_space_constraint(operand, pltpu.HBM)
            for operand in (
                plane_index.reshape(1, held),
                block_group.T,
                visibilities.reshape(held * 2 * chans, SU),
                coords.reshape(held * 2, SU),
                offsets.transpose(0, 2, 1),
                facet_centre.T,
                antenna_gain,
                own_table,
            )
        )
    )
    arrived = [
        lax.ppermute(pieces[shift], "bl", [(g, (g + shift) % groups) for g in range(groups)])
        for shift in [1, *range(groups - 1, 1, -1)]
    ]
    vis_rows = groups * rows
    joined = local(
        functools.partial(join_kernel, rows),
        [half, pieces[0], *arrived],
        (vis_rows + 4 * SU, SU),
        "join",
    )
    blocks = [joined] + [exchange(joined, "facet", shift) for shift in range(1, facets)]
    def grid(some):
        lines = len(some) * groups * cap
        return pl.pallas_call(
            functools.partial(grid_kernel, (facets, groups, chans, cap, rows, len(some))),
            out_shape=jax.ShapeDtypeStruct((slots, SU, 2 * SU), jnp.float32),
            in_specs=[VMEM] * (1 + len(some)),
            out_specs=VMEM,
            scratch_shapes=[
                pltpu.SMEM((lines + UNROLL,), jnp.int32),
            ]
            + [pltpu.VMEM((lines * chans + 8, SU), jnp.float32)] * 4
            + [pltpu.VMEM((SU, SU), jnp.float32)],
            compiler_params=PARAMS,
            cost_estimate=pl.CostEstimate(
                flops=len(some) * 1_000_000_000,
                bytes_accessed=1_000_000,
                transcendentals=len(some) * 1_000_000,
            ),
            name="grid",
        )(joined, *some)

    grids = [grid(blocks[:1]), grid(blocks[-1:])]
    blocks, grids = lax.optimization_barrier((blocks, grids))
    fetched = local(
        functools.partial(collect_kernel, vis_rows), blocks, (facets * 4 * SU, SU), "collect"
    )
    swapped = lax.ppermute(fetched, "chan", [(c, 1 - c) for c in range(chan_count)])
    grids.append(grid(blocks[1:-1]))
    mine, other = pl.pallas_call(
        functools.partial(table_kernel, (slots, meta_row), norm),
        out_shape=[jax.ShapeDtypeStruct((half_rows, 2 * SU), jnp.float32)] * 2,
        in_specs=[VMEM] * (3 + len(grids)),
        out_specs=[VMEM, VMEM],
        scratch_shapes=[
            pltpu.VMEM((SU, 2 * SU), jnp.float32),
        ],
        compiler_params=PARAMS,
        cost_estimate=pl.CostEstimate(
            flops=1_000_000_000, bytes_accessed=2_000_000, transcendentals=0
        ),
        name="apply_tables",
    )(joined, fetched, swapped, *grids)
    summand = lax.ppermute(other, "chan", [(c, 1 - c) for c in range(chan_count)])
    return (mine + summand).reshape(1, 1, half_rows, 2, SU)


def solution(mesh):
    in_specs = (
        P(("facet", "bl"), "chan", None, None),
        P(("facet", "bl"), None, None),
        P(("facet", "bl")),
        P(("facet", "bl"), None),
        P(),
        P(),
        P(("facet", "bl"), None, None, None, None),
        P("bl", None, None),
    )
    out_specs = P("facet", "bl", "chan", None, None)
    return jax.shard_map(body, mesh=mesh, in_specs=in_specs, out_specs=out_specs, check_vma=False)
```

```python
import functools
import math

import jax
import jax.numpy as jnp
from jax import lax
from jax.experimental import pallas as pl
from jax.experimental.pallas import tpu as pltpu
from jax.sharding import PartitionSpec as P

SU = 128
CH = 8
KERNEL_SPREAD = 1.5
ALPHA = math.sqrt(math.log2(math.e) / (2.0 * KERNEL_SPREAD * KERNEL_SPREAD))
UNROLL = 4
REST = 2
NT = (((1,), (1,)), ((), ()))
VMEM = pl.BlockSpec(memory_space=pltpu.VMEM)
HBM = pl.BlockSpec(memory_space=pltpu.HBM)
PARAMS = pltpu.CompilerParams(vmem_limit_bytes=32 * 1024 * 1024)


def cos_sin(turns):
    quarter = jnp.floor(4.0 * turns + 0.5)
    angle = (2.0 * math.pi) * (turns - 0.25 * quarter)
    sq = angle * angle
    sine = angle * (
        1.0 + sq * (-1.0 / 6 + sq * (1.0 / 120 + sq * (-1.0 / 5040 + sq * (1.0 / 362880))))
    )
    cosine = 1.0 + sq * (
        -0.5 + sq * (1.0 / 24 + sq * (-1.0 / 720 + sq * (1.0 / 40320 + sq * (-1.0 / 3628800))))
    )
    turn = quarter.astype(jnp.int32) & 3
    odd = (turn & 1) == 1
    cos_out = jnp.where(odd, sine, cosine)
    sin_out = jnp.where(odd, cosine, sine)
    cos_out = jnp.where((turn == 1) | (turn == 2), -cos_out, cos_out)
    sin_out = jnp.where(turn >= 2, -sin_out, sin_out)
    return cos_out, sin_out


def split_bf16(x):
    high = x.astype(jnp.bfloat16)
    low = (x - high.astype(jnp.float32)).astype(jnp.bfloat16)
    return high, low


def three_parts(x):
    parts = []
    for _ in range(3):
        part = x.astype(jnp.bfloat16)
        x = x - part.astype(jnp.float32)
        parts.append(part.astype(jnp.float32))
    return parts


def sort_kernel(sizes, *refs):
    groups, held, chans, cap, rows = sizes
    table_hbm, outs, half = refs[7], refs[8 : 8 + groups], refs[8 + groups]
    targets = refs[9 + groups : 16 + groups]
    plane_ref, group_ref, samples_b, place_b, offsets_ref, centre_ref, gain_ref = targets
    samples, place, sorted_, filled, table_b, table_f, sems = refs[16 + groups :]
    facet = lax.axis_index("facet")
    copies = [
        pltpu.make_async_copy(source, target, sems.at[n])
        for n, (source, target) in enumerate(zip(refs[:7], targets))
    ]
    table = pltpu.make_async_copy(table_hbm.at[lax.axis_index("chan")], table_b, sems.at[7])
    for copy in copies + [table]:
        copy.start()
    sorted_[...] = jnp.zeros_like(sorted_)
    for g in range(groups):
        filled[g] = 0
    for copy in copies:
        copy.wait()
    samples[...] = samples_b[...].astype(jnp.float32)
    place[...] = place_b[...].astype(jnp.float32)
    lane = lax.broadcasted_iota(jnp.int32, (1, SU), 1)
    meta = 2 * cap * (chans + 1)
    centre = [
        part
        for axis in range(2)
        for part in three_parts(jnp.full((1, SU), centre_ref[axis, facet], jnp.float32))
    ]
    gains = three_parts(gain_ref[0])
    for g in range(groups):
        numbers = jnp.zeros((1, SU), jnp.float32)
        for axis in range(2):
            offset = offsets_ref[facet, axis, g].astype(jnp.float32)
            numbers = jnp.where(lane == axis, offset, numbers)
        for n, part in enumerate(centre):
            numbers = jnp.where(lane == 2 + n, part, numbers)
        sorted_[g, meta + 1 : meta + 2, :] = numbers
        for n, part in enumerate(gains):
            sorted_[g, meta + 2 + 2 * n : meta + 4 + 2 * n, :] = part
    for i in range(held):
        g = group_ref[0, i]
        k = filled[g]
        filled[g] = k + 1
        for part in range(2):
            at = part * cap * chans + k * chans
            sorted_[g, pl.ds(at, chans), :] = samples[pl.ds(2 * chans * i + part, chans, stride=2), :]
            at = 2 * cap * chans + part * cap + k
            sorted_[g, pl.ds(at, 1), :] = place[2 * i + part : 2 * i + part + 1, :]
        sorted_[g, meta : meta + 1, :] += jnp.where(
            lane == k, (plane_ref[0, i] + 1).astype(jnp.float32), 0.0
        )
    for shift, out_ref in enumerate(outs):
        g = lax.rem(lax.axis_index("bl") + shift, groups)
        out_ref[:rows, :] = sorted_[g].astype(jnp.bfloat16)
    table.wait()
    table_f[...] = table_b[...].astype(jnp.float32)
    for part in range(2):
        matrix = table_f[pl.ds(part, SU, stride=2), :]
        matrix = jnp.where(lax.axis_index("chan") == 0, matrix, matrix.T).astype(jnp.bfloat16)
        half[part * SU : (part + 1) * SU, :] = matrix
        outs[1][rows + part * SU : rows + (part + 1) * SU, :] = matrix


def join_kernel(rows, half, *refs):
    *pieces, joined = refs
    for n, ref in enumerate(pieces):
        joined[n * rows : (n + 1) * rows, :] = ref[:rows, :]
    at = len(pieces) * rows
    joined[at : at + 2 * SU, :] = half[...]
    joined[at + 2 * SU :, :] = pieces[1][rows:, :]


def collect_kernel(skip, *refs):
    for n, ref in enumerate(refs[:-1]):
        refs[-1][n * 4 * SU : (n + 1) * 4 * SU, :] = ref[skip:, :]


def grid_kernel(sizes, *refs):
    facets, groups, chans, cap, rows, count_here = sizes
    own_ref = refs[0]
    before = refs[1 + count_here : -7]
    grids = refs[-7]
    order, spots_u, spots_v, turns_real, turns_imag, cells = refs[-6:]
    pieces = [
        ref.at[pl.ds(n * rows, rows)] for ref in refs[1 : 1 + count_here] for n in range(groups)
    ]
    devices = len(pieces)
    slots = 2 * facets
    lines = cap * chans
    meta_row = 2 * (lines + cap)
    tail = meta_row // 16 * 16
    facet = lax.axis_index("facet")
    group = lax.axis_index("bl")
    chan = lax.axis_index("chan")

    lane = lax.broadcasted_iota(jnp.int32, (1, SU), 1)
    own = own_ref[tail : tail + 16, :].astype(jnp.float32)
    numbers = own[meta_row - tail + 1 : meta_row - tail + 2]
    codes = []
    for d in range(devices):
        meta = pieces[d][tail : tail + 16, :].astype(jnp.float32)
        plane = meta[meta_row - tail : meta_row - tail + 1].astype(jnp.int32) - 1
        set_id = jnp.where(lax.rem(plane, groups) == group, 0, 1)
        code = (d * cap + lane) * slots + 2 * (lax.div(plane, groups) ^ facet) + set_id
        codes.append(jnp.where(plane >= 0, code, -1))
    grids[...] = before[0][...] if before else jnp.zeros_like(grids)

    def number(n):
        return jnp.broadcast_to(numbers[:, n : n + 1], (lines, SU))

    offset_u = number(0)
    offset_v = number(1)
    along_l = number(2) + number(3) + number(4)
    along_m = number(5) + number(6) + number(7)
    line = lax.broadcasted_iota(jnp.int32, (lines, SU), 0)
    channel = (chan * chans + lax.rem(line, chans)).astype(jnp.float32)
    scale = 1.0 + 0.01 * (channel - 0.5 * (CH - 1))

    def spread_lines(place):
        return jnp.concatenate(
            [jnp.broadcast_to(place[k : k + 1], (chans, SU)) for k in range(cap)], axis=0
        )

    for d in range(devices):
        at = d * lines
        wide = pieces[d][...].astype(jnp.float32)
        real = wide[:lines]
        imag = wide[lines : 2 * lines]
        along_u = spread_lines(wide[2 * lines : 2 * lines + cap])
        along_v = spread_lines(wide[2 * lines + cap : 2 * (lines + cap)])
        cosine, sine = cos_sin((1.0 / SU) * (scale * (along_u * along_l + along_v * along_m)))
        spots_u[at : at + lines, :] = ALPHA * (scale * along_u - offset_u)
        spots_v[at : at + lines, :] = ALPHA * (scale * along_v - offset_v)
        turns_real[at : at + lines, :] = real * cosine - imag * sine
        turns_imag[at : at + lines, :] = real * sine + imag * cosine
    last = devices * lines
    for ref in (spots_u, spots_v, turns_real, turns_imag):
        ref[last : last + 8, :] = jnp.zeros((8, SU), jnp.float32)

    count = jnp.int32(0)
    for d in range(devices):
        for k in range(cap):
            code = codes[d][0, k]
            order[count] = code
            count = count + jnp.where(code >= 0, 1, 0)
    for i in range(UNROLL):
        order[count + i] = devices * cap * slots

    cells[...] = ALPHA * lax.broadcasted_iota(jnp.int32, (SU, SU), 0).astype(jnp.float32)

    def profile(spot):
        apart = spot - cells[...]
        return jnp.exp2(-((apart * apart).astype(jnp.bfloat16)))

    def tiled(row):
        return jnp.broadcast_to(row, (16, SU)).astype(jnp.bfloat16)[None]

    def one_block(at):
        code = order[at]
        slot = lax.rem(code, slots)
        base = lax.div(code, slots) * chans
        lefts_real, lefts_imag, rights = [], [], []
        for c in range(chans):
            here = pl.ds(base + c, 1)
            left = profile(spots_u[here, :]).reshape(SU // 16, 16, SU)
            lefts_real.append((left * tiled(turns_real[here, :])).reshape(SU, SU))
            lefts_imag.append((left * tiled(turns_imag[here, :])).reshape(SU, SU))
            rights.append(profile(spots_v[here, :]))
        left = jnp.concatenate(
            [jnp.concatenate(lefts_real, axis=1), jnp.concatenate(lefts_imag, axis=1)], axis=0
        )
        right = jnp.concatenate(rights, axis=1)
        return slot, lax.dot_general(right, left, NT, preferred_element_type=jnp.float32)

    def steps(first, blocks, number):
        def step(k, carry):
            for slot, part in [one_block(first + k * blocks + i) for i in range(blocks)]:
                grids[slot] += part
            return carry

        lax.fori_loop(0, number, step, 0)

    whole = lax.div(count, UNROLL)
    steps(0, UNROLL, whole)
    steps(whole * UNROLL, REST, lax.div(lax.rem(count, UNROLL) + REST - 1, REST))


def local(kernel, operands, shape, name):
    return pl.pallas_call(
        kernel,
        out_shape=jax.ShapeDtypeStruct(shape, jnp.bfloat16),
        in_specs=[VMEM] * len(operands),
        out_specs=VMEM,
        compiler_params=PARAMS,
        cost_estimate=pl.CostEstimate(flops=0, bytes_accessed=400_000, transcendentals=0),
        name=name,
    )(*operands)


def exchange(value, axis, shift):
    return lax.ppermute(value, axis, [(n, n ^ shift) for n in range(lax.axis_size(axis))])


def table_kernel(sizes, norm, packed, ours, theirs, grids, mine_ref, other_ref, total):
    slots, meta_row = sizes
    chan = lax.axis_index("chan")
    first = chan == 0

    result = jnp.zeros((SU, 2 * SU), jnp.float32)
    for s in range(slots):
        at = slice(2 * SU * s, 2 * SU * (s + 1))
        fetched = ours[at, :]
        swapped = theirs[at, :]
        v_table = jnp.where(first, swapped, fetched)
        v_side = jnp.concatenate([v_table[:SU], v_table[SU:]], axis=1)
        high, low = (
            jnp.concatenate(
                [
                    part,
                    jnp.concatenate([-part[:, SU:], part[:, :SU]], axis=1),
                ],
                axis=0,
            )
            for part in split_bf16(grids[s])
        )
        half = jnp.dot(v_side, high, preferred_element_type=jnp.float32) + jnp.dot(
            v_side, low, preferred_element_type=jnp.float32
        )
        u_table = jnp.where(first, fetched, swapped)
        u_side = jnp.concatenate(
            [
                jnp.concatenate([u_table[:SU], u_table[SU:]], axis=1),
                jnp.concatenate([-u_table[SU:], u_table[:SU]], axis=1),
            ],
            axis=0,
        )
        both = jnp.dot(
            jnp.concatenate(split_bf16(half), axis=0), u_side, preferred_element_type=jnp.float32
        )
        result = result + both[:SU] + both[SU:]
    result = jnp.concatenate([result[:, :SU].T, result[:, SU:].T], axis=1)
    tail = meta_row // 16 * 16
    wide = packed[tail : tail + 16, :].astype(jnp.float32)
    at = meta_row - tail + 2
    gain = (wide[at : at + 2] + wide[at + 2 : at + 4]) + wide[at + 4 : at + 6]
    gain_u = jnp.broadcast_to(gain[0:1], (SU, SU)).T
    gains = gain_u * gain[1:2] * norm
    total[...] = result * jnp.concatenate([gains, gains], axis=1)
    half_rows = mine_ref.shape[0]
    mine_ref[...] = total[pl.ds(pl.multiple_of(chan * half_rows, half_rows), half_rows), :]
    other_ref[...] = total[pl.ds(pl.multiple_of((1 - chan) * half_rows, half_rows), half_rows), :]


def body(
    visibilities, coords, plane_index, block_group, offsets, facet_centre, tables, antenna_gain
):
    facets = lax.axis_size("facet")
    groups = lax.axis_size("bl")
    chan_count = lax.axis_size("chan")
    held, chans = visibilities.shape[:2]
    devices = facets * groups
    slots = 2 * facets
    cap = max(2, 2 * held // groups)
    meta_row = 2 * cap * (chans + 1)
    rows = -(-(meta_row + 8) // 16) * 16
    half_rows = SU // chan_count
    norm = SU / math.sqrt(visibilities.shape[3] * held * facets * CH)

    own_table = tables.reshape(2, 2 * SU, SU)
    *pieces, half = pl.pallas_call(
        functools.partial(sort_kernel, (groups, held, chans, cap, rows)),
        out_shape=[
            jax.ShapeDtypeStruct((rows + (2 * SU if shift == 1 else 0), SU), jnp.bfloat16)
            for shift in range(groups)
        ]
        + [jax.ShapeDtypeStruct((2 * SU, SU), jnp.bfloat16)],
        in_specs=[HBM] * 8,
        out_specs=[VMEM] * (groups + 1),
        scratch_shapes=[
            pltpu.SMEM((1, held), jnp.int32),
            pltpu.SMEM((1, held), jnp.int32),
            pltpu.VMEM((held * 2 * chans, SU), jnp.bfloat16),
            pltpu.VMEM((held * 2, SU), jnp.bfloat16),
            pltpu.SMEM((facets, 2, groups), jnp.int32),
            pltpu.SMEM((2, facets), jnp.float32),
            pltpu.VMEM((1, 2, SU), jnp.float32),
            pltpu.VMEM((held * 2 * chans, SU), jnp.float32),
            pltpu.VMEM((held * 2, SU), jnp.float32),
            pltpu.VMEM((groups, rows, SU), jnp.float32),
            pltpu.SMEM((groups,), jnp.int32),
            pltpu.VMEM((2 * SU, SU), jnp.bfloat16),
            pltpu.VMEM((2 * SU, SU), jnp.float32),
            pltpu.SemaphoreType.DMA((8,)),
        ],
        compiler_params=PARAMS,
        cost_estimate=pl.CostEstimate(flops=100_000, bytes_accessed=100_000, transcendentals=0),
        name="sort_blocks",
    )(
        *(
            pltpu.with_memory_space_constraint(operand, pltpu.HBM)
            for operand in (
                plane_index.reshape(1, held),
                block_group.T,
                visibilities.reshape(held * 2 * chans, SU),
                coords.reshape(held * 2, SU),
                offsets.transpose(0, 2, 1),
                facet_centre.T,
                antenna_gain,
                own_table,
            )
        )
    )
    arrived = [
        lax.ppermute(pieces[shift], "bl", [(g, (g + shift) % groups) for g in range(groups)])
        for shift in [1, *range(groups - 1, 1, -1)]
    ]
    vis_rows = groups * rows
    joined = local(
        functools.partial(join_kernel, rows),
        [half, pieces[0], *arrived],
        (vis_rows + 4 * SU, SU),
        "join",
    )
    blocks = [joined] + [exchange(joined, "facet", shift) for shift in range(1, facets)]
    def grid(some, before=()):
        lines = len(some) * groups * cap
        return pl.pallas_call(
            functools.partial(grid_kernel, (facets, groups, chans, cap, rows, len(some))),
            out_shape=jax.ShapeDtypeStruct((slots, SU, 2 * SU), jnp.float32),
            in_specs=[VMEM] * (1 + len(some) + len(before)),
            out_specs=VMEM,
            scratch_shapes=[
                pltpu.SMEM((lines + UNROLL,), jnp.int32),
            ]
            + [pltpu.VMEM((lines * chans + 8, SU), jnp.float32)] * 4
            + [pltpu.VMEM((SU, SU), jnp.float32)],
            compiler_params=PARAMS,
            cost_estimate=pl.CostEstimate(
                flops=len(some) * 1_000_000_000,
                bytes_accessed=1_000_000,
                transcendentals=len(some) * 1_000_000,
            ),
            name="grid",
        )(joined, *some, *before)

    grids = grid(blocks[-1:], [grid(blocks[:1])])
    blocks, grids = lax.optimization_barrier((blocks, grids))
    fetched = local(
        functools.partial(collect_kernel, vis_rows), blocks, (facets * 4 * SU, SU), "collect"
    )
    swapped = lax.ppermute(fetched, "chan", [(c, 1 - c) for c in range(chan_count)])
    grids = grid(blocks[1:-1], [grids])
    mine, other = pl.pallas_call(
        functools.partial(table_kernel, (slots, meta_row), norm),
        out_shape=[jax.ShapeDtypeStruct((half_rows, 2 * SU), jnp.float32)] * 2,
        in_specs=[VMEM] * 4,
        out_specs=[VMEM, VMEM],
        scratch_shapes=[
            pltpu.VMEM((SU, 2 * SU), jnp.float32),
        ],
        compiler_params=PARAMS,
        cost_estimate=pl.CostEstimate(
            flops=1_000_000_000, bytes_accessed=2_000_000, transcendentals=0
        ),
        name="apply_tables",
    )(joined, fetched, swapped, grids)
    summand = lax.ppermute(other, "chan", [(c, 1 - c) for c in range(chan_count)])
    return (mine + summand).reshape(1, 1, half_rows, 2, SU)


def solution(mesh):
    in_specs = (
        P(("facet", "bl"), "chan", None, None),
        P(("facet", "bl"), None, None),
        P(("facet", "bl")),
        P(("facet", "bl"), None),
        P(),
        P(),
        P(("facet", "bl"), None, None, None, None),
        P("bl", None, None),
    )
    out_specs = P("facet", "bl", "chan", None, None)
    return jax.shard_map(body, mesh=mesh, in_specs=in_specs, out_specs=out_specs, check_vma=False)
```

```python
import functools
import math

import jax
import jax.numpy as jnp
from jax import lax
from jax.experimental import pallas as pl
from jax.experimental.pallas import tpu as pltpu
from jax.sharding import PartitionSpec as P

SU = 128
CH = 8
KERNEL_SPREAD = 1.5
ALPHA = math.sqrt(math.log2(math.e) / (2.0 * KERNEL_SPREAD * KERNEL_SPREAD))
UNROLL = 4
REST = 2
NT = (((1,), (1,)), ((), ()))
VMEM = pl.BlockSpec(memory_space=pltpu.VMEM)
HBM = pl.BlockSpec(memory_space=pltpu.HBM)
PARAMS = pltpu.CompilerParams(vmem_limit_bytes=32 * 1024 * 1024)


def cos_sin(turns):
    quarter = jnp.floor(4.0 * turns + 0.5)
    angle = (2.0 * math.pi) * (turns - 0.25 * quarter)
    sq = angle * angle
    sine = angle * (
        1.0 + sq * (-1.0 / 6 + sq * (1.0 / 120 + sq * (-1.0 / 5040 + sq * (1.0 / 362880))))
    )
    cosine = 1.0 + sq * (
        -0.5 + sq * (1.0 / 24 + sq * (-1.0 / 720 + sq * (1.0 / 40320 + sq * (-1.0 / 3628800))))
    )
    turn = quarter.astype(jnp.int32) & 3
    odd = (turn & 1) == 1
    cos_out = jnp.where(odd, sine, cosine)
    sin_out = jnp.where(odd, cosine, sine)
    cos_out = jnp.where((turn == 1) | (turn == 2), -cos_out, cos_out)
    sin_out = jnp.where(turn >= 2, -sin_out, sin_out)
    return cos_out, sin_out


def split_bf16(x):
    high = x.astype(jnp.bfloat16)
    low = (x - high.astype(jnp.float32)).astype(jnp.bfloat16)
    return high, low


def three_parts(x):
    parts = []
    for _ in range(3):
        part = x.astype(jnp.bfloat16)
        x = x - part.astype(jnp.float32)
        parts.append(part.astype(jnp.float32))
    return parts


def sort_kernel(sizes, *refs):
    groups, held, chans, cap, rows = sizes
    table_hbm, outs, half = refs[7], refs[8 : 8 + groups], refs[8 + groups]
    targets = refs[9 + groups : 16 + groups]
    plane_ref, group_ref, samples_b, place_b, offsets_ref, centre_ref, gain_ref = targets
    samples, place, sorted_, filled, table_b, table_f, sems = refs[16 + groups :]
    facet = lax.axis_index("facet")
    copies = [
        pltpu.make_async_copy(source, target, sems.at[n])
        for n, (source, target) in enumerate(zip(refs[:7], targets))
    ]
    table = pltpu.make_async_copy(table_hbm.at[lax.axis_index("chan")], table_b, sems.at[7])
    for copy in copies + [table]:
        copy.start()
    sorted_[...] = jnp.zeros_like(sorted_)
    for g in range(groups):
        filled[g] = 0
    for copy in copies:
        copy.wait()
    samples[...] = samples_b[...].astype(jnp.float32)
    place[...] = place_b[...].astype(jnp.float32)
    lane = lax.broadcasted_iota(jnp.int32, (1, SU), 1)
    meta = 2 * cap * (chans + 1)
    centre = [
        part
        for axis in range(2)
        for part in three_parts(jnp.full((1, SU), centre_ref[axis, facet], jnp.float32))
    ]
    gains = three_parts(gain_ref[0])
    for g in range(groups):
        numbers = jnp.zeros((1, SU), jnp.float32)
        for axis in range(2):
            offset = offsets_ref[facet, axis, g].astype(jnp.float32)
            numbers = jnp.where(lane == axis, offset, numbers)
        for n, part in enumerate(centre):
            numbers = jnp.where(lane == 2 + n, part, numbers)
        sorted_[g, meta + 1 : meta + 2, :] = numbers
        for n, part in enumerate(gains):
            sorted_[g, meta + 2 + 2 * n : meta + 4 + 2 * n, :] = part
    for i in range(held):
        g = group_ref[0, i]
        k = filled[g]
        filled[g] = k + 1
        for part in range(2):
            at = part * cap * chans + k * chans
            sorted_[g, pl.ds(at, chans), :] = samples[pl.ds(2 * chans * i + part, chans, stride=2), :]
            at = 2 * cap * chans + part * cap + k
            sorted_[g, pl.ds(at, 1), :] = place[2 * i + part : 2 * i + part + 1, :]
        sorted_[g, meta : meta + 1, :] += jnp.where(
            lane == k, (plane_ref[0, i] + 1).astype(jnp.float32), 0.0
        )
    for shift, out_ref in enumerate(outs):
        out_ref[...] = sorted_[lax.axis_index("bl") ^ shift].astype(jnp.bfloat16)
    table.wait()
    table_f[...] = table_b[...].astype(jnp.float32)
    for part in range(2):
        matrix = table_f[pl.ds(part, SU, stride=2), :]
        matrix = jnp.where(lax.axis_index("chan") == 0, matrix, matrix.T).astype(jnp.bfloat16)
        half[part * SU : (part + 1) * SU, :] = matrix


def join_kernel(rows, half, shifted, *refs):
    *pieces, joined = refs
    for n, ref in enumerate(pieces):
        joined[n * rows : (n + 1) * rows, :] = ref[...]
    at = len(pieces) * rows
    joined[at : at + 2 * SU, :] = half[...]
    joined[at + 2 * SU :, :] = shifted[...]


def collect_kernel(skip, *refs):
    for n, ref in enumerate(refs[:-1]):
        refs[-1][n * 4 * SU : (n + 1) * 4 * SU, :] = ref[skip:, :]


def grid_kernel(sizes, *refs):
    facets, groups, chans, cap, rows, count_here = sizes
    own_ref, grids = refs[0], refs[1 + count_here]
    order, spots_u, spots_v, turns_real, turns_imag, cells = refs[2 + count_here :]
    pieces = [
        ref.at[pl.ds(n * rows, rows)] for ref in refs[1 : 1 + count_here] for n in range(groups)
    ]
    devices = len(pieces)
    slots = 2 * facets
    lines = cap * chans
    meta_row = 2 * (lines + cap)
    tail = meta_row // 16 * 16
    facet = lax.axis_index("facet")
    group = lax.axis_index("bl")
    chan = lax.axis_index("chan")

    lane = lax.broadcasted_iota(jnp.int32, (1, SU), 1)
    own = own_ref[tail : tail + 16, :].astype(jnp.float32)
    numbers = own[meta_row - tail + 1 : meta_row - tail + 2]
    codes = []
    for d in range(devices):
        meta = pieces[d][tail : tail + 16, :].astype(jnp.float32)
        plane = meta[meta_row - tail : meta_row - tail + 1].astype(jnp.int32) - 1
        set_id = jnp.where(lax.rem(plane, groups) == group, 0, 1)
        code = (d * cap + lane) * slots + 2 * (lax.div(plane, groups) ^ facet) + set_id
        codes.append(jnp.where(plane >= 0, code, -1))
    grids[...] = jnp.zeros_like(grids)

    def number(n):
        return jnp.broadcast_to(numbers[:, n : n + 1], (lines, SU))

    offset_u = number(0)
    offset_v = number(1)
    along_l = number(2) + number(3) + number(4)
    along_m = number(5) + number(6) + number(7)
    line = lax.broadcasted_iota(jnp.int32, (lines, SU), 0)
    channel = (chan * chans + lax.rem(line, chans)).astype(jnp.float32)
    scale = 1.0 + 0.01 * (channel - 0.5 * (CH - 1))

    def spread_lines(place):
        return jnp.concatenate(
            [jnp.broadcast_to(place[k : k + 1], (chans, SU)) for k in range(cap)], axis=0
        )

    for d in range(devices):
        at = d * lines
        wide = pieces[d][...].astype(jnp.float32)
        real = wide[:lines]
        imag = wide[lines : 2 * lines]
        along_u = spread_lines(wide[2 * lines : 2 * lines + cap])
        along_v = spread_lines(wide[2 * lines + cap : 2 * (lines + cap)])
        cosine, sine = cos_sin((1.0 / SU) * (scale * (along_u * along_l + along_v * along_m)))
        spots_u[at : at + lines, :] = ALPHA * (scale * along_u - offset_u)
        spots_v[at : at + lines, :] = ALPHA * (scale * along_v - offset_v)
        turns_real[at : at + lines, :] = real * cosine - imag * sine
        turns_imag[at : at + lines, :] = real * sine + imag * cosine
    last = devices * lines
    for ref in (spots_u, spots_v, turns_real, turns_imag):
        ref[last : last + 8, :] = jnp.zeros((8, SU), jnp.float32)

    count = jnp.int32(0)
    for d in range(devices):
        for k in range(cap):
            code = codes[d][0, k]
            order[count] = code
            count = count + jnp.where(code >= 0, 1, 0)
    for i in range(UNROLL):
        order[count + i] = devices * cap * slots

    cells[...] = ALPHA * lax.broadcasted_iota(jnp.int32, (SU, SU), 0).astype(jnp.float32)

    def profile(spot):
        apart = spot - cells[...]
        return jnp.exp2(-((apart * apart).astype(jnp.bfloat16)))

    def tiled(row):
        return jnp.broadcast_to(row, (16, SU)).astype(jnp.bfloat16)[None]

    def one_block(at):
        code = order[at]
        slot = lax.rem(code, slots)
        base = lax.div(code, slots) * chans
        lefts_real, lefts_imag, rights = [], [], []
        for c in range(chans):
            here = pl.ds(base + c, 1)
            left = profile(spots_u[here, :]).reshape(SU // 16, 16, SU)
            lefts_real.append((left * tiled(turns_real[here, :])).reshape(SU, SU))
            lefts_imag.append((left * tiled(turns_imag[here, :])).reshape(SU, SU))
            rights.append(profile(spots_v[here, :]))
        left = jnp.concatenate(
            [jnp.concatenate(lefts_real, axis=1), jnp.concatenate(lefts_imag, axis=1)], axis=0
        )
        right = jnp.concatenate(rights, axis=1)
        return slot, lax.dot_general(right, left, NT, preferred_element_type=jnp.float32)

    def steps(first, blocks, number):
        def step(k, carry):
            for slot, part in [one_block(first + k * blocks + i) for i in range(blocks)]:
                grids[slot] += part
            return carry

        lax.fori_loop(0, number, step, 0)

    whole = lax.div(count, UNROLL)
    steps(0, UNROLL, whole)
    steps(whole * UNROLL, REST, lax.div(lax.rem(count, UNROLL) + REST - 1, REST))


def local(kernel, operands, shape, name):
    return pl.pallas_call(
        kernel,
        out_shape=jax.ShapeDtypeStruct(shape, jnp.bfloat16),
        in_specs=[VMEM] * len(operands),
        out_specs=VMEM,
        compiler_params=PARAMS,
        cost_estimate=pl.CostEstimate(flops=0, bytes_accessed=400_000, transcendentals=0),
        name=name,
    )(*operands)


def exchange(value, axis, shift):
    return lax.ppermute(value, axis, [(n, n ^ shift) for n in range(lax.axis_size(axis))])


def table_kernel(sizes, norm, packed, ours, theirs, *refs):
    slots, meta_row = sizes
    grids, (mine_ref, other_ref, total) = refs[:-3], refs[-3:]
    chan = lax.axis_index("chan")
    first = chan == 0

    result = jnp.zeros((SU, 2 * SU), jnp.float32)
    for s in range(slots):
        at = slice(2 * SU * s, 2 * SU * (s + 1))
        fetched = ours[at, :]
        swapped = theirs[at, :]
        v_table = jnp.where(first, swapped, fetched)
        v_side = jnp.concatenate([v_table[:SU], v_table[SU:]], axis=1)
        grid = sum(ref[s] for ref in grids)
        high, low = (
            jnp.concatenate(
                [
                    part,
                    jnp.concatenate([-part[:, SU:], part[:, :SU]], axis=1),
                ],
                axis=0,
            )
            for part in split_bf16(grid)
        )
        half = jnp.dot(v_side, high, preferred_element_type=jnp.float32) + jnp.dot(
            v_side, low, preferred_element_type=jnp.float32
        )
        u_table = jnp.where(first, fetched, swapped)
        u_side = jnp.concatenate(
            [
                jnp.concatenate([u_table[:SU], u_table[SU:]], axis=1),
                jnp.concatenate([-u_table[SU:], u_table[:SU]], axis=1),
            ],
            axis=0,
        )
        high, low = split_bf16(half)
        result = (
            result
            + jnp.dot(high, u_side, preferred_element_type=jnp.float32)
            + jnp.dot(low, u_side, preferred_element_type=jnp.float32)
        )
    result = jnp.concatenate([result[:, :SU].T, result[:, SU:].T], axis=1)
    tail = meta_row // 16 * 16
    wide = packed[tail : tail + 16, :].astype(jnp.float32)
    at = meta_row - tail + 2
    gain = (wide[at : at + 2] + wide[at + 2 : at + 4]) + wide[at + 4 : at + 6]
    gain_u = jnp.broadcast_to(gain[0:1], (SU, SU)).T
    gains = gain_u * gain[1:2] * norm
    total[...] = result * jnp.concatenate([gains, gains], axis=1)
    half_rows = mine_ref.shape[0]
    mine_ref[...] = total[pl.ds(pl.multiple_of(chan * half_rows, half_rows), half_rows), :]
    other_ref[...] = total[pl.ds(pl.multiple_of((1 - chan) * half_rows, half_rows), half_rows), :]


def body(
    visibilities, coords, plane_index, block_group, offsets, facet_centre, tables, antenna_gain
):
    facets = lax.axis_size("facet")
    groups = lax.axis_size("bl")
    chan_count = lax.axis_size("chan")
    held, chans = visibilities.shape[:2]
    devices = facets * groups
    slots = 2 * facets
    cap = max(2, 2 * held // groups)
    meta_row = 2 * cap * (chans + 1)
    rows = -(-(meta_row + 8) // 16) * 16
    half_rows = SU // chan_count
    norm = SU / math.sqrt(visibilities.shape[3] * held * facets * CH)

    own_table = tables.reshape(2, 2 * SU, SU)
    *pieces, half = pl.pallas_call(
        functools.partial(sort_kernel, (groups, held, chans, cap, rows)),
        out_shape=[jax.ShapeDtypeStruct((rows, SU), jnp.bfloat16)] * groups
        + [jax.ShapeDtypeStruct((2 * SU, SU), jnp.bfloat16)],
        in_specs=[HBM] * 8,
        out_specs=[VMEM] * (groups + 1),
        scratch_shapes=[
            pltpu.SMEM((1, held), jnp.int32),
            pltpu.SMEM((1, held), jnp.int32),
            pltpu.VMEM((held * 2 * chans, SU), jnp.bfloat16),
            pltpu.VMEM((held * 2, SU), jnp.bfloat16),
            pltpu.SMEM((facets, 2, groups), jnp.int32),
            pltpu.SMEM((2, facets), jnp.float32),
            pltpu.VMEM((1, 2, SU), jnp.float32),
            pltpu.VMEM((held * 2 * chans, SU), jnp.float32),
            pltpu.VMEM((held * 2, SU), jnp.float32),
            pltpu.VMEM((groups, rows, SU), jnp.float32),
            pltpu.SMEM((groups,), jnp.int32),
            pltpu.VMEM((2 * SU, SU), jnp.bfloat16),
            pltpu.VMEM((2 * SU, SU), jnp.float32),
            pltpu.SemaphoreType.DMA((8,)),
        ],
        compiler_params=PARAMS,
        cost_estimate=pl.CostEstimate(flops=100_000, bytes_accessed=100_000, transcendentals=0),
        name="sort_blocks",
    )(
        *(
            pltpu.with_memory_space_constraint(operand, pltpu.HBM)
            for operand in (
                plane_index.reshape(1, held),
                block_group.T,
                visibilities.reshape(held * 2 * chans, SU),
                coords.reshape(held * 2, SU),
                offsets.transpose(0, 2, 1),
                facet_centre.T,
                antenna_gain,
                own_table,
            )
        )
    )
    shifted = lax.ppermute(half, "bl", [(g, (g + 1) % groups) for g in range(groups)])
    arrived = [exchange(pieces[shift], "bl", shift) for shift in range(groups - 1, 0, -1)]
    vis_rows = groups * rows
    joined = local(
        functools.partial(join_kernel, rows),
        [half, shifted, pieces[0], *arrived],
        (vis_rows + 4 * SU, SU),
        "join",
    )
    blocks = [joined] + [exchange(joined, "facet", shift) for shift in range(1, facets)]
    def grid(some):
        lines = len(some) * groups * cap
        return pl.pallas_call(
            functools.partial(grid_kernel, (facets, groups, chans, cap, rows, len(some))),
            out_shape=jax.ShapeDtypeStruct((slots, SU, 2 * SU), jnp.float32),
            in_specs=[VMEM] * (1 + len(some)),
            out_specs=VMEM,
            scratch_shapes=[
                pltpu.SMEM((lines + UNROLL,), jnp.int32),
            ]
            + [pltpu.VMEM((lines * chans + 8, SU), jnp.float32)] * 4
            + [pltpu.VMEM((SU, SU), jnp.float32)],
            compiler_params=PARAMS,
            cost_estimate=pl.CostEstimate(
                flops=len(some) * 1_000_000_000,
                bytes_accessed=1_000_000,
                transcendentals=len(some) * 1_000_000,
            ),
            name="grid",
        )(joined, *some)

    grids = [grid(blocks[:1]), grid(blocks[-1:])]
    blocks, grids = lax.optimization_barrier((blocks, grids))
    fetched = local(
        functools.partial(collect_kernel, vis_rows), blocks, (facets * 4 * SU, SU), "collect"
    )
    swapped = lax.ppermute(fetched, "chan", [(c, 1 - c) for c in range(chan_count)])
    grids.append(grid(blocks[1:-1]))
    mine, other = pl.pallas_call(
        functools.partial(table_kernel, (slots, meta_row), norm),
        out_shape=[jax.ShapeDtypeStruct((half_rows, 2 * SU), jnp.float32)] * 2,
        in_specs=[VMEM] * (3 + len(grids)),
        out_specs=[VMEM, VMEM],
        scratch_shapes=[
            pltpu.VMEM((SU, 2 * SU), jnp.float32),
        ],
        compiler_params=PARAMS,
        cost_estimate=pl.CostEstimate(
            flops=1_000_000_000, bytes_accessed=2_000_000, transcendentals=0
        ),
        name="apply_tables",
    )(joined, fetched, swapped, *grids)
    summand = lax.ppermute(other, "chan", [(c, 1 - c) for c in range(chan_count)])
    return (mine + summand).reshape(1, 1, half_rows, 2, SU)


def solution(mesh):
    in_specs = (
        P(("facet", "bl"), "chan", None, None),
        P(("facet", "bl"), None, None),
        P(("facet", "bl")),
        P(("facet", "bl"), None),
        P(),
        P(),
        P(("facet", "bl"), None, None, None, None),
        P("bl", None, None),
    )
    out_specs = P("facet", "bl", "chan", None, None)
    return jax.shard_map(body, mesh=mesh, in_specs=in_specs, out_specs=out_specs, check_vma=False)
```

```python
import functools
import math

import jax
import jax.numpy as jnp
from jax import lax
from jax.experimental import pallas as pl
from jax.experimental.pallas import tpu as pltpu
from jax.sharding import PartitionSpec as P

SU = 128
CH = 8
KERNEL_SPREAD = 1.5
ALPHA = math.sqrt(math.log2(math.e) / (2.0 * KERNEL_SPREAD * KERNEL_SPREAD))
UNROLL = 4
REST = 2
NT = (((1,), (1,)), ((), ()))
VMEM = pl.BlockSpec(memory_space=pltpu.VMEM)
HBM = pl.BlockSpec(memory_space=pltpu.HBM)
PARAMS = pltpu.CompilerParams(vmem_limit_bytes=32 * 1024 * 1024)


def cos_sin(turns):
    quarter = jnp.floor(4.0 * turns + 0.5)
    angle = (2.0 * math.pi) * (turns - 0.25 * quarter)
    sq = angle * angle
    sine = angle * (
        1.0 + sq * (-1.0 / 6 + sq * (1.0 / 120 + sq * (-1.0 / 5040 + sq * (1.0 / 362880))))
    )
    cosine = 1.0 + sq * (
        -0.5 + sq * (1.0 / 24 + sq * (-1.0 / 720 + sq * (1.0 / 40320 + sq * (-1.0 / 3628800))))
    )
    turn = quarter.astype(jnp.int32) & 3
    odd = (turn & 1) == 1
    cos_out = jnp.where(odd, sine, cosine)
    sin_out = jnp.where(odd, cosine, sine)
    cos_out = jnp.where((turn == 1) | (turn == 2), -cos_out, cos_out)
    sin_out = jnp.where(turn >= 2, -sin_out, sin_out)
    return cos_out, sin_out


def split_bf16(x):
    high = x.astype(jnp.bfloat16)
    low = (x - high.astype(jnp.float32)).astype(jnp.bfloat16)
    return high, low


def three_parts(x):
    parts = []
    for _ in range(3):
        part = x.astype(jnp.bfloat16)
        x = x - part.astype(jnp.float32)
        parts.append(part.astype(jnp.float32))
    return parts


def sort_kernel(sizes, *refs):
    groups, held, chans, cap, rows = sizes
    table_hbm, outs, half = refs[7], refs[8 : 8 + groups], refs[8 + groups]
    targets = refs[9 + groups : 16 + groups]
    plane_ref, group_ref, samples_b, place_b, offsets_ref, centre_ref, gain_ref = targets
    samples, place, sorted_, filled, table_b, table_f, sems = refs[16 + groups :]
    facet = lax.axis_index("facet")
    copies = [
        pltpu.make_async_copy(source, target, sems.at[n])
        for n, (source, target) in enumerate(zip(refs[:7], targets))
    ]
    table = pltpu.make_async_copy(table_hbm.at[lax.axis_index("chan")], table_b, sems.at[7])
    for copy in copies + [table]:
        copy.start()
    sorted_[...] = jnp.zeros_like(sorted_)
    for g in range(groups):
        filled[g] = 0
    for copy in copies:
        copy.wait()
    samples[...] = samples_b[...].astype(jnp.float32)
    place[...] = place_b[...].astype(jnp.float32)
    lane = lax.broadcasted_iota(jnp.int32, (1, SU), 1)
    meta = 2 * cap * (chans + 1)
    centre = [
        part
        for axis in range(2)
        for part in three_parts(jnp.full((1, SU), centre_ref[axis, facet], jnp.float32))
    ]
    gains = three_parts(gain_ref[0])
    for g in range(groups):
        numbers = jnp.zeros((1, SU), jnp.float32)
        for axis in range(2):
            offset = offsets_ref[facet, axis, g].astype(jnp.float32)
            numbers = jnp.where(lane == axis, offset, numbers)
        for n, part in enumerate(centre):
            numbers = jnp.where(lane == 2 + n, part, numbers)
        sorted_[g, meta + 1 : meta + 2, :] = numbers
        for n, part in enumerate(gains):
            sorted_[g, meta + 2 + 2 * n : meta + 4 + 2 * n, :] = part
    for i in range(held):
        g = group_ref[0, i]
        k = filled[g]
        filled[g] = k + 1
        for part in range(2):
            at = part * cap * chans + k * chans
            sorted_[g, pl.ds(at, chans), :] = samples[pl.ds(2 * chans * i + part, chans, stride=2), :]
            at = 2 * cap * chans + part * cap + k
            sorted_[g, pl.ds(at, 1), :] = place[2 * i + part : 2 * i + part + 1, :]
        sorted_[g, meta : meta + 1, :] += jnp.where(
            lane == k, (plane_ref[0, i] + 1).astype(jnp.float32), 0.0
        )
    for shift, out_ref in enumerate(outs):
        g = lax.rem(lax.axis_index("bl") + shift, groups)
        out_ref[:rows, :] = sorted_[g].astype(jnp.bfloat16)
    table.wait()
    table_f[...] = table_b[...].astype(jnp.float32)

    def put(turned):
        for part in range(2):
            matrix = table_f[pl.ds(part, SU, stride=2), :]
            matrix = (matrix.T if turned else matrix).astype(jnp.bfloat16)
            half[part * SU : (part + 1) * SU, :] = matrix
            outs[1][rows + part * SU : rows + (part + 1) * SU, :] = matrix

    @pl.when(lax.axis_index("chan") == 0)
    def _():
        put(False)

    @pl.when(lax.axis_index("chan") != 0)
    def _():
        put(True)


def join_kernel(rows, half, *refs):
    *pieces, joined = refs
    for n, ref in enumerate(pieces):
        joined[n * rows : (n + 1) * rows, :] = ref[:rows, :]
    at = len(pieces) * rows
    joined[at : at + 2 * SU, :] = half[...]
    joined[at + 2 * SU :, :] = pieces[1][rows:, :]


def collect_kernel(skip, *refs):
    for n, ref in enumerate(refs[:-1]):
        refs[-1][n * 4 * SU : (n + 1) * 4 * SU, :] = ref[skip:, :]


def grid_kernel(sizes, *refs):
    facets, groups, chans, cap, rows, count_here = sizes
    own_ref, grids = refs[0], refs[1 + count_here]
    order, spots_u, spots_v, turns_real, turns_imag, cells = refs[2 + count_here :]
    pieces = [
        ref.at[pl.ds(n * rows, rows)] for ref in refs[1 : 1 + count_here] for n in range(groups)
    ]
    devices = len(pieces)
    slots = 2 * facets
    lines = cap * chans
    meta_row = 2 * (lines + cap)
    tail = meta_row // 16 * 16
    facet = lax.axis_index("facet")
    group = lax.axis_index("bl")
    chan = lax.axis_index("chan")

    lane = lax.broadcasted_iota(jnp.int32, (1, SU), 1)
    own = own_ref[tail : tail + 16, :].astype(jnp.float32)
    numbers = own[meta_row - tail + 1 : meta_row - tail + 2]
    codes = []
    for d in range(devices):
        meta = pieces[d][tail : tail + 16, :].astype(jnp.float32)
        plane = meta[meta_row - tail : meta_row - tail + 1].astype(jnp.int32) - 1
        set_id = jnp.where(lax.rem(plane, groups) == group, 0, 1)
        code = (d * cap + lane) * slots + 2 * (lax.div(plane, groups) ^ facet) + set_id
        codes.append(jnp.where(plane >= 0, code, -1))
    grids[...] = jnp.zeros_like(grids)

    def number(n):
        return jnp.broadcast_to(numbers[:, n : n + 1], (lines, SU))

    offset_u = number(0)
    offset_v = number(1)
    along_l = number(2) + number(3) + number(4)
    along_m = number(5) + number(6) + number(7)
    line = lax.broadcasted_iota(jnp.int32, (lines, SU), 0)
    channel = (chan * chans + lax.rem(line, chans)).astype(jnp.float32)
    scale = 1.0 + 0.01 * (channel - 0.5 * (CH - 1))

    def spread_lines(place):
        return jnp.concatenate(
            [jnp.broadcast_to(place[k : k + 1], (chans, SU)) for k in range(cap)], axis=0
        )

    for d in range(devices):
        at = d * lines
        wide = pieces[d][...].astype(jnp.float32)
        real = wide[:lines]
        imag = wide[lines : 2 * lines]
        along_u = spread_lines(wide[2 * lines : 2 * lines + cap])
        along_v = spread_lines(wide[2 * lines + cap : 2 * (lines + cap)])
        cosine, sine = cos_sin((1.0 / SU) * (scale * (along_u * along_l + along_v * along_m)))
        spots_u[at : at + lines, :] = ALPHA * (scale * along_u - offset_u)
        spots_v[at : at + lines, :] = ALPHA * (scale * along_v - offset_v)
        turns_real[at : at + lines, :] = real * cosine - imag * sine
        turns_imag[at : at + lines, :] = real * sine + imag * cosine
    last = devices * lines
    for ref in (spots_u, spots_v, turns_real, turns_imag):
        ref[last : last + 8, :] = jnp.zeros((8, SU), jnp.float32)

    count = jnp.int32(0)
    for d in range(devices):
        for k in range(cap):
            code = codes[d][0, k]
            order[count] = code
            count = count + jnp.where(code >= 0, 1, 0)
    for i in range(UNROLL):
        order[count + i] = devices * cap * slots

    cells[...] = ALPHA * lax.broadcasted_iota(jnp.int32, (SU, SU), 0).astype(jnp.float32)

    def profile(spot):
        apart = spot - cells[...]
        return jnp.exp2(-((apart * apart).astype(jnp.bfloat16)))

    def tiled(row):
        return jnp.broadcast_to(row, (16, SU)).astype(jnp.bfloat16)[None]

    def one_block(at):
        code = order[at]
        slot = lax.rem(code, slots)
        base = lax.div(code, slots) * chans
        lefts_real, lefts_imag, rights = [], [], []
        for c in range(chans):
            here = pl.ds(base + c, 1)
            left = profile(spots_u[here, :]).reshape(SU // 16, 16, SU)
            lefts_real.append((left * tiled(turns_real[here, :])).reshape(SU, SU))
            lefts_imag.append((left * tiled(turns_imag[here, :])).reshape(SU, SU))
            rights.append(profile(spots_v[here, :]))
        left = jnp.concatenate(
            [jnp.concatenate(lefts_real, axis=1), jnp.concatenate(lefts_imag, axis=1)], axis=0
        )
        right = jnp.concatenate(rights, axis=1)
        return slot, lax.dot_general(right, left, NT, preferred_element_type=jnp.float32)

    def steps(first, blocks, number):
        def step(k, carry):
            for slot, part in [one_block(first + k * blocks + i) for i in range(blocks)]:
                grids[slot] += part
            return carry

        lax.fori_loop(0, number, step, 0)

    whole = lax.div(count + UNROLL - REST - 1, UNROLL)
    steps(0, UNROLL, whole)
    steps(whole * UNROLL, REST, jnp.where(count > whole * UNROLL, 1, 0))


def local(kernel, operands, shape, name):
    return pl.pallas_call(
        kernel,
        out_shape=jax.ShapeDtypeStruct(shape, jnp.bfloat16),
        in_specs=[VMEM] * len(operands),
        out_specs=VMEM,
        compiler_params=PARAMS,
        cost_estimate=pl.CostEstimate(flops=0, bytes_accessed=400_000, transcendentals=0),
        name=name,
    )(*operands)


def exchange(value, axis, shift):
    return lax.ppermute(value, axis, [(n, n ^ shift) for n in range(lax.axis_size(axis))])


def table_kernel(sizes, norm, packed, ours, theirs, *refs):
    slots, meta_row = sizes
    grids, (mine_ref, other_ref, total) = refs[:-3], refs[-3:]
    chan = lax.axis_index("chan")
    first = chan == 0

    result = jnp.zeros((SU, 2 * SU), jnp.float32)
    for s in range(slots):
        at = slice(2 * SU * s, 2 * SU * (s + 1))
        fetched = ours[at, :]
        swapped = theirs[at, :]
        v_table = jnp.where(first, swapped, fetched)
        v_side = jnp.concatenate([v_table[:SU], v_table[SU:]], axis=1)
        grid = sum(ref[s] for ref in grids)
        high, low = (
            jnp.concatenate(
                [
                    part,
                    jnp.concatenate([-part[:, SU:], part[:, :SU]], axis=1),
                ],
                axis=0,
            )
            for part in split_bf16(grid)
        )
        half = jnp.dot(v_side, high, preferred_element_type=jnp.float32) + jnp.dot(
            v_side, low, preferred_element_type=jnp.float32
        )
        u_table = jnp.where(first, fetched, swapped)
        u_side = jnp.concatenate(
            [
                jnp.concatenate([u_table[:SU], u_table[SU:]], axis=1),
                jnp.concatenate([-u_table[SU:], u_table[:SU]], axis=1),
            ],
            axis=0,
        )
        both = jnp.dot(
            jnp.concatenate(split_bf16(half), axis=0), u_side, preferred_element_type=jnp.float32
        )
        result = result + both[:SU] + both[SU:]
    result = jnp.concatenate([result[:, :SU].T, result[:, SU:].T], axis=1)
    tail = meta_row // 16 * 16
    wide = packed[tail : tail + 16, :].astype(jnp.float32)
    at = meta_row - tail + 2
    gain = (wide[at : at + 2] + wide[at + 2 : at + 4]) + wide[at + 4 : at + 6]
    gain_u = jnp.broadcast_to(gain[0:1], (SU, SU)).T
    gains = gain_u * gain[1:2] * norm
    total[...] = result * jnp.concatenate([gains, gains], axis=1)
    half_rows = mine_ref.shape[0]
    mine_ref[...] = total[pl.ds(pl.multiple_of(chan * half_rows, half_rows), half_rows), :]
    other_ref[...] = total[pl.ds(pl.multiple_of((1 - chan) * half_rows, half_rows), half_rows), :]


def body(
    visibilities, coords, plane_index, block_group, offsets, facet_centre, tables, antenna_gain
):
    facets = lax.axis_size("facet")
    groups = lax.axis_size("bl")
    chan_count = lax.axis_size("chan")
    held, chans = visibilities.shape[:2]
    devices = facets * groups
    slots = 2 * facets
    cap = max(2, 2 * held // groups)
    meta_row = 2 * cap * (chans + 1)
    rows = -(-(meta_row + 8) // 16) * 16
    half_rows = SU // chan_count
    norm = SU / math.sqrt(visibilities.shape[3] * held * facets * CH)

    own_table = tables.reshape(2, 2 * SU, SU)
    *pieces, half = pl.pallas_call(
        functools.partial(sort_kernel, (groups, held, chans, cap, rows)),
        out_shape=[
            jax.ShapeDtypeStruct((rows + (2 * SU if shift == 1 else 0), SU), jnp.bfloat16)
            for shift in range(groups)
        ]
        + [jax.ShapeDtypeStruct((2 * SU, SU), jnp.bfloat16)],
        in_specs=[HBM] * 8,
        out_specs=[VMEM] * (groups + 1),
        scratch_shapes=[
            pltpu.SMEM((1, held), jnp.int32),
            pltpu.SMEM((1, held), jnp.int32),
            pltpu.VMEM((held * 2 * chans, SU), jnp.bfloat16),
            pltpu.VMEM((held * 2, SU), jnp.bfloat16),
            pltpu.SMEM((facets, 2, groups), jnp.int32),
            pltpu.SMEM((2, facets), jnp.float32),
            pltpu.VMEM((1, 2, SU), jnp.float32),
            pltpu.VMEM((held * 2 * chans, SU), jnp.float32),
            pltpu.VMEM((held * 2, SU), jnp.float32),
            pltpu.VMEM((groups, rows, SU), jnp.float32),
            pltpu.SMEM((groups,), jnp.int32),
            pltpu.VMEM((2 * SU, SU), jnp.bfloat16),
            pltpu.VMEM((2 * SU, SU), jnp.float32),
            pltpu.SemaphoreType.DMA((8,)),
        ],
        compiler_params=PARAMS,
        cost_estimate=pl.CostEstimate(flops=100_000, bytes_accessed=100_000, transcendentals=0),
        name="sort_blocks",
    )(
        *(
            pltpu.with_memory_space_constraint(operand, pltpu.HBM)
            for operand in (
                plane_index.reshape(1, held),
                block_group.T,
                visibilities.reshape(held * 2 * chans, SU),
                coords.reshape(held * 2, SU),
                offsets.transpose(0, 2, 1),
                facet_centre.T,
                antenna_gain,
                own_table,
            )
        )
    )
    arrived = [
        lax.ppermute(pieces[shift], "bl", [(g, (g + shift) % groups) for g in range(groups)])
        for shift in [1, *range(groups - 1, 1, -1)]
    ]
    vis_rows = groups * rows
    joined = local(
        functools.partial(join_kernel, rows),
        [half, pieces[0], *arrived],
        (vis_rows + 4 * SU, SU),
        "join",
    )
    blocks = [joined] + [exchange(joined, "facet", shift) for shift in range(1, facets)]
    def grid(some):
        lines = len(some) * groups * cap
        return pl.pallas_call(
            functools.partial(grid_kernel, (facets, groups, chans, cap, rows, len(some))),
            out_shape=jax.ShapeDtypeStruct((slots, SU, 2 * SU), jnp.float32),
            in_specs=[VMEM] * (1 + len(some)),
            out_specs=VMEM,
            scratch_shapes=[
                pltpu.SMEM((lines + UNROLL,), jnp.int32),
            ]
            + [pltpu.VMEM((lines * chans + 8, SU), jnp.float32)] * 4
            + [pltpu.VMEM((SU, SU), jnp.float32)],
            compiler_params=PARAMS,
            cost_estimate=pl.CostEstimate(
                flops=len(some) * 1_000_000_000,
                bytes_accessed=1_000_000,
                transcendentals=len(some) * 1_000_000,
            ),
            name="grid",
        )(joined, *some)

    grids = [grid(blocks[:1]), grid(blocks[-1:])]
    blocks, grids = lax.optimization_barrier((blocks, grids))
    fetched = local(
        functools.partial(collect_kernel, vis_rows), blocks, (facets * 4 * SU, SU), "collect"
    )
    swapped = lax.ppermute(fetched, "chan", [(c, 1 - c) for c in range(chan_count)])
    grids.append(grid(blocks[1:-1]))
    mine, other = pl.pallas_call(
        functools.partial(table_kernel, (slots, meta_row), norm),
        out_shape=[jax.ShapeDtypeStruct((half_rows, 2 * SU), jnp.float32)] * 2,
        in_specs=[VMEM] * (3 + len(grids)),
        out_specs=[VMEM, VMEM],
        scratch_shapes=[
            pltpu.VMEM((SU, 2 * SU), jnp.float32),
        ],
        compiler_params=PARAMS,
        cost_estimate=pl.CostEstimate(
            flops=1_000_000_000, bytes_accessed=2_000_000, transcendentals=0
        ),
        name="apply_tables",
    )(joined, fetched, swapped, *grids)
    summand = lax.ppermute(other, "chan", [(c, 1 - c) for c in range(chan_count)])
    return (mine + summand).reshape(1, 1, half_rows, 2, SU)


def solution(mesh):
    in_specs = (
        P(("facet", "bl"), "chan", None, None),
        P(("facet", "bl"), None, None),
        P(("facet", "bl")),
        P(("facet", "bl"), None),
        P(),
        P(),
        P(("facet", "bl"), None, None, None, None),
        P("bl", None, None),
    )
    out_specs = P("facet", "bl", "chan", None, None)
    return jax.shard_map(body, mesh=mesh, in_specs=in_specs, out_specs=out_specs, check_vma=False)
```

```python
import functools
import math

import jax
import jax.numpy as jnp
from jax import lax
from jax.experimental import pallas as pl
from jax.experimental.pallas import tpu as pltpu
from jax.sharding import PartitionSpec as P

SU = 128
CH = 8
KERNEL_SPREAD = 1.5
ALPHA = math.sqrt(math.log2(math.e) / (2.0 * KERNEL_SPREAD * KERNEL_SPREAD))
UNROLL = 4
REST = 2
NT = (((1,), (1,)), ((), ()))
VMEM = pl.BlockSpec(memory_space=pltpu.VMEM)
HBM = pl.BlockSpec(memory_space=pltpu.HBM)
PARAMS = pltpu.CompilerParams(vmem_limit_bytes=32 * 1024 * 1024)


def cos_sin(turns):
    quarter = jnp.floor(4.0 * turns + 0.5)
    angle = (2.0 * math.pi) * (turns - 0.25 * quarter)
    sq = angle * angle
    sine = angle * (
        1.0 + sq * (-1.0 / 6 + sq * (1.0 / 120 + sq * (-1.0 / 5040 + sq * (1.0 / 362880))))
    )
    cosine = 1.0 + sq * (
        -0.5 + sq * (1.0 / 24 + sq * (-1.0 / 720 + sq * (1.0 / 40320 + sq * (-1.0 / 3628800))))
    )
    turn = quarter.astype(jnp.int32) & 3
    odd = (turn & 1) == 1
    cos_out = jnp.where(odd, sine, cosine)
    sin_out = jnp.where(odd, cosine, sine)
    cos_out = jnp.where((turn == 1) | (turn == 2), -cos_out, cos_out)
    sin_out = jnp.where(turn >= 2, -sin_out, sin_out)
    return cos_out, sin_out


def split_bf16(x):
    high = x.astype(jnp.bfloat16)
    low = (x - high.astype(jnp.float32)).astype(jnp.bfloat16)
    return high, low


def three_parts(x):
    parts = []
    for _ in range(3):
        part = x.astype(jnp.bfloat16)
        x = x - part.astype(jnp.float32)
        parts.append(part.astype(jnp.float32))
    return parts


def sort_kernel(sizes, *refs):
    groups, held, chans, cap, rows = sizes
    table_hbm, outs, half = refs[7], refs[8 : 8 + groups], refs[8 + groups]
    targets = refs[9 + groups : 16 + groups]
    plane_ref, group_ref, samples_b, place_b, offsets_ref, centre_ref, gain_ref = targets
    samples, place, sorted_, filled, table_b, table_f, sems = refs[16 + groups :]
    facet = lax.axis_index("facet")
    copies = [
        pltpu.make_async_copy(source, target, sems.at[n])
        for n, (source, target) in enumerate(zip(refs[:7], targets))
    ]
    table = pltpu.make_async_copy(table_hbm.at[lax.axis_index("chan")], table_b, sems.at[7])
    for copy in copies + [table]:
        copy.start()
    sorted_[...] = jnp.zeros_like(sorted_)
    for g in range(groups):
        filled[g] = 0
    for copy in copies:
        copy.wait()
    samples[...] = samples_b[...].astype(jnp.float32)
    place[...] = place_b[...].astype(jnp.float32)
    lane = lax.broadcasted_iota(jnp.int32, (1, SU), 1)
    meta = 2 * cap * (chans + 1)
    centre = [
        part
        for axis in range(2)
        for part in three_parts(jnp.full((1, SU), centre_ref[axis, facet], jnp.float32))
    ]
    gains = three_parts(gain_ref[0])
    for g in range(groups):
        numbers = jnp.zeros((1, SU), jnp.float32)
        for axis in range(2):
            offset = offsets_ref[facet, axis, g].astype(jnp.float32)
            numbers = jnp.where(lane == axis, offset, numbers)
        for n, part in enumerate(centre):
            numbers = jnp.where(lane == 2 + n, part, numbers)
        sorted_[g, meta + 1 : meta + 2, :] = numbers
        for n, part in enumerate(gains):
            sorted_[g, meta + 2 + 2 * n : meta + 4 + 2 * n, :] = part
    for i in range(held):
        g = group_ref[0, i]
        k = filled[g]
        filled[g] = k + 1
        for part in range(2):
            at = part * cap * chans + k * chans
            sorted_[g, pl.ds(at, chans), :] = samples[pl.ds(2 * chans * i + part, chans, stride=2), :]
            at = 2 * cap * chans + part * cap + k
            sorted_[g, pl.ds(at, 1), :] = place[2 * i + part : 2 * i + part + 1, :]
        sorted_[g, meta : meta + 1, :] += jnp.where(
            lane == k, (plane_ref[0, i] + 1).astype(jnp.float32), 0.0
        )
    for shift, out_ref in enumerate(outs):
        g = lax.rem(lax.axis_index("bl") + shift, groups)
        out_ref[:rows, :] = sorted_[g].astype(jnp.bfloat16)
    table.wait()
    table_f[...] = table_b[...].astype(jnp.float32)
    for part in range(2):
        matrix = table_f[pl.ds(part, SU, stride=2), :]
        matrix = jnp.where(lax.axis_index("chan") == 0, matrix, matrix.T).astype(jnp.bfloat16)
        half[part * SU : (part + 1) * SU, :] = matrix
        outs[1][rows + part * SU : rows + (part + 1) * SU, :] = matrix


def join_kernel(rows, half, *refs):
    *pieces, joined = refs
    for n, ref in enumerate(pieces):
        joined[n * rows : (n + 1) * rows, :] = ref[:rows, :]
    at = len(pieces) * rows
    joined[at : at + 2 * SU, :] = half[...]
    joined[at + 2 * SU :, :] = pieces[1][rows:, :]


def collect_kernel(skip, *refs):
    for n, ref in enumerate(refs[:-1]):
        refs[-1][n * 4 * SU : (n + 1) * 4 * SU, :] = ref[skip:, :]


def grid_kernel(sizes, *refs):
    facets, groups, chans, cap, rows, count_here = sizes
    own_ref, grids = refs[0], refs[1 + count_here]
    order, spots_u, spots_v, turns_real, turns_imag, cells = refs[2 + count_here :]
    pieces = [
        ref.at[pl.ds(n * rows, rows)] for ref in refs[1 : 1 + count_here] for n in range(groups)
    ]
    devices = len(pieces)
    slots = 2 * facets
    lines = cap * chans
    meta_row = 2 * (lines + cap)
    tail = meta_row // 16 * 16
    facet = lax.axis_index("facet")
    group = lax.axis_index("bl")
    chan = lax.axis_index("chan")

    lane = lax.broadcasted_iota(jnp.int32, (1, SU), 1)
    own = own_ref[tail : tail + 16, :].astype(jnp.float32)
    numbers = own[meta_row - tail + 1 : meta_row - tail + 2]
    codes = []
    for d in range(devices):
        meta = pieces[d][tail : tail + 16, :].astype(jnp.float32)
        plane = meta[meta_row - tail : meta_row - tail + 1].astype(jnp.int32) - 1
        set_id = jnp.where(lax.rem(plane, groups) == group, 0, 1)
        code = (d * cap + lane) * slots + 2 * (lax.div(plane, groups) ^ facet) + set_id
        codes.append(jnp.where(plane >= 0, code, -1))
    grids[...] = jnp.zeros_like(grids)

    def number(n):
        return jnp.broadcast_to(numbers[:, n : n + 1], (lines, SU))

    offset_u = number(0)
    offset_v = number(1)
    along_l = number(2) + number(3) + number(4)
    along_m = number(5) + number(6) + number(7)
    line = lax.broadcasted_iota(jnp.int32, (lines, SU), 0)
    channel = (chan * chans + lax.rem(line, chans)).astype(jnp.float32)
    scale = 1.0 + 0.01 * (channel - 0.5 * (CH - 1))

    def spread_lines(place):
        return jnp.concatenate(
            [jnp.broadcast_to(place[k : k + 1], (chans, SU)) for k in range(cap)], axis=0
        )

    for d in range(devices):
        at = d * lines
        wide = pieces[d][...].astype(jnp.float32)
        real = wide[:lines]
        imag = wide[lines : 2 * lines]
        along_u = spread_lines(wide[2 * lines : 2 * lines + cap])
        along_v = spread_lines(wide[2 * lines + cap : 2 * (lines + cap)])
        cosine, sine = cos_sin((1.0 / SU) * (scale * (along_u * along_l + along_v * along_m)))
        spots_u[at : at + lines, :] = ALPHA * (scale * along_u - offset_u)
        spots_v[at : at + lines, :] = ALPHA * (scale * along_v - offset_v)
        turns_real[at : at + lines, :] = real * cosine - imag * sine
        turns_imag[at : at + lines, :] = real * sine + imag * cosine
    last = devices * lines
    for ref in (spots_u, spots_v, turns_real, turns_imag):
        ref[last : last + 8, :] = jnp.zeros((8, SU), jnp.float32)

    count = jnp.int32(0)
    for d in range(devices):
        for k in range(cap):
            code = codes[d][0, k]
            order[count] = code
            count = count + jnp.where(code >= 0, 1, 0)
    for i in range(UNROLL):
        order[count + i] = devices * cap * slots

    cells[...] = ALPHA * lax.broadcasted_iota(jnp.int32, (SU, SU), 0).astype(jnp.float32)

    def profile(spot):
        apart = spot - cells[...]
        return jnp.exp2(-((apart * apart).astype(jnp.bfloat16)))

    def tiled(row):
        return jnp.broadcast_to(row, (16, SU)).astype(jnp.bfloat16)[None]

    def one_block(at):
        code = order[at]
        slot = lax.rem(code, slots)
        base = lax.div(code, slots) * chans
        lefts_real, lefts_imag, rights = [], [], []
        for c in range(chans):
            here = pl.ds(base + c, 1)
            left = profile(spots_u[here, :]).reshape(SU // 16, 16, SU)
            lefts_real.append((left * tiled(turns_real[here, :])).reshape(SU, SU))
            lefts_imag.append((left * tiled(turns_imag[here, :])).reshape(SU, SU))
            rights.append(profile(spots_v[here, :]))
        left = jnp.concatenate(
            [jnp.concatenate(lefts_real, axis=1), jnp.concatenate(lefts_imag, axis=1)], axis=0
        )
        right = jnp.concatenate(rights, axis=1)
        return slot, lax.dot_general(right, left, NT, preferred_element_type=jnp.float32)

    def steps(first, blocks, number):
        def step(k, carry):
            for slot, part in [one_block(first + k * blocks + i) for i in range(blocks)]:
                grids[slot] += part
            return carry

        lax.fori_loop(0, number, step, 0)

    whole = lax.div(count, UNROLL)
    steps(0, UNROLL, whole)
    steps(whole * UNROLL, REST, lax.div(lax.rem(count, UNROLL) + REST - 1, REST))


def local(kernel, operands, shape, name):
    return pl.pallas_call(
        kernel,
        out_shape=jax.ShapeDtypeStruct(shape, jnp.bfloat16),
        in_specs=[VMEM] * len(operands),
        out_specs=VMEM,
        compiler_params=PARAMS,
        cost_estimate=pl.CostEstimate(flops=0, bytes_accessed=400_000, transcendentals=0),
        name=name,
    )(*operands)


def exchange(value, axis, shift):
    return lax.ppermute(value, axis, [(n, n ^ shift) for n in range(lax.axis_size(axis))])


def table_kernel(sizes, norm, packed, ours, theirs, *refs):
    slots, meta_row, own = sizes
    grids, out_ref = refs[:-1], refs[-1]
    first = lax.axis_index("chan") == 0
    half_rows = SU // 2

    def side(low, high):
        return jnp.where(first, low, high) if own else jnp.where(first, high, low)

    result = jnp.zeros((SU, SU), jnp.float32)
    for s in range(slots):
        at = slice(2 * SU * s, 2 * SU * (s + 1))
        fetched = ours[at, :]
        swapped = theirs[at, :]
        v_table = jnp.where(first, swapped, fetched)
        v_side = jnp.concatenate([v_table[:SU], v_table[SU:]], axis=1)
        grid = sum(ref[s] for ref in grids)
        high, low = (
            jnp.concatenate(
                [
                    part,
                    jnp.concatenate([-part[:, SU:], part[:, :SU]], axis=1),
                ],
                axis=0,
            )
            for part in split_bf16(grid)
        )
        half = jnp.dot(v_side, high, preferred_element_type=jnp.float32) + jnp.dot(
            v_side, low, preferred_element_type=jnp.float32
        )
        u_table = jnp.where(first, fetched, swapped)
        u_table = side(u_table[:, :half_rows], u_table[:, half_rows:])
        u_side = jnp.concatenate(
            [
                jnp.concatenate([u_table[:SU], u_table[SU:]], axis=1),
                jnp.concatenate([-u_table[SU:], u_table[:SU]], axis=1),
            ],
            axis=0,
        )
        high, low = split_bf16(half)
        result = (
            result
            + jnp.dot(high, u_side, preferred_element_type=jnp.float32)
            + jnp.dot(low, u_side, preferred_element_type=jnp.float32)
        )
    result = result.T
    result = jnp.concatenate([result[:half_rows], result[half_rows:]], axis=1)
    tail = meta_row // 16 * 16
    wide = packed[tail : tail + 16, :].astype(jnp.float32)
    at = meta_row - tail + 2
    gain = (wide[at : at + 2] + wide[at + 2 : at + 4]) + wide[at + 4 : at + 6]
    gain_u = jnp.broadcast_to(gain[0:1], (SU, SU)).T
    gains = side(gain_u[:half_rows], gain_u[half_rows:]) * gain[1:2] * norm
    out_ref[...] = result * jnp.concatenate([gains, gains], axis=1)


def body(
    visibilities, coords, plane_index, block_group, offsets, facet_centre, tables, antenna_gain
):
    facets = lax.axis_size("facet")
    groups = lax.axis_size("bl")
    chan_count = lax.axis_size("chan")
    held, chans = visibilities.shape[:2]
    devices = facets * groups
    slots = 2 * facets
    cap = max(2, 2 * held // groups)
    meta_row = 2 * cap * (chans + 1)
    rows = -(-(meta_row + 8) // 16) * 16
    half_rows = SU // chan_count
    norm = SU / math.sqrt(visibilities.shape[3] * held * facets * CH)

    own_table = tables.reshape(2, 2 * SU, SU)
    *pieces, half = pl.pallas_call(
        functools.partial(sort_kernel, (groups, held, chans, cap, rows)),
        out_shape=[
            jax.ShapeDtypeStruct((rows + (2 * SU if shift == 1 else 0), SU), jnp.bfloat16)
            for shift in range(groups)
        ]
        + [jax.ShapeDtypeStruct((2 * SU, SU), jnp.bfloat16)],
        in_specs=[HBM] * 8,
        out_specs=[VMEM] * (groups + 1),
        scratch_shapes=[
            pltpu.SMEM((1, held), jnp.int32),
            pltpu.SMEM((1, held), jnp.int32),
            pltpu.VMEM((held * 2 * chans, SU), jnp.bfloat16),
            pltpu.VMEM((held * 2, SU), jnp.bfloat16),
            pltpu.SMEM((facets, 2, groups), jnp.int32),
            pltpu.SMEM((2, facets), jnp.float32),
            pltpu.VMEM((1, 2, SU), jnp.float32),
            pltpu.VMEM((held * 2 * chans, SU), jnp.float32),
            pltpu.VMEM((held * 2, SU), jnp.float32),
            pltpu.VMEM((groups, rows, SU), jnp.float32),
            pltpu.SMEM((groups,), jnp.int32),
            pltpu.VMEM((2 * SU, SU), jnp.bfloat16),
            pltpu.VMEM((2 * SU, SU), jnp.float32),
            pltpu.SemaphoreType.DMA((8,)),
        ],
        compiler_params=PARAMS,
        cost_estimate=pl.CostEstimate(flops=100_000, bytes_accessed=100_000, transcendentals=0),
        name="sort_blocks",
    )(
        *(
            pltpu.with_memory_space_constraint(operand, pltpu.HBM)
            for operand in (
                plane_index.reshape(1, held),
                block_group.T,
                visibilities.reshape(held * 2 * chans, SU),
                coords.reshape(held * 2, SU),
                offsets.transpose(0, 2, 1),
                facet_centre.T,
                antenna_gain,
                own_table,
            )
        )
    )
    arrived = [
        lax.ppermute(pieces[shift], "bl", [(g, (g + shift) % groups) for g in range(groups)])
        for shift in [1, *range(groups - 1, 1, -1)]
    ]
    vis_rows = groups * rows
    joined = local(
        functools.partial(join_kernel, rows),
        [half, pieces[0], *arrived],
        (vis_rows + 4 * SU, SU),
        "join",
    )
    blocks = [joined] + [exchange(joined, "facet", shift) for shift in range(1, facets)]
    def grid(some):
        lines = len(some) * groups * cap
        return pl.pallas_call(
            functools.partial(grid_kernel, (facets, groups, chans, cap, rows, len(some))),
            out_shape=jax.ShapeDtypeStruct((slots, SU, 2 * SU), jnp.float32),
            in_specs=[VMEM] * (1 + len(some)),
            out_specs=VMEM,
            scratch_shapes=[
                pltpu.SMEM((lines + UNROLL,), jnp.int32),
            ]
            + [pltpu.VMEM((lines * chans + 8, SU), jnp.float32)] * 4
            + [pltpu.VMEM((SU, SU), jnp.float32)],
            compiler_params=PARAMS,
            cost_estimate=pl.CostEstimate(
                flops=len(some) * 1_000_000_000,
                bytes_accessed=1_000_000,
                transcendentals=len(some) * 1_000_000,
            ),
            name="grid",
        )(joined, *some)

    grids = [grid(blocks[:1]), grid(blocks[-1:])]
    blocks, grids = lax.optimization_barrier((blocks, grids))
    fetched = local(
        functools.partial(collect_kernel, vis_rows), blocks, (facets * 4 * SU, SU), "collect"
    )
    swapped = lax.ppermute(fetched, "chan", [(c, 1 - c) for c in range(chan_count)])
    grids.append(grid(blocks[1:-1]))
    def apply(own):
        return pl.pallas_call(
            functools.partial(table_kernel, (slots, meta_row, own), norm),
            out_shape=jax.ShapeDtypeStruct((half_rows, 2 * SU), jnp.float32),
            in_specs=[VMEM] * (3 + len(grids)),
            out_specs=VMEM,
            compiler_params=PARAMS,
            cost_estimate=pl.CostEstimate(
                flops=1_000_000_000, bytes_accessed=2_000_000, transcendentals=0
            ),
            name="apply_tables",
        )(joined, fetched, swapped, *grids)

    other = apply(False)
    summand = lax.ppermute(other, "chan", [(c, 1 - c) for c in range(chan_count)])
    mine = apply(True)
    return (mine + summand).reshape(1, 1, half_rows, 2, SU)


def solution(mesh):
    in_specs = (
        P(("facet", "bl"), "chan", None, None),
        P(("facet", "bl"), None, None),
        P(("facet", "bl")),
        P(("facet", "bl"), None),
        P(),
        P(),
        P(("facet", "bl"), None, None, None, None),
        P("bl", None, None),
    )
    out_specs = P("facet", "bl", "chan", None, None)
    return jax.shard_map(body, mesh=mesh, in_specs=in_specs, out_specs=out_specs, check_vma=False)
```

```python
import functools
import math

import jax
import jax.numpy as jnp
from jax import lax
from jax.experimental import pallas as pl
from jax.experimental.pallas import tpu as pltpu
from jax.sharding import PartitionSpec as P

SU = 128
CH = 8
KERNEL_SPREAD = 1.5
ALPHA = math.sqrt(math.log2(math.e) / (2.0 * KERNEL_SPREAD * KERNEL_SPREAD))
UNROLL = 4
REST = 2
NT = (((1,), (1,)), ((), ()))
VMEM = pl.BlockSpec(memory_space=pltpu.VMEM)
HBM = pl.BlockSpec(memory_space=pltpu.HBM)
PARAMS = pltpu.CompilerParams(vmem_limit_bytes=32 * 1024 * 1024)


def cos_sin(turns):
    quarter = jnp.floor(4.0 * turns + 0.5)
    angle = (2.0 * math.pi) * (turns - 0.25 * quarter)
    sq = angle * angle
    sine = angle * (
        1.0 + sq * (-1.0 / 6 + sq * (1.0 / 120 + sq * (-1.0 / 5040 + sq * (1.0 / 362880))))
    )
    cosine = 1.0 + sq * (
        -0.5 + sq * (1.0 / 24 + sq * (-1.0 / 720 + sq * (1.0 / 40320 + sq * (-1.0 / 3628800))))
    )
    turn = quarter.astype(jnp.int32) & 3
    odd = (turn & 1) == 1
    cos_out = jnp.where(odd, sine, cosine)
    sin_out = jnp.where(odd, cosine, sine)
    cos_out = jnp.where((turn == 1) | (turn == 2), -cos_out, cos_out)
    sin_out = jnp.where(turn >= 2, -sin_out, sin_out)
    return cos_out, sin_out


def split_bf16(x):
    high = x.astype(jnp.bfloat16)
    low = (x - high.astype(jnp.float32)).astype(jnp.bfloat16)
    return high, low


def three_parts(x):
    parts = []
    for _ in range(3):
        part = x.astype(jnp.bfloat16)
        x = x - part.astype(jnp.float32)
        parts.append(part.astype(jnp.float32))
    return parts


def sort_kernel(sizes, *refs):
    groups, held, chans, cap, rows = sizes
    table_hbm, outs, half = refs[7], refs[8 : 8 + groups], refs[8 + groups]
    targets = refs[9 + groups : 16 + groups]
    plane_ref, group_ref, samples_b, place_b, offsets_ref, centre_ref, gain_ref = targets
    samples, place, sorted_, filled, table_b, table_f, sems = refs[16 + groups :]
    facet = lax.axis_index("facet")
    copies = [
        pltpu.make_async_copy(source, target, sems.at[n])
        for n, (source, target) in enumerate(zip(refs[:7], targets))
    ]
    table = pltpu.make_async_copy(table_hbm.at[lax.axis_index("chan")], table_b, sems.at[7])
    for copy in copies + [table]:
        copy.start()
    sorted_[...] = jnp.zeros_like(sorted_)
    for g in range(groups):
        filled[g] = 0
    for copy in copies:
        copy.wait()
    samples[...] = samples_b[...].astype(jnp.float32)
    place[...] = place_b[...].astype(jnp.float32)
    lane = lax.broadcasted_iota(jnp.int32, (1, SU), 1)
    meta = 2 * cap * (chans + 1)
    centre = [
        part
        for axis in range(2)
        for part in three_parts(jnp.full((1, SU), centre_ref[axis, facet], jnp.float32))
    ]
    gains = three_parts(gain_ref[0])
    for g in range(groups):
        numbers = jnp.zeros((1, SU), jnp.float32)
        for axis in range(2):
            offset = offsets_ref[facet, axis, g].astype(jnp.float32)
            numbers = jnp.where(lane == axis, offset, numbers)
        for n, part in enumerate(centre):
            numbers = jnp.where(lane == 2 + n, part, numbers)
        sorted_[g, meta + 1 : meta + 2, :] = numbers
        for n, part in enumerate(gains):
            sorted_[g, meta + 2 + 2 * n : meta + 4 + 2 * n, :] = part
    for i in range(held):
        g = group_ref[0, i]
        k = filled[g]
        filled[g] = k + 1
        for part in range(2):
            at = part * cap * chans + k * chans
            sorted_[g, pl.ds(at, chans), :] = samples[pl.ds(2 * chans * i + part, chans, stride=2), :]
            at = 2 * cap * chans + part * cap + k
            sorted_[g, pl.ds(at, 1), :] = place[2 * i + part : 2 * i + part + 1, :]
        sorted_[g, meta : meta + 1, :] += jnp.where(
            lane == k, (plane_ref[0, i] + 1).astype(jnp.float32), 0.0
        )
    for shift, out_ref in enumerate(outs):
        g = lax.rem(lax.axis_index("bl") + shift, groups)
        out_ref[:rows, :] = sorted_[g].astype(jnp.bfloat16)
    table.wait()
    table_f[...] = table_b[...].astype(jnp.float32)

    def put(turned):
        for part in range(2):
            matrix = table_f[pl.ds(part, SU, stride=2), :]
            matrix = (matrix.T if turned else matrix).astype(jnp.bfloat16)
            half[part * SU : (part + 1) * SU, :] = matrix
            outs[1][rows + part * SU : rows + (part + 1) * SU, :] = matrix

    @pl.when(lax.axis_index("chan") == 0)
    def _():
        put(False)

    @pl.when(lax.axis_index("chan") != 0)
    def _():
        put(True)


def join_kernel(rows, half, *refs):
    *pieces, joined = refs
    for n, ref in enumerate(pieces):
        joined[n * rows : (n + 1) * rows, :] = ref[:rows, :]
    at = len(pieces) * rows
    joined[at : at + 2 * SU, :] = half[...]
    joined[at + 2 * SU :, :] = pieces[1][rows:, :]


def collect_kernel(skip, *refs):
    for n, ref in enumerate(refs[:-1]):
        refs[-1][n * 4 * SU : (n + 1) * 4 * SU, :] = ref[skip:, :]


def grid_kernel(sizes, *refs):
    facets, groups, chans, cap, rows, count_here = sizes
    own_ref, grids = refs[0], refs[1 + count_here]
    order, spots_u, spots_v, turns_real, turns_imag, cells = refs[2 + count_here :]
    pieces = [
        ref.at[pl.ds(n * rows, rows)] for ref in refs[1 : 1 + count_here] for n in range(groups)
    ]
    devices = len(pieces)
    slots = 2 * facets
    lines = cap * chans
    meta_row = 2 * (lines + cap)
    tail = meta_row // 16 * 16
    facet = lax.axis_index("facet")
    group = lax.axis_index("bl")
    chan = lax.axis_index("chan")

    lane = lax.broadcasted_iota(jnp.int32, (1, SU), 1)
    own = own_ref[tail : tail + 16, :].astype(jnp.float32)
    numbers = own[meta_row - tail + 1 : meta_row - tail + 2]
    codes = []
    for d in range(devices):
        meta = pieces[d][tail : tail + 16, :].astype(jnp.float32)
        plane = meta[meta_row - tail : meta_row - tail + 1].astype(jnp.int32) - 1
        set_id = jnp.where(lax.rem(plane, groups) == group, 0, 1)
        code = (d * cap + lane) * slots + 2 * (lax.div(plane, groups) ^ facet) + set_id
        codes.append(jnp.where(plane >= 0, code, -1))
    grids[...] = jnp.zeros_like(grids)

    def number(n):
        return jnp.broadcast_to(numbers[:, n : n + 1], (lines, SU))

    offset_u = number(0)
    offset_v = number(1)
    along_l = number(2) + number(3) + number(4)
    along_m = number(5) + number(6) + number(7)
    line = lax.broadcasted_iota(jnp.int32, (lines, SU), 0)
    channel = (chan * chans + lax.rem(line, chans)).astype(jnp.float32)
    scale = 1.0 + 0.01 * (channel - 0.5 * (CH - 1))

    def spread_lines(place):
        return jnp.concatenate(
            [jnp.broadcast_to(place[k : k + 1], (chans, SU)) for k in range(cap)], axis=0
        )

    for d in range(devices):
        at = d * lines
        wide = pieces[d][...].astype(jnp.float32)
        real = wide[:lines]
        imag = wide[lines : 2 * lines]
        along_u = spread_lines(wide[2 * lines : 2 * lines + cap])
        along_v = spread_lines(wide[2 * lines + cap : 2 * (lines + cap)])
        cosine, sine = cos_sin((1.0 / SU) * (scale * (along_u * along_l + along_v * along_m)))
        spots_u[at : at + lines, :] = ALPHA * (scale * along_u - offset_u)
        spots_v[at : at + lines, :] = ALPHA * (scale * along_v - offset_v)
        turns_real[at : at + lines, :] = real * cosine - imag * sine
        turns_imag[at : at + lines, :] = real * sine + imag * cosine
    last = devices * lines
    for ref in (spots_u, spots_v, turns_real, turns_imag):
        ref[last : last + 8, :] = jnp.zeros((8, SU), jnp.float32)

    count = jnp.int32(0)
    for d in range(devices):
        for k in range(cap):
            code = codes[d][0, k]
            order[count] = code
            count = count + jnp.where(code >= 0, 1, 0)
    for i in range(UNROLL):
        order[count + i] = devices * cap * slots

    cells[...] = ALPHA * lax.broadcasted_iota(jnp.int32, (SU, SU), 0).astype(jnp.float32)

    def profile(spot):
        apart = spot - cells[...]
        return jnp.exp2(-((apart * apart).astype(jnp.bfloat16)))

    def tiled(row):
        return jnp.broadcast_to(row, (16, SU)).astype(jnp.bfloat16)[None]

    def one_block(at):
        code = order[at]
        slot = lax.rem(code, slots)
        base = lax.div(code, slots) * chans
        lefts_real, lefts_imag, rights = [], [], []
        for c in range(chans):
            here = pl.ds(base + c, 1)
            left = profile(spots_u[here, :]).reshape(SU // 16, 16, SU)
            lefts_real.append((left * tiled(turns_real[here, :])).reshape(SU, SU))
            lefts_imag.append((left * tiled(turns_imag[here, :])).reshape(SU, SU))
            rights.append(profile(spots_v[here, :]))
        left = jnp.concatenate(
            [jnp.concatenate(lefts_real, axis=1), jnp.concatenate(lefts_imag, axis=1)], axis=0
        )
        right = jnp.concatenate(rights, axis=1)
        return slot, lax.dot_general(right, left, NT, preferred_element_type=jnp.float32)

    def steps(first, blocks, number):
        def step(k, carry):
            for slot, part in [one_block(first + k * blocks + i) for i in range(blocks)]:
                grids[slot] += part
            return carry

        lax.fori_loop(0, number, step, 0)

    whole = lax.div(count, UNROLL)
    steps(0, UNROLL, whole)
    steps(whole * UNROLL, REST, lax.div(lax.rem(count, UNROLL) + REST - 1, REST))


def local(kernel, operands, shape, name):
    return pl.pallas_call(
        kernel,
        out_shape=jax.ShapeDtypeStruct(shape, jnp.bfloat16),
        in_specs=[VMEM] * len(operands),
        out_specs=VMEM,
        compiler_params=PARAMS,
        cost_estimate=pl.CostEstimate(flops=0, bytes_accessed=400_000, transcendentals=0),
        name=name,
    )(*operands)


def exchange(value, axis, shift):
    return lax.ppermute(value, axis, [(n, n ^ shift) for n in range(lax.axis_size(axis))])


def table_kernel(sizes, norm, packed, ours, theirs, *refs):
    slots, meta_row = sizes
    grids, (mine_ref, other_ref, total) = refs[:-3], refs[-3:]
    chan = lax.axis_index("chan")
    first = chan == 0

    result = jnp.zeros((SU, 2 * SU), jnp.float32)
    for s in range(slots):
        at = slice(2 * SU * s, 2 * SU * (s + 1))
        fetched = ours[at, :]
        swapped = theirs[at, :]
        v_table = jnp.where(first, swapped, fetched)
        v_side = jnp.concatenate([v_table[:SU], v_table[SU:]], axis=1)
        grid = sum(ref[s] for ref in grids)
        high, low = (
            jnp.concatenate(
                [
                    part,
                    jnp.concatenate([-part[:, SU:], part[:, :SU]], axis=1),
                ],
                axis=0,
            )
            for part in split_bf16(grid)
        )
        half = jnp.dot(v_side, high, preferred_element_type=jnp.float32) + jnp.dot(
            v_side, low, preferred_element_type=jnp.float32
        )
        u_table = jnp.where(first, fetched, swapped)
        u_side = jnp.concatenate(
            [
                jnp.concatenate([u_table[:SU], u_table[SU:]], axis=1),
                jnp.concatenate([-u_table[SU:], u_table[:SU]], axis=1),
            ],
            axis=0,
        )
        high, low = split_bf16(half)
        result = (
            result
            + jnp.dot(high, u_side, preferred_element_type=jnp.float32)
            + jnp.dot(low, u_side, preferred_element_type=jnp.float32)
        )
    result = jnp.concatenate([result[:, :SU].T, result[:, SU:].T], axis=1)
    tail = meta_row // 16 * 16
    wide = packed[tail : tail + 16, :].astype(jnp.float32)
    at = meta_row - tail + 2
    gain = (wide[at : at + 2] + wide[at + 2 : at + 4]) + wide[at + 4 : at + 6]
    gain_u = jnp.broadcast_to(gain[0:1], (SU, SU)).T
    gains = gain_u * gain[1:2] * norm
    total[...] = result * jnp.concatenate([gains, gains], axis=1)
    half_rows = mine_ref.shape[0]
    mine_ref[...] = total[pl.ds(pl.multiple_of(chan * half_rows, half_rows), half_rows), :]
    other_ref[...] = total[pl.ds(pl.multiple_of((1 - chan) * half_rows, half_rows), half_rows), :]


def body(
    visibilities, coords, plane_index, block_group, offsets, facet_centre, tables, antenna_gain
):
    facets = lax.axis_size("facet")
    groups = lax.axis_size("bl")
    chan_count = lax.axis_size("chan")
    held, chans = visibilities.shape[:2]
    devices = facets * groups
    slots = 2 * facets
    cap = max(2, 2 * held // groups)
    meta_row = 2 * cap * (chans + 1)
    rows = -(-(meta_row + 8) // 16) * 16
    half_rows = SU // chan_count
    norm = SU / math.sqrt(visibilities.shape[3] * held * facets * CH)

    own_table = tables.reshape(2, 2 * SU, SU)
    *pieces, half = pl.pallas_call(
        functools.partial(sort_kernel, (groups, held, chans, cap, rows)),
        out_shape=[
            jax.ShapeDtypeStruct((rows + (2 * SU if shift == 1 else 0), SU), jnp.bfloat16)
            for shift in range(groups)
        ]
        + [jax.ShapeDtypeStruct((2 * SU, SU), jnp.bfloat16)],
        in_specs=[HBM] * 8,
        out_specs=[VMEM] * (groups + 1),
        scratch_shapes=[
            pltpu.SMEM((1, held), jnp.int32),
            pltpu.SMEM((1, held), jnp.int32),
            pltpu.VMEM((held * 2 * chans, SU), jnp.bfloat16),
            pltpu.VMEM((held * 2, SU), jnp.bfloat16),
            pltpu.SMEM((facets, 2, groups), jnp.int32),
            pltpu.SMEM((2, facets), jnp.float32),
            pltpu.VMEM((1, 2, SU), jnp.float32),
            pltpu.VMEM((held * 2 * chans, SU), jnp.float32),
            pltpu.VMEM((held * 2, SU), jnp.float32),
            pltpu.VMEM((groups, rows, SU), jnp.float32),
            pltpu.SMEM((groups,), jnp.int32),
            pltpu.VMEM((2 * SU, SU), jnp.bfloat16),
            pltpu.VMEM((2 * SU, SU), jnp.float32),
            pltpu.SemaphoreType.DMA((8,)),
        ],
        compiler_params=PARAMS,
        cost_estimate=pl.CostEstimate(flops=100_000, bytes_accessed=100_000, transcendentals=0),
        name="sort_blocks",
    )(
        *(
            pltpu.with_memory_space_constraint(operand, pltpu.HBM)
            for operand in (
                plane_index.reshape(1, held),
                block_group.T,
                visibilities.reshape(held * 2 * chans, SU),
                coords.reshape(held * 2, SU),
                offsets.transpose(0, 2, 1),
                facet_centre.T,
                antenna_gain,
                own_table,
            )
        )
    )
    arrived = [
        lax.ppermute(pieces[shift], "bl", [(g, (g + shift) % groups) for g in range(groups)])
        for shift in [1, *range(groups - 1, 1, -1)]
    ]
    vis_rows = groups * rows
    joined = local(
        functools.partial(join_kernel, rows),
        [half, pieces[0], *arrived],
        (vis_rows + 4 * SU, SU),
        "join",
    )
    blocks = [joined] + [exchange(joined, "facet", shift) for shift in range(1, facets)]
    def grid(some):
        lines = len(some) * groups * cap
        return pl.pallas_call(
            functools.partial(grid_kernel, (facets, groups, chans, cap, rows, len(some))),
            out_shape=jax.ShapeDtypeStruct((slots, SU, 2 * SU), jnp.float32),
            in_specs=[VMEM] * (1 + len(some)),
            out_specs=VMEM,
            scratch_shapes=[
                pltpu.SMEM((lines + UNROLL,), jnp.int32),
            ]
            + [pltpu.VMEM((lines * chans + 8, SU), jnp.float32)] * 4
            + [pltpu.VMEM((SU, SU), jnp.float32)],
            compiler_params=PARAMS,
            cost_estimate=pl.CostEstimate(
                flops=len(some) * 1_000_000_000,
                bytes_accessed=1_000_000,
                transcendentals=len(some) * 1_000_000,
            ),
            name="grid",
        )(joined, *some)

    grids = [grid(blocks[:1]), grid(blocks[-1:])]
    blocks, grids = lax.optimization_barrier((blocks, grids))
    fetched = local(
        functools.partial(collect_kernel, vis_rows), blocks, (facets * 4 * SU, SU), "collect"
    )
    swapped = lax.ppermute(fetched, "chan", [(c, 1 - c) for c in range(chan_count)])
    grids.append(grid(blocks[1:-1]))
    mine, other = pl.pallas_call(
        functools.partial(table_kernel, (slots, meta_row), norm),
        out_shape=[jax.ShapeDtypeStruct((half_rows, 2 * SU), jnp.float32)] * 2,
        in_specs=[VMEM] * (3 + len(grids)),
        out_specs=[VMEM, VMEM],
        scratch_shapes=[
            pltpu.VMEM((SU, 2 * SU), jnp.float32),
        ],
        compiler_params=PARAMS,
        cost_estimate=pl.CostEstimate(
            flops=1_000_000_000, bytes_accessed=2_000_000, transcendentals=0
        ),
        name="apply_tables",
    )(joined, fetched, swapped, *grids)
    summand = lax.ppermute(other, "chan", [(c, 1 - c) for c in range(chan_count)])
    return (mine + summand).reshape(1, 1, half_rows, 2, SU)


def solution(mesh):
    in_specs = (
        P(("facet", "bl"), "chan", None, None),
        P(("facet", "bl"), None, None),
        P(("facet", "bl")),
        P(("facet", "bl"), None),
        P(),
        P(),
        P(("facet", "bl"), None, None, None, None),
        P("bl", None, None),
    )
    out_specs = P("facet", "bl", "chan", None, None)
    return jax.shard_map(body, mesh=mesh, in_specs=in_specs, out_specs=out_specs, check_vma=False)
```
